32 devices in a mesh: dp: 4 (over y, x), blk: 8 (over z, core).
Axes of the slice: x: 2, y: 2, z: 4, core: 2. Of those that a mesh axis runs over, the one named last changes fastest.
Arguments:
- tokens: bfloat16 [8, 512, 1024], P('dp', 'blk'), may hold values from -6 to 6
- doc_ids: int32 [8, 512], P('dp', 'blk'), may hold values from 0 to 7, as said below
- w_query: float32 [1024, 1024], P(('dp', 'blk')), may hold values from -0.1875 to 0.1875
- w_key: float32 [1024, 1024], P(('dp', 'blk')), may hold values from -0.1875 to 0.1875
- w_value: float32 [1024, 1024], P(('dp', 'blk')), may hold values from -0.1875 to 0.1875
- w_out: float32 [1024, 1024], P(('dp', 'blk')), may hold values from -0.1875 to 0.1875
- w_up: float32 [1024, 4096], P(('dp', 'blk')), may hold values from -0.1875 to 0.1875
- w_gate: float32 [1024, 4096], P(('dp', 'blk')), may hold values from -0.1875 to 0.1875
- w_down: float32 [4096, 1024], P(('dp', 'blk')), may hold values from -0.09375 to 0.09375
- s_qk: float32 [1024], replicated, may hold values from 1 to 2
- alpha_attn: float32 [1024], replicated, may hold values from 0.2 to 0.8
- s_up: float32 [4096], replicated, may hold values from 0.5 to 2
- s_gate: float32 [4096], replicated, may hold values from 0.5 to 2
- alpha_mlp: float32 [1024], replicated, may hold values from 0.2 to 0.8
- cotangent: bfloat16 [8, 512, 1024], P('dp', 'blk'), may hold values from -6 to 6
Outputs:
- hidden_out: bfloat16 [8, 512, 1024], P('dp', 'blk')
- tokens_grad: float32 [8, 512, 1024], P('dp', 'blk')
- g_query: float32 [1024, 1024], P(('dp', 'blk'))
- g_key: float32 [1024, 1024], P(('dp', 'blk'))
- g_value: float32 [1024, 1024], P(('dp', 'blk'))
- g_out: float32 [1024, 1024], P(('dp', 'blk'))
- g_up: float32 [1024, 4096], P(('dp', 'blk'))
- g_gate: float32 [1024, 4096], P(('dp', 'blk'))
- g_down: float32 [4096, 1024], P(('dp', 'blk'))
- g_sqk: float32 [1024], P(('dp', 'blk'))
- g_alpha_attn: float32 [1024], P(('dp', 'blk'))
- g_s_up: float32 [4096], P(('dp', 'blk'))
- g_s_gate: float32 [4096], P(('dp', 'blk'))
- g_alpha_mlp: float32 [1024], P(('dp', 'blk'))
The draws below stay inside these ranges and needn't reach their ends.
Inputs may be any that keep to these rules, and one draw needn't show every extreme that they name: `doc_ids`: along each row the ids never fall, and every id from 0 to 7 occurs in every row.
All inputs are finite; a program needn't handle non-finite values.
Results may differ from the reference program's by a relative error of at most 0.03.
Values may be sent and summed in bfloat16 or wider, within the bound.
No kernel may reach another device: no remote copies, remote signals or barrier semaphores. Data moves between devices by JAX's collectives and lax.ppermute only.
A program may use at most 320 MiB of HBM per device.

```python
import math
import jax
import jax.numpy as jnp
from jax import lax

D = 1024
HEADS = 16
HEAD_DIM = 64
FF = 4096
SEG_DEV = 64
SEQS = 2
NDOC = 8
ROWS = 8
LEN = 512


def draw_doc_ids(key, part):
    key = jax.random.fold_in(key, 17)
    row_keys = jax.random.split(jax.random.fold_in(key, 1), ROWS)
    crossing_keys = jax.random.split(jax.random.fold_in(key, 2), ROWS)
    chosen = jax.random.randint(jax.random.fold_in(key, 3), (ROWS // SEQS,), 0, SEQS)
    crossing_rows = jnp.arange(ROWS) % SEQS == jnp.repeat(chosen, SEQS)

    def drawn_bounds(row_key):
        return jax.random.permutation(row_key, LEN - 1)[:NDOC - 1] + 1

    def crossing_bounds(row_key):
        selected = jax.random.permutation(row_key, SEG_DEV - 1)[:NDOC - 1] + 1
        return jnp.where(selected < SEG_DEV // 2, selected, selected + LEN - SEG_DEV)
    drawn = jax.vmap(drawn_bounds)(row_keys)
    crossing = jax.vmap(crossing_bounds)(crossing_keys)
    boundaries = jnp.where(crossing_rows[:, None], crossing, drawn)
    position = jnp.arange(LEN)
    above = (position[None, :, None] >= boundaries[:, None, :]).astype(jnp.int32)
    return jnp.sum(above, axis=2).astype(jnp.int32)


def block_levels(own_key, extent, shards, least, high):
    gain = 1.0
    for axis_at, blocks in shards:
        draws = jax.random.uniform(jax.random.fold_in(jax.random.fold_in(own_key, 6), axis_at), (blocks,), jnp.float32, least / len(shards), high / len(shards))
        gain = gain * jnp.repeat(jnp.exp(draws), extent[axis_at] // blocks).reshape((-1,) + (1,) * (len(extent) - 1 - axis_at))
    return gain


def scatter_about(stream_key, shape, width, reach, cuts=(), kind=jnp.bfloat16):
    values = width * jax.random.normal(stream_key, shape, jnp.float32)
    if cuts:
        values = values * block_levels(stream_key, shape, cuts, -0.22, 0.18)
    return jnp.clip(values, -reach, reach).astype(kind)


def setup_inputs(seed: int = 0) -> dict:
    arg_keys = jax.random.split(jax.random.key(seed), 16)
    return {
        "tokens": scatter_about(arg_keys[0], (ROWS, LEN, D), 1.0, 6.0, ((0, 4), (1, 8))),
        "doc_ids": draw_doc_ids(jax.random.fold_in(arg_keys[15], 71), 0),
        "w_query": scatter_about(arg_keys[2], (D, D), D ** -0.5, 0.1875, ((0, 32),), jnp.float32),
        "w_key": scatter_about(arg_keys[3], (D, D), D ** -0.5, 0.1875, ((0, 32),), jnp.float32),
        "w_value": scatter_about(arg_keys[4], (D, D), D ** -0.5, 0.1875, ((0, 32),), jnp.float32),
        "w_out": scatter_about(arg_keys[5], (D, D), D ** -0.5, 0.1875, ((0, 32),), jnp.float32),
        "w_up": scatter_about(arg_keys[6], (D, FF), D ** -0.5, 0.1875, ((0, 32),), jnp.float32),
        "w_gate": scatter_about(arg_keys[7], (D, FF), D ** -0.5, 0.1875, ((0, 32),), jnp.float32),
        "w_down": scatter_about(arg_keys[8], (FF, D), FF ** -0.5, 0.09375, ((0, 32),), jnp.float32),
        "s_qk": jnp.clip(jnp.exp(jax.random.uniform(arg_keys[9], (D,), jnp.float32, math.log(1.0), math.log(2.0))), 1.0, 2.0),
        "alpha_attn": jnp.clip(jnp.exp(jax.random.uniform(arg_keys[10], (D,), jnp.float32, math.log(0.2), math.log(0.8))), 0.2, 0.8),
        "s_up": jnp.clip(jnp.exp(jax.random.uniform(arg_keys[11], (FF,), jnp.float32, math.log(0.5), math.log(2.0))), 0.5, 2.0),
        "s_gate": jnp.clip(jnp.exp(jax.random.uniform(arg_keys[12], (FF,), jnp.float32, math.log(0.5), math.log(2.0))), 0.5, 2.0),
        "alpha_mlp": jnp.clip(jnp.exp(jax.random.uniform(arg_keys[13], (D,), jnp.float32, math.log(0.2), math.log(0.8))), 0.2, 0.8),
        "cotangent": scatter_about(arg_keys[14], (ROWS, LEN, D), 1.0, 6.0, ((0, 4), (1, 8))),
    }


@jax.custom_vjp
def low(v):
    return lax.optimization_barrier(v.astype(jnp.bfloat16)).astype(jnp.float32)

@jax.custom_vjp
def low_back(v):
    return v

def low_keep(v):
    return (low(v), None)

def low_pass(kept, grad):
    return (grad,)

def back_keep(v):
    return (v, None)

def back_low(kept, grad):
    return (low(grad),)
low.defvjp(low_keep, low_pass)
low_back.defvjp(back_keep, back_low)
epsilon = 1e-06

def highest(left, right):
    return jnp.dot(left, right, precision=lax.Precision.HIGHEST)

def rotate(tensor, cosines, sines):
    half_dim = tensor.shape[-1] // 2
    front = tensor[..., :half_dim]
    behind = tensor[..., half_dim:]
    return jnp.concatenate([front * cosines - behind * sines, behind * cosines + front * sines], axis=-1)

def sphere(tensor):
    return tensor * lax.rsqrt(lax.optimization_barrier(jnp.mean(tensor * tensor, axis=-1, keepdims=True)) + epsilon)

def head_unit(tensor, gains):
    return gains * tensor * lax.rsqrt(lax.optimization_barrier(jnp.sum(tensor * tensor, axis=-1, keepdims=True)) + epsilon)

def rope_tables(positions):
    frequency = 10000.0 ** (-jnp.arange(HEAD_DIM // 2, dtype=jnp.float32) / (HEAD_DIM // 2))
    angles = positions.astype(jnp.float32)[..., None] * frequency
    return (jnp.cos(angles)[..., None, :], jnp.sin(angles)[..., None, :])

def layer_row(params, token_row, positions, starts):
    w_query, w_key, w_value, w_out, w_up, w_gate, w_down, s_qk, alpha_attn, s_up, s_gate, alpha_mlp = params
    length = token_row.shape[0]
    cosines, sines = rope_tables(positions)
    head_gains = s_qk.reshape(HEADS, HEAD_DIM)
    q_pre = low_back(highest(token_row, low(w_query)))
    k_pre = low_back(highest(token_row, low(w_key)))
    v_pre = low_back(highest(token_row, low(w_value)))
    q_unit = low(head_unit(rotate(q_pre.reshape(length, HEADS, HEAD_DIM), cosines, sines), head_gains))
    k_unit = low(head_unit(rotate(k_pre.reshape(length, HEADS, HEAD_DIM), cosines, sines), head_gains))
    v_low = low(v_pre).reshape(length, HEADS, HEAD_DIM)
    block_rows = min(512, length)
    key_index = jnp.arange(length, dtype=jnp.int32)
    score_scale = math.sqrt(HEAD_DIM)

    def attend(block_args):
        queries, query_index, query_start = block_args
        scores = low_back(score_scale * jnp.einsum('qhd,khd->hqk', queries, k_unit, precision=lax.Precision.HIGHEST))
        allowed = (key_index[None, :] <= query_index[:, None]) & (key_index[None, :] >= query_start[:, None])
        scores = jnp.where(allowed[None], scores, -1e+30)
        weights_low = low(jax.nn.softmax(scores, axis=-1))
        return jnp.einsum('hqk,khd->qhd', weights_low, v_low, precision=lax.Precision.HIGHEST)
    blocks = length // block_rows
    attended = lax.map(jax.checkpoint(attend), (q_unit.reshape(blocks, block_rows, HEADS, HEAD_DIM), key_index.reshape(blocks, block_rows), starts.reshape(blocks, block_rows)))
    attended = low(low_back(attended.reshape(length, HEADS * HEAD_DIM)))
    h_attn = low_back(highest(attended, low(w_out)))
    h_one = sphere(token_row + alpha_attn * (sphere(h_attn) - token_row))
    h_low = low(h_one)
    up_proj = low_back(highest(h_low, low(w_up)))
    gate_proj = low_back(highest(h_low, low(w_gate)))
    mixed = low(low_back(s_up * up_proj * jax.nn.silu(s_gate * gate_proj)))
    h_mlp = low_back(highest(mixed, low(w_down)))
    return sphere(h_one + alpha_mlp * (sphere(h_mlp) - h_one))

def reference(tokens, doc_ids, w_query, w_key, w_value, w_out, w_up, w_gate, w_down, s_qk, alpha_attn, s_up, s_gate, alpha_mlp, cotangent):
    params = (w_query, w_key, w_value, w_out, w_up, w_gate, w_down, s_qk, alpha_attn, s_up, s_gate, alpha_mlp)

    def one_row(sums_so_far, row_args):
        token_row, doc_row, cot_row = row_args
        onehot_docs = (doc_row[:, None] == jnp.arange(NDOC, dtype=jnp.int32)[None, :]).astype(jnp.int32)
        doc_counts = lax.optimization_barrier(jnp.sum(onehot_docs, axis=0)).astype(jnp.int32)
        doc_firsts = (jnp.cumsum(doc_counts) - doc_counts).astype(jnp.int32)
        starts = lax.optimization_barrier(jnp.sum(onehot_docs * doc_firsts[None, :], axis=1)).astype(jnp.int32)
        positions = (jnp.arange(LEN, dtype=jnp.int32) - starts).astype(jnp.int32)

        def forward(layer_params, row_in):
            return layer_row(layer_params, row_in, positions, starts)
        result, pullback = jax.vjp(forward, params, token_row.astype(jnp.float32))
        param_grads, row_grad = pullback(cot_row.astype(jnp.float32))
        sums_so_far = jax.tree.map(lambda older, newer: older + newer, sums_so_far, param_grads)
        return (sums_so_far, (result.astype(jnp.bfloat16), row_grad))
    zero_grads = jax.tree.map(jnp.zeros_like, params)
    grad_sums, (hidden_out, tokens_grad) = lax.scan(one_row, zero_grads, (tokens, doc_ids, cotangent))
    return (hidden_out, tokens_grad, grad_sums[0], grad_sums[1], grad_sums[2], grad_sums[3], grad_sums[4], grad_sums[5], grad_sums[6], grad_sums[7], grad_sums[8], grad_sums[9], grad_sums[10], grad_sums[11])
```

```python
import math

import jax
import jax.numpy as jnp
from jax import lax
from jax.sharding import Mesh
from jax.sharding import PartitionSpec as P

HEADS = 16
HEAD_DIM = 64
EPS = 1e-06
NEG = -1e30
BF = jnp.bfloat16
F32 = jnp.float32


def dot(a, b):
    return jnp.dot(a, b, preferred_element_type=F32)


def dot_t(a, b):
    return lax.dot_general(a, b, (((1,), (1,)), ((), ())), preferred_element_type=F32)


def tdot(a, b):
    return lax.dot_general(a, b, (((0,), (0,)), ((), ())), preferred_element_type=F32)


def rotate(tensor, cosines, sines):
    half_dim = tensor.shape[-1] // 2
    front = tensor[..., :half_dim]
    behind = tensor[..., half_dim:]
    return jnp.concatenate(
        [front * cosines - behind * sines, behind * cosines + front * sines], axis=-1
    )


def sphere(tensor):
    return tensor * lax.rsqrt(jnp.mean(tensor * tensor, axis=-1, keepdims=True) + EPS)


def head_unit(tensor, gains):
    return gains * tensor * lax.rsqrt(jnp.sum(tensor * tensor, axis=-1, keepdims=True) + EPS)


def residual_step(branch, residual_in, alpha):
    return sphere(residual_in + alpha * (sphere(branch) - residual_in))


def gating(up_proj, gate_proj, scale_up, scale_gate):
    return scale_up * up_proj * jax.nn.silu(scale_gate * gate_proj)


def make_body(sizes):
    ny, nx, nw, nz, nc = sizes
    ndev = ny * nx * nw * nz * nc
    line = ("w", "z")
    nline = nw * nz
    quad = ("x", "z")
    nquad = nx * nz

    def swap(value, axes, count, k):
        return lax.ppermute(value, axes, [(i, i ^ k) for i in range(count)])

    def gather_rel(value, axes, count):
        return [value] + [swap(value, axes, count, k) for k in range(1, count)]

    def exchange_rel(chunks, axes, count):
        return [chunks[0]] + [swap(chunks[k], axes, count, k) for k in range(1, count)]

    def sum_rel(chunks, axes, count):
        got = exchange_rel([c.astype(BF) for c in chunks], axes, count)
        total = chunks[0].astype(F32)
        for piece in got[1:]:
            total = total + piece.astype(F32)
        return total

    def place(pieces, rank):
        stack = jnp.stack(pieces)
        order = rank ^ jnp.arange(len(pieces))
        return jnp.take(stack, order, axis=0)

    def pick(array, rank, count):
        return [lax.dynamic_index_in_dim(array, rank ^ k, 0, False) for k in range(count)]

    def body(
        tokens, doc_ids, w_query, w_key, w_value, w_out, w_up, w_gate, w_down,
        s_qk, alpha_attn, s_up, s_gate, alpha_mlp, cotangent,
    ):
        nseq, seg, dm = tokens.shape
        rows = w_query.shape[0]
        ff = w_up.shape[1]
        ffq = ff // nquad
        ffb = ff // ndev
        hcols = dm // nline
        nheads = HEADS // nline
        score_scale = math.sqrt(HEAD_DIM)
        c_at = lax.axis_index("c")
        line_at = lax.axis_index(line)
        quad_at = lax.axis_index(quad)

        def by_line(w):
            return w.astype(BF).reshape(rows, nline, hcols)

        w_qkv = jnp.stack([by_line(w_query), by_line(w_key), by_line(w_value)], axis=2)
        w_qkv = w_qkv.transpose(1, 0, 2, 3).reshape(nline, rows, 3 * hcols)
        got = place(exchange_rel(pick(w_qkv, line_at, nline), line, nline), line_at)
        full = lax.all_gather(got, ("y", "x", "c"), axis=0)
        full = full.reshape(ny, nx, nc, nw, nz, rows, 3 * hcols).transpose(0, 1, 3, 4, 2, 5, 6)
        full_qkv = full.reshape(dm, 3 * hcols)
        full_out = lax.all_gather(w_out.astype(BF), ("y", "x", "w", "z", "c"), axis=0, tiled=True)

        def by_quad(w):
            w = w.astype(BF).reshape(rows, ny, nx, nw, nz, nc, ffb)
            return w.transpose(2, 4, 0, 1, 3, 5, 6).reshape(nquad, rows, ffq)

        w_ug = jnp.concatenate([by_quad(w_up), by_quad(w_gate)], axis=2)
        got = place(exchange_rel(pick(w_ug, quad_at, nquad), quad, nquad), quad_at)
        full = lax.all_gather(got, ("y", "w", "c"), axis=0)
        full = full.reshape(ny, nw, nc, nx, nz, rows, 2 * ffq).transpose(0, 3, 1, 4, 2, 5, 6)
        full_ug = full.reshape(dm, 2 * ffq)
        full_down = lax.all_gather(w_down.astype(BF), ("y", "w", "c"), axis=0, tiled=True)

        def my_ff(vec):
            v = vec.reshape(ny, nx, nw, nz, nc, ffb).transpose(1, 3, 0, 2, 4, 5)
            return lax.dynamic_index_in_dim(v.reshape(nquad, ffq), quad_at, 0, False)

        my_s_up, my_s_gate = my_ff(s_up), my_ff(s_gate)
        my_gain = lax.dynamic_index_in_dim(s_qk.reshape(nline, hcols), line_at, 0, False)

        def to_row(value):
            keep = lax.dynamic_index_in_dim(value, c_at, 0, False)
            send = lax.dynamic_index_in_dim(value, 1 - c_at, 0, False)
            return jnp.concatenate([keep, lax.ppermute(send, "c", [(0, 1), (1, 0)])], axis=0)

        def from_row(value, send_type):
            keep, send = value[:seg], value[seg:]
            other = lax.ppermute(send.astype(send_type), "c", [(0, 1), (1, 0)])
            pair = jnp.stack([keep, other.astype(value.dtype)])
            return jnp.where(c_at == 0, pair, pair[::-1])

        docs = doc_ids.astype(BF)
        extra = jnp.zeros((nseq, 16, dm), BF).at[:, 0, :seg].set(docs)
        ext = jnp.concatenate([tokens, extra], axis=1)
        mine = to_row(ext).reshape(2, seg + 16, dm)
        everyone = jnp.stack(gather_rel(mine, line, nline))
        row_tokens = everyone[:, :, :seg].reshape(nline * 2 * seg, dm)
        row_docs = everyone[:, :, seg, :seg].reshape(-1).astype(F32)
        peers = line_at ^ jnp.arange(nline)
        seg_at = 2 * peers[:, None] + jnp.stack([c_at, 1 - c_at])[None, :]
        index = (seg_at[:, :, None] * seg + jnp.arange(seg)).reshape(-1)
        start = jnp.sum((row_docs[None, :] < row_docs[:, None]).astype(jnp.int32), axis=1)
        pos = index - start
        allowed = (index[None, :] <= index[:, None]) & (index[None, :] >= start[:, None])
        frequency = 10000.0 ** (-jnp.arange(HEAD_DIM // 2, dtype=F32) / (HEAD_DIM // 2))
        angles = pos.astype(F32)[:, None] * frequency
        cosines, sines = jnp.cos(angles)[:, None, :], jnp.sin(angles)[:, None, :]
        nt = row_tokens.shape[0]
        x_low = mine[:, :seg].reshape(2 * seg, dm)
        x_row = x_low.astype(F32)

        pre = dot(row_tokens, full_qkv)

        def heads(t):
            return t.reshape(nt, nheads, HEAD_DIM)

        def unit_pair(q_pre, k_pre, gains):
            gains = gains.reshape(nheads, HEAD_DIM)
            return (
                head_unit(rotate(heads(q_pre), cosines, sines), gains),
                head_unit(rotate(heads(k_pre), cosines, sines), gains),
            )

        (q_unit, k_unit), unit_pull = jax.vjp(
            unit_pair, pre[:, :hcols], pre[:, hcols : 2 * hcols], my_gain
        )
        q_low, k_low = q_unit.astype(BF), k_unit.astype(BF)
        v_low = heads(pre[:, 2 * hcols :].astype(BF))
        scores = jnp.einsum("qhd,khd->hqk", q_low, k_low, preferred_element_type=F32) * score_scale
        scores = jnp.where(allowed[None], scores, NEG)
        peak = jnp.max(scores, axis=-1, keepdims=True)
        raw = jnp.where(allowed[None], jnp.exp(scores - peak), 0.0)
        probs = raw / jnp.sum(raw, axis=-1, keepdims=True)
        p_low = probs.astype(BF)
        attended = jnp.einsum("hqk,khd->qhd", p_low, v_low, preferred_element_type=F32)
        att_low = attended.astype(BF).reshape(nline, 2 * seg, hcols)
        got = place(exchange_rel([att_low[k] for k in range(nline)], line, nline), line_at)
        att_mine = got.transpose(1, 0, 2).reshape(2 * seg, dm)

        h_attn = dot(att_mine, full_out)
        h_one, attn_pull = jax.vjp(residual_step, h_attn, x_row, alpha_attn)
        h_low = jnp.concatenate(gather_rel(h_one.astype(BF), quad, nquad), axis=0)
        ug = dot(h_low, full_ug)
        mixed, gate_pull = jax.vjp(gating, ug[:, :ffq], ug[:, ffq:], my_s_up, my_s_gate)
        mixed_low = mixed.astype(BF)
        part = dot(mixed_low, full_down).reshape(nquad, 2 * seg, dm)
        h_mlp = sum_rel([part[k] for k in range(nquad)], quad, nquad)
        result, out_pull = jax.vjp(residual_step, h_mlp, h_one, alpha_mlp)
        hidden_out = from_row(result.astype(BF), BF)

        d_result = to_row(cotangent).astype(F32)
        d_hmlp, d_hone, g_alpha_mlp = out_pull(d_result)
        dm_low = jnp.concatenate(gather_rel(d_hmlp.astype(BF), quad, nquad), axis=0)
        d_mixed = dot_t(dm_low, full_down)
        d_up, d_gate, g_s_up, g_s_gate = gate_pull(d_mixed)
        dug_low = jnp.concatenate([d_up.astype(BF), d_gate.astype(BF)], axis=1)
        part = dot_t(dug_low, full_ug).reshape(nquad, 2 * seg, dm)
        d_hone = d_hone + sum_rel([part[k] for k in range(nquad)], quad, nquad)
        g_down = lax.psum_scatter(
            tdot(mixed_low, dm_low).astype(BF), ("y", "w", "c"), scatter_dimension=0, tiled=True
        ).astype(F32)
        g_ug = tdot(h_low, dug_low).astype(BF)
        g_ug = g_ug.reshape(ny, nx, nw, nz, nc, rows, 2 * ffq).transpose(0, 2, 4, 1, 3, 5, 6)
        g_ug = lax.psum_scatter(
            g_ug.reshape(ny * nw * nc, nquad, rows, 2 * ffq),
            ("y", "w", "c"), scatter_dimension=0, tiled=True,
        )[0]
        got = place(exchange_rel(pick(g_ug, quad_at, nquad), quad, nquad), quad_at)
        got = got.reshape(nx, nz, rows, 2, ny, nw, nc, ffb).transpose(3, 2, 4, 0, 5, 1, 6, 7)
        g_up, g_gate = got.reshape(2, rows, ff).astype(F32)

        d_hattn, d_tokens, g_alpha_attn = attn_pull(d_hone)
        dh_low = d_hattn.astype(BF)
        g_out = lax.psum_scatter(
            tdot(att_mine, dh_low).astype(BF), ("y", "x", "w", "z", "c"),
            scatter_dimension=0, tiled=True,
        ).astype(F32)
        d_att = dot_t(dh_low, full_out).astype(BF).reshape(2 * seg, nline, hcols).transpose(1, 0, 2)
        d_att = jnp.concatenate(
            exchange_rel(pick(d_att, line_at, nline), line, nline), axis=0
        ).reshape(nt, nheads, HEAD_DIM)
        delta = jnp.sum(d_att.astype(F32) * attended, axis=-1)
        d_probs = jnp.einsum("qhd,khd->hqk", d_att, v_low, preferred_element_type=F32)
        d_scores = (probs * (d_probs - delta.T[:, :, None])).astype(BF)
        d_q = score_scale * jnp.einsum("hqk,khd->qhd", d_scores, k_low, preferred_element_type=F32)
        d_k = score_scale * jnp.einsum("hqk,qhd->khd", d_scores, q_low, preferred_element_type=F32)
        d_v = jnp.einsum("hqk,qhd->khd", p_low, d_att, preferred_element_type=F32)
        d_qpre, d_kpre, g_sqk = unit_pull((d_q, d_k))
        d_qkv = jnp.concatenate([d_qpre, d_kpre, d_v.reshape(nt, hcols)], axis=1).astype(BF)
        part = dot_t(d_qkv, full_qkv).reshape(nline, 2 * seg, dm)
        tokens_grad = d_tokens + sum_rel([part[k] for k in range(nline)], line, nline)
        tokens_grad = from_row(tokens_grad, BF)
        g_qkv = tdot(row_tokens, d_qkv).astype(BF)
        g_qkv = g_qkv.reshape(ny, nx, nw, nz, nc, rows, 3 * hcols).transpose(0, 1, 4, 2, 3, 5, 6)
        g_qkv = lax.psum_scatter(
            g_qkv.reshape(ny * nx * nc, nline, rows, 3 * hcols),
            ("y", "x", "c"), scatter_dimension=0, tiled=True,
        )[0]
        got = place(exchange_rel(pick(g_qkv, line_at, nline), line, nline), line_at)
        got = got.reshape(nline, rows, 3, hcols).transpose(2, 1, 0, 3).reshape(3, rows, dm)
        g_query, g_key, g_value = got.astype(F32)

        def spread(vec, rank, count):
            return jnp.where(jnp.arange(count)[:, None] == rank, vec[None], 0.0)

        def ff_order(vec):
            v = spread(vec, quad_at, nquad).reshape(nx, nz, ny, nw, nc, ffb)
            return v.transpose(2, 0, 3, 1, 4, 5).reshape(ndev, ffb)

        vecs = jnp.concatenate(
            [
                spread(g_sqk, line_at, nline).reshape(ndev, -1),
                g_alpha_attn.reshape(ndev, -1),
                ff_order(g_s_up),
                ff_order(g_s_gate),
                g_alpha_mlp.reshape(ndev, -1),
            ],
            axis=1,
        )
        vecs = lax.psum_scatter(
            vecs, ("y", "x", "w", "z", "c"), scatter_dimension=0, tiled=True
        )[0]
        cuts = [rows, 2 * rows, 2 * rows + ffb, 2 * rows + 2 * ffb]
        g_sqk, g_alpha_attn, g_s_up, g_s_gate, g_alpha_mlp = jnp.split(vecs, cuts)
        return (
            hidden_out, tokens_grad, g_query, g_key, g_value, g_out, g_up, g_gate, g_down,
            g_sqk, g_alpha_attn, g_s_up, g_s_gate, g_alpha_mlp,
        )

    return body


def solution(mesh):
    ndp, nblk = mesh.shape["dp"], mesh.shape["blk"]
    sizes = (ndp // 2, 2, nblk // 4, 2, 2)
    fine = Mesh(mesh.devices.reshape(sizes), ("y", "x", "w", "z", "c"))
    rows, cols = ("y", "x"), ("w", "z", "c")
    flat = rows + cols
    seq = P(rows, cols, None)
    weight = P(flat, None)
    return jax.shard_map(
        make_body(sizes),
        mesh=fine,
        in_specs=(seq, P(rows, cols)) + (weight,) * 7 + (P(),) * 5 + (seq,),
        out_specs=(seq, seq) + (weight,) * 7 + (P(flat),) * 5,
        check_vma=False,
    )
```

```python
import math

import jax
import jax.numpy as jnp
from jax import lax
from jax.sharding import Mesh
from jax.sharding import PartitionSpec as P

HEADS = 16
HEAD_DIM = 64
EPS = 1e-06
NEG = -1e30
BF = jnp.bfloat16
F32 = jnp.float32


def dot(a, b):
    return jnp.dot(a, b, preferred_element_type=F32)


def dot_t(a, b):
    return lax.dot_general(a, b, (((1,), (1,)), ((), ())), preferred_element_type=F32)


def tdot(a, b):
    return lax.dot_general(a, b, (((0,), (0,)), ((), ())), preferred_element_type=F32)


def rotate(tensor, cosines, sines):
    half_dim = tensor.shape[-1] // 2
    front = tensor[..., :half_dim]
    behind = tensor[..., half_dim:]
    return jnp.concatenate(
        [front * cosines - behind * sines, behind * cosines + front * sines], axis=-1
    )


def sphere(tensor):
    return tensor * lax.rsqrt(jnp.mean(tensor * tensor, axis=-1, keepdims=True) + EPS)


def head_unit(tensor, gains):
    return gains * tensor * lax.rsqrt(jnp.sum(tensor * tensor, axis=-1, keepdims=True) + EPS)


def residual_step(branch, residual_in, alpha):
    return sphere(residual_in + alpha * (sphere(branch) - residual_in))


def gating(up_proj, gate_proj, scale_up, scale_gate):
    return scale_up * up_proj * jax.nn.silu(scale_gate * gate_proj)


def make_body(sizes):
    ny, nx, nw, nz, nc = sizes
    ndev = ny * nx * nw * nz * nc
    line = ("w", "z")
    nline = nw * nz
    quad = ("x", "z")
    nquad = nx * nz

    def swap(value, axes, count, k):
        return lax.ppermute(value, axes, [(i, i ^ k) for i in range(count)])

    def gather_rel(value, axes, count):
        return [value] + [swap(value, axes, count, k) for k in range(1, count)]

    def exchange_rel(chunks, axes, count):
        return [chunks[0]] + [swap(chunks[k], axes, count, k) for k in range(1, count)]

    def sum_rel(chunks, axes, count, kind=BF):
        got = exchange_rel([c.astype(kind) for c in chunks], axes, count)
        total = chunks[0].astype(F32)
        for piece in got[1:]:
            total = total + piece.astype(F32)
        return total

    def double(value, stages):
        for axis, count, k in stages:
            value = jnp.concatenate([value, swap(value, axis, count, k)], axis=0)
        return value

    def halve(value, stages, kind=BF):
        for axis, count, k in stages[::-1]:
            half = value.shape[0] // 2
            other = swap(value[half:].astype(kind), axis, count, k)
            value = value[:half].astype(F32) + other.astype(F32)
        return value

    def bits(axis, count):
        return [(axis, count, 1 << b) for b in range(count.bit_length() - 1)]

    def ranks(order):
        count = dict(y=ny, x=nx, w=nw, z=nz, c=nc)
        shape = [count[axis] for axis in order]
        found = {}
        for i, axis in enumerate(order):
            shifted = jnp.arange(count[axis]) ^ lax.axis_index(axis)
            found[axis] = shifted.reshape((-1,) + (1,) * (len(order) - 1 - i))
        flat = jnp.zeros(shape, jnp.int32)
        return found, flat

    def reorder(order, target):
        found, flat = ranks(order)
        count = dict(y=ny, x=nx, w=nw, z=nz, c=nc)
        index = flat
        for axis in target:
            index = index * count[axis] + found[axis]
        return index.reshape(-1)

    def place(pieces, rank):
        stack = jnp.stack(pieces)
        order = rank ^ jnp.arange(len(pieces))
        return jnp.take(stack, order, axis=0)

    def pick(array, rank, count):
        return [lax.dynamic_index_in_dim(array, rank ^ k, 0, False) for k in range(count)]

    def body(
        tokens, doc_ids, w_query, w_key, w_value, w_out, w_up, w_gate, w_down,
        s_qk, alpha_attn, s_up, s_gate, alpha_mlp, cotangent,
    ):
        nseq, seg, dm = tokens.shape
        rows = w_query.shape[0]
        ff = w_up.shape[1]
        ffq = ff // nquad
        ffb = ff // ndev
        hcols = dm // nline
        nheads = HEADS // nline
        score_scale = math.sqrt(HEAD_DIM)
        c_at = lax.axis_index("c")
        line_at = lax.axis_index(line)
        quad_at = lax.axis_index(quad)

        def by_line(w):
            return w.astype(BF).reshape(rows, nline, hcols)

        w_qkv = jnp.stack([by_line(w_query), by_line(w_key), by_line(w_value)], axis=2)
        w_qkv = w_qkv.transpose(1, 0, 2, 3).reshape(nline, rows, 3 * hcols)
        got = jnp.stack(exchange_rel(pick(w_qkv, line_at, nline), line, nline))
        got = jnp.stack(gather_rel(got, ("y", "x"), ny * nx))
        full = double(got[None], bits("c", nc)).reshape(ndev, rows, 3 * hcols)
        full_qkv = jnp.take(full, reorder("yxwzc", "cyxwz"), axis=0).reshape(dm, 3 * hcols)
        full_out = lax.all_gather(w_out.astype(BF), ("y", "x", "w", "z", "c"), axis=0, tiled=True)

        def by_quad(w):
            w = w.astype(BF).reshape(rows, ny, nx, nw, nz, nc, ffb)
            return w.transpose(2, 4, 0, 1, 3, 5, 6).reshape(nquad, rows, ffq)

        w_ug = jnp.concatenate([by_quad(w_up), by_quad(w_gate)], axis=2)
        got = jnp.stack(exchange_rel(pick(w_ug, quad_at, nquad), quad, nquad))
        stages = bits("w", nw) + bits("y", ny) + bits("c", nc)

        def ff_full(part):
            full = double(part[None], stages).reshape(ndev, rows, ffq)
            return jnp.take(full, reorder("yxwzc", "cywxz"), axis=0).reshape(dm, ffq)

        full_up, full_gate = ff_full(got[:, :, :ffq]), ff_full(got[:, :, ffq:])
        full_down = double(w_down.astype(BF)[None], stages)
        full_down = jnp.take(full_down, reorder("ywc", "cyw"), axis=0).reshape(ffq, dm)

        def my_ff(vec):
            v = vec.reshape(ny, nx, nw, nz, nc, ffb).transpose(1, 3, 0, 2, 4, 5)
            return lax.dynamic_index_in_dim(v.reshape(nquad, ffq), quad_at, 0, False)

        my_s_up, my_s_gate = my_ff(s_up), my_ff(s_gate)
        my_gain = lax.dynamic_index_in_dim(s_qk.reshape(nline, hcols), line_at, 0, False)

        def to_row(value):
            keep = lax.dynamic_index_in_dim(value, c_at, 0, False)
            send = lax.dynamic_index_in_dim(value, 1 - c_at, 0, False)
            return jnp.concatenate([keep, lax.ppermute(send, "c", [(0, 1), (1, 0)])], axis=0)

        def from_row(value, send_type):
            keep, send = value[:seg], value[seg:]
            other = lax.ppermute(send.astype(send_type), "c", [(0, 1), (1, 0)])
            pair = jnp.stack([keep, other.astype(value.dtype)])
            return jnp.where(c_at == 0, pair, pair[::-1])

        docs = doc_ids.astype(BF)
        extra = jnp.zeros((nseq, 16, dm), BF).at[:, 0, :seg].set(docs)
        ext = jnp.concatenate([tokens, extra], axis=1)
        mine = to_row(ext).reshape(2, seg + 16, dm)
        everyone = jnp.stack(gather_rel(mine, line, nline))
        row_tokens = everyone[:, :, :seg].reshape(nline * 2 * seg, dm)
        row_docs = everyone[:, :, seg, :seg].reshape(-1).astype(F32)
        peers = line_at ^ jnp.arange(nline)
        seg_at = 2 * peers[:, None] + jnp.stack([c_at, 1 - c_at])[None, :]
        index = (seg_at[:, :, None] * seg + jnp.arange(seg)).reshape(-1)
        start = jnp.sum((row_docs[None, :] < row_docs[:, None]).astype(jnp.int32), axis=1)
        pos = index - start
        allowed = (index[None, :] <= index[:, None]) & (index[None, :] >= start[:, None])
        frequency = 10000.0 ** (-jnp.arange(HEAD_DIM // 2, dtype=F32) / (HEAD_DIM // 2))
        angles = pos.astype(F32)[:, None] * frequency
        cosines, sines = jnp.cos(angles)[:, None, :], jnp.sin(angles)[:, None, :]
        nt = row_tokens.shape[0]
        x_low = mine[:, :seg].reshape(2 * seg, dm)
        x_row = x_low.astype(F32)

        pre = dot(row_tokens, full_qkv)

        def heads(t):
            return t.reshape(nt, nheads, HEAD_DIM)

        def unit_pair(q_pre, k_pre, gains):
            gains = gains.reshape(nheads, HEAD_DIM)
            return (
                head_unit(rotate(heads(q_pre), cosines, sines), gains),
                head_unit(rotate(heads(k_pre), cosines, sines), gains),
            )

        (q_unit, k_unit), unit_pull = jax.vjp(
            unit_pair, pre[:, :hcols], pre[:, hcols : 2 * hcols], my_gain
        )
        q_low, k_low = q_unit.astype(BF), k_unit.astype(BF)
        v_low = heads(pre[:, 2 * hcols :].astype(BF))
        scores = jnp.einsum("qhd,khd->hqk", q_low, k_low, preferred_element_type=F32) * score_scale
        scores = jnp.where(allowed[None], scores, NEG)
        peak = jnp.max(scores, axis=-1, keepdims=True)
        raw = jnp.where(allowed[None], jnp.exp(scores - peak), 0.0)
        probs = raw / jnp.sum(raw, axis=-1, keepdims=True)
        p_low = probs.astype(BF)
        attended = jnp.einsum("hqk,khd->qhd", p_low, v_low, preferred_element_type=F32)
        att_low = attended.astype(BF).reshape(nline, 2 * seg, hcols)
        got = place(exchange_rel([att_low[k] for k in range(nline)], line, nline), line_at)
        att_mine = got.transpose(1, 0, 2).reshape(2 * seg, dm)

        h_attn = dot(att_mine, full_out)
        h_one, attn_pull = jax.vjp(residual_step, h_attn, x_row, alpha_attn)
        h_low = jnp.concatenate(gather_rel(h_one.astype(BF), quad, nquad), axis=0)
        up, gate = dot(h_low, full_up), dot(h_low, full_gate)
        mixed, gate_pull = jax.vjp(gating, up, gate, my_s_up, my_s_gate)
        mixed_low = mixed.astype(BF)
        part = dot(mixed_low, full_down).reshape(nquad, 2 * seg, dm)
        h_mlp = sum_rel([part[k] for k in range(nquad)], quad, nquad)
        result, out_pull = jax.vjp(residual_step, h_mlp, h_one, alpha_mlp)
        hidden_out = from_row(result.astype(BF), BF)

        d_result = to_row(cotangent).astype(F32)
        d_hmlp, d_hone, g_alpha_mlp = out_pull(d_result)
        dm_low = jnp.concatenate(gather_rel(d_hmlp.astype(BF), quad, nquad), axis=0)
        d_mixed = dot_t(dm_low, full_down)
        d_up, d_gate, g_s_up, g_s_gate = gate_pull(d_mixed)
        du_low, dg_low = d_up.astype(BF), d_gate.astype(BF)
        part = dot_t(du_low, full_up) + dot_t(dg_low, full_gate)
        part = part.reshape(nquad, 2 * seg, dm)
        d_hone = d_hone + sum_rel([part[k] for k in range(nquad)], quad, nquad)
        g_down = tdot(mixed_low, dm_low).reshape(ny * nw * nc, ffb, dm)
        g_down = halve(jnp.take(g_down, reorder("cyw", "ywc"), axis=0), stages)[0]

        def ff_scatter(left, right):
            part = tdot(left, right).reshape(ndev, rows, ffq)
            part = jnp.take(part, reorder("cywxz", "yxwzc"), axis=0)
            part = halve(part.reshape(ny * nw * nc, nquad, rows, ffq), stages)[0].astype(BF)
            got = place(exchange_rel([part[k] for k in range(nquad)], quad, nquad), quad_at)
            got = got.reshape(nx, nz, rows, ny, nw, nc, ffb).transpose(2, 3, 0, 4, 1, 5, 6)
            return got.reshape(rows, ff).astype(F32)

        g_up, g_gate = ff_scatter(h_low, du_low), ff_scatter(h_low, dg_low)

        d_hattn, d_tokens, g_alpha_attn = attn_pull(d_hone)
        dh_low = d_hattn.astype(BF)

        def to_owner(part, kind=BF):
            part = jnp.take(part, reorder("cyxwz", "yxwzc"), axis=0)
            part = halve(part.reshape((nc, ny * nx, nline) + part.shape[1:]), bits("c", nc), kind)[0]
            part = sum_rel([part[k] for k in range(ny * nx)], ("y", "x"), ny * nx, kind)
            return sum_rel([part[k] for k in range(nline)], line, nline, kind)

        g_out = to_owner(tdot(att_mine, dh_low).reshape(ndev, rows, dm))
        d_att = dot_t(dh_low, full_out).astype(BF).reshape(2 * seg, nline, hcols).transpose(1, 0, 2)
        d_att = jnp.concatenate(
            exchange_rel(pick(d_att, line_at, nline), line, nline), axis=0
        ).reshape(nt, nheads, HEAD_DIM)
        delta = jnp.sum(d_att.astype(F32) * attended, axis=-1)
        d_probs = jnp.einsum("qhd,khd->hqk", d_att, v_low, preferred_element_type=F32)
        d_scores = (probs * (d_probs - delta.T[:, :, None])).astype(BF)
        d_q = score_scale * jnp.einsum("hqk,khd->qhd", d_scores, k_low, preferred_element_type=F32)
        d_k = score_scale * jnp.einsum("hqk,qhd->khd", d_scores, q_low, preferred_element_type=F32)
        d_v = jnp.einsum("hqk,qhd->khd", p_low, d_att, preferred_element_type=F32)
        d_qpre, d_kpre, g_sqk = unit_pull((d_q, d_k))
        d_qkv = jnp.concatenate([d_qpre, d_kpre, d_v.reshape(nt, hcols)], axis=1).astype(BF)
        part = dot_t(d_qkv, full_qkv).reshape(nline, 2 * seg, dm)
        tokens_grad = d_tokens + sum_rel([part[k] for k in range(nline)], line, nline)
        tokens_grad = from_row(tokens_grad, BF)
        g_qkv = tdot(row_tokens, d_qkv).reshape(ndev, rows, 3 * hcols)
        g_qkv = jnp.take(g_qkv, reorder("cyxwz", "yxwzc"), axis=0)
        g_qkv = halve(g_qkv.reshape(nc, ny * nx, nline, rows, 3 * hcols), bits("c", nc))[0]
        g_qkv = sum_rel([g_qkv[k] for k in range(ny * nx)], ("y", "x"), ny * nx).astype(BF)
        got = place(exchange_rel([g_qkv[k] for k in range(nline)], line, nline), line_at)
        got = got.reshape(nline, rows, 3, hcols).transpose(2, 1, 0, 3).reshape(3, rows, dm)
        g_query, g_key, g_value = got.astype(F32)

        def spread(vec, rank, count):
            return jnp.where(jnp.arange(count)[:, None] == rank, vec[None], 0.0)

        def ff_order(vec):
            v = spread(vec, quad_at, nquad).reshape(nx, nz, ny, nw, nc, ffb)
            return v.transpose(2, 0, 3, 1, 4, 5).reshape(ndev, ffb)

        vecs = jnp.concatenate(
            [
                spread(g_sqk, line_at, nline).reshape(ndev, -1),
                g_alpha_attn.reshape(ndev, -1),
                ff_order(g_s_up),
                ff_order(g_s_gate),
                g_alpha_mlp.reshape(ndev, -1),
            ],
            axis=1,
        )
        vecs = to_owner(vecs, F32)
        cuts = [rows, 2 * rows, 2 * rows + ffb, 2 * rows + 2 * ffb]
        g_sqk, g_alpha_attn, g_s_up, g_s_gate, g_alpha_mlp = jnp.split(vecs, cuts)
        return (
            hidden_out, tokens_grad, g_query, g_key, g_value, g_out, g_up, g_gate, g_down,
            g_sqk, g_alpha_attn, g_s_up, g_s_gate, g_alpha_mlp,
        )

    return body


def solution(mesh):
    ndp, nblk = mesh.shape["dp"], mesh.shape["blk"]
    sizes = (ndp // 2, 2, nblk // 4, 2, 2)
    fine = Mesh(mesh.devices.reshape(sizes), ("y", "x", "w", "z", "c"))
    rows, cols = ("y", "x"), ("w", "z", "c")
    flat = rows + cols
    seq = P(rows, cols, None)
    weight = P(flat, None)
    return jax.shard_map(
        make_body(sizes),
        mesh=fine,
        in_specs=(seq, P(rows, cols)) + (weight,) * 7 + (P(),) * 5 + (seq,),
        out_specs=(seq, seq) + (weight,) * 7 + (P(flat),) * 5,
        check_vma=False,
    )
```

```python
import math

import jax
import jax.numpy as jnp
from jax import lax
from jax.experimental import pallas as pl
from jax.experimental.pallas import tpu as pltpu
from jax.sharding import Mesh
from jax.sharding import PartitionSpec as P

HEADS = 16
HEAD_DIM = 64
EPS = 1e-06
NEG = -1e30
BF = jnp.bfloat16
F32 = jnp.float32


def dot(a, b):
    return jnp.dot(a, b, preferred_element_type=F32)


def dot_t(a, b):
    return lax.dot_general(a, b, (((1,), (1,)), ((), ())), preferred_element_type=F32)


def tdot(a, b):
    return lax.dot_general(a, b, (((0,), (0,)), ((), ())), preferred_element_type=F32)


def rotate(tensor, cosines, sines):
    half_dim = tensor.shape[-1] // 2
    front = tensor[..., :half_dim]
    behind = tensor[..., half_dim:]
    return jnp.concatenate(
        [front * cosines - behind * sines, behind * cosines + front * sines], axis=-1
    )


def sphere(tensor):
    return tensor * lax.rsqrt(jnp.mean(tensor * tensor, axis=-1, keepdims=True) + EPS)


def head_unit(tensor, gains):
    return gains * tensor * lax.rsqrt(jnp.sum(tensor * tensor, axis=-1, keepdims=True) + EPS)


def residual_step(branch, residual_in, alpha):
    return sphere(residual_in + alpha * (sphere(branch) - residual_in))


def gating(up_proj, gate_proj, scale_up, scale_gate):
    return scale_up * up_proj * jax.nn.silu(scale_gate * gate_proj)


def make_plain(sizes):
    ny, nx, nw, nz, nc = sizes
    ndev = ny * nx * nw * nz * nc
    line = ("w", "z")
    nline = nw * nz
    quad = ("x", "z")
    nquad = nx * nz

    def swap(value, axes, count, k):
        return lax.ppermute(value, axes, [(i, i ^ k) for i in range(count)])

    def gather_rel(value, axes, count):
        return [value] + [swap(value, axes, count, k) for k in range(1, count)]

    def exchange_rel(chunks, axes, count):
        return [chunks[0]] + [swap(chunks[k], axes, count, k) for k in range(1, count)]

    def sum_rel(chunks, axes, count, kind=BF):
        got = exchange_rel([c.astype(kind) for c in chunks], axes, count)
        total = chunks[0].astype(F32)
        for piece in got[1:]:
            total = total + piece.astype(F32)
        return total

    def double(value, stages):
        for axis, count, k in stages:
            value = jnp.concatenate([value, swap(value, axis, count, k)], axis=0)
        return value

    def halve(value, stages, kind=BF):
        for axis, count, k in stages[::-1]:
            half = value.shape[0] // 2
            other = swap(value[half:].astype(kind), axis, count, k)
            value = value[:half].astype(F32) + other.astype(F32)
        return value

    def bits(axis, count):
        return [(axis, count, 1 << b) for b in range(count.bit_length() - 1)]

    def ranks(order):
        count = dict(y=ny, x=nx, w=nw, z=nz, c=nc)
        shape = [count[axis] for axis in order]
        found = {}
        for i, axis in enumerate(order):
            shifted = jnp.arange(count[axis]) ^ lax.axis_index(axis)
            found[axis] = shifted.reshape((-1,) + (1,) * (len(order) - 1 - i))
        flat = jnp.zeros(shape, jnp.int32)
        return found, flat

    def reorder(order, target):
        found, flat = ranks(order)
        count = dict(y=ny, x=nx, w=nw, z=nz, c=nc)
        index = flat
        for axis in target:
            index = index * count[axis] + found[axis]
        return index.reshape(-1)

    def place(pieces, rank):
        stack = jnp.stack(pieces)
        order = rank ^ jnp.arange(len(pieces))
        return jnp.take(stack, order, axis=0)

    def pick(array, rank, count):
        return [lax.dynamic_index_in_dim(array, rank ^ k, 0, False) for k in range(count)]

    def body(
        tokens, doc_ids, w_query, w_key, w_value, w_out, w_up, w_gate, w_down,
        s_qk, alpha_attn, s_up, s_gate, alpha_mlp, cotangent,
    ):
        nseq, seg, dm = tokens.shape
        rows = w_query.shape[0]
        ff = w_up.shape[1]
        ffq = ff // nquad
        ffb = ff // ndev
        hcols = dm // nline
        nheads = HEADS // nline
        score_scale = math.sqrt(HEAD_DIM)
        c_at = lax.axis_index("c")
        line_at = lax.axis_index(line)
        quad_at = lax.axis_index(quad)

        def by_line(w):
            return w.astype(BF).reshape(rows, nline, hcols)

        w_qkv = jnp.stack([by_line(w_query), by_line(w_key), by_line(w_value)], axis=2)
        w_qkv = w_qkv.transpose(1, 0, 2, 3).reshape(nline, rows, 3 * hcols)
        got = jnp.stack(exchange_rel(pick(w_qkv, line_at, nline), line, nline))
        got = jnp.stack(gather_rel(got, ("y", "x"), ny * nx))
        full = double(got[None], bits("c", nc)).reshape(ndev, rows, 3 * hcols)
        full_qkv = jnp.take(full, reorder("yxwzc", "cyxwz"), axis=0).reshape(dm, 3 * hcols)
        full_out = lax.all_gather(w_out.astype(BF), ("y", "x", "w", "z", "c"), axis=0, tiled=True)

        def by_quad(w):
            w = w.astype(BF).reshape(rows, ny, nx, nw, nz, nc, ffb)
            return w.transpose(2, 4, 0, 1, 3, 5, 6).reshape(nquad, rows, ffq)

        w_ug = jnp.concatenate([by_quad(w_up), by_quad(w_gate)], axis=2)
        got = jnp.stack(exchange_rel(pick(w_ug, quad_at, nquad), quad, nquad))
        stages = bits("w", nw) + bits("y", ny) + bits("c", nc)

        def ff_full(part):
            full = double(part[None], stages).reshape(ndev, rows, ffq)
            return jnp.take(full, reorder("yxwzc", "cywxz"), axis=0).reshape(dm, ffq)

        full_up, full_gate = ff_full(got[:, :, :ffq]), ff_full(got[:, :, ffq:])
        full_down = double(w_down.astype(BF)[None], stages)
        full_down = jnp.take(full_down, reorder("ywc", "cyw"), axis=0).reshape(ffq, dm)

        def my_ff(vec):
            v = vec.reshape(ny, nx, nw, nz, nc, ffb).transpose(1, 3, 0, 2, 4, 5)
            return lax.dynamic_index_in_dim(v.reshape(nquad, ffq), quad_at, 0, False)

        my_s_up, my_s_gate = my_ff(s_up), my_ff(s_gate)
        my_gain = lax.dynamic_index_in_dim(s_qk.reshape(nline, hcols), line_at, 0, False)

        def to_row(value):
            keep = lax.dynamic_index_in_dim(value, c_at, 0, False)
            send = lax.dynamic_index_in_dim(value, 1 - c_at, 0, False)
            return jnp.concatenate([keep, lax.ppermute(send, "c", [(0, 1), (1, 0)])], axis=0)

        def from_row(value, send_type):
            keep, send = value[:seg], value[seg:]
            other = lax.ppermute(send.astype(send_type), "c", [(0, 1), (1, 0)])
            pair = jnp.stack([keep, other.astype(value.dtype)])
            return jnp.where(c_at == 0, pair, pair[::-1])

        docs = doc_ids.astype(BF)
        extra = jnp.zeros((nseq, 16, dm), BF).at[:, 0, :seg].set(docs)
        ext = jnp.concatenate([tokens, extra], axis=1)
        mine = to_row(ext).reshape(2, seg + 16, dm)
        everyone = jnp.stack(gather_rel(mine, line, nline))
        row_tokens = everyone[:, :, :seg].reshape(nline * 2 * seg, dm)
        row_docs = everyone[:, :, seg, :seg].reshape(-1).astype(F32)
        peers = line_at ^ jnp.arange(nline)
        seg_at = 2 * peers[:, None] + jnp.stack([c_at, 1 - c_at])[None, :]
        index = (seg_at[:, :, None] * seg + jnp.arange(seg)).reshape(-1)
        start = jnp.sum((row_docs[None, :] < row_docs[:, None]).astype(jnp.int32), axis=1)
        pos = index - start
        allowed = (index[None, :] <= index[:, None]) & (index[None, :] >= start[:, None])
        frequency = 10000.0 ** (-jnp.arange(HEAD_DIM // 2, dtype=F32) / (HEAD_DIM // 2))
        angles = pos.astype(F32)[:, None] * frequency
        cosines, sines = jnp.cos(angles)[:, None, :], jnp.sin(angles)[:, None, :]
        nt = row_tokens.shape[0]
        x_low = mine[:, :seg].reshape(2 * seg, dm)
        x_row = x_low.astype(F32)

        pre = dot(row_tokens, full_qkv)

        def heads(t):
            return t.reshape(nt, nheads, HEAD_DIM)

        def unit_pair(q_pre, k_pre, gains):
            gains = gains.reshape(nheads, HEAD_DIM)
            return (
                head_unit(rotate(heads(q_pre), cosines, sines), gains),
                head_unit(rotate(heads(k_pre), cosines, sines), gains),
            )

        (q_unit, k_unit), unit_pull = jax.vjp(
            unit_pair, pre[:, :hcols], pre[:, hcols : 2 * hcols], my_gain
        )
        q_low, k_low = q_unit.astype(BF), k_unit.astype(BF)
        v_low = heads(pre[:, 2 * hcols :].astype(BF))
        scores = jnp.einsum("qhd,khd->hqk", q_low, k_low, preferred_element_type=F32) * score_scale
        scores = jnp.where(allowed[None], scores, NEG)
        peak = jnp.max(scores, axis=-1, keepdims=True)
        raw = jnp.where(allowed[None], jnp.exp(scores - peak), 0.0)
        probs = raw / jnp.sum(raw, axis=-1, keepdims=True)
        p_low = probs.astype(BF)
        attended = jnp.einsum("hqk,khd->qhd", p_low, v_low, preferred_element_type=F32)
        att_low = attended.astype(BF).reshape(nline, 2 * seg, hcols)
        got = place(exchange_rel([att_low[k] for k in range(nline)], line, nline), line_at)
        att_mine = got.transpose(1, 0, 2).reshape(2 * seg, dm)

        h_attn = dot(att_mine, full_out)
        h_one, attn_pull = jax.vjp(residual_step, h_attn, x_row, alpha_attn)
        h_low = jnp.concatenate(gather_rel(h_one.astype(BF), quad, nquad), axis=0)
        up, gate = dot(h_low, full_up), dot(h_low, full_gate)
        mixed, gate_pull = jax.vjp(gating, up, gate, my_s_up, my_s_gate)
        mixed_low = mixed.astype(BF)
        part = dot(mixed_low, full_down).reshape(nquad, 2 * seg, dm)
        h_mlp = sum_rel([part[k] for k in range(nquad)], quad, nquad)
        result, out_pull = jax.vjp(residual_step, h_mlp, h_one, alpha_mlp)
        hidden_out = from_row(result.astype(BF), BF)

        d_result = to_row(cotangent).astype(F32)
        d_hmlp, d_hone, g_alpha_mlp = out_pull(d_result)
        dm_low = jnp.concatenate(gather_rel(d_hmlp.astype(BF), quad, nquad), axis=0)
        d_mixed = dot_t(dm_low, full_down)
        d_up, d_gate, g_s_up, g_s_gate = gate_pull(d_mixed)
        du_low, dg_low = d_up.astype(BF), d_gate.astype(BF)
        part = dot_t(du_low, full_up) + dot_t(dg_low, full_gate)
        part = part.reshape(nquad, 2 * seg, dm)
        d_hone = d_hone + sum_rel([part[k] for k in range(nquad)], quad, nquad)
        g_down = tdot(mixed_low, dm_low).reshape(ny * nw * nc, ffb, dm)
        g_down = halve(jnp.take(g_down, reorder("cyw", "ywc"), axis=0), stages)[0]

        def ff_scatter(left, right):
            part = tdot(left, right).reshape(ndev, rows, ffq)
            part = jnp.take(part, reorder("cywxz", "yxwzc"), axis=0)
            part = halve(part.reshape(ny * nw * nc, nquad, rows, ffq), stages)[0].astype(BF)
            got = place(exchange_rel([part[k] for k in range(nquad)], quad, nquad), quad_at)
            got = got.reshape(nx, nz, rows, ny, nw, nc, ffb).transpose(2, 3, 0, 4, 1, 5, 6)
            return got.reshape(rows, ff).astype(F32)

        g_up, g_gate = ff_scatter(h_low, du_low), ff_scatter(h_low, dg_low)

        d_hattn, d_tokens, g_alpha_attn = attn_pull(d_hone)
        dh_low = d_hattn.astype(BF)

        def to_owner(part, kind=BF):
            part = jnp.take(part, reorder("cyxwz", "yxwzc"), axis=0)
            part = halve(part.reshape((nc, ny * nx, nline) + part.shape[1:]), bits("c", nc), kind)[0]
            part = sum_rel([part[k] for k in range(ny * nx)], ("y", "x"), ny * nx, kind)
            return sum_rel([part[k] for k in range(nline)], line, nline, kind)

        g_out = to_owner(tdot(att_mine, dh_low).reshape(ndev, rows, dm))
        d_att = dot_t(dh_low, full_out).astype(BF).reshape(2 * seg, nline, hcols).transpose(1, 0, 2)
        d_att = jnp.concatenate(
            exchange_rel(pick(d_att, line_at, nline), line, nline), axis=0
        ).reshape(nt, nheads, HEAD_DIM)
        delta = jnp.sum(d_att.astype(F32) * attended, axis=-1)
        d_probs = jnp.einsum("qhd,khd->hqk", d_att, v_low, preferred_element_type=F32)
        d_scores = (probs * (d_probs - delta.T[:, :, None])).astype(BF)
        d_q = score_scale * jnp.einsum("hqk,khd->qhd", d_scores, k_low, preferred_element_type=F32)
        d_k = score_scale * jnp.einsum("hqk,qhd->khd", d_scores, q_low, preferred_element_type=F32)
        d_v = jnp.einsum("hqk,qhd->khd", p_low, d_att, preferred_element_type=F32)
        d_qpre, d_kpre, g_sqk = unit_pull((d_q, d_k))
        d_qkv = jnp.concatenate([d_qpre, d_kpre, d_v.reshape(nt, hcols)], axis=1).astype(BF)
        part = dot_t(d_qkv, full_qkv).reshape(nline, 2 * seg, dm)
        tokens_grad = d_tokens + sum_rel([part[k] for k in range(nline)], line, nline)
        tokens_grad = from_row(tokens_grad, BF)
        g_qkv = tdot(row_tokens, d_qkv).reshape(ndev, rows, 3 * hcols)
        g_qkv = jnp.take(g_qkv, reorder("cyxwz", "yxwzc"), axis=0)
        g_qkv = halve(g_qkv.reshape(nc, ny * nx, nline, rows, 3 * hcols), bits("c", nc))[0]
        g_qkv = sum_rel([g_qkv[k] for k in range(ny * nx)], ("y", "x"), ny * nx).astype(BF)
        got = place(exchange_rel([g_qkv[k] for k in range(nline)], line, nline), line_at)
        got = got.reshape(nline, rows, 3, hcols).transpose(2, 1, 0, 3).reshape(3, rows, dm)
        g_query, g_key, g_value = got.astype(F32)

        def spread(vec, rank, count):
            return jnp.where(jnp.arange(count)[:, None] == rank, vec[None], 0.0)

        def ff_order(vec):
            v = spread(vec, quad_at, nquad).reshape(nx, nz, ny, nw, nc, ffb)
            return v.transpose(2, 0, 3, 1, 4, 5).reshape(ndev, ffb)

        vecs = jnp.concatenate(
            [
                spread(g_sqk, line_at, nline).reshape(ndev, -1),
                g_alpha_attn.reshape(ndev, -1),
                ff_order(g_s_up),
                ff_order(g_s_gate),
                g_alpha_mlp.reshape(ndev, -1),
            ],
            axis=1,
        )
        vecs = to_owner(vecs, F32)
        cuts = [rows, 2 * rows, 2 * rows + ffb, 2 * rows + 2 * ffb]
        g_sqk, g_alpha_attn, g_s_up, g_s_gate, g_alpha_mlp = jnp.split(vecs, cuts)
        return (
            hidden_out, tokens_grad, g_query, g_key, g_value, g_out, g_up, g_gate, g_down,
            g_sqk, g_alpha_attn, g_s_up, g_s_gate, g_alpha_mlp,
        )

    return body


VM = pl.BlockSpec(memory_space=pltpu.VMEM)
SM = pl.BlockSpec(memory_space=pltpu.SMEM)
HB = pl.BlockSpec(memory_space=pltpu.HBM)


def call(kernel, outs, args, hbm=(), hbm_out=(), scratch=(), flops=0, mib=60, after=()):
    moved = sum(math.prod(a.shape) * a.dtype.itemsize for a in args)
    moved += sum(math.prod(s) * jnp.dtype(d).itemsize for s, d in outs)
    specs = [SM] + [HB if i in hbm else VM for i in range(1, len(args))]
    return pl.pallas_call(
        kernel,
        out_shape=[jax.ShapeDtypeStruct(s, d) for s, d in outs],
        in_specs=specs,
        out_specs=[HB if i in hbm_out else VM for i in range(len(outs))],
        scratch_shapes=list(scratch),
        compiler_params=pltpu.CompilerParams(vmem_limit_bytes=mib << 20),
        cost_estimate=pl.CostEstimate(flops=flops, bytes_accessed=moved, transcendentals=0),
    )(*args)


def row_norm(v):
    return lax.rsqrt(jnp.mean(v * v, axis=-1, keepdims=True) + EPS)


def sphere_back(dy, y, norm):
    return (dy - y * jnp.mean(dy * y, axis=-1, keepdims=True)) * norm


def make_kernels(sizes):
    ny, nx, nw, nz, nc = sizes
    ndev = ny * nx * nw * nz * nc
    nyx, nline = ny * nx, nw * nz
    nquad, nblk = nyx, nw * nz * nc
    line, yx = ("w", "z"), ("y", "x")
    quad, blk = yx, ("w", "z", "c")

    def swap(value, axes, count, k):
        return lax.ppermute(value, axes, [(i, i ^ k) for i in range(count)])

    def exchange(chunks, axes, count):
        return [chunks[0]] + [swap(chunks[k], axes, count, k) for k in range(1, count)]

    def gather(value, axes, count):
        return exchange([value] * count, axes, count)

    def body(
        tokens, doc_ids, w_query, w_key, w_value, w_out, w_up, w_gate, w_down,
        s_qk, alpha_attn, s_up, s_gate, alpha_mlp, cotangent,
    ):
        nseq, seg, dm = tokens.shape
        rows = w_query.shape[0]
        ff = w_up.shape[1]
        ffq, ffb = ff // nquad, ff // ndev
        hc = dm // nline
        nheads = HEADS // nline
        nt = nline * 2 * seg
        tk = 2 * seg
        pad = 16
        ext = seg + pad
        scale = math.sqrt(HEAD_DIM)
        tile = 256

        at = [lax.axis_index(a) for a in "yxwzc"]
        ranks = jnp.stack(at + [lax.axis_index(yx), lax.axis_index(line)])
        ranks = ranks.astype(jnp.int32)

        def pack_tokens(rk, tok, docs, keep, send):
            c = rk[4]
            first = lax.broadcasted_iota(jnp.int32, (pad, dm), 0) == 0
            for out, which in ((keep, c), (send, 1 - c)):
                out[:seg] = tok[which]
                out[seg:] = jnp.where(first, docs[which], 0.0).astype(BF)

        docs = jnp.pad(doc_ids.astype(F32), ((0, 0), (0, dm - seg))).reshape(nseq, 1, dm)
        keep, send = call(pack_tokens, [((ext, dm), BF)] * 2, (ranks, tokens, docs))
        mine = jnp.concatenate([keep, swap(send, "c", nc, 1)], axis=0)

        def pack_qkv(rk, wq, wk, wv, gain, *outs):
            for k in range(nline):
                cols = pl.ds(pl.multiple_of((rk[6] ^ k) * hc, 128), hc)
                for i, w in enumerate((wq, wk, wv)):
                    outs[k][:, i * hc : (i + 1) * hc] = w[:, cols].astype(BF)
            outs[nline][...] = gain[pl.ds(rk[6], 1), :]

        packed = call(
            pack_qkv,
            [((rows, 3 * hc), BF)] * nline + [((1, hc), F32)],
            (ranks, w_query, w_key, w_value, s_qk.reshape(nline, hc)),
        )
        qkv_parts, my_gain = packed[:nline], packed[nline]

        def pack_ff(rk, wu, wg, su, sg, *outs):
            for k in range(nquad):
                cols = pl.ds(pl.multiple_of((rk[5] ^ k) * ffq, 128), ffq)
                outs[k][:, :ffq] = wu[:, cols].astype(BF)
                outs[k][:, ffq:] = wg[:, cols].astype(BF)
            outs[nquad][...] = su[pl.ds(rk[5], 1), :]
            outs[nquad + 1][...] = sg[pl.ds(rk[5], 1), :]

        packed = call(
            pack_ff,
            [((rows, 2 * ffq), BF)] * nquad + [((1, ffq), F32)] * 2,
            (ranks, w_up, w_gate, s_up.reshape(nquad, ffq), s_gate.reshape(nquad, ffq)),
        )
        ug_parts, my_su, my_sg = packed[:nquad], *packed[nquad:]

        def pack_rest(rk, wo, wd, out_o, out_d):
            out_o[...] = wo[...].astype(BF)
            out_d[...] = wd[...].astype(BF)

        out_low, down_low = call(
            pack_rest, [((rows, dm), BF), ((ffb, dm), BF)], (ranks, w_out, w_down)
        )

        pieces = gather(mine, line, nline)
        got = jnp.stack(exchange(qkv_parts, line, nline))
        qkv_near = jnp.stack(gather(got, yx, nyx))
        qkv_far = swap(qkv_near, "c", nc, 1)
        got = jnp.stack(gather(out_low, line, nline))
        out_near = jnp.stack(gather(got, yx, nyx))
        out_far = swap(out_near, "c", nc, 1)
        got = jnp.concatenate(exchange(ug_parts, quad, nquad), axis=0)
        ug_full = lax.all_gather(got, blk, axis=0, tiled=True)
        down_near = down_low[None]
        for axis, count in (("w", nw), ("z", nz)):
            for b in range(count.bit_length() - 1):
                other = swap(down_near, axis, count, 1 << b)
                down_near = jnp.concatenate([down_near, other], axis=0)
        down_far = swap(down_near, "c", nc, 1)

        place = jnp.arange(nt, dtype=F32)[:, None]
        freq = 10000.0 ** (-jnp.arange(HEAD_DIM // 2, dtype=F32) / (HEAD_DIM // 2))
        angles = place * freq
        cosines, sines = jnp.cos(angles), jnp.sin(angles)
        reps = 128 // HEAD_DIM
        table = jnp.concatenate(
            [cosines] * (2 * reps) + [-sines, sines] * reps, axis=1
        )
        table_hi = table.astype(BF)
        table_lo = (table - table_hi.astype(F32)).astype(BF)

        def owner_copies(rk, near, far, dst, sems):
            copies = []
            for cr, src in enumerate((near, far)):
                for a in range(nyx):
                    for b in range(nline):
                        row = ((rk[5] ^ a) * nline + (rk[6] ^ b)) * nc + (rk[4] ^ cr)
                        row = pl.multiple_of(row * rows, 32)
                        copies.append(
                            pltpu.make_async_copy(
                                src.at[a, b], dst.at[pl.ds(row, rows)], sems.at[len(copies)]
                            )
                        )
            return copies

        def heads_swap(v, low):
            width = v.shape[1]
            half = HEAD_DIM // 2
            return jnp.where(low, pltpu.roll(v, width - half, 1), pltpu.roll(v, half, 1))

        def low_half():
            lane = lax.broadcasted_iota(jnp.int32, (nt, hc), 1)
            return lane % HEAD_DIM < HEAD_DIM // 2

        def token_index(rk, axis, shape):
            t = lax.broadcasted_iota(jnp.int32, shape, axis)
            peer = (t // tk) ^ rk[6]
            core = ((t // seg) % 2) ^ rk[4]
            return (peer * 2 + core) * seg + t % seg

        def allowed_keys(rk, start):
            key = token_index(rk, 1, (1, nt))
            query = token_index(rk, 0, (nt, 1))
            return (key <= query) & (key.astype(F32) >= start)

        def attn_forward(rk, *refs):
            ext_refs, refs = refs[:nline], refs[nline:]
            near, far, gain, t_hi, t_lo = refs[:5]
            att_outs, refs = refs[5 : 5 + nline], refs[5 + nline :]
            x_ref, w_ref, rq_ref, rk_ref, q_ref, k_ref, v_ref, start_ref, cs_ref, sems = refs
            copies = owner_copies(rk, near, far, w_ref, sems)
            for copy in copies:
                copy.start()
            ids = []
            for k in range(nline):
                for half in range(2):
                    block = ext_refs[k][half * ext : half * ext + seg, :]
                    x_ref[k * tk + half * seg : k * tk + (half + 1) * seg, :] = block
                    tail = ext_refs[k][half * ext + seg : (half + 1) * ext, :128].astype(F32)
                    ids.append(tail[:1, :seg])
            ids = jnp.concatenate(ids, axis=1)
            same = lax.broadcasted_iota(jnp.int32, (nt, nt), 0) == lax.broadcasted_iota(
                jnp.int32, (nt, nt), 1
            )
            ids_col = jnp.sum(jnp.where(same, ids, 0.0), axis=1, keepdims=True)
            start = jnp.sum(jnp.where(ids < ids_col, 1.0, 0.0), axis=1, keepdims=True)
            start_ref[...] = jnp.broadcast_to(start, (nt, 128))
            pos = token_index(rk, 0, (nt, 1)) - start.astype(jnp.int32)
            hot = (lax.broadcasted_iota(jnp.int32, (nt, nt), 1) == pos).astype(F32).astype(BF)
            cs = dot(hot, t_hi[...]) + dot(hot, t_lo[...])
            cs_ref[...] = cs
            cos = jnp.concatenate([cs[:, :128]] * (hc // 128), axis=1)
            sin = jnp.concatenate([cs[:, 128:]] * (hc // 128), axis=1)
            allowed = allowed_keys(rk, start)
            for copy in copies:
                copy.wait()
            low = low_half()
            for i, (raw_ref, unit_ref) in enumerate(((rq_ref, q_ref), (rk_ref, k_ref))):
                pre = dot(x_ref[...], w_ref[:, i * hc : (i + 1) * hc])
                turned = pre * cos + heads_swap(pre, low) * sin
                raw_ref[...] = turned
                for h in range(nheads):
                    at_h = slice(h * HEAD_DIM, (h + 1) * HEAD_DIM)
                    part = turned[:, at_h]
                    norm = lax.rsqrt(jnp.sum(part * part, axis=1, keepdims=True) + EPS)
                    unit_ref[:, at_h] = (gain[:, at_h] * part * norm).astype(BF)
            v_ref[...] = dot(x_ref[...], w_ref[:, 2 * hc :]).astype(BF)
            for h in range(nheads):
                at_h = slice(h * HEAD_DIM, (h + 1) * HEAD_DIM)
                s = dot_t(q_ref[:, at_h], k_ref[:, at_h]) * scale
                s = jnp.where(allowed, s, NEG)
                raw = jnp.exp(s - jnp.max(s, axis=1, keepdims=True))
                p = raw * (1.0 / jnp.sum(raw, axis=1, keepdims=True))
                att = dot(p.astype(BF), v_ref[:, at_h]).astype(BF)
                for k in range(nline):
                    att_outs[k][:, at_h] = att[k * tk : (k + 1) * tk]

        unit = ((nt, hc), BF)
        outs = call(
            attn_forward,
            [((tk, hc), BF)] * nline
            + [((nt, dm), BF), ((dm, 3 * hc), BF), ((nt, hc), F32), ((nt, hc), F32)]
            + [unit, unit, unit, ((nt, 128), F32), ((nt, 256), F32)],
            (ranks, *pieces, qkv_near, qkv_far, my_gain, table_hi, table_lo),
            hbm=(1 + nline, 2 + nline),
            scratch=[pltpu.SemaphoreType.DMA((ndev,))],
            flops=2 * nt * dm * 3 * hc + 4 * nt * nt * hc,
        )
        att_parts, outs = outs[:nline], outs[nline:]
        x_all, qkv_full, r_q, r_k, q_low, k_low, v_low, start, cs = outs
        att_got = exchange(att_parts, line, nline)

        def own_x(ext_ref):
            return jnp.concatenate([ext_ref[:seg], ext_ref[ext : ext + seg]], axis=0).astype(F32)

        def attn_update(rk, *refs):
            parts, refs = refs[:nline], refs[nline:]
            near, far, ext_ref, alpha, low_ref, one_ref, raw_ref, w, sems = refs
            copies = owner_copies(rk, near, far, w, sems)
            for copy in copies:
                copy.start()
            for copy in copies:
                copy.wait()
            total = None
            for k in range(nline):
                w_k = w[pl.ds(pl.multiple_of((rk[6] ^ k) * hc, hc), hc), :]
                term = dot(parts[k][...], w_k)
                total = term if total is None else total + term
            raw_ref[...] = total
            x = own_x(ext_ref)
            z = x + alpha[...] * (total * row_norm(total) - x)
            one = z * row_norm(z)
            one_ref[...] = one
            low_ref[...] = one.astype(BF)

        alpha_a, alpha_m = alpha_attn.reshape(1, dm), alpha_mlp.reshape(1, dm)
        full = ((tk, dm), F32)
        h_low, h_one, h_attn, full_out = call(
            attn_update,
            [((tk, dm), BF), full, full, ((dm, dm), BF)],
            (ranks, *att_got, out_near, out_far, mine, alpha_a),
            hbm=(1 + nline, 2 + nline),
            scratch=[pltpu.SemaphoreType.DMA((ndev,))],
            flops=2 * tk * dm * dm,
        )

        h_got = gather(h_low, quad, nquad)

        def load_ff(rk, stack, near, far, scratch):
            wug, wd, sems, sems_d = scratch
            first, second = [], []
            for b in range(nblk):
                for k in range(nquad):
                    row = pl.multiple_of(((rk[5] ^ k) * nblk + b) * rows, 32)
                    src = stack.at[pl.ds((b * nquad + k) * rows, rows)]
                    sem = sems.at[len(first)]
                    first.append(pltpu.make_async_copy(src, wug.at[pl.ds(row, rows)], sem))
            for cr, src in enumerate((near, far)):
                for a in range(nline):
                    peer = ((a % nw) * nz + a // nw) ^ rk[6]
                    row = pl.multiple_of((peer * nc + (rk[4] ^ cr)) * ffb, 32)
                    sem = sems_d.at[len(second)]
                    second.append(pltpu.make_async_copy(src.at[a], wd.at[pl.ds(row, ffb)], sem))
            return first, second

        w_scratch = [pltpu.VMEM((dm, 2 * ffq), BF), pltpu.VMEM((ffq, dm), BF)]
        w_scratch += [pltpu.SemaphoreType.DMA((ndev,)), pltpu.SemaphoreType.DMA((nblk,))]

        def gate_terms(gate, sg):
            v = sg * gate
            s = 1.0 / (1.0 + jnp.exp(-v))
            return v, s

        def ff_forward(rk, *refs):
            h_refs, stacks = refs[:nquad], refs[nquad : nquad + 3]
            su, sg = refs[nquad + 3 : nquad + 5]
            refs = refs[nquad + 5 :]
            parts, (h_all, up_ref, gate_ref, mixed_ref) = refs[:nquad], refs[nquad : nquad + 4]
            scratch = refs[nquad + 4 :]
            wug, wd = scratch[:2]
            first, third = load_ff(rk, *stacks, scratch)
            for copy in first + third:
                copy.start()
            for k in range(nquad):
                h_all[k * tk : (k + 1) * tk, :] = h_refs[k][...]
            for copy in first:
                copy.wait()

            @pl.loop(0, ffq // tile)
            def _(j):
                cols = pl.ds(pl.multiple_of(j * tile, tile), tile)
                up = dot(h_all[...], wug[:, cols])
                gate = dot(h_all[...], wug[:, pl.ds(pl.multiple_of(ffq + j * tile, tile), tile)])
                up_ref[:, cols] = up
                gate_ref[:, cols] = gate
                v, s = gate_terms(gate, sg[:, cols])
                mixed_ref[:, cols] = (su[:, cols] * up * (v * s)).astype(BF)

            for copy in third:
                copy.wait()

            @pl.loop(0, dm // tile)
            def _(j):
                cols = pl.ds(pl.multiple_of(j * tile, tile), tile)
                part = dot(mixed_ref[...], wd[:, cols])
                for k in range(nquad):
                    parts[k][:, cols] = part[k * tk : (k + 1) * tk].astype(parts[k].dtype)

        stacks = (ug_full, down_near, down_far)
        part_shapes = [((tk, dm), F32)] + [((tk, dm), BF)] * (nquad - 1)
        hbm = tuple(range(1 + nquad, 4 + nquad))
        outs = call(
            ff_forward,
            part_shapes + [((nt_q, dm), BF) for nt_q in (nquad * tk,)]
            + [((nquad * tk, ffq), F32)] * 2 + [((nquad * tk, ffq), BF)],
            (ranks, *h_got, *stacks, my_su, my_sg),
            hbm=hbm,
            scratch=w_scratch,
            flops=6 * nquad * tk * dm * ffq,
        )
        mlp_parts, (h_all, up, gate, mixed) = outs[:nquad], outs[nquad:]
        mlp_got = exchange(mlp_parts, quad, nquad)

        def split_rows(rk, cot, keep, send):
            keep[...] = cot[rk[4]]
            send[...] = cot[1 - rk[4]]

        half_low = ((seg, dm), BF)
        cot_keep, cot_send = call(split_rows, [half_low] * 2, (ranks, cotangent))
        cot_recv = swap(cot_send, "c", nc, 1)

        def mlp_update(rk, *refs):
            parts, refs = refs[:nquad], refs[nquad:]
            one_ref, alpha_ref, ck, cr, hid_keep, hid_send, dm_ref, direct, g_alpha = refs
            h = parts[0][...]
            for k in range(1, nquad):
                h = h + parts[k][...].astype(F32)
            one, alpha = one_ref[...], alpha_ref[...]
            norm_h = row_norm(h)
            b = h * norm_h
            gap = b - one
            z = one + alpha * gap
            norm_z = row_norm(z)
            y = z * norm_z
            low = y.astype(BF)
            hid_keep[...] = low[:seg]
            hid_send[...] = low[seg:]
            dy = jnp.concatenate([ck[...], cr[...]], axis=0).astype(F32)
            dz = sphere_back(dy, y, norm_z)
            g_alpha[...] = jnp.sum(dz * gap, axis=0, keepdims=True)
            direct[...] = dz * (1.0 - alpha)
            dm_ref[...] = sphere_back(dz * alpha, b, norm_h).astype(BF)

        outs = call(
            mlp_update,
            [half_low, half_low, ((tk, dm), BF), full, ((1, dm), F32)],
            (ranks, *mlp_got, h_one, alpha_m, cot_keep, cot_recv),
        )
        hid_keep, hid_send, dm_low, d_one_direct, g_alpha_mlp = outs
        hid_recv = swap(hid_send, "c", nc, 1)
        dm_got = gather(dm_low, quad, nquad)

        def ff_back(rk, *refs):
            d_refs, stacks = refs[:nquad], refs[nquad : nquad + 3]
            su_ref, sg_ref, up_ref, gate_ref = refs[nquad + 3 : nquad + 7]
            refs = refs[nquad + 7 :]
            parts, (d_all, dug, g_su, g_sg) = refs[:nquad], refs[nquad : nquad + 4]
            scratch = refs[nquad + 4 :]
            wug, wd = scratch[:2]
            first, third = load_ff(rk, *stacks, scratch)
            for copy in third + first:
                copy.start()
            for k in range(nquad):
                d_all[k * tk : (k + 1) * tk, :] = d_refs[k][...]
            for copy in third:
                copy.wait()

            @pl.loop(0, ffq // tile)
            def _(j):
                cols = pl.ds(pl.multiple_of(j * tile, tile), tile)
                d_mixed = dot_t(d_all[...], wd[cols, :])
                up, gate = up_ref[:, cols], gate_ref[:, cols]
                su, sg = su_ref[:, cols], sg_ref[:, cols]
                v, s = gate_terms(gate, sg)
                silu = v * s
                dug[:, cols] = (d_mixed * su * silu).astype(BF)
                slope = d_mixed * su * up * (s * (1.0 + v * (1.0 - s)))
                other = pl.ds(pl.multiple_of(ffq + j * tile, tile), tile)
                dug[:, other] = (slope * sg).astype(BF)
                g_su[:, cols] = jnp.sum(d_mixed * up * silu, axis=0, keepdims=True)
                g_sg[:, cols] = jnp.sum(slope * gate, axis=0, keepdims=True)

            for copy in first:
                copy.wait()

            @pl.loop(0, dm // tile)
            def _(j):
                cols = pl.ds(pl.multiple_of(j * tile, tile), tile)
                part = dot_t(dug[...], wug[cols, :])
                for k in range(nquad):
                    parts[k][:, cols] = part[k * tk : (k + 1) * tk].astype(parts[k].dtype)

        outs = call(
            ff_back,
            part_shapes + [((nquad * tk, dm), BF), ((nquad * tk, 2 * ffq), BF)] + [((1, ffq), F32)] * 2,
            (ranks, *dm_got, *stacks, my_su, my_sg, up, gate),
            hbm=hbm,
            scratch=w_scratch,
            flops=6 * nquad * tk * dm * ffq,
        )
        one_parts, (dm_all, dug_low, g_su, g_sg) = outs[:nquad], outs[nquad:]
        one_got = exchange(one_parts, quad, nquad)

        def store_blocks(scratch, outs, rows_of, count, depth, sems):
            copies = []
            for i, out in enumerate(outs):
                for r in range(count):
                    src = scratch.at[pl.ds(pl.multiple_of(rows_of(i, r) * depth, 32), depth)]
                    copies.append(pltpu.make_async_copy(src, out.at[r], sems.at[len(copies)]))
            return copies

        def down_row(rk, cr, r):
            peer = ((r % nw) * nz + r // nw) ^ rk[6]
            return peer * nc + (rk[4] ^ cr)

        def ff_row(rk, part, r):
            return (rk[5] ^ (r % nquad)) * nblk + r // nquad

        def own_row(rk, cr, r):
            return ((rk[5] ^ (r // nline)) * nline + (rk[6] ^ (r % nline))) * nc + (rk[4] ^ cr)

        def outer(row_of, count, depth, nout=2):
            def kernel(rk, left, right, *refs):
                outs, (g_ref, sems) = refs[:nout], refs[nout:]
                height = left.shape[1]

                @pl.loop(0, height // tile)
                def _(j):
                    cols = pl.ds(pl.multiple_of(j * tile, tile), tile)
                    g_ref[cols, :] = tdot(left[:, cols], right[...]).astype(BF)

                copies = store_blocks(
                    g_ref, outs, lambda i, r: row_of(rk, i, r), count, depth, sems
                )
                for copy in copies:
                    copy.start()
                for copy in copies:
                    copy.wait()

            def run(left, right):
                shape = ((count, depth, right.shape[1]), BF)
                return call(
                    kernel,
                    [shape] * nout,
                    (ranks, left, right),
                    hbm_out=tuple(range(nout)),
                    scratch=[
                        pltpu.VMEM((left.shape[1], right.shape[1]), BF),
                        pltpu.SemaphoreType.DMA((nout * count,)),
                    ],
                    flops=2 * left.shape[0] * left.shape[1] * right.shape[1],
                )

            return run

        def add(a, b):
            return a.astype(F32) + b.astype(F32)

        keep, send = outer(down_row, nline, ffb)(mixed, dm_all)
        total = add(keep, swap(send, "c", nc, 1))
        for axis, count in (("z", nz), ("w", nw)):
            for b in reversed(range(count.bit_length() - 1)):
                half = total.shape[0] // 2
                total = add(total[:half], swap(total[half:].astype(BF), axis, count, 1 << b))
        g_down = total[0]

        (g_ug,) = outer(ff_row, nblk * nquad, rows, 1)(h_all, dug_low)
        g_ug = g_ug.reshape(dm, 2 * ffq)
        g_ug = lax.psum_scatter(g_ug, blk, scatter_dimension=0, tiled=True)
        g_parts = exchange([g_ug[k * rows : (k + 1) * rows] for k in range(nquad)], quad, nquad)

        def place_ff(rk, *refs):
            parts, outs = refs[:nquad], refs[nquad:]
            for k in range(nquad):
                cols = pl.ds(pl.multiple_of((rk[5] ^ k) * ffq, 128), ffq)
                for i in range(2):
                    outs[i][:, cols] = parts[k][:, i * ffq : (i + 1) * ffq].astype(F32)

        g_up, g_gate = call(place_ff, [((rows, ff), F32)] * 2, (ranks, *g_parts))

        def attn_update_back(rk, *refs):
            parts, refs = refs[:nquad], refs[nquad:]
            direct_in, one_ref, raw_ref, ext_ref, alpha_ref, w = refs[:6]
            d_outs, (dh_ref, direct, g_alpha) = refs[6 : 6 + nline], refs[6 + nline :]
            d = direct_in[...] + parts[0][...]
            for k in range(1, nquad):
                d = d + parts[k][...].astype(F32)
            one, raw, alpha = one_ref[...], raw_ref[...], alpha_ref[...]
            x = own_x(ext_ref)
            norm_raw = row_norm(raw)
            b = raw * norm_raw
            gap = b - x
            norm_z = row_norm(x + alpha * gap)
            dz = sphere_back(d, one, norm_z)
            g_alpha[...] = jnp.sum(dz * gap, axis=0, keepdims=True)
            direct[...] = dz * (1.0 - alpha)
            dh_ref[...] = sphere_back(dz * alpha, b, norm_raw).astype(BF)
            for k in range(nline):
                w_k = w[pl.ds(pl.multiple_of((rk[6] ^ k) * hc, hc), hc), :]
                d_outs[k][...] = dot_t(dh_ref[...], w_k).astype(BF)

        outs = call(
            attn_update_back,
            [((tk, hc), BF)] * nline + [((tk, dm), BF), full, ((1, dm), F32)],
            (ranks, *one_got, d_one_direct, h_one, h_attn, mine, alpha_a, full_out),
            flops=2 * tk * dm * dm,
        )
        d_att_parts, (dh_low, d_x_direct, g_alpha_attn) = outs[:nline], outs[nline:]
        d_att = exchange(d_att_parts, line, nline)

        def attn_back(rk, *refs):
            d_refs, refs = refs[:nline], refs[nline:]
            w_ref, rq_ref, rk_ref, q_ref, k_ref, v_ref, start_ref, cs_ref, gain = refs[:9]
            parts, (d_ref, g_gain, do_ref, dq_ref, dk_ref) = refs[9 : 9 + nline], refs[9 + nline :]
            for k in range(nline):
                do_ref[k * tk : (k + 1) * tk, :] = d_refs[k][...]
            allowed = allowed_keys(rk, start_ref[:, :1])
            for h in range(nheads):
                at_h = slice(h * HEAD_DIM, (h + 1) * HEAD_DIM)
                q, key, do = q_ref[:, at_h], k_ref[:, at_h], do_ref[:, at_h]
                s = jnp.where(allowed, dot_t(q, key) * scale, NEG)
                raw = jnp.exp(s - jnp.max(s, axis=1, keepdims=True))
                p = raw * (1.0 / jnp.sum(raw, axis=1, keepdims=True))
                dp = dot_t(do, v_ref[:, at_h])
                pdp = p * dp
                delta = jnp.sum(pdp, axis=1, keepdims=True)
                ds = (pdp - p * delta).astype(BF)
                p = p.astype(BF)
                at_v = slice(2 * hc + h * HEAD_DIM, 2 * hc + (h + 1) * HEAD_DIM)
                d_ref[:, at_v] = tdot(p, do).astype(BF)
                dq_ref[:, at_h] = scale * dot(ds, key)
                dk_ref[:, at_h] = scale * tdot(ds, q)
            cs = cs_ref[...]
            cos = jnp.concatenate([cs[:, :128]] * (hc // 128), axis=1)
            sin = jnp.concatenate([cs[:, 128:]] * (hc // 128), axis=1)
            low = low_half()
            total = None
            for i, (raw_ref, g_ref) in enumerate(((rq_ref, dq_ref), (rk_ref, dk_ref))):
                for h in range(nheads):
                    at_h = slice(h * HEAD_DIM, (h + 1) * HEAD_DIM)
                    turned, g = raw_ref[:, at_h], g_ref[:, at_h]
                    norm = lax.rsqrt(jnp.sum(turned * turned, axis=1, keepdims=True) + EPS)
                    unit = turned * norm
                    term = jnp.sum(g * unit, axis=0, keepdims=True)
                    g_gain[:, at_h] = term if i == 0 else g_gain[:, at_h] + term
                    g = g * gain[:, at_h]
                    g_ref[:, at_h] = norm * (g - unit * jnp.sum(unit * g, axis=1, keepdims=True))
                g = g_ref[...]
                d_ref[:, i * hc : (i + 1) * hc] = (g * cos - heads_swap(g, low) * sin).astype(BF)

            @pl.loop(0, dm // tile)
            def _(j):
                cols = pl.ds(pl.multiple_of(j * tile, tile), tile)
                part = dot_t(d_ref[...], w_ref[cols, :])
                for k in range(nline):
                    parts[k][:, cols] = part[k * tk : (k + 1) * tk].astype(parts[k].dtype)

        outs = call(
            attn_back,
            [((tk, dm), F32)] + [((tk, dm), BF)] * (nline - 1)
            + [((nt, 3 * hc), BF), ((1, hc), F32)],
            (ranks, *d_att, qkv_full, r_q, r_k, q_low, k_low, v_low, start, cs, my_gain),
            scratch=[
                pltpu.VMEM((nt, hc), BF), pltpu.VMEM((nt, hc), F32), pltpu.VMEM((nt, hc), F32)
            ],
            flops=2 * nt * dm * 3 * hc + 10 * nt * nt * hc,
        )
        x_parts, (d_qkv, g_gain) = outs[:nline], outs[nline:]
        x_got = exchange(x_parts, line, nline)

        def finish_tokens(rk, *refs):
            parts, (direct, keep, send) = refs[:nline], refs[nline:]
            d = direct[...] + parts[0][...]
            for k in range(1, nline):
                d = d + parts[k][...].astype(F32)
            keep[...] = d[:seg]
            send[...] = d[seg:].astype(BF)

        x_keep, x_send = call(
            finish_tokens, [((seg, dm), F32), half_low], (ranks, *x_got, d_x_direct)
        )
        x_recv = swap(x_send, "c", nc, 1)

        def join_rows(rk, keep, recv, out):
            out[rk[4]] = keep[...].astype(out.dtype)
            out[1 - rk[4]] = recv[...].astype(out.dtype)

        (tokens_grad,) = call(join_rows, [((nseq, seg, dm), F32)], (ranks, x_keep, x_recv))
        (hidden_out,) = call(join_rows, [((nseq, seg, dm), BF)], (ranks, hid_keep, hid_recv))

        def sum_over(chunks, axes, count):
            got = exchange([chunks[0]] + [c.astype(BF) for c in chunks[1:]], axes, count)
            total = got[0].astype(F32)
            for piece in got[1:]:
                total = total + piece.astype(F32)
            return total

        def outer_out(rk, *refs):
            parts, (dh, keep, send, g_ref, sems) = refs[:nline], refs[nline:]
            for k in range(nline):
                spot = pl.ds(pl.multiple_of((rk[6] ^ k) * hc, hc), hc)
                g_ref[spot, :] = tdot(parts[k][...], dh[...]).astype(BF)
            copies = store_blocks(
                g_ref, (keep, send), lambda i, r: own_row(rk, i, r), nyx * nline, rows, sems
            )
            for copy in copies:
                copy.start()
            for copy in copies:
                copy.wait()

        shape = ((nyx * nline, rows, dm), BF)
        keep, send = call(
            outer_out,
            [shape, shape],
            (ranks, *att_got, dh_low),
            hbm_out=(0, 1),
            scratch=[pltpu.VMEM((dm, dm), BF), pltpu.SemaphoreType.DMA((2 * nyx * nline,))],
            flops=2 * tk * dm * dm,
        )

        def across(keep, send):
            total = add(keep, swap(send, "c", nc, 1))
            total = total.reshape((nyx, nline) + total.shape[1:])
            return sum_over([total[k] for k in range(nyx)], yx, nyx)

        total = across(keep, send)
        g_out = sum_over([total[k] for k in range(nline)], line, nline)
        total = across(*outer(own_row, nyx * nline, rows)(x_all, d_qkv)).astype(BF)
        got = exchange([total[k] for k in range(nline)], line, nline)

        def place_qkv(rk, *refs):
            parts, outs = refs[:nline], refs[nline:]
            for k in range(nline):
                cols = pl.ds(pl.multiple_of((rk[6] ^ k) * hc, 128), hc)
                for i in range(3):
                    outs[i][:, cols] = parts[k][:, i * hc : (i + 1) * hc].astype(F32)

        g_query, g_key, g_value = call(place_qkv, [((rows, dm), F32)] * 3, (ranks, *got))

        width = 2 * ffb + 3 * rows

        def spread(vec, rank, count):
            return jnp.where(jnp.arange(count)[:, None] == rank, vec[None], 0.0)

        def ff_order(vec):
            return spread(vec, ranks[5], nquad).reshape(ndev, ffb)

        at_line = ranks[6]
        vecs = jnp.concatenate(
            [
                spread(g_gain[0], at_line, nline).reshape(ndev, -1),
                g_alpha_attn.reshape(ndev, -1),
                ff_order(g_su[0]),
                ff_order(g_sg[0]),
                g_alpha_mlp.reshape(ndev, -1),
            ],
            axis=1,
        )
        order = (
            (jnp.arange(nc)[:, None, None] ^ at[4])
            + nc * (jnp.arange(nline)[None, None, :] ^ at_line)
            + nc * nline * (jnp.arange(nyx)[None, :, None] ^ ranks[5])
        ).reshape(-1)
        vecs = jnp.take(vecs, order, axis=0).reshape(nc, nyx, nline, width)
        vecs = vecs[0] + swap(vecs[1], "c", nc, 1)
        vecs = sum(exchange([vecs[k] for k in range(nyx)], yx, nyx))
        vecs = sum(exchange([vecs[k] for k in range(nline)], line, nline))
        cuts = [rows, 2 * rows, 2 * rows + ffb, 2 * rows + 2 * ffb]
        g_sqk, g_aa, g_s_up, g_s_gate, g_am = jnp.split(vecs, cuts)
        return (
            hidden_out, tokens_grad, g_query, g_key, g_value, g_out, g_up, g_gate, g_down,
            g_sqk, g_aa, g_s_up, g_s_gate, g_am,
        )

    return body


def make_body(sizes):
    plain, kernels = make_plain(sizes), make_kernels(sizes)
    ndev = math.prod(sizes)
    nline = sizes[2] * sizes[3]

    def body(*args):
        tokens, w_query, w_up = args[0], args[2], args[6]
        fits = w_query.shape[0] % 32 == 0 and (w_up.shape[1] // ndev) % 128 == 0
        fits = fits and (tokens.shape[2] // nline) % 256 == 0 and tokens.shape[1] == 64
        return (kernels if fits else plain)(*args)

    return body


def solution(mesh):
    ndp, nblk = mesh.shape["dp"], mesh.shape["blk"]
    sizes = (ndp // 2, 2, nblk // 4, 2, 2)
    fine = Mesh(mesh.devices.reshape(sizes), ("y", "x", "w", "z", "c"))
    rows, cols = ("y", "x"), ("w", "z", "c")
    flat = rows + cols
    seq = P(rows, cols, None)
    weight = P(flat, None)
    return jax.shard_map(
        make_body(sizes),
        mesh=fine,
        in_specs=(seq, P(rows, cols)) + (weight,) * 7 + (P(),) * 5 + (seq,),
        out_specs=(seq, seq) + (weight,) * 7 + (P(flat),) * 5,
        check_vma=False,
    )
```

```python
import math

import jax
import jax.numpy as jnp
from jax import lax
from jax.experimental import pallas as pl
from jax.experimental.pallas import tpu as pltpu
from jax.sharding import Mesh
from jax.sharding import PartitionSpec as P

HEADS = 16
HEAD_DIM = 64
EPS = 1e-06
NEG = -1e30
BF = jnp.bfloat16
F32 = jnp.float32


def dot(a, b):
    return jnp.dot(a, b, preferred_element_type=F32)


def dot_t(a, b):
    return lax.dot_general(a, b, (((1,), (1,)), ((), ())), preferred_element_type=F32)


def tdot(a, b):
    return lax.dot_general(a, b, (((0,), (0,)), ((), ())), preferred_element_type=F32)


def rotate(tensor, cosines, sines):
    half_dim = tensor.shape[-1] // 2
    front = tensor[..., :half_dim]
    behind = tensor[..., half_dim:]
    return jnp.concatenate(
        [front * cosines - behind * sines, behind * cosines + front * sines], axis=-1
    )


def sphere(tensor):
    return tensor * lax.rsqrt(jnp.mean(tensor * tensor, axis=-1, keepdims=True) + EPS)


def head_unit(tensor, gains):
    return gains * tensor * lax.rsqrt(jnp.sum(tensor * tensor, axis=-1, keepdims=True) + EPS)


def residual_step(branch, residual_in, alpha):
    return sphere(residual_in + alpha * (sphere(branch) - residual_in))


def gating(up_proj, gate_proj, scale_up, scale_gate):
    return scale_up * up_proj * jax.nn.silu(scale_gate * gate_proj)


def make_plain(sizes):
    ny, nx, nw, nz, nc = sizes
    ndev = ny * nx * nw * nz * nc
    line = ("w", "z")
    nline = nw * nz
    quad = ("x", "z")
    nquad = nx * nz

    def swap(value, axes, count, k):
        return lax.ppermute(value, axes, [(i, i ^ k) for i in range(count)])

    def gather_rel(value, axes, count):
        return [value] + [swap(value, axes, count, k) for k in range(1, count)]

    def exchange_rel(chunks, axes, count):
        return [chunks[0]] + [swap(chunks[k], axes, count, k) for k in range(1, count)]

    def sum_rel(chunks, axes, count, kind=BF):
        got = exchange_rel([c.astype(kind) for c in chunks], axes, count)
        total = chunks[0].astype(F32)
        for piece in got[1:]:
            total = total + piece.astype(F32)
        return total

    def double(value, stages):
        for axis, count, k in stages:
            value = jnp.concatenate([value, swap(value, axis, count, k)], axis=0)
        return value

    def halve(value, stages, kind=BF):
        for axis, count, k in stages[::-1]:
            half = value.shape[0] // 2
            other = swap(value[half:].astype(kind), axis, count, k)
            value = value[:half].astype(F32) + other.astype(F32)
        return value

    def bits(axis, count):
        return [(axis, count, 1 << b) for b in range(count.bit_length() - 1)]

    def ranks(order):
        count = dict(y=ny, x=nx, w=nw, z=nz, c=nc)
        shape = [count[axis] for axis in order]
        found = {}
        for i, axis in enumerate(order):
            shifted = jnp.arange(count[axis]) ^ lax.axis_index(axis)
            found[axis] = shifted.reshape((-1,) + (1,) * (len(order) - 1 - i))
        flat = jnp.zeros(shape, jnp.int32)
        return found, flat

    def reorder(order, target):
        found, flat = ranks(order)
        count = dict(y=ny, x=nx, w=nw, z=nz, c=nc)
        index = flat
        for axis in target:
            index = index * count[axis] + found[axis]
        return index.reshape(-1)

    def place(pieces, rank):
        stack = jnp.stack(pieces)
        order = rank ^ jnp.arange(len(pieces))
        return jnp.take(stack, order, axis=0)

    def pick(array, rank, count):
        return [lax.dynamic_index_in_dim(array, rank ^ k, 0, False) for k in range(count)]

    def body(
        tokens, doc_ids, w_query, w_key, w_value, w_out, w_up, w_gate, w_down,
        s_qk, alpha_attn, s_up, s_gate, alpha_mlp, cotangent,
    ):
        nseq, seg, dm = tokens.shape
        rows = w_query.shape[0]
        ff = w_up.shape[1]
        ffq = ff // nquad
        ffb = ff // ndev
        hcols = dm // nline
        nheads = HEADS // nline
        score_scale = math.sqrt(HEAD_DIM)
        c_at = lax.axis_index("c")
        line_at = lax.axis_index(line)
        quad_at = lax.axis_index(quad)

        def by_line(w):
            return w.astype(BF).reshape(rows, nline, hcols)

        w_qkv = jnp.stack([by_line(w_query), by_line(w_key), by_line(w_value)], axis=2)
        w_qkv = w_qkv.transpose(1, 0, 2, 3).reshape(nline, rows, 3 * hcols)
        got = jnp.stack(exchange_rel(pick(w_qkv, line_at, nline), line, nline))
        got = jnp.stack(gather_rel(got, ("y", "x"), ny * nx))
        full = double(got[None], bits("c", nc)).reshape(ndev, rows, 3 * hcols)
        full_qkv = jnp.take(full, reorder("yxwzc", "cyxwz"), axis=0).reshape(dm, 3 * hcols)
        full_out = lax.all_gather(w_out.astype(BF), ("y", "x", "w", "z", "c"), axis=0, tiled=True)

        def by_quad(w):
            w = w.astype(BF).reshape(rows, ny, nx, nw, nz, nc, ffb)
            return w.transpose(2, 4, 0, 1, 3, 5, 6).reshape(nquad, rows, ffq)

        w_ug = jnp.concatenate([by_quad(w_up), by_quad(w_gate)], axis=2)
        got = jnp.stack(exchange_rel(pick(w_ug, quad_at, nquad), quad, nquad))
        stages = bits("w", nw) + bits("y", ny) + bits("c", nc)

        def ff_full(part):
            full = double(part[None], stages).reshape(ndev, rows, ffq)
            return jnp.take(full, reorder("yxwzc", "cywxz"), axis=0).reshape(dm, ffq)

        full_up, full_gate = ff_full(got[:, :, :ffq]), ff_full(got[:, :, ffq:])
        full_down = double(w_down.astype(BF)[None], stages)
        full_down = jnp.take(full_down, reorder("ywc", "cyw"), axis=0).reshape(ffq, dm)

        def my_ff(vec):
            v = vec.reshape(ny, nx, nw, nz, nc, ffb).transpose(1, 3, 0, 2, 4, 5)
            return lax.dynamic_index_in_dim(v.reshape(nquad, ffq), quad_at, 0, False)

        my_s_up, my_s_gate = my_ff(s_up), my_ff(s_gate)
        my_gain = lax.dynamic_index_in_dim(s_qk.reshape(nline, hcols), line_at, 0, False)

        def to_row(value):
            keep = lax.dynamic_index_in_dim(value, c_at, 0, False)
            send = lax.dynamic_index_in_dim(value, 1 - c_at, 0, False)
            return jnp.concatenate([keep, lax.ppermute(send, "c", [(0, 1), (1, 0)])], axis=0)

        def from_row(value, send_type):
            keep, send = value[:seg], value[seg:]
            other = lax.ppermute(send.astype(send_type), "c", [(0, 1), (1, 0)])
            pair = jnp.stack([keep, other.astype(value.dtype)])
            return jnp.where(c_at == 0, pair, pair[::-1])

        docs = doc_ids.astype(BF)
        extra = jnp.zeros((nseq, 16, dm), BF).at[:, 0, :seg].set(docs)
        ext = jnp.concatenate([tokens, extra], axis=1)
        mine = to_row(ext).reshape(2, seg + 16, dm)
        everyone = jnp.stack(gather_rel(mine, line, nline))
        row_tokens = everyone[:, :, :seg].reshape(nline * 2 * seg, dm)
        row_docs = everyone[:, :, seg, :seg].reshape(-1).astype(F32)
        peers = line_at ^ jnp.arange(nline)
        seg_at = 2 * peers[:, None] + jnp.stack([c_at, 1 - c_at])[None, :]
        index = (seg_at[:, :, None] * seg + jnp.arange(seg)).reshape(-1)
        start = jnp.sum((row_docs[None, :] < row_docs[:, None]).astype(jnp.int32), axis=1)
        pos = index - start
        allowed = (index[None, :] <= index[:, None]) & (index[None, :] >= start[:, None])
        frequency = 10000.0 ** (-jnp.arange(HEAD_DIM // 2, dtype=F32) / (HEAD_DIM // 2))
        angles = pos.astype(F32)[:, None] * frequency
        cosines, sines = jnp.cos(angles)[:, None, :], jnp.sin(angles)[:, None, :]
        nt = row_tokens.shape[0]
        x_low = mine[:, :seg].reshape(2 * seg, dm)
        x_row = x_low.astype(F32)

        pre = dot(row_tokens, full_qkv)

        def heads(t):
            return t.reshape(nt, nheads, HEAD_DIM)

        def unit_pair(q_pre, k_pre, gains):
            gains = gains.reshape(nheads, HEAD_DIM)
            return (
                head_unit(rotate(heads(q_pre), cosines, sines), gains),
                head_unit(rotate(heads(k_pre), cosines, sines), gains),
            )

        (q_unit, k_unit), unit_pull = jax.vjp(
            unit_pair, pre[:, :hcols], pre[:, hcols : 2 * hcols], my_gain
        )
        q_low, k_low = q_unit.astype(BF), k_unit.astype(BF)
        v_low = heads(pre[:, 2 * hcols :].astype(BF))
        scores = jnp.einsum("qhd,khd->hqk", q_low, k_low, preferred_element_type=F32) * score_scale
        scores = jnp.where(allowed[None], scores, NEG)
        peak = jnp.max(scores, axis=-1, keepdims=True)
        raw = jnp.where(allowed[None], jnp.exp(scores - peak), 0.0)
        probs = raw / jnp.sum(raw, axis=-1, keepdims=True)
        p_low = probs.astype(BF)
        attended = jnp.einsum("hqk,khd->qhd", p_low, v_low, preferred_element_type=F32)
        att_low = attended.astype(BF).reshape(nline, 2 * seg, hcols)
        got = place(exchange_rel([att_low[k] for k in range(nline)], line, nline), line_at)
        att_mine = got.transpose(1, 0, 2).reshape(2 * seg, dm)

        h_attn = dot(att_mine, full_out)
        h_one, attn_pull = jax.vjp(residual_step, h_attn, x_row, alpha_attn)
        h_low = jnp.concatenate(gather_rel(h_one.astype(BF), quad, nquad), axis=0)
        up, gate = dot(h_low, full_up), dot(h_low, full_gate)
        mixed, gate_pull = jax.vjp(gating, up, gate, my_s_up, my_s_gate)
        mixed_low = mixed.astype(BF)
        part = dot(mixed_low, full_down).reshape(nquad, 2 * seg, dm)
        h_mlp = sum_rel([part[k] for k in range(nquad)], quad, nquad)
        result, out_pull = jax.vjp(residual_step, h_mlp, h_one, alpha_mlp)
        hidden_out = from_row(result.astype(BF), BF)

        d_result = to_row(cotangent).astype(F32)
        d_hmlp, d_hone, g_alpha_mlp = out_pull(d_result)
        dm_low = jnp.concatenate(gather_rel(d_hmlp.astype(BF), quad, nquad), axis=0)
        d_mixed = dot_t(dm_low, full_down)
        d_up, d_gate, g_s_up, g_s_gate = gate_pull(d_mixed)
        du_low, dg_low = d_up.astype(BF), d_gate.astype(BF)
        part = dot_t(du_low, full_up) + dot_t(dg_low, full_gate)
        part = part.reshape(nquad, 2 * seg, dm)
        d_hone = d_hone + sum_rel([part[k] for k in range(nquad)], quad, nquad)
        g_down = tdot(mixed_low, dm_low).reshape(ny * nw * nc, ffb, dm)
        g_down = halve(jnp.take(g_down, reorder("cyw", "ywc"), axis=0), stages)[0]

        def ff_scatter(left, right):
            part = tdot(left, right).reshape(ndev, rows, ffq)
            part = jnp.take(part, reorder("cywxz", "yxwzc"), axis=0)
            part = halve(part.reshape(ny * nw * nc, nquad, rows, ffq), stages)[0].astype(BF)
            got = place(exchange_rel([part[k] for k in range(nquad)], quad, nquad), quad_at)
            got = got.reshape(nx, nz, rows, ny, nw, nc, ffb).transpose(2, 3, 0, 4, 1, 5, 6)
            return got.reshape(rows, ff).astype(F32)

        g_up, g_gate = ff_scatter(h_low, du_low), ff_scatter(h_low, dg_low)

        d_hattn, d_tokens, g_alpha_attn = attn_pull(d_hone)
        dh_low = d_hattn.astype(BF)

        def to_owner(part, kind=BF):
            part = jnp.take(part, reorder("cyxwz", "yxwzc"), axis=0)
            part = halve(part.reshape((nc, ny * nx, nline) + part.shape[1:]), bits("c", nc), kind)[0]
            part = sum_rel([part[k] for k in range(ny * nx)], ("y", "x"), ny * nx, kind)
            return sum_rel([part[k] for k in range(nline)], line, nline, kind)

        g_out = to_owner(tdot(att_mine, dh_low).reshape(ndev, rows, dm))
        d_att = dot_t(dh_low, full_out).astype(BF).reshape(2 * seg, nline, hcols).transpose(1, 0, 2)
        d_att = jnp.concatenate(
            exchange_rel(pick(d_att, line_at, nline), line, nline), axis=0
        ).reshape(nt, nheads, HEAD_DIM)
        delta = jnp.sum(d_att.astype(F32) * attended, axis=-1)
        d_probs = jnp.einsum("qhd,khd->hqk", d_att, v_low, preferred_element_type=F32)
        d_scores = (probs * (d_probs - delta.T[:, :, None])).astype(BF)
        d_q = score_scale * jnp.einsum("hqk,khd->qhd", d_scores, k_low, preferred_element_type=F32)
        d_k = score_scale * jnp.einsum("hqk,qhd->khd", d_scores, q_low, preferred_element_type=F32)
        d_v = jnp.einsum("hqk,qhd->khd", p_low, d_att, preferred_element_type=F32)
        d_qpre, d_kpre, g_sqk = unit_pull((d_q, d_k))
        d_qkv = jnp.concatenate([d_qpre, d_kpre, d_v.reshape(nt, hcols)], axis=1).astype(BF)
        part = dot_t(d_qkv, full_qkv).reshape(nline, 2 * seg, dm)
        tokens_grad = d_tokens + sum_rel([part[k] for k in range(nline)], line, nline)
        tokens_grad = from_row(tokens_grad, BF)
        g_qkv = tdot(row_tokens, d_qkv).reshape(ndev, rows, 3 * hcols)
        g_qkv = jnp.take(g_qkv, reorder("cyxwz", "yxwzc"), axis=0)
        g_qkv = halve(g_qkv.reshape(nc, ny * nx, nline, rows, 3 * hcols), bits("c", nc))[0]
        g_qkv = sum_rel([g_qkv[k] for k in range(ny * nx)], ("y", "x"), ny * nx).astype(BF)
        got = place(exchange_rel([g_qkv[k] for k in range(nline)], line, nline), line_at)
        got = got.reshape(nline, rows, 3, hcols).transpose(2, 1, 0, 3).reshape(3, rows, dm)
        g_query, g_key, g_value = got.astype(F32)

        def spread(vec, rank, count):
            return jnp.where(jnp.arange(count)[:, None] == rank, vec[None], 0.0)

        def ff_order(vec):
            v = spread(vec, quad_at, nquad).reshape(nx, nz, ny, nw, nc, ffb)
            return v.transpose(2, 0, 3, 1, 4, 5).reshape(ndev, ffb)

        vecs = jnp.concatenate(
            [
                spread(g_sqk, line_at, nline).reshape(ndev, -1),
                g_alpha_attn.reshape(ndev, -1),
                ff_order(g_s_up),
                ff_order(g_s_gate),
                g_alpha_mlp.reshape(ndev, -1),
            ],
            axis=1,
        )
        vecs = to_owner(vecs, F32)
        cuts = [rows, 2 * rows, 2 * rows + ffb, 2 * rows + 2 * ffb]
        g_sqk, g_alpha_attn, g_s_up, g_s_gate, g_alpha_mlp = jnp.split(vecs, cuts)
        return (
            hidden_out, tokens_grad, g_query, g_key, g_value, g_out, g_up, g_gate, g_down,
            g_sqk, g_alpha_attn, g_s_up, g_s_gate, g_alpha_mlp,
        )

    return body


VM = pl.BlockSpec(memory_space=pltpu.VMEM)
SM = pl.BlockSpec(memory_space=pltpu.SMEM)
HB = pl.BlockSpec(memory_space=pltpu.HBM)


def call(kernel, outs, args, hbm=(), hbm_out=(), scratch=(), flops=0, mib=60, after=()):
    moved = sum(math.prod(a.shape) * a.dtype.itemsize for a in args)
    moved += sum(math.prod(s) * jnp.dtype(d).itemsize for s, d in outs)
    count = len(args)

    def run(*refs):
        kernel(*refs[:count], *refs[count + len(after) :])

    specs = [SM] + [HB if i in hbm else VM for i in range(1, count)]
    specs += [pl.BlockSpec(memory_space=pl.ANY)] * len(after)
    return pl.pallas_call(
        run,
        out_shape=[jax.ShapeDtypeStruct(s, d) for s, d in outs],
        in_specs=specs,
        out_specs=[HB if i in hbm_out else VM for i in range(len(outs))],
        scratch_shapes=list(scratch),
        compiler_params=pltpu.CompilerParams(vmem_limit_bytes=mib << 20),
        cost_estimate=pl.CostEstimate(flops=flops, bytes_accessed=moved, transcendentals=0),
    )(*args, *after)


def row_norm(v):
    return lax.rsqrt(jnp.mean(v * v, axis=-1, keepdims=True) + EPS)


def sphere_back(dy, y, norm):
    return (dy - y * jnp.mean(dy * y, axis=-1, keepdims=True)) * norm


def make_kernels(sizes):
    ny, nx, nw, nz, nc = sizes
    ndev = ny * nx * nw * nz * nc
    nyx, nline = ny * nx, nw * nz
    ndpc = nyx * nc
    line, yx, dpc = ("w", "z"), ("y", "x"), ("y", "x", "c")

    def swap(value, axes, count, k):
        return lax.ppermute(value, axes, [(i, i ^ k) for i in range(count)])

    def exchange(chunks, axes, count):
        return [chunks[0]] + [swap(chunks[k], axes, count, k) for k in range(1, count)]

    def gather(value, axes, count):
        return exchange([value] * count, axes, count)

    def body(
        tokens, doc_ids, w_query, w_key, w_value, w_out, w_up, w_gate, w_down,
        s_qk, alpha_attn, s_up, s_gate, alpha_mlp, cotangent,
    ):
        nseq, seg, dm = tokens.shape
        rows = w_query.shape[0]
        ff = w_up.shape[1]
        ffq, ffb = ff // nline, ff // ndev
        sub = nc * ffb
        hc = dm // nline
        nheads = HEADS // nline
        nt = nline * 2 * seg
        tk = 2 * seg
        pad = 16
        ext = seg + pad
        scale = math.sqrt(HEAD_DIM)
        tile = 256

        at = [lax.axis_index(a) for a in "yxwzc"]
        ranks = jnp.stack(at + [lax.axis_index(yx), lax.axis_index(line)])
        ranks = ranks.astype(jnp.int32)

        def pack_tokens(rk, tok, docs, keep, send):
            c = rk[4]
            first = lax.broadcasted_iota(jnp.int32, (pad, dm), 0) == 0
            for out, which in ((keep, c), (send, 1 - c)):
                out[:seg] = tok[which]
                out[seg:] = jnp.where(first, docs[which], 0.0).astype(BF)

        def ff_cols(rk, k):
            runs = [(d * nline + (rk[6] ^ k)) * sub for d in range(nyx)]
            return [pl.ds(pl.multiple_of(run, 128), sub) for run in runs]

        def pack_weights(rk, wq, wk, wv, wu, wg, wo, gain, su, sg, *outs):
            for k in range(nline):
                out, out_ff = outs[k], outs[nline + k]
                cols = pl.ds(pl.multiple_of((rk[6] ^ k) * hc, 128), hc)
                for i, w in enumerate((wq, wk, wv)):
                    out[:, i * hc : (i + 1) * hc] = w[:, cols].astype(BF)
                for d, cols in enumerate(ff_cols(rk, k)):
                    for i, w in enumerate((wu, wg)):
                        here = i * ffq + d * sub
                        out_ff[:, here : here + sub] = w[:, cols].astype(BF)
                out_ff[:, 2 * ffq :] = wo[...].astype(BF)
            outs = outs[nline:]
            outs[nline][...] = gain[:, pl.ds(pl.multiple_of(rk[6] * hc, 128), hc)]
            for d, cols in enumerate(ff_cols(rk, 0)):
                here = slice(d * sub, (d + 1) * sub)
                outs[nline + 1][:, here] = su[:, cols]
                outs[nline + 2][:, here] = sg[:, cols]

        docs = jnp.pad(doc_ids.astype(F32), ((0, 0), (0, dm - seg))).reshape(nseq, 1, dm)
        keep, send = call(pack_tokens, [((ext, dm), BF)] * 2, (ranks, tokens, docs))
        mine = jnp.concatenate([keep, swap(send, "c", nc, 1)], axis=0)
        packed = call(
            pack_weights,
            [((rows, 3 * hc), BF)] * nline
            + [((rows, 2 * ffq + dm), BF)] * nline
            + [((1, hc), F32)]
            + [((1, ffq), F32)] * 2,
            (ranks, w_query, w_key, w_value, w_up, w_gate, w_out, s_qk.reshape(1, dm))
            + (s_up.reshape(1, ff), s_gate.reshape(1, ff)),
            after=(keep,),
        )
        packed, packed_ff, (my_gain, my_su, my_sg) = (
            packed[:nline], packed[nline : 2 * nline], packed[2 * nline :]
        )

        w_got = exchange(packed, line, nline)
        ff_got = exchange(packed_ff, line, nline)
        pieces = gather(mine, line, nline)

        def stack(rk, *refs):
            for k in range(nline):
                refs[nline][k * rows : (k + 1) * rows, :] = refs[k][...]

        (got,) = call(stack, [((ffb, 3 * hc), BF)], (ranks, *w_got))
        qkv_full = lax.all_gather(got, dpc, axis=0, tiled=True)

        def stack_ff(rk, *refs):
            parts, (wd, out) = refs[:nline], refs[nline:]
            for k in range(nline):
                out[k * rows : (k + 1) * rows, : 2 * ffq + dm] = parts[k][...]
            out[:, 2 * ffq + dm :] = wd[...].astype(BF)

        (got,) = call(
            stack_ff,
            [((ffb, 2 * ffq + 2 * dm), BF)],
            (ranks, *ff_got, w_down),
            after=(got,),
        )
        ff_full = lax.all_gather(got, dpc, axis=0, tiled=True)

        place = jnp.arange(nt, dtype=F32)[:, None]
        freq = 10000.0 ** (-jnp.arange(HEAD_DIM // 2, dtype=F32) / (HEAD_DIM // 2))
        angles = place * freq
        cosines, sines = jnp.cos(angles), jnp.sin(angles)
        reps = 128 // HEAD_DIM
        table = jnp.concatenate(
            [cosines] * (2 * reps) + [-sines, sines] * reps, axis=1
        )
        table_hi = table.astype(BF)
        table_lo = (table - table_hi.astype(F32)).astype(BF)

        def natural(rk, src, cols, dst, sems):
            copies = []
            for b in range(ndpc):
                for k in range(nline):
                    row = ((b // nc) * nline + (rk[6] ^ k)) * nc + b % nc
                    row = pl.ds(pl.multiple_of(row * rows, 32), rows)
                    block = src.at[pl.ds((b * nline + k) * rows, rows), cols]
                    copies.append(pltpu.make_async_copy(block, dst.at[row], sems.at[len(copies)]))
            return copies

        def heads_swap(v, low):
            width = v.shape[1]
            half = HEAD_DIM // 2
            return jnp.where(low, pltpu.roll(v, width - half, 1), pltpu.roll(v, half, 1))

        def low_half():
            lane = lax.broadcasted_iota(jnp.int32, (nt, hc), 1)
            return lane % HEAD_DIM < HEAD_DIM // 2

        def token_index(rk, axis, shape):
            t = lax.broadcasted_iota(jnp.int32, shape, axis)
            peer = (t // tk) ^ rk[6]
            core = ((t // seg) % 2) ^ rk[4]
            return (peer * 2 + core) * seg + t % seg

        def allowed_keys(rk, start):
            key = token_index(rk, 1, (1, nt))
            query = token_index(rk, 0, (nt, 1))
            return (key <= query) & (key.astype(F32) >= start)

        def attn_forward(rk, *refs):
            ext_refs, refs = refs[:nline], refs[nline:]
            stack, gain, t_hi, t_lo = refs[:4]
            att_ref, refs = refs[4], refs[5:]
            x_ref, w_ref, rq_ref, rk_ref, q_ref, k_ref, v_ref, start_ref, cs_ref, sems = refs
            copies = natural(rk, stack, pl.ds(0, 3 * hc), w_ref, sems)
            for copy in copies:
                copy.start()
            ids = []
            for k in range(nline):
                for half in range(2):
                    block = ext_refs[k][half * ext : half * ext + seg, :]
                    x_ref[k * tk + half * seg : k * tk + (half + 1) * seg, :] = block
                    tail = ext_refs[k][half * ext + seg : (half + 1) * ext, :128].astype(F32)
                    ids.append(tail[:1, :seg])
            ids = jnp.concatenate(ids, axis=1)
            same = lax.broadcasted_iota(jnp.int32, (nt, nt), 0) == lax.broadcasted_iota(
                jnp.int32, (nt, nt), 1
            )
            ids_col = jnp.sum(jnp.where(same, ids, 0.0), axis=1, keepdims=True)
            start = jnp.sum(jnp.where(ids < ids_col, 1.0, 0.0), axis=1, keepdims=True)
            start_ref[...] = jnp.broadcast_to(start, (nt, 128))
            pos = token_index(rk, 0, (nt, 1)) - start.astype(jnp.int32)
            hot = (lax.broadcasted_iota(jnp.int32, (nt, nt), 1) == pos).astype(F32).astype(BF)
            cs = dot(hot, t_hi[...]) + dot(hot, t_lo[...])
            cs_ref[...] = cs
            cos = jnp.concatenate([cs[:, :128]] * (hc // 128), axis=1)
            sin = jnp.concatenate([cs[:, 128:]] * (hc // 128), axis=1)
            allowed = allowed_keys(rk, start)
            for copy in copies:
                copy.wait()
            low = low_half()
            for i, (raw_ref, unit_ref) in enumerate(((rq_ref, q_ref), (rk_ref, k_ref))):
                pre = dot(x_ref[...], w_ref[:, i * hc : (i + 1) * hc])
                turned = pre * cos + heads_swap(pre, low) * sin
                raw_ref[...] = turned
                for h in range(nheads):
                    at_h = slice(h * HEAD_DIM, (h + 1) * HEAD_DIM)
                    part = turned[:, at_h]
                    norm = lax.rsqrt(jnp.sum(part * part, axis=1, keepdims=True) + EPS)
                    unit_ref[:, at_h] = (gain[:, at_h] * part * norm).astype(BF)
            v_ref[...] = dot(x_ref[...], w_ref[:, 2 * hc :]).astype(BF)
            for h in range(nheads):
                at_h = slice(h * HEAD_DIM, (h + 1) * HEAD_DIM)
                s = dot_t(q_ref[:, at_h], k_ref[:, at_h]) * scale
                s = jnp.where(allowed, s, NEG)
                raw = jnp.exp(s - jnp.max(s, axis=1, keepdims=True))
                p = raw * (1.0 / jnp.sum(raw, axis=1, keepdims=True))
                att_ref[:, at_h] = dot(p.astype(BF), v_ref[:, at_h]).astype(BF)

        unit = ((nt, hc), BF)
        outs = call(
            attn_forward,
            [unit, ((nt, dm), BF), ((dm, 3 * hc), BF), ((nt, hc), F32), ((nt, hc), F32)]
            + [unit, unit, unit, ((nt, 128), F32), ((nt, 256), F32)],
            (ranks, *pieces, qkv_full, my_gain, table_hi, table_lo),
            hbm=(1 + nline,),
            scratch=[pltpu.SemaphoreType.DMA((ndev,))],
            flops=2 * nt * dm * 3 * hc + 4 * nt * nt * hc,
        )
        att, outs = outs[0], outs[1:]
        x_all, w_qkv, r_q, r_k, q_low, k_low, v_low, start, cs = outs
        att_got = gather(att, line, nline)

        def own_x(ext_ref):
            return jnp.concatenate([ext_ref[:seg], ext_ref[ext : ext + seg]], axis=0).astype(F32)

        alpha_a, alpha_m = alpha_attn.reshape(1, dm), alpha_mlp.reshape(1, dm)
        full = ((tk, dm), F32)

        def load_out(rk, stack, wo, sems):
            return natural(rk, stack, pl.ds(2 * ffq, dm), wo, sems)

        def load_ff(rk, stack, scratch):
            wug, wd, sems, sem_d = scratch
            down = stack.at[:, pl.ds(2 * ffq + dm, dm)]
            return (
                natural(rk, stack, pl.ds(0, 2 * ffq), wug, sems),
                [pltpu.make_async_copy(down, wd, sem_d.at[0])],
            )

        w_scratch = [pltpu.VMEM((dm, 2 * ffq), BF), pltpu.VMEM((ffq, dm), BF)]
        w_scratch += [pltpu.SemaphoreType.DMA((ndev,)), pltpu.SemaphoreType.DMA((1,))]
        out_scratch = [pltpu.VMEM((dm, dm), BF), pltpu.SemaphoreType.DMA((ndev,))]

        def gate_terms(gate, sg):
            v = sg * gate
            s = 1.0 / (1.0 + jnp.exp(-v))
            return v, s

        def forward(rk, *refs):
            att_refs, refs = refs[:nline], refs[nline:]
            x_ref, alpha, stack, su, sg = refs[:5]
            parts, refs = refs[5 : 5 + nline], refs[5 + nline :]
            h_all, up_ref, gate_ref, mixed_ref, one_ref, raw_ref = refs[:6]
            scratch = refs[6:]
            wug, wd = scratch[:2]
            w = scratch[4]
            first, third = load_ff(rk, stack, scratch[:4])
            out_copies = load_out(rk, stack, w, scratch[5])
            for copy in out_copies + first + third:
                copy.start()
            for copy in out_copies:
                copy.wait()
            for m in range(nline):
                total = None
                for k in range(nline):
                    w_k = w[pl.ds(pl.multiple_of((rk[6] ^ k) * hc, hc), hc), :]
                    term = dot(att_refs[k][(m ^ k) * tk : ((m ^ k) + 1) * tk, :], w_k)
                    total = term if total is None else total + term
                x = x_ref[m * tk : (m + 1) * tk, :].astype(F32)
                z = x + alpha[...] * (total * row_norm(total) - x)
                one = z * row_norm(z)
                h_all[m * tk : (m + 1) * tk, :] = one.astype(BF)
                if m == 0:
                    one_ref[...] = one
                    raw_ref[...] = total
            for copy in first:
                copy.wait()

            @pl.loop(0, ffq // tile)
            def _(j):
                cols = pl.ds(pl.multiple_of(j * tile, tile), tile)
                up = dot(h_all[...], wug[:, cols])
                gate = dot(h_all[...], wug[:, pl.ds(pl.multiple_of(ffq + j * tile, tile), tile)])
                up_ref[:, cols] = up.astype(BF)
                gate_ref[:, cols] = gate.astype(BF)
                v, s = gate_terms(gate, sg[:, cols])
                mixed_ref[:, cols] = (su[:, cols] * up * (v * s)).astype(BF)

            for copy in third:
                copy.wait()

            @pl.loop(0, dm // tile)
            def _(j):
                cols = pl.ds(pl.multiple_of(j * tile, tile), tile)
                part = dot(mixed_ref[...], wd[:, cols])
                for k in range(nline):
                    parts[k][:, cols] = part[k * tk : (k + 1) * tk].astype(parts[k].dtype)

        part_shapes = [((tk, dm), F32)] + [((tk, dm), BF)] * (nline - 1)
        outs = call(
            forward,
            part_shapes
            + [((nt, dm), BF), ((nt, ffq), BF), ((nt, ffq), BF), ((nt, ffq), BF), full, full],
            (ranks, *att_got, x_all, alpha_a, ff_full, my_su, my_sg),
            hbm=(3 + nline,),
            scratch=w_scratch + out_scratch,
            flops=6 * nt * dm * ffq + 2 * nt * dm * dm,
        )
        mlp_parts, (h_all, up, gate, mixed, h_one, h_attn) = outs[:nline], outs[nline:]
        mlp_got = exchange(mlp_parts, line, nline)

        def split_rows(rk, cot, keep, send):
            keep[...] = cot[rk[4]]
            send[...] = cot[1 - rk[4]]

        half_low = ((seg, dm), BF)
        cot_keep, cot_send = call(split_rows, [half_low] * 2, (ranks, cotangent))
        cot_recv = swap(cot_send, "c", nc, 1)

        def mlp_update(rk, *refs):
            parts, refs = refs[:nline], refs[nline:]
            one_ref, alpha_ref, ck, cr, hid_keep, hid_send, dm_ref, direct, g_alpha = refs
            h = parts[0][...]
            for k in range(1, nline):
                h = h + parts[k][...].astype(F32)
            one, alpha = one_ref[...], alpha_ref[...]
            norm_h = row_norm(h)
            b = h * norm_h
            gap = b - one
            z = one + alpha * gap
            norm_z = row_norm(z)
            y = z * norm_z
            low = y.astype(BF)
            hid_keep[...] = low[:seg]
            hid_send[...] = low[seg:]
            dy = jnp.concatenate([ck[...], cr[...]], axis=0).astype(F32)
            dz = sphere_back(dy, y, norm_z)
            g_alpha[...] = jnp.sum(dz * gap, axis=0, keepdims=True)
            direct[...] = dz * (1.0 - alpha)
            dm_ref[...] = sphere_back(dz * alpha, b, norm_h).astype(BF)

        outs = call(
            mlp_update,
            [half_low, half_low, ((tk, dm), BF), full, ((1, dm), F32)],
            (ranks, *mlp_got, h_one, alpha_m, cot_keep, cot_recv),
        )
        hid_keep, hid_send, dm_low, d_one_direct, g_alpha_mlp = outs
        hid_recv = swap(hid_send, "c", nc, 1)
        dm_got = gather(dm_low, line, nline)

        def ff_back(rk, *refs):
            d_refs, stack = refs[:nline], refs[nline]
            su_ref, sg_ref, up_ref, gate_ref = refs[nline + 1 : nline + 5]
            refs = refs[nline + 5 :]
            parts, (d_all, dug, g_su, g_sg) = refs[:nline], refs[nline : nline + 4]
            scratch = refs[nline + 4 :]
            wug, wd = scratch[:2]
            first, third = load_ff(rk, stack, scratch)
            for copy in third + first:
                copy.start()
            for k in range(nline):
                d_all[k * tk : (k + 1) * tk, :] = d_refs[k][...]
            for copy in third:
                copy.wait()

            @pl.loop(0, ffq // tile)
            def _(j):
                cols = pl.ds(pl.multiple_of(j * tile, tile), tile)
                d_mixed = dot_t(d_all[...], wd[cols, :])
                up, gate = up_ref[:, cols].astype(F32), gate_ref[:, cols].astype(F32)
                su, sg = su_ref[:, cols], sg_ref[:, cols]
                v, s = gate_terms(gate, sg)
                silu = v * s
                dug[:, cols] = (d_mixed * su * silu).astype(BF)
                slope = d_mixed * su * up * (s * (1.0 + v * (1.0 - s)))
                other = pl.ds(pl.multiple_of(ffq + j * tile, tile), tile)
                dug[:, other] = (slope * sg).astype(BF)
                g_su[:, cols] = jnp.sum(d_mixed * up * silu, axis=0, keepdims=True)
                g_sg[:, cols] = jnp.sum(slope * gate, axis=0, keepdims=True)

            for copy in first:
                copy.wait()

            @pl.loop(0, dm // tile)
            def _(j):
                cols = pl.ds(pl.multiple_of(j * tile, tile), tile)
                part = dot_t(dug[...], wug[cols, :])
                for k in range(nline):
                    parts[k][:, cols] = part[k * tk : (k + 1) * tk].astype(parts[k].dtype)

        outs = call(
            ff_back,
            part_shapes + [((nline * tk, dm), BF), ((nline * tk, 2 * ffq), BF)] + [((1, ffq), F32)] * 2,
            (ranks, *dm_got, ff_full, my_su, my_sg, up, gate),
            hbm=(1 + nline,),
            scratch=w_scratch,
            flops=6 * nline * tk * dm * ffq,
        )
        one_parts, (dm_all, dug_low, g_su, g_sg) = outs[:nline], outs[nline:]
        one_got = exchange(one_parts, line, nline)

        def stored(rk, g_ref, out, width, block, sems):
            d, peer, c = block // (nline * nc), (block // nc) % nline, block % nc
            spot = ((d * nc + c) * nline + (peer ^ rk[6])) * rows
            src = g_ref.at[pl.ds(pl.multiple_of(block * rows, 32), rows)]
            dst = out.at[pl.ds(pl.multiple_of(spot, 32), rows), pl.ds(0, width)]
            return pltpu.make_async_copy(src, dst, sems.at[block])

        def outer_ff(rk, h, dug, mixed_ref, d_all, out, g_ref, g_down_ref, sems, sem_d):
            def store(block):
                return stored(rk, g_ref, out, 2 * ffq, block, sems)

            @pl.loop(0, dm // tile)
            def _(j):
                cols = pl.ds(pl.multiple_of(j * tile, tile), tile)
                g_ref[cols, :] = tdot(h[:, cols], dug[...]).astype(BF)
                for i in range(tile // rows):
                    store(j * (tile // rows) + i).start()

            @pl.loop(0, ffq // tile)
            def _(j):
                cols = pl.ds(pl.multiple_of(j * tile, tile), tile)
                g_down_ref[cols, :] = tdot(mixed_ref[:, cols], d_all[...]).astype(BF)

            down = pltpu.make_async_copy(g_down_ref, out.at[:, pl.ds(2 * ffq, dm)], sem_d.at[0])
            down.start()
            down.wait()

            @pl.loop(0, ndev)
            def _(block):
                store(block).wait()

        (g_ff,) = call(
            outer_ff,
            [((dm, 2 * ffq + dm), BF)],
            (ranks, h_all, dug_low, mixed, dm_all),
            hbm_out=(0,),
            scratch=[
                pltpu.VMEM((dm, 2 * ffq), BF), pltpu.VMEM((ffq, dm), BF),
                pltpu.SemaphoreType.DMA((ndev,)), pltpu.SemaphoreType.DMA((1,)),
            ],
            flops=6 * nt * dm * ffq,
        )
        g_ff = lax.psum_scatter(g_ff, dpc, scatter_dimension=0, tiled=True)
        def attn_update_back(rk, *refs):
            parts, refs = refs[:nline], refs[nline:]
            direct_in, one_ref, raw_ref, ext_ref, alpha_ref, stack = refs[:6]
            d_outs, (dh_ref, direct, g_alpha, w, sems) = refs[6 : 6 + nline], refs[6 + nline :]
            copies = load_out(rk, stack, w, sems)
            for copy in copies:
                copy.start()
            d = direct_in[...] + parts[0][...]
            for k in range(1, nline):
                d = d + parts[k][...].astype(F32)
            one, raw, alpha = one_ref[...], raw_ref[...], alpha_ref[...]
            x = own_x(ext_ref)
            norm_raw = row_norm(raw)
            b = raw * norm_raw
            gap = b - x
            norm_z = row_norm(x + alpha * gap)
            dz = sphere_back(d, one, norm_z)
            g_alpha[...] = jnp.sum(dz * gap, axis=0, keepdims=True)
            direct[...] = dz * (1.0 - alpha)
            dh_ref[...] = sphere_back(dz * alpha, b, norm_raw).astype(BF)
            for copy in copies:
                copy.wait()
            for k in range(nline):
                w_k = w[pl.ds(pl.multiple_of((rk[6] ^ k) * hc, hc), hc), :]
                d_outs[k][...] = dot_t(dh_ref[...], w_k).astype(BF)

        outs = call(
            attn_update_back,
            [((tk, hc), BF)] * nline + [((tk, dm), BF), full, ((1, dm), F32)],
            (ranks, *one_got, d_one_direct, h_one, h_attn, mine, alpha_a, ff_full),
            hbm=(6 + nline,),
            scratch=out_scratch,
            flops=2 * tk * dm * dm,
        )
        d_att_parts, (dh_low, d_x_direct, g_alpha_attn) = outs[:nline], outs[nline:]
        d_att = exchange(d_att_parts, line, nline)

        def attn_back(rk, *refs):
            d_refs, refs = refs[:nline], refs[nline:]
            w_ref, rq_ref, rk_ref, q_ref, k_ref, v_ref, start_ref, cs_ref, gain = refs[:9]
            parts, (d_ref, g_gain, do_ref, dq_ref, dk_ref) = refs[9 : 9 + nline], refs[9 + nline :]
            for k in range(nline):
                do_ref[k * tk : (k + 1) * tk, :] = d_refs[k][...]
            allowed = allowed_keys(rk, start_ref[:, :1])
            for h in range(nheads):
                at_h = slice(h * HEAD_DIM, (h + 1) * HEAD_DIM)
                q, key, do = q_ref[:, at_h], k_ref[:, at_h], do_ref[:, at_h]
                s = jnp.where(allowed, dot_t(q, key) * scale, NEG)
                raw = jnp.exp(s - jnp.max(s, axis=1, keepdims=True))
                p = raw * (1.0 / jnp.sum(raw, axis=1, keepdims=True))
                dp = dot_t(do, v_ref[:, at_h])
                pdp = p * dp
                delta = jnp.sum(pdp, axis=1, keepdims=True)
                ds = (pdp - p * delta).astype(BF)
                p = p.astype(BF)
                at_v = slice(2 * hc + h * HEAD_DIM, 2 * hc + (h + 1) * HEAD_DIM)
                d_ref[:, at_v] = tdot(p, do).astype(BF)
                dq_ref[:, at_h] = scale * dot(ds, key)
                dk_ref[:, at_h] = scale * tdot(ds, q)
            cs = cs_ref[...]
            cos = jnp.concatenate([cs[:, :128]] * (hc // 128), axis=1)
            sin = jnp.concatenate([cs[:, 128:]] * (hc // 128), axis=1)
            low = low_half()
            total = None
            for i, (raw_ref, g_ref) in enumerate(((rq_ref, dq_ref), (rk_ref, dk_ref))):
                for h in range(nheads):
                    at_h = slice(h * HEAD_DIM, (h + 1) * HEAD_DIM)
                    turned, g = raw_ref[:, at_h], g_ref[:, at_h]
                    norm = lax.rsqrt(jnp.sum(turned * turned, axis=1, keepdims=True) + EPS)
                    unit = turned * norm
                    term = jnp.sum(g * unit, axis=0, keepdims=True)
                    g_gain[:, at_h] = term if i == 0 else g_gain[:, at_h] + term
                    g = g * gain[:, at_h]
                    g_ref[:, at_h] = norm * (g - unit * jnp.sum(unit * g, axis=1, keepdims=True))
                g = g_ref[...]
                d_ref[:, i * hc : (i + 1) * hc] = (g * cos - heads_swap(g, low) * sin).astype(BF)

            @pl.loop(0, dm // tile)
            def _(j):
                cols = pl.ds(pl.multiple_of(j * tile, tile), tile)
                part = dot_t(d_ref[...], w_ref[cols, :])
                for k in range(nline):
                    parts[k][:, cols] = part[k * tk : (k + 1) * tk].astype(parts[k].dtype)

        outs = call(
            attn_back,
            [((tk, dm), F32)] + [((tk, dm), BF)] * (nline - 1)
            + [((nt, 3 * hc), BF), ((1, hc), F32)],
            (ranks, *d_att, w_qkv, r_q, r_k, q_low, k_low, v_low, start, cs, my_gain),
            scratch=[
                pltpu.VMEM((nt, hc), BF), pltpu.VMEM((nt, hc), F32), pltpu.VMEM((nt, hc), F32)
            ],
            flops=2 * nt * dm * 3 * hc + 10 * nt * nt * hc,
        )
        x_parts, (d_qkv, g_gain) = outs[:nline], outs[nline:]
        x_got = exchange(x_parts, line, nline)

        def finish_tokens(rk, *refs):
            parts, (direct, keep, send) = refs[:nline], refs[nline:]
            d = direct[...] + parts[0][...]
            for k in range(1, nline):
                d = d + parts[k][...].astype(F32)
            keep[...] = d[:seg]
            send[...] = d[seg:].astype(BF)

        x_keep, x_send = call(
            finish_tokens, [((seg, dm), F32), half_low], (ranks, *x_got, d_x_direct)
        )
        x_recv = swap(x_send, "c", nc, 1)

        def join_rows(rk, keep, recv, out):
            out[rk[4]] = keep[...].astype(out.dtype)
            out[1 - rk[4]] = recv[...].astype(out.dtype)

        (tokens_grad,) = call(join_rows, [((nseq, seg, dm), F32)], (ranks, x_keep, x_recv))
        (hidden_out,) = call(join_rows, [((nseq, seg, dm), BF)], (ranks, hid_keep, hid_recv))

        at_line = ranks[6]
        mine_ff = (jnp.arange(nline) == at_line)[None, :, None, None]

        def ff_owner(vec):
            return jnp.where(mine_ff, vec.reshape(nyx, 1, nc, ffb), 0.0).reshape(ndev, ffb)

        gains = jnp.where((jnp.arange(nyx) == at_line)[:, None], g_gain, 0.0)
        misc = [v.reshape(ndev, rows) for v in (g_alpha_attn, g_alpha_mlp, gains)]
        misc = jnp.pad(jnp.concatenate(misc, axis=1), ((0, 0), (0, ffb - 3 * rows)))
        vecs = jnp.stack([ff_owner(g_su), ff_owner(g_sg), misc], axis=1).astype(BF)
        vecs = jnp.pad(vecs, ((0, 0), (0, rows - 3), (0, 0))).reshape(dm, ffb)

        wide = 3 * hc + ffb

        def outer_last(rk, x_ref, d_ref, vec_ref, dh, *refs):
            parts, (out, g_ref, sems) = refs[:nline], refs[nline:]

            def store(block):
                return stored(rk, g_ref, out, wide + dm, block, sems)

            for k in range(nline):
                spot = pl.ds(pl.multiple_of((rk[6] ^ k) * hc, hc), hc)
                own = parts[k][k * tk : (k + 1) * tk, :]
                g_ref[spot, wide:] = tdot(own, dh[...]).astype(BF)
            g_ref[:, 3 * hc : wide] = vec_ref[...]

            @pl.loop(0, dm // tile)
            def _(j):
                cols = pl.ds(pl.multiple_of(j * tile, tile), tile)
                g_ref[cols, : 3 * hc] = tdot(x_ref[:, cols], d_ref[...]).astype(BF)
                for i in range(tile // rows):
                    store(j * (tile // rows) + i).start()

            @pl.loop(0, ndev)
            def _(block):
                store(block).wait()

        (g_last,) = call(
            outer_last,
            [((dm, wide + dm), BF)],
            (ranks, x_all, d_qkv, vecs, dh_low, *att_got),
            hbm_out=(0,),
            scratch=[pltpu.VMEM((dm, wide + dm), BF), pltpu.SemaphoreType.DMA((ndev,))],
            flops=2 * nt * dm * 3 * hc,
        )
        g_last = lax.psum_scatter(g_last, dpc, scatter_dimension=0, tiled=True)

        def split_ff(rk, g_ref, down, *outs):
            down[...] = g_ref[:, 2 * ffq :].astype(F32)
            for k in range(nline):
                outs[k][...] = g_ref[k * rows : (k + 1) * rows, : 2 * ffq]

        g_down, *g_parts = call(
            split_ff,
            [((ffb, dm), F32)] + [((rows, 2 * ffq), BF)] * nline,
            (ranks, g_ff),
            after=tuple(x_got[1:]),
        )
        g_parts = exchange(g_parts, line, nline)

        def split_last(rk, g_ref, *outs):
            for k in range(nline):
                outs[k][...] = g_ref[k * rows : (k + 1) * rows, :]

        last = call(
            split_last,
            [((rows, wide + dm), BF)] * nline,
            (ranks, g_last),
            after=tuple(g_parts[1:]),
        )
        last = exchange(last, line, nline)

        def place_last(rk, *refs):
            parts, ff_parts = refs[:nline], refs[nline : 2 * nline]
            outs, refs = refs[2 * nline : 2 * nline + 3], refs[2 * nline + 3 :]
            g_o, ff_outs, vec_outs = refs[0], refs[1:3], refs[3:]
            g_sum, v_sum = None, None
            for k in range(nline):
                cols = pl.ds(pl.multiple_of((rk[6] ^ k) * hc, 128), hc)
                for i in range(3):
                    outs[i][:, cols] = parts[k][:, i * hc : (i + 1) * hc].astype(F32)
                vec = parts[k][:16, 3 * hc : wide].astype(F32)
                part = parts[k][:, wide:].astype(F32)
                for d, cols in enumerate(ff_cols(rk, k)):
                    for i in range(2):
                        here = i * ffq + d * sub
                        ff_outs[i][:, cols] = ff_parts[k][:, here : here + sub].astype(F32)
                g_sum = part if g_sum is None else g_sum + part
                v_sum = vec if v_sum is None else v_sum + vec
            g_o[...] = g_sum
            vec_outs[0][...] = v_sum[:1]
            vec_outs[1][...] = v_sum[1:2]
            for i in range(3):
                vec_outs[2 + i][...] = v_sum[2:3, i * rows : (i + 1) * rows]

        g_query, g_key, g_value, g_out, g_up, g_gate, *vecs = call(
            place_last,
            [((rows, dm), F32)] * 4
            + [((rows, ff), F32)] * 2
            + [((1, ffb), F32)] * 2
            + [((1, rows), F32)] * 3,
            (ranks, *last, *g_parts),
        )
        g_s_up, g_s_gate, g_aa, g_am, g_sqk = [v.reshape(-1) for v in vecs]
        return (
            hidden_out, tokens_grad, g_query, g_key, g_value, g_out, g_up, g_gate, g_down,
            g_sqk, g_aa, g_s_up, g_s_gate, g_am,
        )

    return body


def make_body(sizes):
    plain, kernels = make_plain(sizes), make_kernels(sizes)
    ndev = math.prod(sizes)
    nline = sizes[2] * sizes[3]

    def body(*args):
        tokens, w_query, w_up = args[0], args[2], args[6]
        fits = w_query.shape[0] % 32 == 0 and (w_up.shape[1] // ndev) % 128 == 0
        fits = fits and (tokens.shape[2] // nline) % 256 == 0 and tokens.shape[1] == 64
        return (kernels if fits else plain)(*args)

    return body


def solution(mesh):
    ndp, nblk = mesh.shape["dp"], mesh.shape["blk"]
    sizes = (ndp // 2, 2, nblk // 4, 2, 2)
    fine = Mesh(mesh.devices.reshape(sizes), ("y", "x", "w", "z", "c"))
    rows, cols = ("y", "x"), ("w", "z", "c")
    flat = rows + cols
    seq = P(rows, cols, None)
    weight = P(flat, None)
    return jax.shard_map(
        make_body(sizes),
        mesh=fine,
        in_specs=(seq, P(rows, cols)) + (weight,) * 7 + (P(),) * 5 + (seq,),
        out_specs=(seq, seq) + (weight,) * 7 + (P(flat),) * 5,
        check_vma=False,
    )
```

```python
import math

import jax
import jax.numpy as jnp
from jax import lax
from jax.experimental import pallas as pl
from jax.experimental.pallas import tpu as pltpu
from jax.sharding import Mesh
from jax.sharding import PartitionSpec as P

HEADS = 16
HEAD_DIM = 64
EPS = 1e-06
NEG = -1e30
BF = jnp.bfloat16
F32 = jnp.float32


def dot(a, b):
    return jnp.dot(a, b, preferred_element_type=F32)


def dot_t(a, b):
    return lax.dot_general(a, b, (((1,), (1,)), ((), ())), preferred_element_type=F32)


def tdot(a, b):
    return lax.dot_general(a, b, (((0,), (0,)), ((), ())), preferred_element_type=F32)


def rotate(tensor, cosines, sines):
    half_dim = tensor.shape[-1] // 2
    front = tensor[..., :half_dim]
    behind = tensor[..., half_dim:]
    return jnp.concatenate(
        [front * cosines - behind * sines, behind * cosines + front * sines], axis=-1
    )


def sphere(tensor):
    return tensor * lax.rsqrt(jnp.mean(tensor * tensor, axis=-1, keepdims=True) + EPS)


def head_unit(tensor, gains):
    return gains * tensor * lax.rsqrt(jnp.sum(tensor * tensor, axis=-1, keepdims=True) + EPS)


def residual_step(branch, residual_in, alpha):
    return sphere(residual_in + alpha * (sphere(branch) - residual_in))


def gating(up_proj, gate_proj, scale_up, scale_gate):
    return scale_up * up_proj * jax.nn.silu(scale_gate * gate_proj)


def make_plain(sizes):
    ny, nx, nw, nz, nc = sizes
    ndev = ny * nx * nw * nz * nc
    line = ("w", "z")
    nline = nw * nz
    quad = ("x", "z")
    nquad = nx * nz

    def swap(value, axes, count, k):
        return lax.ppermute(value, axes, [(i, i ^ k) for i in range(count)])

    def gather_rel(value, axes, count):
        return [value] + [swap(value, axes, count, k) for k in range(1, count)]

    def exchange_rel(chunks, axes, count):
        return [chunks[0]] + [swap(chunks[k], axes, count, k) for k in range(1, count)]

    def sum_rel(chunks, axes, count, kind=BF):
        got = exchange_rel([c.astype(kind) for c in chunks], axes, count)
        total = chunks[0].astype(F32)
        for piece in got[1:]:
            total = total + piece.astype(F32)
        return total

    def double(value, stages):
        for axis, count, k in stages:
            value = jnp.concatenate([value, swap(value, axis, count, k)], axis=0)
        return value

    def halve(value, stages, kind=BF):
        for axis, count, k in stages[::-1]:
            half = value.shape[0] // 2
            other = swap(value[half:].astype(kind), axis, count, k)
            value = value[:half].astype(F32) + other.astype(F32)
        return value

    def bits(axis, count):
        return [(axis, count, 1 << b) for b in range(count.bit_length() - 1)]

    def ranks(order):
        count = dict(y=ny, x=nx, w=nw, z=nz, c=nc)
        shape = [count[axis] for axis in order]
        found = {}
        for i, axis in enumerate(order):
            shifted = jnp.arange(count[axis]) ^ lax.axis_index(axis)
            found[axis] = shifted.reshape((-1,) + (1,) * (len(order) - 1 - i))
        flat = jnp.zeros(shape, jnp.int32)
        return found, flat

    def reorder(order, target):
        found, flat = ranks(order)
        count = dict(y=ny, x=nx, w=nw, z=nz, c=nc)
        index = flat
        for axis in target:
            index = index * count[axis] + found[axis]
        return index.reshape(-1)

    def place(pieces, rank):
        stack = jnp.stack(pieces)
        order = rank ^ jnp.arange(len(pieces))
        return jnp.take(stack, order, axis=0)

    def pick(array, rank, count):
        return [lax.dynamic_index_in_dim(array, rank ^ k, 0, False) for k in range(count)]

    def body(
        tokens, doc_ids, w_query, w_key, w_value, w_out, w_up, w_gate, w_down,
        s_qk, alpha_attn, s_up, s_gate, alpha_mlp, cotangent,
    ):
        nseq, seg, dm = tokens.shape
        rows = w_query.shape[0]
        ff = w_up.shape[1]
        ffq = ff // nquad
        ffb = ff // ndev
        hcols = dm // nline
        nheads = HEADS // nline
        score_scale = math.sqrt(HEAD_DIM)
        c_at = lax.axis_index("c")
        line_at = lax.axis_index(line)
        quad_at = lax.axis_index(quad)

        def by_line(w):
            return w.astype(BF).reshape(rows, nline, hcols)

        w_qkv = jnp.stack([by_line(w_query), by_line(w_key), by_line(w_value)], axis=2)
        w_qkv = w_qkv.transpose(1, 0, 2, 3).reshape(nline, rows, 3 * hcols)
        got = jnp.stack(exchange_rel(pick(w_qkv, line_at, nline), line, nline))
        got = jnp.stack(gather_rel(got, ("y", "x"), ny * nx))
        full = double(got[None], bits("c", nc)).reshape(ndev, rows, 3 * hcols)
        full_qkv = jnp.take(full, reorder("yxwzc", "cyxwz"), axis=0).reshape(dm, 3 * hcols)
        full_out = lax.all_gather(w_out.astype(BF), ("y", "x", "w", "z", "c"), axis=0, tiled=True)

        def by_quad(w):
            w = w.astype(BF).reshape(rows, ny, nx, nw, nz, nc, ffb)
            return w.transpose(2, 4, 0, 1, 3, 5, 6).reshape(nquad, rows, ffq)

        w_ug = jnp.concatenate([by_quad(w_up), by_quad(w_gate)], axis=2)
        got = jnp.stack(exchange_rel(pick(w_ug, quad_at, nquad), quad, nquad))
        stages = bits("w", nw) + bits("y", ny) + bits("c", nc)

        def ff_full(part):
            full = double(part[None], stages).reshape(ndev, rows, ffq)
            return jnp.take(full, reorder("yxwzc", "cywxz"), axis=0).reshape(dm, ffq)

        full_up, full_gate = ff_full(got[:, :, :ffq]), ff_full(got[:, :, ffq:])
        full_down = double(w_down.astype(BF)[None], stages)
        full_down = jnp.take(full_down, reorder("ywc", "cyw"), axis=0).reshape(ffq, dm)

        def my_ff(vec):
            v = vec.reshape(ny, nx, nw, nz, nc, ffb).transpose(1, 3, 0, 2, 4, 5)
            return lax.dynamic_index_in_dim(v.reshape(nquad, ffq), quad_at, 0, False)

        my_s_up, my_s_gate = my_ff(s_up), my_ff(s_gate)
        my_gain = lax.dynamic_index_in_dim(s_qk.reshape(nline, hcols), line_at, 0, False)

        def to_row(value):
            keep = lax.dynamic_index_in_dim(value, c_at, 0, False)
            send = lax.dynamic_index_in_dim(value, 1 - c_at, 0, False)
            return jnp.concatenate([keep, lax.ppermute(send, "c", [(0, 1), (1, 0)])], axis=0)

        def from_row(value, send_type):
            keep, send = value[:seg], value[seg:]
            other = lax.ppermute(send.astype(send_type), "c", [(0, 1), (1, 0)])
            pair = jnp.stack([keep, other.astype(value.dtype)])
            return jnp.where(c_at == 0, pair, pair[::-1])

        docs = doc_ids.astype(BF)
        extra = jnp.zeros((nseq, 16, dm), BF).at[:, 0, :seg].set(docs)
        ext = jnp.concatenate([tokens, extra], axis=1)
        mine = to_row(ext).reshape(2, seg + 16, dm)
        everyone = jnp.stack(gather_rel(mine, line, nline))
        row_tokens = everyone[:, :, :seg].reshape(nline * 2 * seg, dm)
        row_docs = everyone[:, :, seg, :seg].reshape(-1).astype(F32)
        peers = line_at ^ jnp.arange(nline)
        seg_at = 2 * peers[:, None] + jnp.stack([c_at, 1 - c_at])[None, :]
        index = (seg_at[:, :, None] * seg + jnp.arange(seg)).reshape(-1)
        start = jnp.sum((row_docs[None, :] < row_docs[:, None]).astype(jnp.int32), axis=1)
        pos = index - start
        allowed = (index[None, :] <= index[:, None]) & (index[None, :] >= start[:, None])
        frequency = 10000.0 ** (-jnp.arange(HEAD_DIM // 2, dtype=F32) / (HEAD_DIM // 2))
        angles = pos.astype(F32)[:, None] * frequency
        cosines, sines = jnp.cos(angles)[:, None, :], jnp.sin(angles)[:, None, :]
        nt = row_tokens.shape[0]
        x_low = mine[:, :seg].reshape(2 * seg, dm)
        x_row = x_low.astype(F32)

        pre = dot(row_tokens, full_qkv)

        def heads(t):
            return t.reshape(nt, nheads, HEAD_DIM)

        def unit_pair(q_pre, k_pre, gains):
            gains = gains.reshape(nheads, HEAD_DIM)
            return (
                head_unit(rotate(heads(q_pre), cosines, sines), gains),
                head_unit(rotate(heads(k_pre), cosines, sines), gains),
            )

        (q_unit, k_unit), unit_pull = jax.vjp(
            unit_pair, pre[:, :hcols], pre[:, hcols : 2 * hcols], my_gain
        )
        q_low, k_low = q_unit.astype(BF), k_unit.astype(BF)
        v_low = heads(pre[:, 2 * hcols :].astype(BF))
        scores = jnp.einsum("qhd,khd->hqk", q_low, k_low, preferred_element_type=F32) * score_scale
        scores = jnp.where(allowed[None], scores, NEG)
        peak = jnp.max(scores, axis=-1, keepdims=True)
        raw = jnp.where(allowed[None], jnp.exp(scores - peak), 0.0)
        probs = raw / jnp.sum(raw, axis=-1, keepdims=True)
        p_low = probs.astype(BF)
        attended = jnp.einsum("hqk,khd->qhd", p_low, v_low, preferred_element_type=F32)
        att_low = attended.astype(BF).reshape(nline, 2 * seg, hcols)
        got = place(exchange_rel([att_low[k] for k in range(nline)], line, nline), line_at)
        att_mine = got.transpose(1, 0, 2).reshape(2 * seg, dm)

        h_attn = dot(att_mine, full_out)
        h_one, attn_pull = jax.vjp(residual_step, h_attn, x_row, alpha_attn)
        h_low = jnp.concatenate(gather_rel(h_one.astype(BF), quad, nquad), axis=0)
        up, gate = dot(h_low, full_up), dot(h_low, full_gate)
        mixed, gate_pull = jax.vjp(gating, up, gate, my_s_up, my_s_gate)
        mixed_low = mixed.astype(BF)
        part = dot(mixed_low, full_down).reshape(nquad, 2 * seg, dm)
        h_mlp = sum_rel([part[k] for k in range(nquad)], quad, nquad)
        result, out_pull = jax.vjp(residual_step, h_mlp, h_one, alpha_mlp)
        hidden_out = from_row(result.astype(BF), BF)

        d_result = to_row(cotangent).astype(F32)
        d_hmlp, d_hone, g_alpha_mlp = out_pull(d_result)
        dm_low = jnp.concatenate(gather_rel(d_hmlp.astype(BF), quad, nquad), axis=0)
        d_mixed = dot_t(dm_low, full_down)
        d_up, d_gate, g_s_up, g_s_gate = gate_pull(d_mixed)
        du_low, dg_low = d_up.astype(BF), d_gate.astype(BF)
        part = dot_t(du_low, full_up) + dot_t(dg_low, full_gate)
        part = part.reshape(nquad, 2 * seg, dm)
        d_hone = d_hone + sum_rel([part[k] for k in range(nquad)], quad, nquad)
        g_down = tdot(mixed_low, dm_low).reshape(ny * nw * nc, ffb, dm)
        g_down = halve(jnp.take(g_down, reorder("cyw", "ywc"), axis=0), stages)[0]

        def ff_scatter(left, right):
            part = tdot(left, right).reshape(ndev, rows, ffq)
            part = jnp.take(part, reorder("cywxz", "yxwzc"), axis=0)
            part = halve(part.reshape(ny * nw * nc, nquad, rows, ffq), stages)[0].astype(BF)
            got = place(exchange_rel([part[k] for k in range(nquad)], quad, nquad), quad_at)
            got = got.reshape(nx, nz, rows, ny, nw, nc, ffb).transpose(2, 3, 0, 4, 1, 5, 6)
            return got.reshape(rows, ff).astype(F32)

        g_up, g_gate = ff_scatter(h_low, du_low), ff_scatter(h_low, dg_low)

        d_hattn, d_tokens, g_alpha_attn = attn_pull(d_hone)
        dh_low = d_hattn.astype(BF)

        def to_owner(part, kind=BF):
            part = jnp.take(part, reorder("cyxwz", "yxwzc"), axis=0)
            part = halve(part.reshape((nc, ny * nx, nline) + part.shape[1:]), bits("c", nc), kind)[0]
            part = sum_rel([part[k] for k in range(ny * nx)], ("y", "x"), ny * nx, kind)
            return sum_rel([part[k] for k in range(nline)], line, nline, kind)

        g_out = to_owner(tdot(att_mine, dh_low).reshape(ndev, rows, dm))
        d_att = dot_t(dh_low, full_out).astype(BF).reshape(2 * seg, nline, hcols).transpose(1, 0, 2)
        d_att = jnp.concatenate(
            exchange_rel(pick(d_att, line_at, nline), line, nline), axis=0
        ).reshape(nt, nheads, HEAD_DIM)
        delta = jnp.sum(d_att.astype(F32) * attended, axis=-1)
        d_probs = jnp.einsum("qhd,khd->hqk", d_att, v_low, preferred_element_type=F32)
        d_scores = (probs * (d_probs - delta.T[:, :, None])).astype(BF)
        d_q = score_scale * jnp.einsum("hqk,khd->qhd", d_scores, k_low, preferred_element_type=F32)
        d_k = score_scale * jnp.einsum("hqk,qhd->khd", d_scores, q_low, preferred_element_type=F32)
        d_v = jnp.einsum("hqk,qhd->khd", p_low, d_att, preferred_element_type=F32)
        d_qpre, d_kpre, g_sqk = unit_pull((d_q, d_k))
        d_qkv = jnp.concatenate([d_qpre, d_kpre, d_v.reshape(nt, hcols)], axis=1).astype(BF)
        part = dot_t(d_qkv, full_qkv).reshape(nline, 2 * seg, dm)
        tokens_grad = d_tokens + sum_rel([part[k] for k in range(nline)], line, nline)
        tokens_grad = from_row(tokens_grad, BF)
        g_qkv = tdot(row_tokens, d_qkv).reshape(ndev, rows, 3 * hcols)
        g_qkv = jnp.take(g_qkv, reorder("cyxwz", "yxwzc"), axis=0)
        g_qkv = halve(g_qkv.reshape(nc, ny * nx, nline, rows, 3 * hcols), bits("c", nc))[0]
        g_qkv = sum_rel([g_qkv[k] for k in range(ny * nx)], ("y", "x"), ny * nx).astype(BF)
        got = place(exchange_rel([g_qkv[k] for k in range(nline)], line, nline), line_at)
        got = got.reshape(nline, rows, 3, hcols).transpose(2, 1, 0, 3).reshape(3, rows, dm)
        g_query, g_key, g_value = got.astype(F32)

        def spread(vec, rank, count):
            return jnp.where(jnp.arange(count)[:, None] == rank, vec[None], 0.0)

        def ff_order(vec):
            v = spread(vec, quad_at, nquad).reshape(nx, nz, ny, nw, nc, ffb)
            return v.transpose(2, 0, 3, 1, 4, 5).reshape(ndev, ffb)

        vecs = jnp.concatenate(
            [
                spread(g_sqk, line_at, nline).reshape(ndev, -1),
                g_alpha_attn.reshape(ndev, -1),
                ff_order(g_s_up),
                ff_order(g_s_gate),
                g_alpha_mlp.reshape(ndev, -1),
            ],
            axis=1,
        )
        vecs = to_owner(vecs, F32)
        cuts = [rows, 2 * rows, 2 * rows + ffb, 2 * rows + 2 * ffb]
        g_sqk, g_alpha_attn, g_s_up, g_s_gate, g_alpha_mlp = jnp.split(vecs, cuts)
        return (
            hidden_out, tokens_grad, g_query, g_key, g_value, g_out, g_up, g_gate, g_down,
            g_sqk, g_alpha_attn, g_s_up, g_s_gate, g_alpha_mlp,
        )

    return body


VM = pl.BlockSpec(memory_space=pltpu.VMEM)
SM = pl.BlockSpec(memory_space=pltpu.SMEM)
HB = pl.BlockSpec(memory_space=pltpu.HBM)


def call(kernel, outs, args, hbm=(), hbm_out=(), scratch=(), flops=0, mib=60, after=()):
    moved = sum(math.prod(a.shape) * a.dtype.itemsize for a in args)
    moved += sum(math.prod(s) * jnp.dtype(d).itemsize for s, d in outs)
    count = len(args)

    def run(*refs):
        kernel(*refs[:count], *refs[count + len(after) :])

    specs = [SM] + [HB if i in hbm else VM for i in range(1, count)]
    specs += [pl.BlockSpec(memory_space=pl.ANY)] * len(after)
    return pl.pallas_call(
        run,
        out_shape=[jax.ShapeDtypeStruct(s, d) for s, d in outs],
        in_specs=specs,
        out_specs=[HB if i in hbm_out else VM for i in range(len(outs))],
        scratch_shapes=list(scratch),
        compiler_params=pltpu.CompilerParams(vmem_limit_bytes=mib << 20),
        cost_estimate=pl.CostEstimate(flops=flops, bytes_accessed=moved, transcendentals=0),
    )(*args, *after)


def row_norm(v):
    return lax.rsqrt(jnp.mean(v * v, axis=-1, keepdims=True) + EPS)


def sphere_back(dy, y, norm):
    return (dy - y * jnp.mean(dy * y, axis=-1, keepdims=True)) * norm


def make_kernels(sizes):
    ny, nx, nw, nz, nc = sizes
    ndev = ny * nx * nw * nz * nc
    nyx, nline = ny * nx, nw * nz
    ndpc = nyx * nc
    line, yx, dpc = ("w", "z"), ("y", "x"), ("y", "x", "c")

    def swap(value, axes, count, k):
        return lax.ppermute(value, axes, [(i, i ^ k) for i in range(count)])

    def exchange(chunks, axes, count):
        return [chunks[0]] + [swap(chunks[k], axes, count, k) for k in range(1, count)]

    def gather(value, axes, count):
        return exchange([value] * count, axes, count)

    def body(
        tokens, doc_ids, w_query, w_key, w_value, w_out, w_up, w_gate, w_down,
        s_qk, alpha_attn, s_up, s_gate, alpha_mlp, cotangent,
    ):
        nseq, seg, dm = tokens.shape
        rows = w_query.shape[0]
        ff = w_up.shape[1]
        ffq, ffb = ff // nline, ff // ndev
        sub = nc * ffb
        hc = dm // nline
        nheads = HEADS // nline
        nt = nline * 2 * seg
        tk = 2 * seg
        pad = 16
        ext = seg + pad
        scale = math.sqrt(HEAD_DIM)
        tile = 256

        at = [lax.axis_index(a) for a in "yxwzc"]
        ranks = jnp.stack(at + [lax.axis_index(yx), lax.axis_index(line)])
        ranks = ranks.astype(jnp.int32)

        def pack_tokens(rk, tok, docs, keep, send):
            c = rk[4]
            first = lax.broadcasted_iota(jnp.int32, (pad, dm), 0) == 0
            for out, which in ((keep, c), (send, 1 - c)):
                out[:seg] = tok[which]
                out[seg:] = jnp.where(first, docs[which], 0.0).astype(BF)

        def ff_cols(rk, k):
            runs = [(d * nline + (rk[6] ^ k)) * sub for d in range(nyx)]
            return [pl.ds(pl.multiple_of(run, 128), sub) for run in runs]

        def pack_weights(rk, wq, wk, wv, wu, wg, wo, gain, su, sg, *outs):
            for k in range(nline):
                out, out_ff = outs[k], outs[nline + k]
                cols = pl.ds(pl.multiple_of((rk[6] ^ k) * hc, 128), hc)
                for i, w in enumerate((wq, wk, wv)):
                    out[:, i * hc : (i + 1) * hc] = w[:, cols].astype(BF)
                for d, cols in enumerate(ff_cols(rk, k)):
                    for i, w in enumerate((wu, wg)):
                        here = i * ffq + d * sub
                        out_ff[:, here : here + sub] = w[:, cols].astype(BF)
                out_ff[:, 2 * ffq :] = wo[...].astype(BF)
            outs = outs[nline:]
            outs[nline][...] = gain[:, pl.ds(pl.multiple_of(rk[6] * hc, 128), hc)]
            for d, cols in enumerate(ff_cols(rk, 0)):
                here = slice(d * sub, (d + 1) * sub)
                outs[nline + 1][:, here] = su[:, cols]
                outs[nline + 2][:, here] = sg[:, cols]

        docs = jnp.pad(doc_ids.astype(F32), ((0, 0), (0, dm - seg))).reshape(nseq, 1, dm)
        keep, send = call(pack_tokens, [((ext, dm), BF)] * 2, (ranks, tokens, docs))

        def join_tokens(rk, near, far, out):
            out[:seg] = near[:seg]
            out[seg:tk] = far[:seg]
            row = lax.broadcasted_iota(jnp.int32, (pad, dm), 0)
            ids = far[seg:].astype(F32)[:1]
            out[tk:] = jnp.where(row == 1, ids, near[seg:].astype(F32)).astype(BF)

        (mine,) = call(join_tokens, [((tk + pad, dm), BF)], (ranks, keep, swap(send, "c", nc, 1)))
        packed = call(
            pack_weights,
            [((rows, 3 * hc), BF)] * nline
            + [((rows, 2 * ffq + dm), BF)] * nline
            + [((1, hc), F32)]
            + [((1, ffq), F32)] * 2,
            (ranks, w_query, w_key, w_value, w_up, w_gate, w_out, s_qk.reshape(1, dm))
            + (s_up.reshape(1, ff), s_gate.reshape(1, ff)),
            after=(keep,),
        )
        packed, packed_ff, (my_gain, my_su, my_sg) = (
            packed[:nline], packed[nline : 2 * nline], packed[2 * nline :]
        )

        w_got = exchange(packed, line, nline)
        ff_got = exchange(packed_ff, line, nline)
        pieces = gather(mine, line, nline)

        def stack(rk, *refs):
            for k in range(nline):
                refs[nline][k * rows : (k + 1) * rows, :] = refs[k][...]

        (got,) = call(stack, [((ffb, 3 * hc), BF)], (ranks, *w_got))
        qkv_full = lax.all_gather(got, dpc, axis=0, tiled=True)

        def stack_ff(rk, *refs):
            parts, (wd, out) = refs[:nline], refs[nline:]
            for k in range(nline):
                out[k * rows : (k + 1) * rows, : 2 * ffq + dm] = parts[k][...]
            out[:, 2 * ffq + dm :] = wd[...].astype(BF)

        (got,) = call(
            stack_ff,
            [((ffb, 2 * ffq + 2 * dm), BF)],
            (ranks, *ff_got, w_down),
            after=(got,),
        )
        ff_full = lax.all_gather(got, dpc, axis=0, tiled=True)

        place = jnp.arange(nt, dtype=F32)[:, None]
        freq = 10000.0 ** (-jnp.arange(HEAD_DIM // 2, dtype=F32) / (HEAD_DIM // 2))
        angles = place * freq
        cosines, sines = jnp.cos(angles), jnp.sin(angles)
        reps = 128 // HEAD_DIM
        table = jnp.concatenate(
            [cosines] * (2 * reps) + [-sines, sines] * reps, axis=1
        )
        table_hi = table.astype(BF)
        table_lo = (table - table_hi.astype(F32)).astype(BF)

        def natural(rk, src, cols, dst, sems):
            copies = []
            for b in range(ndpc):
                for k in range(nline):
                    row = ((b // nc) * nline + (rk[6] ^ k)) * nc + b % nc
                    row = pl.ds(pl.multiple_of(row * rows, 32), rows)
                    block = src.at[pl.ds((b * nline + k) * rows, rows), cols]
                    copies.append(pltpu.make_async_copy(block, dst.at[row], sems.at[len(copies)]))
            return copies

        def heads_swap(v, low):
            width = v.shape[1]
            half = HEAD_DIM // 2
            return jnp.where(low, pltpu.roll(v, width - half, 1), pltpu.roll(v, half, 1))

        def low_half():
            lane = lax.broadcasted_iota(jnp.int32, (nt, hc), 1)
            return lane % HEAD_DIM < HEAD_DIM // 2

        def token_index(rk, axis, shape):
            t = lax.broadcasted_iota(jnp.int32, shape, axis)
            peer = (t // tk) ^ rk[6]
            core = ((t // seg) % 2) ^ rk[4]
            return (peer * 2 + core) * seg + t % seg

        def allowed_keys(rk, start):
            key = token_index(rk, 1, (1, nt))
            query = token_index(rk, 0, (nt, 1))
            return (key <= query) & (key.astype(F32) >= start)

        def attn_forward(rk, *refs):
            ext_refs, refs = refs[:nline], refs[nline:]
            stack, gain, t_hi, t_lo = refs[:4]
            att_ref, refs = refs[4], refs[5:]
            x_ref, w_ref, rq_ref, rk_ref, q_ref, k_ref, v_ref, bias_ref, cs_ref = refs[:9]
            full_ref, inv_ref, sems = refs[9:]
            copies = natural(rk, stack, pl.ds(0, 3 * hc), w_ref, sems)
            for copy in copies:
                copy.start()
            ids = []
            for k in range(nline):
                x_ref[k * tk : (k + 1) * tk, :] = ext_refs[k][:tk, :]
                tail = ext_refs[k][tk:, :128].astype(F32)
                ids += [tail[:1, :seg], tail[1:2, :seg]]
            ids = jnp.concatenate(ids, axis=1)
            same = lax.broadcasted_iota(jnp.int32, (nt, nt), 0) == lax.broadcasted_iota(
                jnp.int32, (nt, nt), 1
            )
            ids_col = jnp.sum(jnp.where(same, ids, 0.0), axis=1, keepdims=True)
            start = jnp.sum(jnp.where(ids < ids_col, 1.0, 0.0), axis=1, keepdims=True)
            pos = token_index(rk, 0, (nt, 1)) - start.astype(jnp.int32)
            hot = (lax.broadcasted_iota(jnp.int32, (nt, nt), 1) == pos).astype(F32).astype(BF)
            cs = dot(hot, t_hi[...]) + dot(hot, t_lo[...])
            cs_ref[...] = cs
            cos = jnp.concatenate([cs[:, :128]] * (hc // 128), axis=1)
            sin = jnp.concatenate([cs[:, 128:]] * (hc // 128), axis=1)
            bias_ref[...] = jnp.where(allowed_keys(rk, start), 0.0, NEG).astype(BF)
            for copy in copies:
                copy.wait()
            low = low_half()
            for i, (raw_ref, unit_ref) in enumerate(((rq_ref, q_ref), (rk_ref, k_ref))):
                pre = dot(x_ref[...], w_ref[:, i * hc : (i + 1) * hc])
                turned = pre * cos + heads_swap(pre, low) * sin
                raw_ref[...] = turned
                for h in range(nheads):
                    at_h = slice(h * HEAD_DIM, (h + 1) * HEAD_DIM)
                    part = turned[:, at_h]
                    norm = lax.rsqrt(jnp.sum(part * part, axis=1, keepdims=True) + EPS)
                    unit = (gain[:, at_h] * part * norm).astype(BF)
                    unit_ref[:, at_h] = unit * (scale if i == 0 else 1)
            v_ref[...] = dot(x_ref[...], w_ref[:, 2 * hc :]).astype(BF)
            for h in range(nheads):
                at_h = slice(h * HEAD_DIM, (h + 1) * HEAD_DIM)
                raw = jnp.exp(dot_t(q_ref[:, at_h], k_ref[:, at_h]) + bias_ref[...].astype(F32))
                inv = 1.0 / jnp.sum(raw, axis=1, keepdims=True)
                att_h = dot(raw.astype(BF), v_ref[:, at_h]) * inv
                full_ref[:, at_h] = att_h
                att_ref[:, at_h] = att_h.astype(BF)
                inv_ref[:, h : h + 1] = inv

        unit = ((nt, hc), BF)
        outs = call(
            attn_forward,
            [unit, ((nt, dm), BF), ((dm, 3 * hc), BF), ((nt, hc), F32), ((nt, hc), F32)]
            + [unit, unit, unit, ((nt, nt), BF), ((nt, 256), F32), ((nt, hc), F32), ((nt, 128), F32)],
            (ranks, *pieces, qkv_full, my_gain, table_hi, table_lo),
            hbm=(1 + nline,),
            scratch=[pltpu.SemaphoreType.DMA((ndev,))],
            flops=2 * nt * dm * 3 * hc + 4 * nt * nt * hc,
        )
        att, outs = outs[0], outs[1:]
        x_all, w_qkv, r_q, r_k, q_low, k_low, v_low, bias, cs, att_full, inv = outs
        att_got = gather(att, line, nline)

        def own_x(ext_ref):
            return ext_ref[:tk].astype(F32)

        alpha_a, alpha_m = alpha_attn.reshape(1, dm), alpha_mlp.reshape(1, dm)
        full = ((tk, dm), F32)

        def load_out(rk, stack, wo, sems):
            return natural(rk, stack, pl.ds(2 * ffq, dm), wo, sems)

        def load_ff(rk, stack, scratch):
            wug, wd, sems, sem_d = scratch
            down = stack.at[:, pl.ds(2 * ffq + dm, dm)]
            return (
                natural(rk, stack, pl.ds(0, 2 * ffq), wug, sems),
                [pltpu.make_async_copy(down, wd, sem_d.at[0])],
            )

        w_scratch = [pltpu.VMEM((dm, 2 * ffq), BF), pltpu.VMEM((ffq, dm), BF)]
        w_scratch += [pltpu.SemaphoreType.DMA((ndev,)), pltpu.SemaphoreType.DMA((1,))]
        out_scratch = [pltpu.VMEM((dm, dm), BF), pltpu.SemaphoreType.DMA((ndev,))]

        def gate_terms(gate, sg):
            v = sg * gate
            s = 1.0 / (1.0 + jnp.exp(-v))
            return v, s

        def forward(rk, *refs):
            att_refs, refs = refs[:nline], refs[nline:]
            x_ref, alpha, stack, su, sg = refs[:5]
            parts, refs = refs[5 : 5 + nline], refs[5 + nline :]
            h_all, up_ref, gate_ref, mixed_ref, one_ref, raw_ref = refs[:6]
            scratch = refs[6:]
            wug, wd = scratch[:2]
            w, a_ref = scratch[4], scratch[6]
            first, third = load_ff(rk, stack, scratch[:4])
            out_copies = load_out(rk, stack, w, scratch[5])
            for copy in out_copies + first + third:
                copy.start()
            for k in range(nline):
                spot = pl.ds(pl.multiple_of((rk[6] ^ k) * hc, hc), hc)
                for m in range(nline):
                    block = att_refs[k][(m ^ k) * tk : ((m ^ k) + 1) * tk, :]
                    a_ref[m * tk : (m + 1) * tk, spot] = block
            for copy in out_copies:
                copy.wait()
            for m in range(nline):
                total = dot(a_ref[m * tk : (m + 1) * tk, :], w[...])
                x = x_ref[m * tk : (m + 1) * tk, :].astype(F32)
                z = x + alpha[...] * (total * row_norm(total) - x)
                one = z * row_norm(z)
                h_all[m * tk : (m + 1) * tk, :] = one.astype(BF)
                if m == 0:
                    one_ref[...] = one
                    raw_ref[...] = total
            for copy in first:
                copy.wait()

            @pl.loop(0, ffq // tile, unroll=True)
            def _(j):
                cols = pl.ds(pl.multiple_of(j * tile, tile), tile)
                up = dot(h_all[...], wug[:, cols])
                gate = dot(h_all[...], wug[:, pl.ds(pl.multiple_of(ffq + j * tile, tile), tile)])
                up_ref[:, cols] = up.astype(BF)
                gate_ref[:, cols] = gate.astype(BF)
                v, s = gate_terms(gate, sg[:, cols])
                mixed_ref[:, cols] = (su[:, cols] * up * (v * s)).astype(BF)

            for copy in third:
                copy.wait()

            @pl.loop(0, dm // tile, unroll=True)
            def _(j):
                cols = pl.ds(pl.multiple_of(j * tile, tile), tile)
                part = dot(mixed_ref[...], wd[:, cols])
                for k in range(nline):
                    parts[k][:, cols] = part[k * tk : (k + 1) * tk].astype(parts[k].dtype)

        part_shapes = [((tk, dm), F32)] + [((tk, dm), BF)] * (nline - 1)
        outs = call(
            forward,
            part_shapes
            + [((nt, dm), BF), ((nt, ffq), BF), ((nt, ffq), BF), ((nt, ffq), BF), full, full],
            (ranks, *att_got, x_all, alpha_a, ff_full, my_su, my_sg),
            hbm=(3 + nline,),
            scratch=w_scratch + out_scratch + [pltpu.VMEM((nt, dm), BF)],
            flops=6 * nt * dm * ffq + 2 * nt * dm * dm,
        )
        mlp_parts, (h_all, up, gate, mixed, h_one, h_attn) = outs[:nline], outs[nline:]
        mlp_got = exchange(mlp_parts, line, nline)

        def split_rows(rk, cot, keep, send):
            keep[...] = cot[rk[4]]
            send[...] = cot[1 - rk[4]]

        half_low = ((seg, dm), BF)
        cot_keep, cot_send = call(split_rows, [half_low] * 2, (ranks, cotangent))
        cot_recv = swap(cot_send, "c", nc, 1)

        def mlp_update(rk, *refs):
            parts, refs = refs[:nline], refs[nline:]
            one_ref, alpha_ref, ck, cr, hid_keep, hid_send, dm_ref, direct, g_alpha = refs
            h = parts[0][...]
            for k in range(1, nline):
                h = h + parts[k][...].astype(F32)
            one, alpha = one_ref[...], alpha_ref[...]
            norm_h = row_norm(h)
            b = h * norm_h
            gap = b - one
            z = one + alpha * gap
            norm_z = row_norm(z)
            y = z * norm_z
            low = y.astype(BF)
            hid_keep[...] = low[:seg]
            hid_send[...] = low[seg:]
            dy = jnp.concatenate([ck[...], cr[...]], axis=0).astype(F32)
            dz = sphere_back(dy, y, norm_z)
            g_alpha[...] = jnp.sum(dz * gap, axis=0, keepdims=True)
            direct[...] = dz * (1.0 - alpha)
            dm_ref[...] = sphere_back(dz * alpha, b, norm_h).astype(BF)

        outs = call(
            mlp_update,
            [half_low, half_low, ((tk, dm), BF), full, ((1, dm), F32)],
            (ranks, *mlp_got, h_one, alpha_m, cot_keep, cot_recv),
        )
        hid_keep, hid_send, dm_low, d_one_direct, g_alpha_mlp = outs
        hid_recv = swap(hid_send, "c", nc, 1)
        dm_got = gather(dm_low, line, nline)

        def ff_back(rk, late, *refs):
            d_refs, stack = refs[:nline], refs[nline]
            su_ref, sg_ref, up_ref, gate_ref = refs[nline + 1 : nline + 5]
            refs = refs[nline + 5 :]
            parts, (d_all, dug, g_su, g_sg) = refs[:nline], refs[nline : nline + 4]
            scratch = refs[nline + 4 :]
            wug, wd = scratch[:2]
            first, third = load_ff(rk, stack, scratch)
            for copy in third + late[:2] + first + late[2:]:
                copy.start()
            for k in range(nline):
                d_all[k * tk : (k + 1) * tk, :] = d_refs[k][...]
            for copy in third + late[:2]:
                copy.wait()

            @pl.loop(0, ffq // tile, unroll=True)
            def _(j):
                cols = pl.ds(pl.multiple_of(j * tile, tile), tile)
                d_mixed = dot_t(d_all[...], wd[cols, :])
                up, gate = up_ref[:, cols].astype(F32), gate_ref[:, cols].astype(F32)
                su, sg = su_ref[:, cols], sg_ref[:, cols]
                v, s = gate_terms(gate, sg)
                silu = v * s
                dug[:, cols] = (d_mixed * su * silu).astype(BF)
                slope = d_mixed * su * up * (s * (1.0 + v * (1.0 - s)))
                other = pl.ds(pl.multiple_of(ffq + j * tile, tile), tile)
                dug[:, other] = (slope * sg).astype(BF)
                g_su[:, cols] = jnp.sum(d_mixed * up * silu, axis=0, keepdims=True)
                g_sg[:, cols] = jnp.sum(slope * gate, axis=0, keepdims=True)

            for copy in first:
                copy.wait()

            @pl.loop(0, dm // tile, unroll=True)
            def _(j):
                cols = pl.ds(pl.multiple_of(j * tile, tile), tile)
                part = dot_t(dug[...], wug[cols, :])
                for k in range(nline):
                    parts[k][:, cols] = part[k * tk : (k + 1) * tk].astype(parts[k].dtype)


        def stored(rk, g_ref, out, width, block, sems):
            d, peer, c = block // (nline * nc), (block // nc) % nline, block % nc
            spot = ((d * nc + c) * nline + (peer ^ rk[6])) * rows
            src = g_ref.at[pl.ds(pl.multiple_of(block * rows, 32), rows)]
            dst = out.at[pl.ds(pl.multiple_of(spot, 32), rows), pl.ds(0, width)]
            return pltpu.make_async_copy(src, dst, sems.at[block])

        def outer_ff(rk, h, dug, mixed_ref, d_all, out, g_ref, g_down_ref, sems, sem_d):
            def store(block):
                return stored(rk, g_ref, out, 2 * ffq, block, sems)

            @pl.loop(0, dm // tile, unroll=True)
            def _(j):
                cols = pl.ds(pl.multiple_of(j * tile, tile), tile)
                g_ref[cols, :] = tdot(h[:, cols], dug[...]).astype(BF)
                for i in range(tile // rows):
                    store(j * (tile // rows) + i).start()

            @pl.loop(0, ffq // tile, unroll=True)
            def _(j):
                cols = pl.ds(pl.multiple_of(j * tile, tile), tile)
                g_down_ref[cols, :] = tdot(mixed_ref[:, cols], d_all[...]).astype(BF)

            down = pltpu.make_async_copy(g_down_ref, out.at[:, pl.ds(2 * ffq, dm)], sem_d.at[0])
            down.start()
            down.wait()

            @pl.loop(0, ndev)
            def _(block):
                store(block).wait()

        def ff_back_all(rk, *refs):
            ins, refs = list(refs[: nline + 7]), refs[nline + 7 :]
            parts, (g_su, g_sg, out) = refs[:nline], refs[nline : nline + 3]
            d_all, dug, wug, wd, s_u, s_d, g_ref, g_down_ref, sems, sem_d = refs[nline + 3 : nline + 13]
            *held, late_sems = refs[nline + 13 :]
            late = []
            for i, dst in enumerate(held):
                late.append(pltpu.make_async_copy(ins[nline + 3 + i], dst, late_sems.at[i]))
            ins[nline + 3 :] = held
            scratch = (d_all, dug, g_su, g_sg, wug, wd, s_u, s_d)
            ff_back(rk, late, *ins[: nline + 5], *parts, *scratch)
            h, mixed_ref = ins[nline + 5 :]
            for copy in late[2:]:
                copy.wait()
            outer_ff(rk, h, dug, mixed_ref, d_all, out, g_ref, g_down_ref, sems, sem_d)

        *one_parts, g_su, g_sg, g_ff = call(
            ff_back_all,
            part_shapes + [((1, ffq), F32)] * 2 + [((dm, 2 * ffq + dm), BF)],
            (ranks, *dm_got, ff_full, my_su, my_sg, up, gate, h_all, mixed),
            hbm=(1 + nline, 4 + nline, 5 + nline, 6 + nline, 7 + nline),
            hbm_out=(nline + 2,),
            scratch=[pltpu.VMEM((nt, dm), BF), pltpu.VMEM((nt, 2 * ffq), BF)]
            + w_scratch
            + [pltpu.VMEM((dm, 2 * ffq), BF), pltpu.VMEM((ffq, dm), BF)]
            + [pltpu.SemaphoreType.DMA((ndev,)), pltpu.SemaphoreType.DMA((1,))]
            + [pltpu.VMEM((nt, ffq), BF)] * 2
            + [pltpu.VMEM((nt, dm), BF), pltpu.VMEM((nt, ffq), BF)]
            + [pltpu.SemaphoreType.DMA((4,))],
            flops=12 * nt * dm * ffq,
        )
        one_got = exchange(one_parts, line, nline)
        g_ff = lax.psum_scatter(g_ff, dpc, scatter_dimension=0, tiled=True)
        def attn_update_back(rk, *refs):
            parts, refs = refs[:nline], refs[nline:]
            direct_in, one_ref, raw_ref, ext_ref, alpha_ref, stack = refs[:6]
            d_outs, (dh_ref, direct, g_alpha, w, sems) = refs[6 : 6 + nline], refs[6 + nline :]
            copies = load_out(rk, stack, w, sems)
            for copy in copies:
                copy.start()
            d = direct_in[...] + parts[0][...]
            for k in range(1, nline):
                d = d + parts[k][...].astype(F32)
            one, raw, alpha = one_ref[...], raw_ref[...], alpha_ref[...]
            x = own_x(ext_ref)
            norm_raw = row_norm(raw)
            b = raw * norm_raw
            gap = b - x
            norm_z = row_norm(x + alpha * gap)
            dz = sphere_back(d, one, norm_z)
            g_alpha[...] = jnp.sum(dz * gap, axis=0, keepdims=True)
            direct[...] = dz * (1.0 - alpha)
            dh_ref[...] = sphere_back(dz * alpha, b, norm_raw).astype(BF)
            for copy in copies:
                copy.wait()
            for k in range(nline):
                w_k = w[pl.ds(pl.multiple_of((rk[6] ^ k) * hc, hc), hc), :]
                d_outs[k][...] = dot_t(dh_ref[...], w_k).astype(BF)

        outs = call(
            attn_update_back,
            [((tk, hc), BF)] * nline + [((tk, dm), BF), full, ((1, dm), F32)],
            (ranks, *one_got, d_one_direct, h_one, h_attn, mine, alpha_a, ff_full),
            hbm=(6 + nline,),
            scratch=out_scratch,
            flops=2 * tk * dm * dm,
        )
        d_att_parts, (dh_low, d_x_direct, g_alpha_attn) = outs[:nline], outs[nline:]
        d_att = exchange(d_att_parts, line, nline)

        def attn_back(rk, late, *refs):
            d_refs, refs = refs[:nline], refs[nline:]
            w_ref, rq_ref, rk_ref, q_ref, k_ref, v_ref, bias_ref, cs_ref, gain = refs[:9]
            full_ref, inv_ref, refs = refs[9], refs[10], refs[11:]
            parts, (d_ref, g_gain, do_ref, dq_ref, dk_ref) = refs[:nline], refs[nline:]
            for k in range(nline):
                do_ref[k * tk : (k + 1) * tk, :] = d_refs[k][...]
            for h in range(nheads):
                at_h = slice(h * HEAD_DIM, (h + 1) * HEAD_DIM)
                q, key, do = q_ref[:, at_h], k_ref[:, at_h], do_ref[:, at_h]
                raw = jnp.exp(dot_t(q, key) + bias_ref[...].astype(F32))
                p = raw * inv_ref[:, h : h + 1]
                delta = jnp.sum(do.astype(F32) * full_ref[:, at_h], axis=1, keepdims=True)
                ds = (p * (dot_t(do, v_ref[:, at_h]) - delta)).astype(BF)
                p = p.astype(BF)
                at_v = slice(2 * hc + h * HEAD_DIM, 2 * hc + (h + 1) * HEAD_DIM)
                d_ref[:, at_v] = tdot(p, do).astype(BF)
                dq_ref[:, at_h] = scale * dot(ds, key)
                dk_ref[:, at_h] = tdot(ds, q)
            for copy in late:
                copy.wait()
            cs = cs_ref[...]
            cos = jnp.concatenate([cs[:, :128]] * (hc // 128), axis=1)
            sin = jnp.concatenate([cs[:, 128:]] * (hc // 128), axis=1)
            low = low_half()
            for i, (raw_ref, g_ref) in enumerate(((rq_ref, dq_ref), (rk_ref, dk_ref))):
                for h in range(nheads):
                    at_h = slice(h * HEAD_DIM, (h + 1) * HEAD_DIM)
                    turned, g = raw_ref[:, at_h], g_ref[:, at_h]
                    norm = lax.rsqrt(jnp.sum(turned * turned, axis=1, keepdims=True) + EPS)
                    unit = turned * norm
                    term = jnp.sum(g * unit, axis=0, keepdims=True)
                    g_gain[:, at_h] = term if i == 0 else g_gain[:, at_h] + term
                    g = g * gain[:, at_h]
                    g_ref[:, at_h] = norm * (g - unit * jnp.sum(unit * g, axis=1, keepdims=True))
                g = g_ref[...]
                d_ref[:, i * hc : (i + 1) * hc] = (g * cos - heads_swap(g, low) * sin).astype(BF)

            @pl.loop(0, dm // tile, unroll=True)
            def _(j):
                cols = pl.ds(pl.multiple_of(j * tile, tile), tile)
                part = dot_t(d_ref[...], w_ref[cols, :])
                for k in range(nline):
                    parts[k][:, cols] = part[k * tk : (k + 1) * tk].astype(parts[k].dtype)


        at_line = ranks[6]
        mine_ff = (jnp.arange(nline) == at_line)[None, :, None, None]

        def ff_owner(vec):
            return jnp.where(mine_ff, vec.reshape(nyx, 1, nc, ffb), 0.0).reshape(ndev, ffb)

        misc = [v.reshape(ndev, rows) for v in (g_alpha_attn, g_alpha_mlp)]
        misc = jnp.pad(jnp.concatenate(misc, axis=1), ((0, 0), (0, ffb - 2 * rows)))
        vecs = jnp.stack([ff_owner(g_su), ff_owner(g_sg), misc], axis=1).astype(BF)
        vecs = jnp.pad(vecs, ((0, 0), (0, rows - 3), (0, 0))).reshape(dm, ffb)

        wide = 3 * hc + ffb

        def outer_out(rk, dh, *refs):
            parts, outs, (g_ref, sems) = refs[:nline], refs[nline : nline + 2], refs[nline + 2 :]
            for k in range(nline):
                spot = pl.ds(pl.multiple_of((rk[6] ^ k) * hc, hc), hc)
                own = parts[k][k * tk : (k + 1) * tk, :]
                g_ref[spot, :] = tdot(own, dh[...]).astype(BF)
            copies = []
            for cr in range(nc):
                for a in range(nyx):
                    for b in range(nline):
                        row = ((rk[5] ^ a) * nline + (rk[6] ^ b)) * nc + (rk[4] ^ cr)
                        src = g_ref.at[pl.ds(pl.multiple_of(row * rows, 32), rows)]
                        dst = outs[cr].at[pl.ds((a * nline + b) * rows, rows)]
                        copies.append(pltpu.make_async_copy(src, dst, sems.at[len(copies)]))
            for copy in copies:
                copy.start()
            for copy in copies:
                copy.wait()

        keep, send = call(
            outer_out,
            [((dm // nc, dm), BF)] * nc,
            (ranks, dh_low, *att_got),
            hbm_out=(0, 1),
            scratch=[pltpu.VMEM((dm, dm), BF), pltpu.SemaphoreType.DMA((ndev,))],
            flops=2 * tk * dm * dm,
        )

        def core_add(rk, a, b, *outs):
            for i in range(nyx):
                here = slice(i * ffb, (i + 1) * ffb)
                outs[i][...] = (a[here, :].astype(F32) + b[here, :].astype(F32)).astype(BF)

        out_sum = call(
            core_add, [((ffb, dm), BF)] * nyx, (ranks, keep, swap(send, "c", nc, 1))
        )
        out_got = exchange(out_sum, yx, nyx)

        def outer_last(rk, x_ref, d_ref, vec_ref, g_gain, out, g_ref, sems):

            def store(block):
                return stored(rk, g_ref, out, wide, block, sems)

            g_ref[:, 3 * hc : wide] = vec_ref[...]
            third = lax.broadcasted_iota(jnp.int32, (16, ffb), 0) == 2
            for i in range(hc // rows):
                spot = pl.ds(pl.multiple_of((rk[6] * (hc // rows) + i) * rows, 32), 16)
                run = [jnp.zeros((1, 2 * rows), F32), g_gain[:, i * rows : (i + 1) * rows]]
                run = jnp.concatenate(run + [jnp.zeros((1, ffb - 3 * rows), F32)], axis=1)
                held = g_ref[spot, 3 * hc : wide].astype(F32)
                g_ref[spot, 3 * hc : wide] = (held + jnp.where(third, run, 0.0)).astype(BF)

            @pl.loop(0, dm // tile, unroll=True)
            def _(j):
                cols = pl.ds(pl.multiple_of(j * tile, tile), tile)
                g_ref[cols, : 3 * hc] = tdot(x_ref[:, cols], d_ref[...]).astype(BF)
                for i in range(tile // rows):
                    store(j * (tile // rows) + i).start()

            @pl.loop(0, ndev)
            def _(block):
                store(block).wait()

        def attn_back_all(rk, *refs):
            ins, refs = list(refs[: nline + 13]), refs[nline + 13 :]
            parts, out = refs[:nline], refs[nline]
            d_ref, g_gain, do_ref, dq_ref, dk_ref, g_ref, sems = refs[nline + 1 : nline + 8]
            *held, late_sems = refs[nline + 8 :]
            late = []
            for i, (at_in, dst) in enumerate(zip(late_back, held)):
                late.append(pltpu.make_async_copy(ins[at_in - 1], dst, late_sems.at[i]))
                ins[at_in - 1] = dst
            for copy in late:
                copy.start()
            x_ref, vec_ref = ins[nline + 11 :]
            scratch = (d_ref, g_gain, do_ref, dq_ref, dk_ref)
            attn_back(rk, late, *ins[: nline + 11], *parts, *scratch)
            outer_last(rk, x_ref, d_ref, vec_ref, g_gain, out, g_ref, sems)

        late_back = [1 + nline, 2 + nline, 3 + nline, 8 + nline, 12 + nline]
        late_shapes = [((dm, 3 * hc), BF), ((nt, hc), F32), ((nt, hc), F32), ((nt, 256), F32)]
        late_shapes.append(((nt, dm), BF))

        *x_parts, g_last = call(
            attn_back_all,
            part_shapes + [((dm, wide), BF)],
            (ranks, *d_att, w_qkv, r_q, r_k, q_low, k_low, v_low, bias, cs, my_gain, att_full, inv)
            + (x_all, vecs),
            hbm=late_back,
            hbm_out=(nline,),
            scratch=[
                pltpu.VMEM((nt, 3 * hc), BF), pltpu.VMEM((1, hc), F32),
                pltpu.VMEM((nt, hc), BF), pltpu.VMEM((nt, hc), F32), pltpu.VMEM((nt, hc), F32),
                pltpu.VMEM((dm, wide), BF), pltpu.SemaphoreType.DMA((ndev,)),
                *[pltpu.VMEM(*shape) for shape in late_shapes], pltpu.SemaphoreType.DMA((5,)),
            ],
            flops=4 * nt * dm * 3 * hc + 10 * nt * nt * hc,
        )
        x_got = exchange(x_parts, line, nline)

        def finish_tokens(rk, *refs):
            parts, (direct, keep, send) = refs[:nline], refs[nline:]
            d = direct[...] + parts[0][...]
            for k in range(1, nline):
                d = d + parts[k][...].astype(F32)
            keep[...] = d[:seg]
            send[...] = d[seg:].astype(BF)

        x_keep, x_send = call(
            finish_tokens, [((seg, dm), F32), half_low], (ranks, *x_got, d_x_direct)
        )
        x_recv = swap(x_send, "c", nc, 1)

        def join_rows(rk, keep, recv, out):
            out[rk[4]] = keep[...].astype(out.dtype)
            out[1 - rk[4]] = recv[...].astype(out.dtype)

        (tokens_grad,) = call(join_rows, [((nseq, seg, dm), F32)], (ranks, x_keep, x_recv))
        (hidden_out,) = call(join_rows, [((nseq, seg, dm), BF)], (ranks, hid_keep, hid_recv))

        g_last = lax.psum_scatter(g_last, dpc, scatter_dimension=0, tiled=True)

        def split_ff(rk, g_ref, down, *outs):
            down[...] = g_ref[:, 2 * ffq :].astype(F32)
            for k in range(nline):
                outs[k][...] = g_ref[k * rows : (k + 1) * rows, : 2 * ffq]

        g_down, *g_parts = call(
            split_ff,
            [((ffb, dm), F32)] + [((rows, 2 * ffq), BF)] * nline,
            (ranks, g_ff),
            after=tuple(x_got[1:]),
        )
        g_parts = exchange(g_parts, line, nline)

        def split_last(rk, g_ref, *refs):
            parts, outs = refs[:nyx], refs[nyx:]
            for k in range(nline):
                here = slice(k * rows, (k + 1) * rows)
                outs[k][:, :wide] = g_ref[here, :]
                total = parts[0][here, :].astype(F32)
                for j in range(1, nyx):
                    total = total + parts[j][here, :].astype(F32)
                outs[k][:, wide:] = total.astype(BF)

        last = call(
            split_last,
            [((rows, wide + dm), BF)] * nline,
            (ranks, g_last, *out_got),
            after=tuple(g_parts[1:]),
        )
        last = exchange(last, line, nline)

        def place_last(rk, *refs):
            parts, ff_parts = refs[:nline], refs[nline : 2 * nline]
            outs, refs = refs[2 * nline : 2 * nline + 3], refs[2 * nline + 3 :]
            g_o, ff_outs, vec_outs = refs[0], refs[1:3], refs[3:]
            g_sum, v_sum = None, None
            for k in range(nline):
                cols = pl.ds(pl.multiple_of((rk[6] ^ k) * hc, 128), hc)
                for i in range(3):
                    outs[i][:, cols] = parts[k][:, i * hc : (i + 1) * hc].astype(F32)
                vec = parts[k][:16, 3 * hc : wide].astype(F32)
                part = parts[k][:, wide:].astype(F32)
                for d, cols in enumerate(ff_cols(rk, k)):
                    for i in range(2):
                        here = i * ffq + d * sub
                        ff_outs[i][:, cols] = ff_parts[k][:, here : here + sub].astype(F32)
                g_sum = part if g_sum is None else g_sum + part
                v_sum = vec if v_sum is None else v_sum + vec
            g_o[...] = g_sum
            vec_outs[0][...] = v_sum[:1]
            vec_outs[1][...] = v_sum[1:2]
            for i in range(3):
                vec_outs[2 + i][...] = v_sum[2:3, i * rows : (i + 1) * rows]

        g_query, g_key, g_value, g_out, g_up, g_gate, *vecs = call(
            place_last,
            [((rows, dm), F32)] * 4
            + [((rows, ff), F32)] * 2
            + [((1, ffb), F32)] * 2
            + [((1, rows), F32)] * 3,
            (ranks, *last, *g_parts),
        )
        g_s_up, g_s_gate, g_aa, g_am, g_sqk = [v.reshape(-1) for v in vecs]
        return (
            hidden_out, tokens_grad, g_query, g_key, g_value, g_out, g_up, g_gate, g_down,
            g_sqk, g_aa, g_s_up, g_s_gate, g_am,
        )

    return body


def make_body(sizes):
    plain, kernels = make_plain(sizes), make_kernels(sizes)
    ndev = math.prod(sizes)
    nline = sizes[2] * sizes[3]

    def body(*args):
        tokens, w_query, w_up = args[0], args[2], args[6]
        fits = w_query.shape[0] % 32 == 0 and (w_up.shape[1] // ndev) % 128 == 0
        fits = fits and (tokens.shape[2] // nline) % 256 == 0 and tokens.shape[1] == 64
        return (kernels if fits else plain)(*args)

    return body


def solution(mesh):
    ndp, nblk = mesh.shape["dp"], mesh.shape["blk"]
    sizes = (ndp // 2, 2, nblk // 4, 2, 2)
    fine = Mesh(mesh.devices.reshape(sizes), ("y", "x", "w", "z", "c"))
    rows, cols = ("y", "x"), ("w", "z", "c")
    flat = rows + cols
    seq = P(rows, cols, None)
    weight = P(flat, None)
    return jax.shard_map(
        make_body(sizes),
        mesh=fine,
        in_specs=(seq, P(rows, cols)) + (weight,) * 7 + (P(),) * 5 + (seq,),
        out_specs=(seq, seq) + (weight,) * 7 + (P(flat),) * 5,
        check_vma=False,
    )
```

```python
import math

import jax
import jax.numpy as jnp
from jax import lax
from jax.experimental import pallas as pl
from jax.experimental.pallas import tpu as pltpu
from jax.sharding import Mesh
from jax.sharding import PartitionSpec as P

HEADS = 16
HEAD_DIM = 64
EPS = 1e-06
NEG = -1e30
BF = jnp.bfloat16
F32 = jnp.float32


def dot(a, b):
    return jnp.dot(a, b, preferred_element_type=F32)


def dot_t(a, b):
    return lax.dot_general(a, b, (((1,), (1,)), ((), ())), preferred_element_type=F32)


def tdot(a, b):
    return lax.dot_general(a, b, (((0,), (0,)), ((), ())), preferred_element_type=F32)


def rotate(tensor, cosines, sines):
    half_dim = tensor.shape[-1] // 2
    front = tensor[..., :half_dim]
    behind = tensor[..., half_dim:]
    return jnp.concatenate(
        [front * cosines - behind * sines, behind * cosines + front * sines], axis=-1
    )


def sphere(tensor):
    return tensor * lax.rsqrt(jnp.mean(tensor * tensor, axis=-1, keepdims=True) + EPS)


def head_unit(tensor, gains):
    return gains * tensor * lax.rsqrt(jnp.sum(tensor * tensor, axis=-1, keepdims=True) + EPS)


def residual_step(branch, residual_in, alpha):
    return sphere(residual_in + alpha * (sphere(branch) - residual_in))


def gating(up_proj, gate_proj, scale_up, scale_gate):
    return scale_up * up_proj * jax.nn.silu(scale_gate * gate_proj)


def make_plain(sizes):
    ny, nx, nw, nz, nc = sizes
    ndev = ny * nx * nw * nz * nc
    line = ("w", "z")
    nline = nw * nz
    quad = ("x", "z")
    nquad = nx * nz

    def swap(value, axes, count, k):
        return lax.ppermute(value, axes, [(i, i ^ k) for i in range(count)])

    def gather_rel(value, axes, count):
        return [value] + [swap(value, axes, count, k) for k in range(1, count)]

    def exchange_rel(chunks, axes, count):
        return [chunks[0]] + [swap(chunks[k], axes, count, k) for k in range(1, count)]

    def sum_rel(chunks, axes, count, kind=BF):
        got = exchange_rel([c.astype(kind) for c in chunks], axes, count)
        total = chunks[0].astype(F32)
        for piece in got[1:]:
            total = total + piece.astype(F32)
        return total

    def double(value, stages):
        for axis, count, k in stages:
            value = jnp.concatenate([value, swap(value, axis, count, k)], axis=0)
        return value

    def halve(value, stages, kind=BF):
        for axis, count, k in stages[::-1]:
            half = value.shape[0] // 2
            other = swap(value[half:].astype(kind), axis, count, k)
            value = value[:half].astype(F32) + other.astype(F32)
        return value

    def bits(axis, count):
        return [(axis, count, 1 << b) for b in range(count.bit_length() - 1)]

    def ranks(order):
        count = dict(y=ny, x=nx, w=nw, z=nz, c=nc)
        shape = [count[axis] for axis in order]
        found = {}
        for i, axis in enumerate(order):
            shifted = jnp.arange(count[axis]) ^ lax.axis_index(axis)
            found[axis] = shifted.reshape((-1,) + (1,) * (len(order) - 1 - i))
        flat = jnp.zeros(shape, jnp.int32)
        return found, flat

    def reorder(order, target):
        found, flat = ranks(order)
        count = dict(y=ny, x=nx, w=nw, z=nz, c=nc)
        index = flat
        for axis in target:
            index = index * count[axis] + found[axis]
        return index.reshape(-1)

    def place(pieces, rank):
        stack = jnp.stack(pieces)
        order = rank ^ jnp.arange(len(pieces))
        return jnp.take(stack, order, axis=0)

    def pick(array, rank, count):
        return [lax.dynamic_index_in_dim(array, rank ^ k, 0, False) for k in range(count)]

    def body(
        tokens, doc_ids, w_query, w_key, w_value, w_out, w_up, w_gate, w_down,
        s_qk, alpha_attn, s_up, s_gate, alpha_mlp, cotangent,
    ):
        nseq, seg, dm = tokens.shape
        rows = w_query.shape[0]
        ff = w_up.shape[1]
        ffq = ff // nquad
        ffb = ff // ndev
        hcols = dm // nline
        nheads = HEADS // nline
        score_scale = math.sqrt(HEAD_DIM)
        c_at = lax.axis_index("c")
        line_at = lax.axis_index(line)
        quad_at = lax.axis_index(quad)

        def by_line(w):
            return w.astype(BF).reshape(rows, nline, hcols)

        w_qkv = jnp.stack([by_line(w_query), by_line(w_key), by_line(w_value)], axis=2)
        w_qkv = w_qkv.transpose(1, 0, 2, 3).reshape(nline, rows, 3 * hcols)
        got = jnp.stack(exchange_rel(pick(w_qkv, line_at, nline), line, nline))
        got = jnp.stack(gather_rel(got, ("y", "x"), ny * nx))
        full = double(got[None], bits("c", nc)).reshape(ndev, rows, 3 * hcols)
        full_qkv = jnp.take(full, reorder("yxwzc", "cyxwz"), axis=0).reshape(dm, 3 * hcols)
        full_out = lax.all_gather(w_out.astype(BF), ("y", "x", "w", "z", "c"), axis=0, tiled=True)

        def by_quad(w):
            w = w.astype(BF).reshape(rows, ny, nx, nw, nz, nc, ffb)
            return w.transpose(2, 4, 0, 1, 3, 5, 6).reshape(nquad, rows, ffq)

        w_ug = jnp.concatenate([by_quad(w_up), by_quad(w_gate)], axis=2)
        got = jnp.stack(exchange_rel(pick(w_ug, quad_at, nquad), quad, nquad))
        stages = bits("w", nw) + bits("y", ny) + bits("c", nc)

        def ff_full(part):
            full = double(part[None], stages).reshape(ndev, rows, ffq)
            return jnp.take(full, reorder("yxwzc", "cywxz"), axis=0).reshape(dm, ffq)

        full_up, full_gate = ff_full(got[:, :, :ffq]), ff_full(got[:, :, ffq:])
        full_down = double(w_down.astype(BF)[None], stages)
        full_down = jnp.take(full_down, reorder("ywc", "cyw"), axis=0).reshape(ffq, dm)

        def my_ff(vec):
            v = vec.reshape(ny, nx, nw, nz, nc, ffb).transpose(1, 3, 0, 2, 4, 5)
            return lax.dynamic_index_in_dim(v.reshape(nquad, ffq), quad_at, 0, False)

        my_s_up, my_s_gate = my_ff(s_up), my_ff(s_gate)
        my_gain = lax.dynamic_index_in_dim(s_qk.reshape(nline, hcols), line_at, 0, False)

        def to_row(value):
            keep = lax.dynamic_index_in_dim(value, c_at, 0, False)
            send = lax.dynamic_index_in_dim(value, 1 - c_at, 0, False)
            return jnp.concatenate([keep, lax.ppermute(send, "c", [(0, 1), (1, 0)])], axis=0)

        def from_row(value, send_type):
            keep, send = value[:seg], value[seg:]
            other = lax.ppermute(send.astype(send_type), "c", [(0, 1), (1, 0)])
            pair = jnp.stack([keep, other.astype(value.dtype)])
            return jnp.where(c_at == 0, pair, pair[::-1])

        docs = doc_ids.astype(BF)
        extra = jnp.zeros((nseq, 16, dm), BF).at[:, 0, :seg].set(docs)
        ext = jnp.concatenate([tokens, extra], axis=1)
        mine = to_row(ext).reshape(2, seg + 16, dm)
        everyone = jnp.stack(gather_rel(mine, line, nline))
        row_tokens = everyone[:, :, :seg].reshape(nline * 2 * seg, dm)
        row_docs = everyone[:, :, seg, :seg].reshape(-1).astype(F32)
        peers = line_at ^ jnp.arange(nline)
        seg_at = 2 * peers[:, None] + jnp.stack([c_at, 1 - c_at])[None, :]
        index = (seg_at[:, :, None] * seg + jnp.arange(seg)).reshape(-1)
        start = jnp.sum((row_docs[None, :] < row_docs[:, None]).astype(jnp.int32), axis=1)
        pos = index - start
        allowed = (index[None, :] <= index[:, None]) & (index[None, :] >= start[:, None])
        frequency = 10000.0 ** (-jnp.arange(HEAD_DIM // 2, dtype=F32) / (HEAD_DIM // 2))
        angles = pos.astype(F32)[:, None] * frequency
        cosines, sines = jnp.cos(angles)[:, None, :], jnp.sin(angles)[:, None, :]
        nt = row_tokens.shape[0]
        x_low = mine[:, :seg].reshape(2 * seg, dm)
        x_row = x_low.astype(F32)

        pre = dot(row_tokens, full_qkv)

        def heads(t):
            return t.reshape(nt, nheads, HEAD_DIM)

        def unit_pair(q_pre, k_pre, gains):
            gains = gains.reshape(nheads, HEAD_DIM)
            return (
                head_unit(rotate(heads(q_pre), cosines, sines), gains),
                head_unit(rotate(heads(k_pre), cosines, sines), gains),
            )

        (q_unit, k_unit), unit_pull = jax.vjp(
            unit_pair, pre[:, :hcols], pre[:, hcols : 2 * hcols], my_gain
        )
        q_low, k_low = q_unit.astype(BF), k_unit.astype(BF)
        v_low = heads(pre[:, 2 * hcols :].astype(BF))
        scores = jnp.einsum("qhd,khd->hqk", q_low, k_low, preferred_element_type=F32) * score_scale
        scores = jnp.where(allowed[None], scores, NEG)
        peak = jnp.max(scores, axis=-1, keepdims=True)
        raw = jnp.where(allowed[None], jnp.exp(scores - peak), 0.0)
        probs = raw / jnp.sum(raw, axis=-1, keepdims=True)
        p_low = probs.astype(BF)
        attended = jnp.einsum("hqk,khd->qhd", p_low, v_low, preferred_element_type=F32)
        att_low = attended.astype(BF).reshape(nline, 2 * seg, hcols)
        got = place(exchange_rel([att_low[k] for k in range(nline)], line, nline), line_at)
        att_mine = got.transpose(1, 0, 2).reshape(2 * seg, dm)

        h_attn = dot(att_mine, full_out)
        h_one, attn_pull = jax.vjp(residual_step, h_attn, x_row, alpha_attn)
        h_low = jnp.concatenate(gather_rel(h_one.astype(BF), quad, nquad), axis=0)
        up, gate = dot(h_low, full_up), dot(h_low, full_gate)
        mixed, gate_pull = jax.vjp(gating, up, gate, my_s_up, my_s_gate)
        mixed_low = mixed.astype(BF)
        part = dot(mixed_low, full_down).reshape(nquad, 2 * seg, dm)
        h_mlp = sum_rel([part[k] for k in range(nquad)], quad, nquad)
        result, out_pull = jax.vjp(residual_step, h_mlp, h_one, alpha_mlp)
        hidden_out = from_row(result.astype(BF), BF)

        d_result = to_row(cotangent).astype(F32)
        d_hmlp, d_hone, g_alpha_mlp = out_pull(d_result)
        dm_low = jnp.concatenate(gather_rel(d_hmlp.astype(BF), quad, nquad), axis=0)
        d_mixed = dot_t(dm_low, full_down)
        d_up, d_gate, g_s_up, g_s_gate = gate_pull(d_mixed)
        du_low, dg_low = d_up.astype(BF), d_gate.astype(BF)
        part = dot_t(du_low, full_up) + dot_t(dg_low, full_gate)
        part = part.reshape(nquad, 2 * seg, dm)
        d_hone = d_hone + sum_rel([part[k] for k in range(nquad)], quad, nquad)
        g_down = tdot(mixed_low, dm_low).reshape(ny * nw * nc, ffb, dm)
        g_down = halve(jnp.take(g_down, reorder("cyw", "ywc"), axis=0), stages)[0]

        def ff_scatter(left, right):
            part = tdot(left, right).reshape(ndev, rows, ffq)
            part = jnp.take(part, reorder("cywxz", "yxwzc"), axis=0)
            part = halve(part.reshape(ny * nw * nc, nquad, rows, ffq), stages)[0].astype(BF)
            got = place(exchange_rel([part[k] for k in range(nquad)], quad, nquad), quad_at)
            got = got.reshape(nx, nz, rows, ny, nw, nc, ffb).transpose(2, 3, 0, 4, 1, 5, 6)
            return got.reshape(rows, ff).astype(F32)

        g_up, g_gate = ff_scatter(h_low, du_low), ff_scatter(h_low, dg_low)

        d_hattn, d_tokens, g_alpha_attn = attn_pull(d_hone)
        dh_low = d_hattn.astype(BF)

        def to_owner(part, kind=BF):
            part = jnp.take(part, reorder("cyxwz", "yxwzc"), axis=0)
            part = halve(part.reshape((nc, ny * nx, nline) + part.shape[1:]), bits("c", nc), kind)[0]
            part = sum_rel([part[k] for k in range(ny * nx)], ("y", "x"), ny * nx, kind)
            return sum_rel([part[k] for k in range(nline)], line, nline, kind)

        g_out = to_owner(tdot(att_mine, dh_low).reshape(ndev, rows, dm))
        d_att = dot_t(dh_low, full_out).astype(BF).reshape(2 * seg, nline, hcols).transpose(1, 0, 2)
        d_att = jnp.concatenate(
            exchange_rel(pick(d_att, line_at, nline), line, nline), axis=0
        ).reshape(nt, nheads, HEAD_DIM)
        delta = jnp.sum(d_att.astype(F32) * attended, axis=-1)
        d_probs = jnp.einsum("qhd,khd->hqk", d_att, v_low, preferred_element_type=F32)
        d_scores = (probs * (d_probs - delta.T[:, :, None])).astype(BF)
        d_q = score_scale * jnp.einsum("hqk,khd->qhd", d_scores, k_low, preferred_element_type=F32)
        d_k = score_scale * jnp.einsum("hqk,qhd->khd", d_scores, q_low, preferred_element_type=F32)
        d_v = jnp.einsum("hqk,qhd->khd", p_low, d_att, preferred_element_type=F32)
        d_qpre, d_kpre, g_sqk = unit_pull((d_q, d_k))
        d_qkv = jnp.concatenate([d_qpre, d_kpre, d_v.reshape(nt, hcols)], axis=1).astype(BF)
        part = dot_t(d_qkv, full_qkv).reshape(nline, 2 * seg, dm)
        tokens_grad = d_tokens + sum_rel([part[k] for k in range(nline)], line, nline)
        tokens_grad = from_row(tokens_grad, BF)
        g_qkv = tdot(row_tokens, d_qkv).reshape(ndev, rows, 3 * hcols)
        g_qkv = jnp.take(g_qkv, reorder("cyxwz", "yxwzc"), axis=0)
        g_qkv = halve(g_qkv.reshape(nc, ny * nx, nline, rows, 3 * hcols), bits("c", nc))[0]
        g_qkv = sum_rel([g_qkv[k] for k in range(ny * nx)], ("y", "x"), ny * nx).astype(BF)
        got = place(exchange_rel([g_qkv[k] for k in range(nline)], line, nline), line_at)
        got = got.reshape(nline, rows, 3, hcols).transpose(2, 1, 0, 3).reshape(3, rows, dm)
        g_query, g_key, g_value = got.astype(F32)

        def spread(vec, rank, count):
            return jnp.where(jnp.arange(count)[:, None] == rank, vec[None], 0.0)

        def ff_order(vec):
            v = spread(vec, quad_at, nquad).reshape(nx, nz, ny, nw, nc, ffb)
            return v.transpose(2, 0, 3, 1, 4, 5).reshape(ndev, ffb)

        vecs = jnp.concatenate(
            [
                spread(g_sqk, line_at, nline).reshape(ndev, -1),
                g_alpha_attn.reshape(ndev, -1),
                ff_order(g_s_up),
                ff_order(g_s_gate),
                g_alpha_mlp.reshape(ndev, -1),
            ],
            axis=1,
        )
        vecs = to_owner(vecs, F32)
        cuts = [rows, 2 * rows, 2 * rows + ffb, 2 * rows + 2 * ffb]
        g_sqk, g_alpha_attn, g_s_up, g_s_gate, g_alpha_mlp = jnp.split(vecs, cuts)
        return (
            hidden_out, tokens_grad, g_query, g_key, g_value, g_out, g_up, g_gate, g_down,
            g_sqk, g_alpha_attn, g_s_up, g_s_gate, g_alpha_mlp,
        )

    return body


VM = pl.BlockSpec(memory_space=pltpu.VMEM)
SM = pl.BlockSpec(memory_space=pltpu.SMEM)
HB = pl.BlockSpec(memory_space=pltpu.HBM)


def call(kernel, outs, args, hbm=(), hbm_out=(), scratch=(), flops=0, mib=60, after=()):
    moved = sum(math.prod(a.shape) * a.dtype.itemsize for a in args)
    moved += sum(math.prod(s) * jnp.dtype(d).itemsize for s, d in outs)
    count = len(args)

    def run(*refs):
        kernel(*refs[:count], *refs[count + len(after) :])

    specs = [SM] + [HB if i in hbm else VM for i in range(1, count)]
    specs += [pl.BlockSpec(memory_space=pl.ANY)] * len(after)
    return pl.pallas_call(
        run,
        out_shape=[jax.ShapeDtypeStruct(s, d) for s, d in outs],
        in_specs=specs,
        out_specs=[HB if i in hbm_out else VM for i in range(len(outs))],
        scratch_shapes=list(scratch),
        compiler_params=pltpu.CompilerParams(vmem_limit_bytes=mib << 20),
        cost_estimate=pl.CostEstimate(flops=flops, bytes_accessed=moved, transcendentals=0),
    )(*args, *after)


def row_norm(v):
    return lax.rsqrt(jnp.mean(v * v, axis=-1, keepdims=True) + EPS)


def sphere_back(dy, y, norm):
    return (dy - y * jnp.mean(dy * y, axis=-1, keepdims=True)) * norm


def make_kernels(sizes):
    ny, nx, nw, nz, nc = sizes
    ndev = ny * nx * nw * nz * nc
    nyx, nline = ny * nx, nw * nz
    ndpc = nyx * nc
    line, yx, dpc = ("w", "z"), ("y", "x"), ("y", "x", "c")

    def swap(value, axes, count, k):
        return lax.ppermute(value, axes, [(i, i ^ k) for i in range(count)])

    def exchange(chunks, axes, count):
        return [chunks[0]] + [swap(chunks[k], axes, count, k) for k in range(1, count)]

    def gather(value, axes, count):
        return exchange([value] * count, axes, count)

    def body(
        tokens, doc_ids, w_query, w_key, w_value, w_out, w_up, w_gate, w_down,
        s_qk, alpha_attn, s_up, s_gate, alpha_mlp, cotangent,
    ):
        nseq, seg, dm = tokens.shape
        rows = w_query.shape[0]
        ff = w_up.shape[1]
        ffq, ffb = ff // nline, ff // ndev
        sub = nc * ffb
        hc = dm // nline
        nheads = HEADS // nline
        nt = nline * 2 * seg
        tk = 2 * seg
        pad = 16
        ext = seg + pad
        scale = math.sqrt(HEAD_DIM)
        tile = 256

        at = [lax.axis_index(a) for a in "yxwzc"]
        ranks = jnp.stack(at + [lax.axis_index(yx), lax.axis_index(line)])
        ranks = ranks.astype(jnp.int32)

        def pack_tokens(rk, tok, docs, keep, send):
            c = rk[4]
            first = lax.broadcasted_iota(jnp.int32, (pad, dm), 0) == 0
            for out, which in ((keep, c), (send, 1 - c)):
                out[:seg] = tok[which]
                out[seg:] = jnp.where(first, docs[which], 0.0).astype(BF)

        def ff_cols(rk, k):
            runs = [(d * nline + (rk[6] ^ k)) * sub for d in range(nyx)]
            return [pl.ds(pl.multiple_of(run, 128), sub) for run in runs]

        def pack_qkv(rk, wq, wk, wv, *outs):
            for k in range(nline):
                cols = pl.ds(pl.multiple_of((rk[6] ^ k) * hc, 128), hc)
                for i, w in enumerate((wq, wk, wv)):
                    outs[k][:, i * hc : (i + 1) * hc] = w[:, cols].astype(BF)

        def pack_weights(rk, wu, wg, wo, gain, su, sg, *outs):
            for k in range(nline):
                out_ff = outs[k]
                for d, cols in enumerate(ff_cols(rk, k)):
                    for i, w in enumerate((wu, wg)):
                        here = i * ffq + d * sub
                        out_ff[:, here : here + sub] = w[:, cols].astype(BF)
                out_ff[:, 2 * ffq :] = wo[...].astype(BF)
            outs[nline][...] = gain[:, pl.ds(pl.multiple_of(rk[6] * hc, 128), hc)]
            for d, cols in enumerate(ff_cols(rk, 0)):
                here = slice(d * sub, (d + 1) * sub)
                outs[nline + 1][:, here] = su[:, cols]
                outs[nline + 2][:, here] = sg[:, cols]

        docs = jnp.pad(doc_ids.astype(F32), ((0, 0), (0, dm - seg))).reshape(nseq, 1, dm)
        packed = call(
            pack_qkv, [((rows, 3 * hc), BF)] * nline, (ranks, w_query, w_key, w_value)
        )
        keep, send = call(pack_tokens, [((ext, dm), BF)] * 2, (ranks, tokens, docs), after=(packed[0],))

        def join_tokens(rk, near, far, out):
            out[:seg] = near[:seg]
            out[seg:tk] = far[:seg]
            row = lax.broadcasted_iota(jnp.int32, (pad, dm), 0)
            ids = far[seg:].astype(F32)[:1]
            out[tk:] = jnp.where(row == 1, ids, near[seg:].astype(F32)).astype(BF)

        (mine,) = call(join_tokens, [((tk + pad, dm), BF)], (ranks, keep, swap(send, "c", nc, 1)))
        packed_ff = call(
            pack_weights,
            [((rows, 2 * ffq + dm), BF)] * nline
            + [((1, hc), F32)]
            + [((1, ffq), F32)] * 2,
            (ranks, w_up, w_gate, w_out, s_qk.reshape(1, dm))
            + (s_up.reshape(1, ff), s_gate.reshape(1, ff)),
            after=(keep,),
        )
        packed_ff, (my_gain, my_su, my_sg) = packed_ff[:nline], packed_ff[nline:]

        w_got = exchange(packed, line, nline)
        ff_got = exchange(packed_ff, line, nline)
        pieces = gather(mine, line, nline)

        def stack(rk, *refs):
            for k in range(nline):
                refs[nline][k * rows : (k + 1) * rows, :] = refs[k][...]

        (got,) = call(stack, [((ffb, 3 * hc), BF)], (ranks, *w_got))
        qkv_full = lax.all_gather(got, dpc, axis=0, tiled=True)

        def stack_ff(rk, *refs):
            parts, (wd, out) = refs[:nline], refs[nline:]
            for k in range(nline):
                out[k * rows : (k + 1) * rows, : 2 * ffq + dm] = parts[k][...]
            out[:, 2 * ffq + dm :] = wd[...].astype(BF)

        (got,) = call(
            stack_ff,
            [((ffb, 2 * ffq + 2 * dm), BF)],
            (ranks, *ff_got, w_down),
            after=(got, mine),
        )
        ff_full = lax.all_gather(got, dpc, axis=0, tiled=True)

        place = jnp.arange(nt, dtype=F32)[:, None]
        freq = 10000.0 ** (-jnp.arange(HEAD_DIM // 2, dtype=F32) / (HEAD_DIM // 2))
        angles = place * freq
        cosines, sines = jnp.cos(angles), jnp.sin(angles)
        reps = 128 // HEAD_DIM
        table = jnp.concatenate(
            [cosines] * (2 * reps) + [-sines, sines] * reps, axis=1
        )
        table_hi = table.astype(BF)
        table_lo = (table - table_hi.astype(F32)).astype(BF)

        def natural(rk, src, cols, dst, sems):
            copies = []
            for b in range(ndpc):
                for k in range(nline):
                    row = ((b // nc) * nline + (rk[6] ^ k)) * nc + b % nc
                    row = pl.ds(pl.multiple_of(row * rows, 32), rows)
                    block = src.at[pl.ds((b * nline + k) * rows, rows), cols]
                    copies.append(pltpu.make_async_copy(block, dst.at[row], sems.at[len(copies)]))
            return copies

        def heads_swap(v, low):
            width = v.shape[1]
            half = HEAD_DIM // 2
            return jnp.where(low, pltpu.roll(v, width - half, 1), pltpu.roll(v, half, 1))

        def low_half():
            lane = lax.broadcasted_iota(jnp.int32, (nt, hc), 1)
            return lane % HEAD_DIM < HEAD_DIM // 2

        def token_index(rk, axis, shape):
            t = lax.broadcasted_iota(jnp.int32, shape, axis)
            peer = (t // tk) ^ rk[6]
            core = ((t // seg) % 2) ^ rk[4]
            return (peer * 2 + core) * seg + t % seg

        def allowed_keys(rk, start):
            key = token_index(rk, 1, (1, nt))
            query = token_index(rk, 0, (nt, 1))
            return (key <= query) & (key.astype(F32) >= start)

        def attn_forward(rk, *refs):
            ext_refs, refs = refs[:nline], refs[nline:]
            stack, gain, t_hi, t_lo = refs[:4]
            att_ref, refs = refs[4], refs[5:]
            x_ref, w_ref, rq_ref, rk_ref, q_ref, k_ref, v_ref, bias_ref, cs_ref = refs[:9]
            full_ref, inv_ref, sems = refs[9:]
            copies = natural(rk, stack, pl.ds(0, 3 * hc), w_ref, sems)
            for copy in copies:
                copy.start()
            ids = []
            for k in range(nline):
                x_ref[k * tk : (k + 1) * tk, :] = ext_refs[k][:tk, :]
                tail = ext_refs[k][tk:, :128].astype(F32)
                ids += [tail[:1, :seg], tail[1:2, :seg]]
            ids = jnp.concatenate(ids, axis=1)
            same = lax.broadcasted_iota(jnp.int32, (nt, nt), 0) == lax.broadcasted_iota(
                jnp.int32, (nt, nt), 1
            )
            ids_col = jnp.sum(jnp.where(same, ids, 0.0), axis=1, keepdims=True)
            start = jnp.sum(jnp.where(ids < ids_col, 1.0, 0.0), axis=1, keepdims=True)
            pos = token_index(rk, 0, (nt, 1)) - start.astype(jnp.int32)
            hot = (lax.broadcasted_iota(jnp.int32, (nt, nt), 1) == pos).astype(F32).astype(BF)
            cs = dot(hot, t_hi[...]) + dot(hot, t_lo[...])
            cs_ref[...] = cs
            cos = jnp.concatenate([cs[:, :128]] * (hc // 128), axis=1)
            sin = jnp.concatenate([cs[:, 128:]] * (hc // 128), axis=1)
            bias_ref[...] = jnp.where(allowed_keys(rk, start), 0.0, NEG).astype(BF)
            for copy in copies:
                copy.wait()
            low = low_half()
            for i, (raw_ref, unit_ref) in enumerate(((rq_ref, q_ref), (rk_ref, k_ref))):
                pre = dot(x_ref[...], w_ref[:, i * hc : (i + 1) * hc])
                turned = pre * cos + heads_swap(pre, low) * sin
                raw_ref[...] = turned
                for h in range(nheads):
                    at_h = slice(h * HEAD_DIM, (h + 1) * HEAD_DIM)
                    part = turned[:, at_h]
                    norm = lax.rsqrt(jnp.sum(part * part, axis=1, keepdims=True) + EPS)
                    unit = (gain[:, at_h] * part * norm).astype(BF)
                    unit_ref[:, at_h] = unit * (scale if i == 0 else 1)
            v_ref[...] = dot(x_ref[...], w_ref[:, 2 * hc :]).astype(BF)
            for h in range(nheads):
                at_h = slice(h * HEAD_DIM, (h + 1) * HEAD_DIM)
                raw = jnp.exp(dot_t(q_ref[:, at_h], k_ref[:, at_h]) + bias_ref[...].astype(F32))
                inv = 1.0 / jnp.sum(raw, axis=1, keepdims=True)
                att_h = dot(raw.astype(BF), v_ref[:, at_h]) * inv
                full_ref[:, at_h] = att_h
                att_ref[:, at_h] = att_h.astype(BF)
                inv_ref[:, h : h + 1] = inv

        unit = ((nt, hc), BF)
        outs = call(
            attn_forward,
            [unit, ((nt, dm), BF), ((dm, 3 * hc), BF), ((nt, hc), F32), ((nt, hc), F32)]
            + [unit, unit, unit, ((nt, nt), BF), ((nt, 256), F32), ((nt, hc), F32), ((nt, 128), F32)],
            (ranks, *pieces, qkv_full, my_gain, table_hi, table_lo),
            hbm=(1 + nline,),
            scratch=[pltpu.SemaphoreType.DMA((ndev,))],
            flops=2 * nt * dm * 3 * hc + 4 * nt * nt * hc,
        )
        att, outs = outs[0], outs[1:]
        x_all, w_qkv, r_q, r_k, q_low, k_low, v_low, bias, cs, att_full, inv = outs
        att_got = gather(att, line, nline)

        def own_x(ext_ref):
            return ext_ref[:tk].astype(F32)

        alpha_a, alpha_m = alpha_attn.reshape(1, dm), alpha_mlp.reshape(1, dm)
        full = ((tk, dm), F32)

        def load_out(rk, stack, wo, sems):
            return natural(rk, stack, pl.ds(2 * ffq, dm), wo, sems)

        def load_ff(rk, stack, scratch):
            wug, wd, sems, sem_d = scratch
            down = stack.at[:, pl.ds(2 * ffq + dm, dm)]
            return (
                natural(rk, stack, pl.ds(0, 2 * ffq), wug, sems),
                [pltpu.make_async_copy(down, wd, sem_d.at[0])],
            )

        w_scratch = [pltpu.VMEM((dm, 2 * ffq), BF), pltpu.VMEM((ffq, dm), BF)]
        w_scratch += [pltpu.SemaphoreType.DMA((ndev,)), pltpu.SemaphoreType.DMA((1,))]
        out_scratch = [pltpu.VMEM((dm, dm), BF), pltpu.SemaphoreType.DMA((ndev,))]

        def gate_terms(gate, sg):
            v = sg * gate
            s = 1.0 / (1.0 + jnp.exp(-v))
            return v, s

        def forward(rk, *refs):
            att_refs, refs = refs[:nline], refs[nline:]
            x_ref, alpha, stack, su, sg = refs[:5]
            parts, refs = refs[5 : 5 + nline], refs[5 + nline :]
            h_all, up_ref, gate_ref, mixed_ref, one_ref, raw_ref = refs[:6]
            scratch = refs[6:]
            wug, wd = scratch[:2]
            w, a_ref = scratch[4], scratch[6]
            first, third = load_ff(rk, stack, scratch[:4])
            out_copies = load_out(rk, stack, w, scratch[5])
            for copy in out_copies + first + third:
                copy.start()
            for k in range(nline):
                spot = pl.ds(pl.multiple_of((rk[6] ^ k) * hc, hc), hc)
                for m in range(nline):
                    block = att_refs[k][(m ^ k) * tk : ((m ^ k) + 1) * tk, :]
                    a_ref[m * tk : (m + 1) * tk, spot] = block
            for copy in out_copies:
                copy.wait()
            for m in range(nline):
                total = dot(a_ref[m * tk : (m + 1) * tk, :], w[...])
                x = x_ref[m * tk : (m + 1) * tk, :].astype(F32)
                z = x + alpha[...] * (total * row_norm(total) - x)
                one = z * row_norm(z)
                h_all[m * tk : (m + 1) * tk, :] = one.astype(BF)
                if m == 0:
                    one_ref[...] = one
                    raw_ref[...] = total
            for copy in first:
                copy.wait()

            @pl.loop(0, ffq // tile, unroll=True)
            def _(j):
                cols = pl.ds(pl.multiple_of(j * tile, tile), tile)
                up = dot(h_all[...], wug[:, cols])
                gate = dot(h_all[...], wug[:, pl.ds(pl.multiple_of(ffq + j * tile, tile), tile)])
                up_ref[:, cols] = up.astype(BF)
                gate_ref[:, cols] = gate.astype(BF)
                v, s = gate_terms(gate, sg[:, cols])
                mixed_ref[:, cols] = (su[:, cols] * up * (v * s)).astype(BF)

            for copy in third:
                copy.wait()

            @pl.loop(0, dm // tile, unroll=True)
            def _(j):
                cols = pl.ds(pl.multiple_of(j * tile, tile), tile)
                part = dot(mixed_ref[...], wd[:, cols])
                for k in range(nline):
                    parts[k][:, cols] = part[k * tk : (k + 1) * tk].astype(parts[k].dtype)

        part_shapes = [((tk, dm), F32)] + [((tk, dm), BF)] * (nline - 1)
        outs = call(
            forward,
            part_shapes
            + [((nt, dm), BF), ((nt, ffq), BF), ((nt, ffq), BF), ((nt, ffq), BF), full, full],
            (ranks, *att_got, x_all, alpha_a, ff_full, my_su, my_sg),
            hbm=(3 + nline,),
            scratch=w_scratch + out_scratch + [pltpu.VMEM((nt, dm), BF)],
            flops=6 * nt * dm * ffq + 2 * nt * dm * dm,
        )
        mlp_parts, (h_all, up, gate, mixed, h_one, h_attn) = outs[:nline], outs[nline:]
        mlp_got = exchange(mlp_parts, line, nline)

        def split_rows(rk, cot, keep, send):
            keep[...] = cot[rk[4]]
            send[...] = cot[1 - rk[4]]

        half_low = ((seg, dm), BF)
        cot_keep, cot_send = call(split_rows, [half_low] * 2, (ranks, cotangent))
        cot_recv = swap(cot_send, "c", nc, 1)

        def mlp_update(rk, *refs):
            parts, refs = refs[:nline], refs[nline:]
            one_ref, alpha_ref, ck, cr, hid_keep, hid_send, dm_ref, direct, g_alpha = refs
            h = parts[0][...]
            for k in range(1, nline):
                h = h + parts[k][...].astype(F32)
            one, alpha = one_ref[...], alpha_ref[...]
            norm_h = row_norm(h)
            b = h * norm_h
            gap = b - one
            z = one + alpha * gap
            norm_z = row_norm(z)
            y = z * norm_z
            low = y.astype(BF)
            hid_keep[...] = low[:seg]
            hid_send[...] = low[seg:]
            dy = jnp.concatenate([ck[...], cr[...]], axis=0).astype(F32)
            dz = sphere_back(dy, y, norm_z)
            g_alpha[...] = jnp.sum(dz * gap, axis=0, keepdims=True)
            direct[...] = dz * (1.0 - alpha)
            dm_ref[...] = sphere_back(dz * alpha, b, norm_h).astype(BF)

        outs = call(
            mlp_update,
            [half_low, half_low, ((tk, dm), BF), full, ((1, dm), F32)],
            (ranks, *mlp_got, h_one, alpha_m, cot_keep, cot_recv),
        )
        hid_keep, hid_send, dm_low, d_one_direct, g_alpha_mlp = outs
        hid_recv = swap(hid_send, "c", nc, 1)
        dm_got = gather(dm_low, line, nline)

        def ff_back(rk, late, *refs):
            d_refs, stack = refs[:nline], refs[nline]
            su_ref, sg_ref, up_ref, gate_ref = refs[nline + 1 : nline + 5]
            refs = refs[nline + 5 :]
            parts, (d_all, dug, g_su, g_sg) = refs[:nline], refs[nline : nline + 4]
            scratch = refs[nline + 4 :]
            wug, wd = scratch[:2]
            first, third = load_ff(rk, stack, scratch)
            for copy in third + late[:2] + first + late[2:]:
                copy.start()
            for k in range(nline):
                d_all[k * tk : (k + 1) * tk, :] = d_refs[k][...]
            for copy in third + late[:2]:
                copy.wait()

            @pl.loop(0, ffq // tile)
            def _(j):
                cols = pl.ds(pl.multiple_of(j * tile, tile), tile)
                d_mixed = dot_t(d_all[...], wd[cols, :])
                up, gate = up_ref[:, cols].astype(F32), gate_ref[:, cols].astype(F32)
                su, sg = su_ref[:, cols], sg_ref[:, cols]
                v, s = gate_terms(gate, sg)
                silu = v * s
                dug[:, cols] = (d_mixed * su * silu).astype(BF)
                slope = d_mixed * su * up * (s * (1.0 + v * (1.0 - s)))
                other = pl.ds(pl.multiple_of(ffq + j * tile, tile), tile)
                dug[:, other] = (slope * sg).astype(BF)
                g_su[:, cols] = jnp.sum(d_mixed * up * silu, axis=0, keepdims=True)
                g_sg[:, cols] = jnp.sum(slope * gate, axis=0, keepdims=True)

            for copy in first:
                copy.wait()

            @pl.loop(0, dm // tile)
            def _(j):
                cols = pl.ds(pl.multiple_of(j * tile, tile), tile)
                part = dot_t(dug[...], wug[cols, :])
                for k in range(nline):
                    parts[k][:, cols] = part[k * tk : (k + 1) * tk].astype(parts[k].dtype)


        def stored(rk, g_ref, out, width, block, sems):
            d, peer, c = block // (nline * nc), (block // nc) % nline, block % nc
            spot = ((d * nc + c) * nline + (peer ^ rk[6])) * rows
            src = g_ref.at[pl.ds(pl.multiple_of(block * rows, 32), rows)]
            dst = out.at[pl.ds(pl.multiple_of(spot, 32), rows), pl.ds(0, width)]
            return pltpu.make_async_copy(src, dst, sems.at[block])

        def outer_ff(rk, h, dug, mixed_ref, d_all, out, g_ref, g_down_ref, sems, sem_d):
            def store(block):
                return stored(rk, g_ref, out, 2 * ffq, block, sems)

            @pl.loop(0, dm // tile, unroll=True)
            def _(j):
                cols = pl.ds(pl.multiple_of(j * tile, tile), tile)
                g_ref[cols, :] = tdot(h[:, cols], dug[...]).astype(BF)
                for i in range(tile // rows):
                    store(j * (tile // rows) + i).start()

            @pl.loop(0, ffq // tile, unroll=True)
            def _(j):
                cols = pl.ds(pl.multiple_of(j * tile, tile), tile)
                g_down_ref[cols, :] = tdot(mixed_ref[:, cols], d_all[...]).astype(BF)

            down = pltpu.make_async_copy(g_down_ref, out.at[:, pl.ds(2 * ffq, dm)], sem_d.at[0])
            down.start()
            down.wait()

            @pl.loop(0, ndev)
            def _(block):
                store(block).wait()

        def ff_back_all(rk, *refs):
            ins, refs = list(refs[: nline + 7]), refs[nline + 7 :]
            parts, (g_su, g_sg, out) = refs[:nline], refs[nline : nline + 3]
            d_all, dug, wug, wd, s_u, s_d, g_ref, g_down_ref, sems, sem_d = refs[nline + 3 : nline + 13]
            *held, late_sems = refs[nline + 13 :]
            late = []
            for i, dst in enumerate(held):
                late.append(pltpu.make_async_copy(ins[nline + 3 + i], dst, late_sems.at[i]))
            ins[nline + 3 :] = held
            scratch = (d_all, dug, g_su, g_sg, wug, wd, s_u, s_d)
            ff_back(rk, late, *ins[: nline + 5], *parts, *scratch)
            h, mixed_ref = ins[nline + 5 :]
            for copy in late[2:]:
                copy.wait()
            outer_ff(rk, h, dug, mixed_ref, d_all, out, g_ref, g_down_ref, sems, sem_d)

        *one_parts, g_su, g_sg, g_ff = call(
            ff_back_all,
            part_shapes + [((1, ffq), F32)] * 2 + [((dm, 2 * ffq + dm), BF)],
            (ranks, *dm_got, ff_full, my_su, my_sg, up, gate, h_all, mixed),
            hbm=(1 + nline, 4 + nline, 5 + nline, 6 + nline, 7 + nline),
            hbm_out=(nline + 2,),
            scratch=[pltpu.VMEM((nt, dm), BF), pltpu.VMEM((nt, 2 * ffq), BF)]
            + w_scratch
            + [pltpu.VMEM((dm, 2 * ffq), BF), pltpu.VMEM((ffq, dm), BF)]
            + [pltpu.SemaphoreType.DMA((ndev,)), pltpu.SemaphoreType.DMA((1,))]
            + [pltpu.VMEM((nt, ffq), BF)] * 2
            + [pltpu.VMEM((nt, dm), BF), pltpu.VMEM((nt, ffq), BF)]
            + [pltpu.SemaphoreType.DMA((4,))],
            flops=12 * nt * dm * ffq,
        )
        one_got = exchange(one_parts, line, nline)
        g_ff = lax.psum_scatter(g_ff, dpc, scatter_dimension=0, tiled=True)
        def attn_update_back(rk, *refs):
            parts, refs = refs[:nline], refs[nline:]
            direct_in, one_ref, raw_ref, ext_ref, alpha_ref, stack = refs[:6]
            d_outs, (dh_ref, direct, g_alpha, w, sems) = refs[6 : 6 + nline], refs[6 + nline :]
            copies = load_out(rk, stack, w, sems)
            for copy in copies:
                copy.start()
            d = direct_in[...] + parts[0][...]
            for k in range(1, nline):
                d = d + parts[k][...].astype(F32)
            one, raw, alpha = one_ref[...], raw_ref[...], alpha_ref[...]
            x = own_x(ext_ref)
            norm_raw = row_norm(raw)
            b = raw * norm_raw
            gap = b - x
            norm_z = row_norm(x + alpha * gap)
            dz = sphere_back(d, one, norm_z)
            g_alpha[...] = jnp.sum(dz * gap, axis=0, keepdims=True)
            direct[...] = dz * (1.0 - alpha)
            dh_ref[...] = sphere_back(dz * alpha, b, norm_raw).astype(BF)
            for copy in copies:
                copy.wait()
            for k in range(nline):
                w_k = w[pl.ds(pl.multiple_of((rk[6] ^ k) * hc, hc), hc), :]
                d_outs[k][...] = dot_t(dh_ref[...], w_k).astype(BF)

        outs = call(
            attn_update_back,
            [((tk, hc), BF)] * nline + [((tk, dm), BF), full, ((1, dm), F32)],
            (ranks, *one_got, d_one_direct, h_one, h_attn, mine, alpha_a, ff_full),
            hbm=(6 + nline,),
            scratch=out_scratch,
            flops=2 * tk * dm * dm,
        )
        d_att_parts, (dh_low, d_x_direct, g_alpha_attn) = outs[:nline], outs[nline:]
        d_att = exchange(d_att_parts, line, nline)

        def attn_back(rk, late, *refs):
            d_refs, refs = refs[:nline], refs[nline:]
            w_ref, rq_ref, rk_ref, q_ref, k_ref, v_ref, bias_ref, cs_ref, gain = refs[:9]
            full_ref, inv_ref, refs = refs[9], refs[10], refs[11:]
            parts, (d_ref, g_gain, do_ref, dq_ref, dk_ref) = refs[:nline], refs[nline:]
            for k in range(nline):
                do_ref[k * tk : (k + 1) * tk, :] = d_refs[k][...]
            for h in range(nheads):
                at_h = slice(h * HEAD_DIM, (h + 1) * HEAD_DIM)
                q, key, do = q_ref[:, at_h], k_ref[:, at_h], do_ref[:, at_h]
                raw = jnp.exp(dot_t(q, key) + bias_ref[...].astype(F32))
                p = raw * inv_ref[:, h : h + 1]
                delta = jnp.sum(do.astype(F32) * full_ref[:, at_h], axis=1, keepdims=True)
                ds = (p * (dot_t(do, v_ref[:, at_h]) - delta)).astype(BF)
                p = p.astype(BF)
                at_v = slice(2 * hc + h * HEAD_DIM, 2 * hc + (h + 1) * HEAD_DIM)
                d_ref[:, at_v] = tdot(p, do).astype(BF)
                dq_ref[:, at_h] = scale * dot(ds, key)
                dk_ref[:, at_h] = tdot(ds, q)
            for copy in late:
                copy.wait()
            cs = cs_ref[...]
            cos = jnp.concatenate([cs[:, :128]] * (hc // 128), axis=1)
            sin = jnp.concatenate([cs[:, 128:]] * (hc // 128), axis=1)
            low = low_half()
            for i, (raw_ref, g_ref) in enumerate(((rq_ref, dq_ref), (rk_ref, dk_ref))):
                for h in range(nheads):
                    at_h = slice(h * HEAD_DIM, (h + 1) * HEAD_DIM)
                    turned, g = raw_ref[:, at_h], g_ref[:, at_h]
                    norm = lax.rsqrt(jnp.sum(turned * turned, axis=1, keepdims=True) + EPS)
                    unit = turned * norm
                    term = jnp.sum(g * unit, axis=0, keepdims=True)
                    g_gain[:, at_h] = term if i == 0 else g_gain[:, at_h] + term
                    g = g * gain[:, at_h]
                    g_ref[:, at_h] = norm * (g - unit * jnp.sum(unit * g, axis=1, keepdims=True))
                g = g_ref[...]
                d_ref[:, i * hc : (i + 1) * hc] = (g * cos - heads_swap(g, low) * sin).astype(BF)

            @pl.loop(0, dm // tile)
            def _(j):
                cols = pl.ds(pl.multiple_of(j * tile, tile), tile)
                part = dot_t(d_ref[...], w_ref[cols, :])
                for k in range(nline):
                    parts[k][:, cols] = part[k * tk : (k + 1) * tk].astype(parts[k].dtype)


        at_line = ranks[6]
        mine_ff = (jnp.arange(nline) == at_line)[None, :, None, None]

        def ff_owner(vec):
            return jnp.where(mine_ff, vec.reshape(nyx, 1, nc, ffb), 0.0).reshape(ndev, ffb)

        misc = [v.reshape(ndev, rows) for v in (g_alpha_attn, g_alpha_mlp)]
        misc = jnp.pad(jnp.concatenate(misc, axis=1), ((0, 0), (0, ffb - 2 * rows)))
        vecs = jnp.stack([ff_owner(g_su), ff_owner(g_sg), misc], axis=1).astype(BF)
        vecs = jnp.pad(vecs, ((0, 0), (0, rows - 3), (0, 0))).reshape(dm, ffb)

        wide = 3 * hc + ffb

        def outer_out(rk, dh, *refs):
            parts, outs, (g_ref, sems) = refs[:nline], refs[nline : nline + 2], refs[nline + 2 :]
            for k in range(nline):
                spot = pl.ds(pl.multiple_of((rk[6] ^ k) * hc, hc), hc)
                own = parts[k][k * tk : (k + 1) * tk, :]
                g_ref[spot, :] = tdot(own, dh[...]).astype(BF)
            copies = []
            for cr in range(nc):
                for a in range(nyx):
                    for b in range(nline):
                        row = ((rk[5] ^ a) * nline + (rk[6] ^ b)) * nc + (rk[4] ^ cr)
                        src = g_ref.at[pl.ds(pl.multiple_of(row * rows, 32), rows)]
                        dst = outs[cr].at[pl.ds((a * nline + b) * rows, rows)]
                        copies.append(pltpu.make_async_copy(src, dst, sems.at[len(copies)]))
            for copy in copies:
                copy.start()
            for copy in copies:
                copy.wait()

        keep, send = call(
            outer_out,
            [((dm // nc, dm), BF)] * nc,
            (ranks, dh_low, *att_got),
            hbm_out=(0, 1),
            scratch=[pltpu.VMEM((dm, dm), BF), pltpu.SemaphoreType.DMA((ndev,))],
            flops=2 * tk * dm * dm,
        )

        def core_add(rk, a, b, *outs):
            for i in range(nyx):
                here = slice(i * ffb, (i + 1) * ffb)
                outs[i][...] = (a[here, :].astype(F32) + b[here, :].astype(F32)).astype(BF)

        out_sum = call(
            core_add, [((ffb, dm), BF)] * nyx, (ranks, keep, swap(send, "c", nc, 1))
        )
        out_got = exchange(out_sum, yx, nyx)

        def outer_last(rk, x_ref, d_ref, vec_ref, g_gain, out, g_ref, sems):

            def store(block):
                return stored(rk, g_ref, out, wide, block, sems)

            g_ref[:, 3 * hc : wide] = vec_ref[...]
            third = lax.broadcasted_iota(jnp.int32, (16, ffb), 0) == 2
            for i in range(hc // rows):
                spot = pl.ds(pl.multiple_of((rk[6] * (hc // rows) + i) * rows, 32), 16)
                run = [jnp.zeros((1, 2 * rows), F32), g_gain[:, i * rows : (i + 1) * rows]]
                run = jnp.concatenate(run + [jnp.zeros((1, ffb - 3 * rows), F32)], axis=1)
                held = g_ref[spot, 3 * hc : wide].astype(F32)
                g_ref[spot, 3 * hc : wide] = (held + jnp.where(third, run, 0.0)).astype(BF)

            @pl.loop(0, dm // tile)
            def _(j):
                cols = pl.ds(pl.multiple_of(j * tile, tile), tile)
                g_ref[cols, : 3 * hc] = tdot(x_ref[:, cols], d_ref[...]).astype(BF)
                for i in range(tile // rows):
                    store(j * (tile // rows) + i).start()

            @pl.loop(0, ndev)
            def _(block):
                store(block).wait()

        def attn_back_all(rk, *refs):
            ins, refs = list(refs[: nline + 13]), refs[nline + 13 :]
            parts, out = refs[:nline], refs[nline]
            d_ref, g_gain, do_ref, dq_ref, dk_ref, g_ref, sems = refs[nline + 1 : nline + 8]
            *held, late_sems = refs[nline + 8 :]
            late = []
            for i, (at_in, dst) in enumerate(zip(late_back, held)):
                late.append(pltpu.make_async_copy(ins[at_in - 1], dst, late_sems.at[i]))
                ins[at_in - 1] = dst
            for copy in late:
                copy.start()
            x_ref, vec_ref = ins[nline + 11 :]
            scratch = (d_ref, g_gain, do_ref, dq_ref, dk_ref)
            attn_back(rk, late, *ins[: nline + 11], *parts, *scratch)
            outer_last(rk, x_ref, d_ref, vec_ref, g_gain, out, g_ref, sems)

        late_back = [1 + nline, 2 + nline, 3 + nline, 8 + nline, 12 + nline]
        late_shapes = [((dm, 3 * hc), BF), ((nt, hc), F32), ((nt, hc), F32), ((nt, 256), F32)]
        late_shapes.append(((nt, dm), BF))

        *x_parts, g_last = call(
            attn_back_all,
            part_shapes + [((dm, wide), BF)],
            (ranks, *d_att, w_qkv, r_q, r_k, q_low, k_low, v_low, bias, cs, my_gain, att_full, inv)
            + (x_all, vecs),
            hbm=late_back,
            hbm_out=(nline,),
            scratch=[
                pltpu.VMEM((nt, 3 * hc), BF), pltpu.VMEM((1, hc), F32),
                pltpu.VMEM((nt, hc), BF), pltpu.VMEM((nt, hc), F32), pltpu.VMEM((nt, hc), F32),
                pltpu.VMEM((dm, wide), BF), pltpu.SemaphoreType.DMA((ndev,)),
                *[pltpu.VMEM(*shape) for shape in late_shapes], pltpu.SemaphoreType.DMA((5,)),
            ],
            flops=4 * nt * dm * 3 * hc + 10 * nt * nt * hc,
        )
        x_got = exchange(x_parts, line, nline)

        def finish_tokens(rk, *refs):
            parts, (direct, keep, send) = refs[:nline], refs[nline:]
            d = direct[...] + parts[0][...]
            for k in range(1, nline):
                d = d + parts[k][...].astype(F32)
            keep[...] = d[:seg]
            send[...] = d[seg:].astype(BF)

        x_keep, x_send = call(
            finish_tokens, [((seg, dm), F32), half_low], (ranks, *x_got, d_x_direct)
        )
        x_recv = swap(x_send, "c", nc, 1)

        def join_rows(rk, keep, recv, out):
            out[rk[4]] = keep[...].astype(out.dtype)
            out[1 - rk[4]] = recv[...].astype(out.dtype)

        (tokens_grad,) = call(join_rows, [((nseq, seg, dm), F32)], (ranks, x_keep, x_recv))
        (hidden_out,) = call(join_rows, [((nseq, seg, dm), BF)], (ranks, hid_keep, hid_recv))

        g_last = lax.psum_scatter(g_last, dpc, scatter_dimension=0, tiled=True)

        def split_ff(rk, g_ref, down, *outs):
            down[...] = g_ref[:, 2 * ffq :].astype(F32)
            for k in range(nline):
                outs[k][...] = g_ref[k * rows : (k + 1) * rows, : 2 * ffq]

        g_down, *g_parts = call(
            split_ff,
            [((ffb, dm), F32)] + [((rows, 2 * ffq), BF)] * nline,
            (ranks, g_ff),
            after=tuple(x_got[1:]),
        )
        g_parts = exchange(g_parts, line, nline)

        def place_ff(rk, *refs):
            parts, outs = refs[:nline], refs[nline:]
            for k in range(nline):
                for d, cols in enumerate(ff_cols(rk, k)):
                    for i in range(2):
                        here = i * ffq + d * sub
                        outs[i][:, cols] = parts[k][:, here : here + sub].astype(F32)

        g_up, g_gate = call(place_ff, [((rows, ff), F32)] * 2, (ranks, *g_parts))

        def sum_out(rk, *refs):
            parts, outs = refs[:nyx], refs[nyx:]
            for k in range(nline):
                here = slice(k * rows, (k + 1) * rows)
                total = parts[0][here, :].astype(F32)
                for j in range(1, nyx):
                    total = total + parts[j][here, :].astype(F32)
                outs[k][...] = total.astype(BF)

        out_sum = call(sum_out, [((rows, dm), BF)] * nline, (ranks, *out_got))
        out_got = exchange(out_sum, line, nline)

        def split_last(rk, g_ref, *outs):
            for k in range(nline):
                outs[k][...] = g_ref[k * rows : (k + 1) * rows, :]

        last = call(
            split_last,
            [((rows, wide), BF)] * nline,
            (ranks, g_last),
            after=(g_up, *out_got[1:]),
        )
        last = exchange(last, line, nline)

        def place_last(rk, *refs):
            parts, out_parts = refs[:nline], refs[nline : 2 * nline]
            outs, refs = refs[2 * nline : 2 * nline + 3], refs[2 * nline + 3 :]
            g_o, vec_outs = refs[0], refs[1:]
            g_sum, v_sum = None, None
            for k in range(nline):
                cols = pl.ds(pl.multiple_of((rk[6] ^ k) * hc, 128), hc)
                for i in range(3):
                    outs[i][:, cols] = parts[k][:, i * hc : (i + 1) * hc].astype(F32)
                vec = parts[k][:16, 3 * hc : wide].astype(F32)
                part = out_parts[k][...].astype(F32)
                g_sum = part if g_sum is None else g_sum + part
                v_sum = vec if v_sum is None else v_sum + vec
            g_o[...] = g_sum
            vec_outs[0][...] = v_sum[:1]
            vec_outs[1][...] = v_sum[1:2]
            for i in range(3):
                vec_outs[2 + i][...] = v_sum[2:3, i * rows : (i + 1) * rows]

        g_query, g_key, g_value, g_out, *vecs = call(
            place_last,
            [((rows, dm), F32)] * 4
            + [((1, ffb), F32)] * 2
            + [((1, rows), F32)] * 3,
            (ranks, *last, *out_got),
        )
        g_s_up, g_s_gate, g_aa, g_am, g_sqk = [v.reshape(-1) for v in vecs]
        return (
            hidden_out, tokens_grad, g_query, g_key, g_value, g_out, g_up, g_gate, g_down,
            g_sqk, g_aa, g_s_up, g_s_gate, g_am,
        )

    return body


def make_body(sizes):
    plain, kernels = make_plain(sizes), make_kernels(sizes)
    ndev = math.prod(sizes)
    nline = sizes[2] * sizes[3]

    def body(*args):
        tokens, w_query, w_up = args[0], args[2], args[6]
        fits = w_query.shape[0] % 32 == 0 and (w_up.shape[1] // ndev) % 128 == 0
        fits = fits and (tokens.shape[2] // nline) % 256 == 0 and tokens.shape[1] == 64
        return (kernels if fits else plain)(*args)

    return body


def solution(mesh):
    ndp, nblk = mesh.shape["dp"], mesh.shape["blk"]
    sizes = (ndp // 2, 2, nblk // 4, 2, 2)
    fine = Mesh(mesh.devices.reshape(sizes), ("y", "x", "w", "z", "c"))
    rows, cols = ("y", "x"), ("w", "z", "c")
    flat = rows + cols
    seq = P(rows, cols, None)
    weight = P(flat, None)
    return jax.shard_map(
        make_body(sizes),
        mesh=fine,
        in_specs=(seq, P(rows, cols)) + (weight,) * 7 + (P(),) * 5 + (seq,),
        out_specs=(seq, seq) + (weight,) * 7 + (P(flat),) * 5,
        check_vma=False,
    )
```

```python
import math

import jax
import jax.numpy as jnp
from jax import lax
from jax.experimental import pallas as pl
from jax.experimental.pallas import tpu as pltpu
from jax.sharding import Mesh
from jax.sharding import PartitionSpec as P

HEADS = 16
HEAD_DIM = 64
EPS = 1e-06
NEG = -1e30
BF = jnp.bfloat16
F32 = jnp.float32


def dot(a, b):
    return jnp.dot(a, b, preferred_element_type=F32)


def dot_t(a, b):
    return lax.dot_general(a, b, (((1,), (1,)), ((), ())), preferred_element_type=F32)


def tdot(a, b):
    return lax.dot_general(a, b, (((0,), (0,)), ((), ())), preferred_element_type=F32)


def rotate(tensor, cosines, sines):
    half_dim = tensor.shape[-1] // 2
    front = tensor[..., :half_dim]
    behind = tensor[..., half_dim:]
    return jnp.concatenate(
        [front * cosines - behind * sines, behind * cosines + front * sines], axis=-1
    )


def sphere(tensor):
    return tensor * lax.rsqrt(jnp.mean(tensor * tensor, axis=-1, keepdims=True) + EPS)


def head_unit(tensor, gains):
    return gains * tensor * lax.rsqrt(jnp.sum(tensor * tensor, axis=-1, keepdims=True) + EPS)


def residual_step(branch, residual_in, alpha):
    return sphere(residual_in + alpha * (sphere(branch) - residual_in))


def gating(up_proj, gate_proj, scale_up, scale_gate):
    return scale_up * up_proj * jax.nn.silu(scale_gate * gate_proj)


def make_plain(sizes):
    ny, nx, nw, nz, nc = sizes
    ndev = ny * nx * nw * nz * nc
    line = ("w", "z")
    nline = nw * nz
    quad = ("x", "z")
    nquad = nx * nz

    def swap(value, axes, count, k):
        return lax.ppermute(value, axes, [(i, i ^ k) for i in range(count)])

    def gather_rel(value, axes, count):
        return [value] + [swap(value, axes, count, k) for k in range(1, count)]

    def exchange_rel(chunks, axes, count):
        return [chunks[0]] + [swap(chunks[k], axes, count, k) for k in range(1, count)]

    def sum_rel(chunks, axes, count, kind=BF):
        got = exchange_rel([c.astype(kind) for c in chunks], axes, count)
        total = chunks[0].astype(F32)
        for piece in got[1:]:
            total = total + piece.astype(F32)
        return total

    def double(value, stages):
        for axis, count, k in stages:
            value = jnp.concatenate([value, swap(value, axis, count, k)], axis=0)
        return value

    def halve(value, stages, kind=BF):
        for axis, count, k in stages[::-1]:
            half = value.shape[0] // 2
            other = swap(value[half:].astype(kind), axis, count, k)
            value = value[:half].astype(F32) + other.astype(F32)
        return value

    def bits(axis, count):
        return [(axis, count, 1 << b) for b in range(count.bit_length() - 1)]

    def ranks(order):
        count = dict(y=ny, x=nx, w=nw, z=nz, c=nc)
        shape = [count[axis] for axis in order]
        found = {}
        for i, axis in enumerate(order):
            shifted = jnp.arange(count[axis]) ^ lax.axis_index(axis)
            found[axis] = shifted.reshape((-1,) + (1,) * (len(order) - 1 - i))
        flat = jnp.zeros(shape, jnp.int32)
        return found, flat

    def reorder(order, target):
        found, flat = ranks(order)
        count = dict(y=ny, x=nx, w=nw, z=nz, c=nc)
        index = flat
        for axis in target:
            index = index * count[axis] + found[axis]
        return index.reshape(-1)

    def place(pieces, rank):
        stack = jnp.stack(pieces)
        order = rank ^ jnp.arange(len(pieces))
        return jnp.take(stack, order, axis=0)

    def pick(array, rank, count):
        return [lax.dynamic_index_in_dim(array, rank ^ k, 0, False) for k in range(count)]

    def body(
        tokens, doc_ids, w_query, w_key, w_value, w_out, w_up, w_gate, w_down,
        s_qk, alpha_attn, s_up, s_gate, alpha_mlp, cotangent,
    ):
        nseq, seg, dm = tokens.shape
        rows = w_query.shape[0]
        ff = w_up.shape[1]
        ffq = ff // nquad
        ffb = ff // ndev
        hcols = dm // nline
        nheads = HEADS // nline
        score_scale = math.sqrt(HEAD_DIM)
        c_at = lax.axis_index("c")
        line_at = lax.axis_index(line)
        quad_at = lax.axis_index(quad)

        def by_line(w):
            return w.astype(BF).reshape(rows, nline, hcols)

        w_qkv = jnp.stack([by_line(w_query), by_line(w_key), by_line(w_value)], axis=2)
        w_qkv = w_qkv.transpose(1, 0, 2, 3).reshape(nline, rows, 3 * hcols)
        got = jnp.stack(exchange_rel(pick(w_qkv, line_at, nline), line, nline))
        got = jnp.stack(gather_rel(got, ("y", "x"), ny * nx))
        full = double(got[None], bits("c", nc)).reshape(ndev, rows, 3 * hcols)
        full_qkv = jnp.take(full, reorder("yxwzc", "cyxwz"), axis=0).reshape(dm, 3 * hcols)
        full_out = lax.all_gather(w_out.astype(BF), ("y", "x", "w", "z", "c"), axis=0, tiled=True)

        def by_quad(w):
            w = w.astype(BF).reshape(rows, ny, nx, nw, nz, nc, ffb)
            return w.transpose(2, 4, 0, 1, 3, 5, 6).reshape(nquad, rows, ffq)

        w_ug = jnp.concatenate([by_quad(w_up), by_quad(w_gate)], axis=2)
        got = jnp.stack(exchange_rel(pick(w_ug, quad_at, nquad), quad, nquad))
        stages = bits("w", nw) + bits("y", ny) + bits("c", nc)

        def ff_full(part):
            full = double(part[None], stages).reshape(ndev, rows, ffq)
            return jnp.take(full, reorder("yxwzc", "cywxz"), axis=0).reshape(dm, ffq)

        full_up, full_gate = ff_full(got[:, :, :ffq]), ff_full(got[:, :, ffq:])
        full_down = double(w_down.astype(BF)[None], stages)
        full_down = jnp.take(full_down, reorder("ywc", "cyw"), axis=0).reshape(ffq, dm)

        def my_ff(vec):
            v = vec.reshape(ny, nx, nw, nz, nc, ffb).transpose(1, 3, 0, 2, 4, 5)
            return lax.dynamic_index_in_dim(v.reshape(nquad, ffq), quad_at, 0, False)

        my_s_up, my_s_gate = my_ff(s_up), my_ff(s_gate)
        my_gain = lax.dynamic_index_in_dim(s_qk.reshape(nline, hcols), line_at, 0, False)

        def to_row(value):
            keep = lax.dynamic_index_in_dim(value, c_at, 0, False)
            send = lax.dynamic_index_in_dim(value, 1 - c_at, 0, False)
            return jnp.concatenate([keep, lax.ppermute(send, "c", [(0, 1), (1, 0)])], axis=0)

        def from_row(value, send_type):
            keep, send = value[:seg], value[seg:]
            other = lax.ppermute(send.astype(send_type), "c", [(0, 1), (1, 0)])
            pair = jnp.stack([keep, other.astype(value.dtype)])
            return jnp.where(c_at == 0, pair, pair[::-1])

        docs = doc_ids.astype(BF)
        extra = jnp.zeros((nseq, 16, dm), BF).at[:, 0, :seg].set(docs)
        ext = jnp.concatenate([tokens, extra], axis=1)
        mine = to_row(ext).reshape(2, seg + 16, dm)
        everyone = jnp.stack(gather_rel(mine, line, nline))
        row_tokens = everyone[:, :, :seg].reshape(nline * 2 * seg, dm)
        row_docs = everyone[:, :, seg, :seg].reshape(-1).astype(F32)
        peers = line_at ^ jnp.arange(nline)
        seg_at = 2 * peers[:, None] + jnp.stack([c_at, 1 - c_at])[None, :]
        index = (seg_at[:, :, None] * seg + jnp.arange(seg)).reshape(-1)
        start = jnp.sum((row_docs[None, :] < row_docs[:, None]).astype(jnp.int32), axis=1)
        pos = index - start
        allowed = (index[None, :] <= index[:, None]) & (index[None, :] >= start[:, None])
        frequency = 10000.0 ** (-jnp.arange(HEAD_DIM // 2, dtype=F32) / (HEAD_DIM // 2))
        angles = pos.astype(F32)[:, None] * frequency
        cosines, sines = jnp.cos(angles)[:, None, :], jnp.sin(angles)[:, None, :]
        nt = row_tokens.shape[0]
        x_low = mine[:, :seg].reshape(2 * seg, dm)
        x_row = x_low.astype(F32)

        pre = dot(row_tokens, full_qkv)

        def heads(t):
            return t.reshape(nt, nheads, HEAD_DIM)

        def unit_pair(q_pre, k_pre, gains):
            gains = gains.reshape(nheads, HEAD_DIM)
            return (
                head_unit(rotate(heads(q_pre), cosines, sines), gains),
                head_unit(rotate(heads(k_pre), cosines, sines), gains),
            )

        (q_unit, k_unit), unit_pull = jax.vjp(
            unit_pair, pre[:, :hcols], pre[:, hcols : 2 * hcols], my_gain
        )
        q_low, k_low = q_unit.astype(BF), k_unit.astype(BF)
        v_low = heads(pre[:, 2 * hcols :].astype(BF))
        scores = jnp.einsum("qhd,khd->hqk", q_low, k_low, preferred_element_type=F32) * score_scale
        scores = jnp.where(allowed[None], scores, NEG)
        peak = jnp.max(scores, axis=-1, keepdims=True)
        raw = jnp.where(allowed[None], jnp.exp(scores - peak), 0.0)
        probs = raw / jnp.sum(raw, axis=-1, keepdims=True)
        p_low = probs.astype(BF)
        attended = jnp.einsum("hqk,khd->qhd", p_low, v_low, preferred_element_type=F32)
        att_low = attended.astype(BF).reshape(nline, 2 * seg, hcols)
        got = place(exchange_rel([att_low[k] for k in range(nline)], line, nline), line_at)
        att_mine = got.transpose(1, 0, 2).reshape(2 * seg, dm)

        h_attn = dot(att_mine, full_out)
        h_one, attn_pull = jax.vjp(residual_step, h_attn, x_row, alpha_attn)
        h_low = jnp.concatenate(gather_rel(h_one.astype(BF), quad, nquad), axis=0)
        up, gate = dot(h_low, full_up), dot(h_low, full_gate)
        mixed, gate_pull = jax.vjp(gating, up, gate, my_s_up, my_s_gate)
        mixed_low = mixed.astype(BF)
        part = dot(mixed_low, full_down).reshape(nquad, 2 * seg, dm)
        h_mlp = sum_rel([part[k] for k in range(nquad)], quad, nquad)
        result, out_pull = jax.vjp(residual_step, h_mlp, h_one, alpha_mlp)
        hidden_out = from_row(result.astype(BF), BF)

        d_result = to_row(cotangent).astype(F32)
        d_hmlp, d_hone, g_alpha_mlp = out_pull(d_result)
        dm_low = jnp.concatenate(gather_rel(d_hmlp.astype(BF), quad, nquad), axis=0)
        d_mixed = dot_t(dm_low, full_down)
        d_up, d_gate, g_s_up, g_s_gate = gate_pull(d_mixed)
        du_low, dg_low = d_up.astype(BF), d_gate.astype(BF)
        part = dot_t(du_low, full_up) + dot_t(dg_low, full_gate)
        part = part.reshape(nquad, 2 * seg, dm)
        d_hone = d_hone + sum_rel([part[k] for k in range(nquad)], quad, nquad)
        g_down = tdot(mixed_low, dm_low).reshape(ny * nw * nc, ffb, dm)
        g_down = halve(jnp.take(g_down, reorder("cyw", "ywc"), axis=0), stages)[0]

        def ff_scatter(left, right):
            part = tdot(left, right).reshape(ndev, rows, ffq)
            part = jnp.take(part, reorder("cywxz", "yxwzc"), axis=0)
            part = halve(part.reshape(ny * nw * nc, nquad, rows, ffq), stages)[0].astype(BF)
            got = place(exchange_rel([part[k] for k in range(nquad)], quad, nquad), quad_at)
            got = got.reshape(nx, nz, rows, ny, nw, nc, ffb).transpose(2, 3, 0, 4, 1, 5, 6)
            return got.reshape(rows, ff).astype(F32)

        g_up, g_gate = ff_scatter(h_low, du_low), ff_scatter(h_low, dg_low)

        d_hattn, d_tokens, g_alpha_attn = attn_pull(d_hone)
        dh_low = d_hattn.astype(BF)

        def to_owner(part, kind=BF):
            part = jnp.take(part, reorder("cyxwz", "yxwzc"), axis=0)
            part = halve(part.reshape((nc, ny * nx, nline) + part.shape[1:]), bits("c", nc), kind)[0]
            part = sum_rel([part[k] for k in range(ny * nx)], ("y", "x"), ny * nx, kind)
            return sum_rel([part[k] for k in range(nline)], line, nline, kind)

        g_out = to_owner(tdot(att_mine, dh_low).reshape(ndev, rows, dm))
        d_att = dot_t(dh_low, full_out).astype(BF).reshape(2 * seg, nline, hcols).transpose(1, 0, 2)
        d_att = jnp.concatenate(
            exchange_rel(pick(d_att, line_at, nline), line, nline), axis=0
        ).reshape(nt, nheads, HEAD_DIM)
        delta = jnp.sum(d_att.astype(F32) * attended, axis=-1)
        d_probs = jnp.einsum("qhd,khd->hqk", d_att, v_low, preferred_element_type=F32)
        d_scores = (probs * (d_probs - delta.T[:, :, None])).astype(BF)
        d_q = score_scale * jnp.einsum("hqk,khd->qhd", d_scores, k_low, preferred_element_type=F32)
        d_k = score_scale * jnp.einsum("hqk,qhd->khd", d_scores, q_low, preferred_element_type=F32)
        d_v = jnp.einsum("hqk,qhd->khd", p_low, d_att, preferred_element_type=F32)
        d_qpre, d_kpre, g_sqk = unit_pull((d_q, d_k))
        d_qkv = jnp.concatenate([d_qpre, d_kpre, d_v.reshape(nt, hcols)], axis=1).astype(BF)
        part = dot_t(d_qkv, full_qkv).reshape(nline, 2 * seg, dm)
        tokens_grad = d_tokens + sum_rel([part[k] for k in range(nline)], line, nline)
        tokens_grad = from_row(tokens_grad, BF)
        g_qkv = tdot(row_tokens, d_qkv).reshape(ndev, rows, 3 * hcols)
        g_qkv = jnp.take(g_qkv, reorder("cyxwz", "yxwzc"), axis=0)
        g_qkv = halve(g_qkv.reshape(nc, ny * nx, nline, rows, 3 * hcols), bits("c", nc))[0]
        g_qkv = sum_rel([g_qkv[k] for k in range(ny * nx)], ("y", "x"), ny * nx).astype(BF)
        got = place(exchange_rel([g_qkv[k] for k in range(nline)], line, nline), line_at)
        got = got.reshape(nline, rows, 3, hcols).transpose(2, 1, 0, 3).reshape(3, rows, dm)
        g_query, g_key, g_value = got.astype(F32)

        def spread(vec, rank, count):
            return jnp.where(jnp.arange(count)[:, None] == rank, vec[None], 0.0)

        def ff_order(vec):
            v = spread(vec, quad_at, nquad).reshape(nx, nz, ny, nw, nc, ffb)
            return v.transpose(2, 0, 3, 1, 4, 5).reshape(ndev, ffb)

        vecs = jnp.concatenate(
            [
                spread(g_sqk, line_at, nline).reshape(ndev, -1),
                g_alpha_attn.reshape(ndev, -1),
                ff_order(g_s_up),
                ff_order(g_s_gate),
                g_alpha_mlp.reshape(ndev, -1),
            ],
            axis=1,
        )
        vecs = to_owner(vecs, F32)
        cuts = [rows, 2 * rows, 2 * rows + ffb, 2 * rows + 2 * ffb]
        g_sqk, g_alpha_attn, g_s_up, g_s_gate, g_alpha_mlp = jnp.split(vecs, cuts)
        return (
            hidden_out, tokens_grad, g_query, g_key, g_value, g_out, g_up, g_gate, g_down,
            g_sqk, g_alpha_attn, g_s_up, g_s_gate, g_alpha_mlp,
        )

    return body


VM = pl.BlockSpec(memory_space=pltpu.VMEM)
SM = pl.BlockSpec(memory_space=pltpu.SMEM)
HB = pl.BlockSpec(memory_space=pltpu.HBM)


def call(kernel, outs, args, hbm=(), hbm_out=(), scratch=(), flops=0, mib=60, after=()):
    moved = sum(math.prod(a.shape) * a.dtype.itemsize for a in args)
    moved += sum(math.prod(s) * jnp.dtype(d).itemsize for s, d in outs)
    count = len(args)

    def run(*refs):
        kernel(*refs[:count], *refs[count + len(after) :])

    specs = [SM] + [HB if i in hbm else VM for i in range(1, count)]
    specs += [pl.BlockSpec(memory_space=pl.ANY)] * len(after)
    return pl.pallas_call(
        run,
        out_shape=[jax.ShapeDtypeStruct(s, d) for s, d in outs],
        in_specs=specs,
        out_specs=[HB if i in hbm_out else VM for i in range(len(outs))],
        scratch_shapes=list(scratch),
        compiler_params=pltpu.CompilerParams(vmem_limit_bytes=mib << 20),
        cost_estimate=pl.CostEstimate(flops=flops, bytes_accessed=moved, transcendentals=0),
    )(*args, *after)


def row_norm(v):
    return lax.rsqrt(jnp.mean(v * v, axis=-1, keepdims=True) + EPS)


def sphere_back(dy, y, norm):
    return (dy - y * jnp.mean(dy * y, axis=-1, keepdims=True)) * norm


def make_kernels(sizes):
    ny, nx, nw, nz, nc = sizes
    ndev = ny * nx * nw * nz * nc
    nyx, nline = ny * nx, nw * nz
    ndpc = nyx * nc
    line, yx, dpc = ("w", "z"), ("y", "x"), ("y", "x", "c")

    def swap(value, axes, count, k):
        return lax.ppermute(value, axes, [(i, i ^ k) for i in range(count)])

    def exchange(chunks, axes, count):
        return [chunks[0]] + [swap(chunks[k], axes, count, k) for k in range(1, count)]

    def gather(value, axes, count):
        return exchange([value] * count, axes, count)

    def body(
        tokens, doc_ids, w_query, w_key, w_value, w_out, w_up, w_gate, w_down,
        s_qk, alpha_attn, s_up, s_gate, alpha_mlp, cotangent,
    ):
        nseq, seg, dm = tokens.shape
        rows = w_query.shape[0]
        ff = w_up.shape[1]
        ffq, ffb = ff // nline, ff // ndev
        sub = nc * ffb
        hc = dm // nline
        nheads = HEADS // nline
        nt = nline * 2 * seg
        tk = 2 * seg
        pad = 16
        ext = seg + pad
        scale = math.sqrt(HEAD_DIM)
        tile = 256

        at = [lax.axis_index(a) for a in "yxwzc"]
        ranks = jnp.stack(at + [lax.axis_index(yx), lax.axis_index(line)])
        ranks = ranks.astype(jnp.int32)

        def pack_tokens(rk, tok, docs, keep, send):
            c = rk[4]
            first = lax.broadcasted_iota(jnp.int32, (pad, dm), 0) == 0
            for out, which in ((keep, c), (send, 1 - c)):
                out[:seg] = tok[which]
                out[seg:] = jnp.where(first, docs[which], 0.0).astype(BF)

        def ff_cols(rk, k):
            runs = [(d * nline + (rk[6] ^ k)) * sub for d in range(nyx)]
            return [pl.ds(pl.multiple_of(run, 128), sub) for run in runs]

        def pack_qkv(rk, wq, wk, wv, *outs):
            for k in range(nline):
                cols = pl.ds(pl.multiple_of((rk[6] ^ k) * hc, 128), hc)
                for i, w in enumerate((wq, wk, wv)):
                    outs[k][:, i * hc : (i + 1) * hc] = w[:, cols].astype(BF)

        def pack_weights(rk, wu, wg, wo, gain, su, sg, *outs):
            for k in range(nline):
                out_ff = outs[k]
                for d, cols in enumerate(ff_cols(rk, k)):
                    for i, w in enumerate((wu, wg)):
                        here = i * ffq + d * sub
                        out_ff[:, here : here + sub] = w[:, cols].astype(BF)
                out_ff[:, 2 * ffq :] = wo[...].astype(BF)
            outs[nline][...] = gain[:, pl.ds(pl.multiple_of(rk[6] * hc, 128), hc)]
            for d, cols in enumerate(ff_cols(rk, 0)):
                here = slice(d * sub, (d + 1) * sub)
                outs[nline + 1][:, here] = su[:, cols]
                outs[nline + 2][:, here] = sg[:, cols]

        docs = jnp.pad(doc_ids.astype(F32), ((0, 0), (0, dm - seg))).reshape(nseq, 1, dm)
        packed = call(
            pack_qkv, [((rows, 3 * hc), BF)] * nline, (ranks, w_query, w_key, w_value)
        )
        keep, send = call(pack_tokens, [((ext, dm), BF)] * 2, (ranks, tokens, docs), after=(packed[0],))

        def join_tokens(rk, near, far, out):
            out[:seg] = near[:seg]
            out[seg:tk] = far[:seg]
            row = lax.broadcasted_iota(jnp.int32, (pad, dm), 0)
            ids = far[seg:].astype(F32)[:1]
            out[tk:] = jnp.where(row == 1, ids, near[seg:].astype(F32)).astype(BF)

        (mine,) = call(join_tokens, [((tk + pad, dm), BF)], (ranks, keep, swap(send, "c", nc, 1)))
        packed_ff = call(
            pack_weights,
            [((rows, 2 * ffq + dm), BF)] * nline
            + [((1, hc), F32)]
            + [((1, ffq), F32)] * 2,
            (ranks, w_up, w_gate, w_out, s_qk.reshape(1, dm))
            + (s_up.reshape(1, ff), s_gate.reshape(1, ff)),
            after=(keep,),
        )
        packed_ff, (my_gain, my_su, my_sg) = packed_ff[:nline], packed_ff[nline:]

        w_got = exchange(packed, line, nline)
        ff_got = exchange(packed_ff, line, nline)
        pieces = gather(mine, line, nline)

        def stack(rk, *refs):
            for k in range(nline):
                refs[nline][k * rows : (k + 1) * rows, :] = refs[k][...]

        (got,) = call(stack, [((ffb, 3 * hc), BF)], (ranks, *w_got))
        qkv_full = lax.all_gather(got, dpc, axis=0, tiled=True)

        def stack_ff(rk, *refs):
            parts, (wd, out) = refs[:nline], refs[nline:]
            for k in range(nline):
                out[k * rows : (k + 1) * rows, : 2 * ffq + dm] = parts[k][...]
            out[:, 2 * ffq + dm :] = wd[...].astype(BF)

        (got,) = call(
            stack_ff,
            [((ffb, 2 * ffq + 2 * dm), BF)],
            (ranks, *ff_got, w_down),
            after=(got, mine),
        )
        ff_full = lax.all_gather(got, dpc, axis=0, tiled=True)

        place = jnp.arange(nt, dtype=F32)[:, None]
        freq = 10000.0 ** (-jnp.arange(HEAD_DIM // 2, dtype=F32) / (HEAD_DIM // 2))
        angles = place * freq
        cosines, sines = jnp.cos(angles), jnp.sin(angles)
        reps = 128 // HEAD_DIM
        table = jnp.concatenate(
            [cosines] * (2 * reps) + [-sines, sines] * reps, axis=1
        )
        table_hi = table.astype(BF)
        table_lo = (table - table_hi.astype(F32)).astype(BF)

        def natural(rk, src, cols, dst, sems):
            copies = []
            for b in range(ndpc):
                for k in range(nline):
                    row = ((b // nc) * nline + (rk[6] ^ k)) * nc + b % nc
                    row = pl.ds(pl.multiple_of(row * rows, 32), rows)
                    block = src.at[pl.ds((b * nline + k) * rows, rows), cols]
                    copies.append(pltpu.make_async_copy(block, dst.at[row], sems.at[len(copies)]))
            return copies

        def heads_swap(v, low):
            width = v.shape[1]
            half = HEAD_DIM // 2
            return jnp.where(low, pltpu.roll(v, width - half, 1), pltpu.roll(v, half, 1))

        def low_half():
            lane = lax.broadcasted_iota(jnp.int32, (nt, hc), 1)
            return lane % HEAD_DIM < HEAD_DIM // 2

        def token_index(rk, axis, shape):
            t = lax.broadcasted_iota(jnp.int32, shape, axis)
            peer = (t // tk) ^ rk[6]
            core = ((t // seg) % 2) ^ rk[4]
            return (peer * 2 + core) * seg + t % seg

        def allowed_keys(rk, start):
            key = token_index(rk, 1, (1, nt))
            query = token_index(rk, 0, (nt, 1))
            return (key <= query) & (key.astype(F32) >= start)

        def attn_forward(rk, *refs):
            ext_refs, refs = refs[:nline], refs[nline:]
            stack, gain, t_hi, t_lo = refs[:4]
            att_ref, refs = refs[4], refs[5:]
            x_ref, w_ref, rq_ref, rk_ref, q_ref, k_ref, v_ref, bias_ref, cs_ref = refs[:9]
            full_ref, inv_ref, sems = refs[9:]
            copies = natural(rk, stack, pl.ds(0, 3 * hc), w_ref, sems)
            for copy in copies:
                copy.start()
            ids = []
            for k in range(nline):
                x_ref[k * tk : (k + 1) * tk, :] = ext_refs[k][:tk, :]
                tail = ext_refs[k][tk:, :128].astype(F32)
                ids += [tail[:1, :seg], tail[1:2, :seg]]
            ids = jnp.concatenate(ids, axis=1)
            same = lax.broadcasted_iota(jnp.int32, (nt, nt), 0) == lax.broadcasted_iota(
                jnp.int32, (nt, nt), 1
            )
            ids_col = jnp.sum(jnp.where(same, ids, 0.0), axis=1, keepdims=True)
            start = jnp.sum(jnp.where(ids < ids_col, 1.0, 0.0), axis=1, keepdims=True)
            pos = token_index(rk, 0, (nt, 1)) - start.astype(jnp.int32)
            hot = (lax.broadcasted_iota(jnp.int32, (nt, nt), 1) == pos).astype(F32).astype(BF)
            cs = dot(hot, t_hi[...]) + dot(hot, t_lo[...])
            cs_ref[...] = cs
            cos = jnp.concatenate([cs[:, :128]] * (hc // 128), axis=1)
            sin = jnp.concatenate([cs[:, 128:]] * (hc // 128), axis=1)
            bias_ref[...] = jnp.where(allowed_keys(rk, start), 0.0, NEG).astype(BF)
            for copy in copies:
                copy.wait()
            low = low_half()
            for i, (raw_ref, unit_ref) in enumerate(((rq_ref, q_ref), (rk_ref, k_ref))):
                pre = dot(x_ref[...], w_ref[:, i * hc : (i + 1) * hc])
                turned = pre * cos + heads_swap(pre, low) * sin
                raw_ref[...] = turned
                for h in range(nheads):
                    at_h = slice(h * HEAD_DIM, (h + 1) * HEAD_DIM)
                    part = turned[:, at_h]
                    norm = lax.rsqrt(jnp.sum(part * part, axis=1, keepdims=True) + EPS)
                    unit = (gain[:, at_h] * part * norm).astype(BF)
                    unit_ref[:, at_h] = unit * (scale if i == 0 else 1)
            v_ref[...] = dot(x_ref[...], w_ref[:, 2 * hc :]).astype(BF)
            for h in range(nheads):
                at_h = slice(h * HEAD_DIM, (h + 1) * HEAD_DIM)
                raw = jnp.exp(dot_t(q_ref[:, at_h], k_ref[:, at_h]) + bias_ref[...].astype(F32))
                inv = 1.0 / jnp.sum(raw, axis=1, keepdims=True)
                att_h = dot(raw.astype(BF), v_ref[:, at_h]) * inv
                full_ref[:, at_h] = att_h
                att_ref[:, at_h] = att_h.astype(BF)
                inv_ref[:, h : h + 1] = inv

        unit = ((nt, hc), BF)
        outs = call(
            attn_forward,
            [unit, ((nt, dm), BF), ((dm, 3 * hc), BF), ((nt, hc), F32), ((nt, hc), F32)]
            + [unit, unit, unit, ((nt, nt), BF), ((nt, 256), F32), ((nt, hc), F32), ((nt, 128), F32)],
            (ranks, *pieces, qkv_full, my_gain, table_hi, table_lo),
            hbm=(1 + nline,),
            scratch=[pltpu.SemaphoreType.DMA((ndev,))],
            flops=2 * nt * dm * 3 * hc + 4 * nt * nt * hc,
        )
        att, outs = outs[0], outs[1:]
        x_all, w_qkv, r_q, r_k, q_low, k_low, v_low, bias, cs, att_full, inv = outs
        att_got = gather(att, line, nline)

        def own_x(ext_ref):
            return ext_ref[:tk].astype(F32)

        alpha_a, alpha_m = alpha_attn.reshape(1, dm), alpha_mlp.reshape(1, dm)
        full = ((tk, dm), F32)

        def load_out(rk, stack, wo, sems):
            return natural(rk, stack, pl.ds(2 * ffq, dm), wo, sems)

        def load_ff(rk, stack, scratch):
            wug, wd, sems, sem_d = scratch
            down = stack.at[:, pl.ds(2 * ffq + dm, dm)]
            return (
                natural(rk, stack, pl.ds(0, 2 * ffq), wug, sems),
                [pltpu.make_async_copy(down, wd, sem_d.at[0])],
            )

        w_scratch = [pltpu.VMEM((dm, 2 * ffq), BF), pltpu.VMEM((ffq, dm), BF)]
        w_scratch += [pltpu.SemaphoreType.DMA((ndev,)), pltpu.SemaphoreType.DMA((1,))]
        out_scratch = [pltpu.VMEM((dm, dm), BF), pltpu.SemaphoreType.DMA((ndev,))]

        def gate_terms(gate, sg):
            v = sg * gate
            s = 1.0 / (1.0 + jnp.exp(-v))
            return v, s

        def forward(rk, *refs):
            att_refs, refs = refs[:nline], refs[nline:]
            x_ref, alpha, stack, su, sg = refs[:5]
            parts, refs = refs[5 : 5 + nline], refs[5 + nline :]
            h_all, up_ref, gate_ref, mixed_ref, one_ref, raw_ref = refs[:6]
            scratch = refs[6:]
            wug, wd = scratch[:2]
            w, a_ref = scratch[4], scratch[6]
            first, third = load_ff(rk, stack, scratch[:4])
            out_copies = load_out(rk, stack, w, scratch[5])
            for copy in out_copies + first + third:
                copy.start()
            for k in range(nline):
                spot = pl.ds(pl.multiple_of((rk[6] ^ k) * hc, hc), hc)
                for m in range(nline):
                    block = att_refs[k][(m ^ k) * tk : ((m ^ k) + 1) * tk, :]
                    a_ref[m * tk : (m + 1) * tk, spot] = block
            for copy in out_copies:
                copy.wait()
            for m in range(nline):
                total = dot(a_ref[m * tk : (m + 1) * tk, :], w[...])
                x = x_ref[m * tk : (m + 1) * tk, :].astype(F32)
                z = x + alpha[...] * (total * row_norm(total) - x)
                one = z * row_norm(z)
                h_all[m * tk : (m + 1) * tk, :] = one.astype(BF)
                if m == 0:
                    one_ref[...] = one
                    raw_ref[...] = total
            for copy in first:
                copy.wait()

            @pl.loop(0, ffq // tile, unroll=True)
            def _(j):
                cols = pl.ds(pl.multiple_of(j * tile, tile), tile)
                up = dot(h_all[...], wug[:, cols])
                gate = dot(h_all[...], wug[:, pl.ds(pl.multiple_of(ffq + j * tile, tile), tile)])
                up_ref[:, cols] = up.astype(BF)
                gate_ref[:, cols] = gate.astype(BF)
                v, s = gate_terms(gate, sg[:, cols])
                mixed_ref[:, cols] = (su[:, cols] * up * (v * s)).astype(BF)

            for copy in third:
                copy.wait()

            @pl.loop(0, dm // tile, unroll=True)
            def _(j):
                cols = pl.ds(pl.multiple_of(j * tile, tile), tile)
                part = dot(mixed_ref[...], wd[:, cols])
                for k in range(nline):
                    parts[k][:, cols] = part[k * tk : (k + 1) * tk].astype(parts[k].dtype)

        part_shapes = [((tk, dm), F32)] + [((tk, dm), BF)] * (nline - 1)
        outs = call(
            forward,
            part_shapes
            + [((nt, dm), BF), ((nt, ffq), BF), ((nt, ffq), BF), ((nt, ffq), BF), full, full],
            (ranks, *att_got, x_all, alpha_a, ff_full, my_su, my_sg),
            hbm=(3 + nline,),
            scratch=w_scratch + out_scratch + [pltpu.VMEM((nt, dm), BF)],
            flops=6 * nt * dm * ffq + 2 * nt * dm * dm,
        )
        mlp_parts, (h_all, up, gate, mixed, h_one, h_attn) = outs[:nline], outs[nline:]
        mlp_got = exchange(mlp_parts, line, nline)

        def split_rows(rk, cot, keep, send):
            keep[...] = cot[rk[4]]
            send[...] = cot[1 - rk[4]]

        half_low = ((seg, dm), BF)
        cot_keep, cot_send = call(split_rows, [half_low] * 2, (ranks, cotangent))
        cot_recv = swap(cot_send, "c", nc, 1)

        def mlp_update(rk, *refs):
            parts, refs = refs[:nline], refs[nline:]
            one_ref, alpha_ref, ck, cr, hid_keep, hid_send, dm_ref, direct, g_alpha = refs
            h = parts[0][...]
            for k in range(1, nline):
                h = h + parts[k][...].astype(F32)
            one, alpha = one_ref[...], alpha_ref[...]
            norm_h = row_norm(h)
            b = h * norm_h
            gap = b - one
            z = one + alpha * gap
            norm_z = row_norm(z)
            y = z * norm_z
            low = y.astype(BF)
            hid_keep[...] = low[:seg]
            hid_send[...] = low[seg:]
            dy = jnp.concatenate([ck[...], cr[...]], axis=0).astype(F32)
            dz = sphere_back(dy, y, norm_z)
            g_alpha[...] = jnp.sum(dz * gap, axis=0, keepdims=True)
            direct[...] = dz * (1.0 - alpha)
            dm_ref[...] = sphere_back(dz * alpha, b, norm_h).astype(BF)

        outs = call(
            mlp_update,
            [half_low, half_low, ((tk, dm), BF), full, ((1, dm), F32)],
            (ranks, *mlp_got, h_one, alpha_m, cot_keep, cot_recv),
        )
        hid_keep, hid_send, dm_low, d_one_direct, g_alpha_mlp = outs
        hid_recv = swap(hid_send, "c", nc, 1)
        dm_got = gather(dm_low, line, nline)

        def ff_back(rk, late, *refs):
            d_refs, stack = refs[:nline], refs[nline]
            su_ref, sg_ref, up_ref, gate_ref = refs[nline + 1 : nline + 5]
            refs = refs[nline + 5 :]
            parts, (d_all, dug, g_su, g_sg) = refs[:nline], refs[nline : nline + 4]
            scratch = refs[nline + 4 :]
            wug, wd = scratch[:2]
            first, third = load_ff(rk, stack, scratch)
            for copy in third + late[:2] + first + late[2:]:
                copy.start()
            for k in range(nline):
                d_all[k * tk : (k + 1) * tk, :] = d_refs[k][...]
            for copy in third + late[:2]:
                copy.wait()

            @pl.loop(0, ffq // tile)
            def _(j):
                cols = pl.ds(pl.multiple_of(j * tile, tile), tile)
                d_mixed = dot_t(d_all[...], wd[cols, :])
                up, gate = up_ref[:, cols].astype(F32), gate_ref[:, cols].astype(F32)
                su, sg = su_ref[:, cols], sg_ref[:, cols]
                v, s = gate_terms(gate, sg)
                silu = v * s
                dug[:, cols] = (d_mixed * su * silu).astype(BF)
                slope = d_mixed * su * up * (s * (1.0 + v * (1.0 - s)))
                other = pl.ds(pl.multiple_of(ffq + j * tile, tile), tile)
                dug[:, other] = (slope * sg).astype(BF)
                g_su[:, cols] = jnp.sum(d_mixed * up * silu, axis=0, keepdims=True)
                g_sg[:, cols] = jnp.sum(slope * gate, axis=0, keepdims=True)

            for copy in first:
                copy.wait()

            @pl.loop(0, dm // tile)
            def _(j):
                cols = pl.ds(pl.multiple_of(j * tile, tile), tile)
                part = dot_t(dug[...], wug[cols, :])
                for k in range(nline):
                    parts[k][:, cols] = part[k * tk : (k + 1) * tk].astype(parts[k].dtype)


        def stored(rk, g_ref, out, width, block, sems):
            d, peer, c = block // (nline * nc), (block // nc) % nline, block % nc
            spot = ((d * nc + c) * nline + (peer ^ rk[6])) * rows
            src = g_ref.at[pl.ds(pl.multiple_of(block * rows, 32), rows)]
            dst = out.at[pl.ds(pl.multiple_of(spot, 32), rows), pl.ds(0, width)]
            return pltpu.make_async_copy(src, dst, sems.at[block])

        def outer_ff(rk, h, dug, mixed_ref, d_all, out, g_ref, g_down_ref, sems, sem_d):
            def store(block):
                return stored(rk, g_ref, out, 2 * ffq, block, sems)

            @pl.loop(0, dm // tile, unroll=True)
            def _(j):
                cols = pl.ds(pl.multiple_of(j * tile, tile), tile)
                g_ref[cols, :] = tdot(h[:, cols], dug[...]).astype(BF)
                for i in range(tile // rows):
                    store(j * (tile // rows) + i).start()

            @pl.loop(0, ffq // tile, unroll=True)
            def _(j):
                cols = pl.ds(pl.multiple_of(j * tile, tile), tile)
                g_down_ref[cols, :] = tdot(mixed_ref[:, cols], d_all[...]).astype(BF)

            down = pltpu.make_async_copy(g_down_ref, out.at[:, pl.ds(2 * ffq, dm)], sem_d.at[0])
            down.start()
            down.wait()

            @pl.loop(0, ndev)
            def _(block):
                store(block).wait()

        def ff_back_all(rk, *refs):
            ins, refs = list(refs[: nline + 7]), refs[nline + 7 :]
            parts, (g_su, g_sg, out) = refs[:nline], refs[nline : nline + 3]
            d_all, dug, wug, wd, s_u, s_d, g_ref, g_down_ref, sems, sem_d = refs[nline + 3 : nline + 13]
            *held, late_sems = refs[nline + 13 :]
            late = []
            for i, dst in enumerate(held):
                late.append(pltpu.make_async_copy(ins[nline + 3 + i], dst, late_sems.at[i]))
            ins[nline + 3 :] = held
            scratch = (d_all, dug, g_su, g_sg, wug, wd, s_u, s_d)
            ff_back(rk, late, *ins[: nline + 5], *parts, *scratch)
            h, mixed_ref = ins[nline + 5 :]
            for copy in late[2:]:
                copy.wait()
            outer_ff(rk, h, dug, mixed_ref, d_all, out, g_ref, g_down_ref, sems, sem_d)

        *one_parts, g_su, g_sg, g_ff = call(
            ff_back_all,
            part_shapes + [((1, ffq), F32)] * 2 + [((dm, 2 * ffq + dm), BF)],
            (ranks, *dm_got, ff_full, my_su, my_sg, up, gate, h_all, mixed),
            hbm=(1 + nline, 4 + nline, 5 + nline, 6 + nline, 7 + nline),
            hbm_out=(nline + 2,),
            scratch=[pltpu.VMEM((nt, dm), BF), pltpu.VMEM((nt, 2 * ffq), BF)]
            + w_scratch
            + [pltpu.VMEM((dm, 2 * ffq), BF), pltpu.VMEM((ffq, dm), BF)]
            + [pltpu.SemaphoreType.DMA((ndev,)), pltpu.SemaphoreType.DMA((1,))]
            + [pltpu.VMEM((nt, ffq), BF)] * 2
            + [pltpu.VMEM((nt, dm), BF), pltpu.VMEM((nt, ffq), BF)]
            + [pltpu.SemaphoreType.DMA((4,))],
            flops=12 * nt * dm * ffq,
        )
        one_got = exchange(one_parts, line, nline)
        g_ff = lax.psum_scatter(g_ff, dpc, scatter_dimension=0, tiled=True)
        def attn_update_back(rk, *refs):
            parts, refs = refs[:nline], refs[nline:]
            direct_in, one_ref, raw_ref, ext_ref, alpha_ref, stack = refs[:6]
            d_outs, (dh_ref, direct, g_alpha, w, sems) = refs[6 : 6 + nline], refs[6 + nline :]
            copies = load_out(rk, stack, w, sems)
            for copy in copies:
                copy.start()
            d = direct_in[...] + parts[0][...]
            for k in range(1, nline):
                d = d + parts[k][...].astype(F32)
            one, raw, alpha = one_ref[...], raw_ref[...], alpha_ref[...]
            x = own_x(ext_ref)
            norm_raw = row_norm(raw)
            b = raw * norm_raw
            gap = b - x
            norm_z = row_norm(x + alpha * gap)
            dz = sphere_back(d, one, norm_z)
            g_alpha[...] = jnp.sum(dz * gap, axis=0, keepdims=True)
            direct[...] = dz * (1.0 - alpha)
            dh_ref[...] = sphere_back(dz * alpha, b, norm_raw).astype(BF)
            for copy in copies:
                copy.wait()
            for k in range(nline):
                w_k = w[pl.ds(pl.multiple_of((rk[6] ^ k) * hc, hc), hc), :]
                d_outs[k][...] = dot_t(dh_ref[...], w_k).astype(BF)

        outs = call(
            attn_update_back,
            [((tk, hc), BF)] * nline + [((tk, dm), BF), full, ((1, dm), F32)],
            (ranks, *one_got, d_one_direct, h_one, h_attn, mine, alpha_a, ff_full),
            hbm=(6 + nline,),
            scratch=out_scratch,
            flops=2 * tk * dm * dm,
        )
        d_att_parts, (dh_low, d_x_direct, g_alpha_attn) = outs[:nline], outs[nline:]
        d_att = exchange(d_att_parts, line, nline)

        def attn_back(rk, late, *refs):
            d_refs, refs = refs[:nline], refs[nline:]
            w_ref, rq_ref, rk_ref, q_ref, k_ref, v_ref, bias_ref, cs_ref, gain = refs[:9]
            full_ref, inv_ref, refs = refs[9], refs[10], refs[11:]
            parts, (d_ref, g_gain, do_ref, dq_ref, dk_ref) = refs[:nline], refs[nline:]
            for k in range(nline):
                do_ref[k * tk : (k + 1) * tk, :] = d_refs[k][...]
            for h in range(nheads):
                at_h = slice(h * HEAD_DIM, (h + 1) * HEAD_DIM)
                q, key, do = q_ref[:, at_h], k_ref[:, at_h], do_ref[:, at_h]
                raw = jnp.exp(dot_t(q, key) + bias_ref[...].astype(F32))
                p = raw * inv_ref[:, h : h + 1]
                delta = jnp.sum(do.astype(F32) * full_ref[:, at_h], axis=1, keepdims=True)
                ds = (p * (dot_t(do, v_ref[:, at_h]) - delta)).astype(BF)
                p = p.astype(BF)
                at_v = slice(2 * hc + h * HEAD_DIM, 2 * hc + (h + 1) * HEAD_DIM)
                d_ref[:, at_v] = tdot(p, do).astype(BF)
                dq_ref[:, at_h] = scale * dot(ds, key)
                dk_ref[:, at_h] = tdot(ds, q)
            for copy in late:
                copy.wait()
            cs = cs_ref[...]
            cos = jnp.concatenate([cs[:, :128]] * (hc // 128), axis=1)
            sin = jnp.concatenate([cs[:, 128:]] * (hc // 128), axis=1)
            low = low_half()
            for i, (raw_ref, g_ref) in enumerate(((rq_ref, dq_ref), (rk_ref, dk_ref))):
                for h in range(nheads):
                    at_h = slice(h * HEAD_DIM, (h + 1) * HEAD_DIM)
                    turned, g = raw_ref[:, at_h], g_ref[:, at_h]
                    norm = lax.rsqrt(jnp.sum(turned * turned, axis=1, keepdims=True) + EPS)
                    unit = turned * norm
                    term = jnp.sum(g * unit, axis=0, keepdims=True)
                    g_gain[:, at_h] = term if i == 0 else g_gain[:, at_h] + term
                    g = g * gain[:, at_h]
                    g_ref[:, at_h] = norm * (g - unit * jnp.sum(unit * g, axis=1, keepdims=True))
                g = g_ref[...]
                d_ref[:, i * hc : (i + 1) * hc] = (g * cos - heads_swap(g, low) * sin).astype(BF)

            @pl.loop(0, dm // tile)
            def _(j):
                cols = pl.ds(pl.multiple_of(j * tile, tile), tile)
                part = dot_t(d_ref[...], w_ref[cols, :])
                for k in range(nline):
                    parts[k][:, cols] = part[k * tk : (k + 1) * tk].astype(parts[k].dtype)


        at_line = ranks[6]
        mine_ff = (jnp.arange(nline) == at_line)[None, :, None, None]

        def ff_owner(vec):
            return jnp.where(mine_ff, vec.reshape(nyx, 1, nc, ffb), 0.0).reshape(ndev, ffb)

        misc = [v.reshape(ndev, rows) for v in (g_alpha_attn, g_alpha_mlp)]
        misc = jnp.pad(jnp.concatenate(misc, axis=1), ((0, 0), (0, ffb - 2 * rows)))
        vecs = jnp.stack([ff_owner(g_su), ff_owner(g_sg), misc], axis=1).astype(BF)
        vecs = jnp.pad(vecs, ((0, 0), (0, rows - 3), (0, 0))).reshape(dm, ffb)

        wide = 3 * hc + ffb

        def outer_out(rk, dh, *refs):
            parts, outs, (g_ref, sems) = refs[:nline], refs[nline : nline + 2], refs[nline + 2 :]
            for k in range(nline):
                spot = pl.ds(pl.multiple_of((rk[6] ^ k) * hc, hc), hc)
                own = parts[k][k * tk : (k + 1) * tk, :]
                g_ref[spot, :] = tdot(own, dh[...]).astype(BF)
            copies = []
            for cr in range(nc):
                for a in range(nyx):
                    for b in range(nline):
                        row = ((rk[5] ^ a) * nline + (rk[6] ^ b)) * nc + (rk[4] ^ cr)
                        src = g_ref.at[pl.ds(pl.multiple_of(row * rows, 32), rows)]
                        dst = outs[cr].at[pl.ds((a * nline + b) * rows, rows)]
                        copies.append(pltpu.make_async_copy(src, dst, sems.at[len(copies)]))
            for copy in copies:
                copy.start()
            for copy in copies:
                copy.wait()

        keep, send = call(
            outer_out,
            [((dm // nc, dm), BF)] * nc,
            (ranks, dh_low, *att_got),
            hbm_out=(0, 1),
            scratch=[pltpu.VMEM((dm, dm), BF), pltpu.SemaphoreType.DMA((ndev,))],
            flops=2 * tk * dm * dm,
        )

        def core_add(rk, a, b, *outs):
            for i in range(nyx):
                here = slice(i * ffb, (i + 1) * ffb)
                outs[i][...] = (a[here, :].astype(F32) + b[here, :].astype(F32)).astype(BF)

        out_sum = call(
            core_add, [((ffb, dm), BF)] * nyx, (ranks, keep, swap(send, "c", nc, 1))
        )
        out_got = exchange(out_sum, yx, nyx)

        def outer_last(rk, x_ref, d_ref, vec_ref, g_gain, out, g_ref, sems):

            def store(block):
                return stored(rk, g_ref, out, wide, block, sems)

            g_ref[:, 3 * hc : wide] = vec_ref[...]
            third = lax.broadcasted_iota(jnp.int32, (16, ffb), 0) == 2
            for i in range(hc // rows):
                spot = pl.ds(pl.multiple_of((rk[6] * (hc // rows) + i) * rows, 32), 16)
                run = [jnp.zeros((1, 2 * rows), F32), g_gain[:, i * rows : (i + 1) * rows]]
                run = jnp.concatenate(run + [jnp.zeros((1, ffb - 3 * rows), F32)], axis=1)
                held = g_ref[spot, 3 * hc : wide].astype(F32)
                g_ref[spot, 3 * hc : wide] = (held + jnp.where(third, run, 0.0)).astype(BF)

            @pl.loop(0, dm // tile)
            def _(j):
                cols = pl.ds(pl.multiple_of(j * tile, tile), tile)
                g_ref[cols, : 3 * hc] = tdot(x_ref[:, cols], d_ref[...]).astype(BF)
                for i in range(tile // rows):
                    store(j * (tile // rows) + i).start()

            @pl.loop(0, ndev)
            def _(block):
                store(block).wait()

        def attn_back_all(rk, *refs):
            ins, refs = list(refs[: nline + 13]), refs[nline + 13 :]
            parts, out = refs[:nline], refs[nline]
            d_ref, g_gain, do_ref, dq_ref, dk_ref, g_ref, sems = refs[nline + 1 : nline + 8]
            *held, late_sems = refs[nline + 8 :]
            late = []
            for i, (at_in, dst) in enumerate(zip(late_back, held)):
                late.append(pltpu.make_async_copy(ins[at_in - 1], dst, late_sems.at[i]))
                ins[at_in - 1] = dst
            for copy in late:
                copy.start()
            x_ref, vec_ref = ins[nline + 11 :]
            scratch = (d_ref, g_gain, do_ref, dq_ref, dk_ref)
            attn_back(rk, late, *ins[: nline + 11], *parts, *scratch)
            outer_last(rk, x_ref, d_ref, vec_ref, g_gain, out, g_ref, sems)

        late_back = [1 + nline, 2 + nline, 3 + nline, 8 + nline, 12 + nline]
        late_shapes = [((dm, 3 * hc), BF), ((nt, hc), F32), ((nt, hc), F32), ((nt, 256), F32)]
        late_shapes.append(((nt, dm), BF))

        *x_parts, g_last = call(
            attn_back_all,
            part_shapes + [((dm, wide), BF)],
            (ranks, *d_att, w_qkv, r_q, r_k, q_low, k_low, v_low, bias, cs, my_gain, att_full, inv)
            + (x_all, vecs),
            hbm=late_back,
            hbm_out=(nline,),
            scratch=[
                pltpu.VMEM((nt, 3 * hc), BF), pltpu.VMEM((1, hc), F32),
                pltpu.VMEM((nt, hc), BF), pltpu.VMEM((nt, hc), F32), pltpu.VMEM((nt, hc), F32),
                pltpu.VMEM((dm, wide), BF), pltpu.SemaphoreType.DMA((ndev,)),
                *[pltpu.VMEM(*shape) for shape in late_shapes], pltpu.SemaphoreType.DMA((5,)),
            ],
            flops=4 * nt * dm * 3 * hc + 10 * nt * nt * hc,
        )
        x_got = exchange(x_parts, line, nline)


        g_last = lax.psum_scatter(g_last, dpc, scatter_dimension=0, tiled=True)

        def split_ff(rk, *refs):
            parts, (g_ref, down), outs = refs[:nyx], refs[nyx : nyx + 2], refs[nyx + 2 :]
            down[...] = g_ref[:, 2 * ffq :].astype(F32)
            for k in range(nline):
                here = slice(k * rows, (k + 1) * rows)
                outs[k][:, : 2 * ffq] = g_ref[here, : 2 * ffq]
                total = parts[0][here, :].astype(F32)
                for j in range(1, nyx):
                    total = total + parts[j][here, :].astype(F32)
                outs[k][:, 2 * ffq :] = total.astype(BF)

        g_down, *g_parts = call(
            split_ff,
            [((ffb, dm), F32)] + [((rows, 2 * ffq + dm), BF)] * nline,
            (ranks, *out_got, g_ff),
            after=tuple(x_got[1:]),
        )
        g_parts = exchange(g_parts, line, nline)

        def place_ff(rk, *refs):
            parts, outs, g_o = refs[:nline], refs[nline : nline + 2], refs[nline + 2]
            total = parts[0][:, 2 * ffq :].astype(F32)
            for k in range(nline):
                for d, cols in enumerate(ff_cols(rk, k)):
                    for i in range(2):
                        here = i * ffq + d * sub
                        outs[i][:, cols] = parts[k][:, here : here + sub].astype(F32)
                if k:
                    total = total + parts[k][:, 2 * ffq :].astype(F32)
            g_o[...] = total

        g_up, g_gate, g_out = call(
            place_ff, [((rows, ff), F32)] * 2 + [((rows, dm), F32)], (ranks, *g_parts)
        )

        def finish_tokens(rk, *refs):
            parts, (direct, keep, send) = refs[:nline], refs[nline:]
            d = direct[...] + parts[0][...]
            for k in range(1, nline):
                d = d + parts[k][...].astype(F32)
            keep[...] = d[:seg]
            send[...] = d[seg:].astype(BF)

        x_keep, x_send = call(
            finish_tokens, [((seg, dm), F32), half_low], (ranks, *x_got, d_x_direct)
        )
        x_recv = swap(x_send, "c", nc, 1)

        def join_rows(rk, keep, recv, out):
            out[rk[4]] = keep[...].astype(out.dtype)
            out[1 - rk[4]] = recv[...].astype(out.dtype)

        (tokens_grad,) = call(join_rows, [((nseq, seg, dm), F32)], (ranks, x_keep, x_recv))
        (hidden_out,) = call(join_rows, [((nseq, seg, dm), BF)], (ranks, hid_keep, hid_recv))

        def split_last(rk, g_ref, *outs):
            for k in range(nline):
                outs[k][...] = g_ref[k * rows : (k + 1) * rows, :]

        last = call(
            split_last,
            [((rows, wide), BF)] * nline,
            (ranks, g_last),
            after=(tokens_grad, hidden_out, g_parts[1]),
        )
        last = exchange(last, line, nline)

        def place_last(rk, *refs):
            parts, outs, vec_outs = refs[:nline], refs[nline : nline + 3], refs[nline + 3 :]
            v_sum = None
            for k in range(nline):
                cols = pl.ds(pl.multiple_of((rk[6] ^ k) * hc, 128), hc)
                for i in range(3):
                    outs[i][:, cols] = parts[k][:, i * hc : (i + 1) * hc].astype(F32)
                vec = parts[k][:16, 3 * hc : wide].astype(F32)
                v_sum = vec if v_sum is None else v_sum + vec
            vec_outs[0][...] = v_sum[:1]
            vec_outs[1][...] = v_sum[1:2]
            for i in range(3):
                vec_outs[2 + i][...] = v_sum[2:3, i * rows : (i + 1) * rows]

        g_query, g_key, g_value, *vecs = call(
            place_last,
            [((rows, dm), F32)] * 3
            + [((1, ffb), F32)] * 2
            + [((1, rows), F32)] * 3,
            (ranks, *last),
        )
        g_s_up, g_s_gate, g_aa, g_am, g_sqk = [v.reshape(-1) for v in vecs]
        return (
            hidden_out, tokens_grad, g_query, g_key, g_value, g_out, g_up, g_gate, g_down,
            g_sqk, g_aa, g_s_up, g_s_gate, g_am,
        )

    return body


def make_body(sizes):
    plain, kernels = make_plain(sizes), make_kernels(sizes)
    ndev = math.prod(sizes)
    nline = sizes[2] * sizes[3]

    def body(*args):
        tokens, w_query, w_up = args[0], args[2], args[6]
        fits = w_query.shape[0] % 32 == 0 and (w_up.shape[1] // ndev) % 128 == 0
        fits = fits and (tokens.shape[2] // nline) % 256 == 0 and tokens.shape[1] == 64
        return (kernels if fits else plain)(*args)

    return body


def solution(mesh):
    ndp, nblk = mesh.shape["dp"], mesh.shape["blk"]
    sizes = (ndp // 2, 2, nblk // 4, 2, 2)
    fine = Mesh(mesh.devices.reshape(sizes), ("y", "x", "w", "z", "c"))
    rows, cols = ("y", "x"), ("w", "z", "c")
    flat = rows + cols
    seq = P(rows, cols, None)
    weight = P(flat, None)
    return jax.shard_map(
        make_body(sizes),
        mesh=fine,
        in_specs=(seq, P(rows, cols)) + (weight,) * 7 + (P(),) * 5 + (seq,),
        out_specs=(seq, seq) + (weight,) * 7 + (P(flat),) * 5,
        check_vma=False,
    )
```

```python
import math

import jax
import jax.numpy as jnp
from jax import lax
from jax.experimental import pallas as pl
from jax.experimental.pallas import tpu as pltpu
from jax.sharding import Mesh
from jax.sharding import PartitionSpec as P

HEADS = 16
HEAD_DIM = 64
EPS = 1e-06
NEG = -1e30
BF = jnp.bfloat16
F32 = jnp.float32


def dot(a, b):
    return jnp.dot(a, b, preferred_element_type=F32)


def dot_t(a, b):
    return lax.dot_general(a, b, (((1,), (1,)), ((), ())), preferred_element_type=F32)


def tdot(a, b):
    return lax.dot_general(a, b, (((0,), (0,)), ((), ())), preferred_element_type=F32)


def rotate(tensor, cosines, sines):
    half_dim = tensor.shape[-1] // 2
    front = tensor[..., :half_dim]
    behind = tensor[..., half_dim:]
    return jnp.concatenate(
        [front * cosines - behind * sines, behind * cosines + front * sines], axis=-1
    )


def sphere(tensor):
    return tensor * lax.rsqrt(jnp.mean(tensor * tensor, axis=-1, keepdims=True) + EPS)


def head_unit(tensor, gains):
    return gains * tensor * lax.rsqrt(jnp.sum(tensor * tensor, axis=-1, keepdims=True) + EPS)


def residual_step(branch, residual_in, alpha):
    return sphere(residual_in + alpha * (sphere(branch) - residual_in))


def gating(up_proj, gate_proj, scale_up, scale_gate):
    return scale_up * up_proj * jax.nn.silu(scale_gate * gate_proj)


def make_plain(sizes):
    ny, nx, nw, nz, nc = sizes
    ndev = ny * nx * nw * nz * nc
    line = ("w", "z")
    nline = nw * nz
    quad = ("x", "z")
    nquad = nx * nz

    def swap(value, axes, count, k):
        return lax.ppermute(value, axes, [(i, i ^ k) for i in range(count)])

    def gather_rel(value, axes, count):
        return [value] + [swap(value, axes, count, k) for k in range(1, count)]

    def exchange_rel(chunks, axes, count):
        return [chunks[0]] + [swap(chunks[k], axes, count, k) for k in range(1, count)]

    def sum_rel(chunks, axes, count, kind=BF):
        got = exchange_rel([c.astype(kind) for c in chunks], axes, count)
        total = chunks[0].astype(F32)
        for piece in got[1:]:
            total = total + piece.astype(F32)
        return total

    def double(value, stages):
        for axis, count, k in stages:
            value = jnp.concatenate([value, swap(value, axis, count, k)], axis=0)
        return value

    def halve(value, stages, kind=BF):
        for axis, count, k in stages[::-1]:
            half = value.shape[0] // 2
            other = swap(value[half:].astype(kind), axis, count, k)
            value = value[:half].astype(F32) + other.astype(F32)
        return value

    def bits(axis, count):
        return [(axis, count, 1 << b) for b in range(count.bit_length() - 1)]

    def ranks(order):
        count = dict(y=ny, x=nx, w=nw, z=nz, c=nc)
        shape = [count[axis] for axis in order]
        found = {}
        for i, axis in enumerate(order):
            shifted = jnp.arange(count[axis]) ^ lax.axis_index(axis)
            found[axis] = shifted.reshape((-1,) + (1,) * (len(order) - 1 - i))
        flat = jnp.zeros(shape, jnp.int32)
        return found, flat

    def reorder(order, target):
        found, flat = ranks(order)
        count = dict(y=ny, x=nx, w=nw, z=nz, c=nc)
        index = flat
        for axis in target:
            index = index * count[axis] + found[axis]
        return index.reshape(-1)

    def place(pieces, rank):
        stack = jnp.stack(pieces)
        order = rank ^ jnp.arange(len(pieces))
        return jnp.take(stack, order, axis=0)

    def pick(array, rank, count):
        return [lax.dynamic_index_in_dim(array, rank ^ k, 0, False) for k in range(count)]

    def body(
        tokens, doc_ids, w_query, w_key, w_value, w_out, w_up, w_gate, w_down,
        s_qk, alpha_attn, s_up, s_gate, alpha_mlp, cotangent,
    ):
        nseq, seg, dm = tokens.shape
        rows = w_query.shape[0]
        ff = w_up.shape[1]
        ffq = ff // nquad
        ffb = ff // ndev
        hcols = dm // nline
        nheads = HEADS // nline
        score_scale = math.sqrt(HEAD_DIM)
        c_at = lax.axis_index("c")
        line_at = lax.axis_index(line)
        quad_at = lax.axis_index(quad)

        def by_line(w):
            return w.astype(BF).reshape(rows, nline, hcols)

        w_qkv = jnp.stack([by_line(w_query), by_line(w_key), by_line(w_value)], axis=2)
        w_qkv = w_qkv.transpose(1, 0, 2, 3).reshape(nline, rows, 3 * hcols)
        got = jnp.stack(exchange_rel(pick(w_qkv, line_at, nline), line, nline))
        got = jnp.stack(gather_rel(got, ("y", "x"), ny * nx))
        full = double(got[None], bits("c", nc)).reshape(ndev, rows, 3 * hcols)
        full_qkv = jnp.take(full, reorder("yxwzc", "cyxwz"), axis=0).reshape(dm, 3 * hcols)
        full_out = lax.all_gather(w_out.astype(BF), ("y", "x", "w", "z", "c"), axis=0, tiled=True)

        def by_quad(w):
            w = w.astype(BF).reshape(rows, ny, nx, nw, nz, nc, ffb)
            return w.transpose(2, 4, 0, 1, 3, 5, 6).reshape(nquad, rows, ffq)

        w_ug = jnp.concatenate([by_quad(w_up), by_quad(w_gate)], axis=2)
        got = jnp.stack(exchange_rel(pick(w_ug, quad_at, nquad), quad, nquad))
        stages = bits("w", nw) + bits("y", ny) + bits("c", nc)

        def ff_full(part):
            full = double(part[None], stages).reshape(ndev, rows, ffq)
            return jnp.take(full, reorder("yxwzc", "cywxz"), axis=0).reshape(dm, ffq)

        full_up, full_gate = ff_full(got[:, :, :ffq]), ff_full(got[:, :, ffq:])
        full_down = double(w_down.astype(BF)[None], stages)
        full_down = jnp.take(full_down, reorder("ywc", "cyw"), axis=0).reshape(ffq, dm)

        def my_ff(vec):
            v = vec.reshape(ny, nx, nw, nz, nc, ffb).transpose(1, 3, 0, 2, 4, 5)
            return lax.dynamic_index_in_dim(v.reshape(nquad, ffq), quad_at, 0, False)

        my_s_up, my_s_gate = my_ff(s_up), my_ff(s_gate)
        my_gain = lax.dynamic_index_in_dim(s_qk.reshape(nline, hcols), line_at, 0, False)

        def to_row(value):
            keep = lax.dynamic_index_in_dim(value, c_at, 0, False)
            send = lax.dynamic_index_in_dim(value, 1 - c_at, 0, False)
            return jnp.concatenate([keep, lax.ppermute(send, "c", [(0, 1), (1, 0)])], axis=0)

        def from_row(value, send_type):
            keep, send = value[:seg], value[seg:]
            other = lax.ppermute(send.astype(send_type), "c", [(0, 1), (1, 0)])
            pair = jnp.stack([keep, other.astype(value.dtype)])
            return jnp.where(c_at == 0, pair, pair[::-1])

        docs = doc_ids.astype(BF)
        extra = jnp.zeros((nseq, 16, dm), BF).at[:, 0, :seg].set(docs)
        ext = jnp.concatenate([tokens, extra], axis=1)
        mine = to_row(ext).reshape(2, seg + 16, dm)
        everyone = jnp.stack(gather_rel(mine, line, nline))
        row_tokens = everyone[:, :, :seg].reshape(nline * 2 * seg, dm)
        row_docs = everyone[:, :, seg, :seg].reshape(-1).astype(F32)
        peers = line_at ^ jnp.arange(nline)
        seg_at = 2 * peers[:, None] + jnp.stack([c_at, 1 - c_at])[None, :]
        index = (seg_at[:, :, None] * seg + jnp.arange(seg)).reshape(-1)
        start = jnp.sum((row_docs[None, :] < row_docs[:, None]).astype(jnp.int32), axis=1)
        pos = index - start
        allowed = (index[None, :] <= index[:, None]) & (index[None, :] >= start[:, None])
        frequency = 10000.0 ** (-jnp.arange(HEAD_DIM // 2, dtype=F32) / (HEAD_DIM // 2))
        angles = pos.astype(F32)[:, None] * frequency
        cosines, sines = jnp.cos(angles)[:, None, :], jnp.sin(angles)[:, None, :]
        nt = row_tokens.shape[0]
        x_low = mine[:, :seg].reshape(2 * seg, dm)
        x_row = x_low.astype(F32)

        pre = dot(row_tokens, full_qkv)

        def heads(t):
            return t.reshape(nt, nheads, HEAD_DIM)

        def unit_pair(q_pre, k_pre, gains):
            gains = gains.reshape(nheads, HEAD_DIM)
            return (
                head_unit(rotate(heads(q_pre), cosines, sines), gains),
                head_unit(rotate(heads(k_pre), cosines, sines), gains),
            )

        (q_unit, k_unit), unit_pull = jax.vjp(
            unit_pair, pre[:, :hcols], pre[:, hcols : 2 * hcols], my_gain
        )
        q_low, k_low = q_unit.astype(BF), k_unit.astype(BF)
        v_low = heads(pre[:, 2 * hcols :].astype(BF))
        scores = jnp.einsum("qhd,khd->hqk", q_low, k_low, preferred_element_type=F32) * score_scale
        scores = jnp.where(allowed[None], scores, NEG)
        peak = jnp.max(scores, axis=-1, keepdims=True)
        raw = jnp.where(allowed[None], jnp.exp(scores - peak), 0.0)
        probs = raw / jnp.sum(raw, axis=-1, keepdims=True)
        p_low = probs.astype(BF)
        attended = jnp.einsum("hqk,khd->qhd", p_low, v_low, preferred_element_type=F32)
        att_low = attended.astype(BF).reshape(nline, 2 * seg, hcols)
        got = place(exchange_rel([att_low[k] for k in range(nline)], line, nline), line_at)
        att_mine = got.transpose(1, 0, 2).reshape(2 * seg, dm)

        h_attn = dot(att_mine, full_out)
        h_one, attn_pull = jax.vjp(residual_step, h_attn, x_row, alpha_attn)
        h_low = jnp.concatenate(gather_rel(h_one.astype(BF), quad, nquad), axis=0)
        up, gate = dot(h_low, full_up), dot(h_low, full_gate)
        mixed, gate_pull = jax.vjp(gating, up, gate, my_s_up, my_s_gate)
        mixed_low = mixed.astype(BF)
        part = dot(mixed_low, full_down).reshape(nquad, 2 * seg, dm)
        h_mlp = sum_rel([part[k] for k in range(nquad)], quad, nquad)
        result, out_pull = jax.vjp(residual_step, h_mlp, h_one, alpha_mlp)
        hidden_out = from_row(result.astype(BF), BF)

        d_result = to_row(cotangent).astype(F32)
        d_hmlp, d_hone, g_alpha_mlp = out_pull(d_result)
        dm_low = jnp.concatenate(gather_rel(d_hmlp.astype(BF), quad, nquad), axis=0)
        d_mixed = dot_t(dm_low, full_down)
        d_up, d_gate, g_s_up, g_s_gate = gate_pull(d_mixed)
        du_low, dg_low = d_up.astype(BF), d_gate.astype(BF)
        part = dot_t(du_low, full_up) + dot_t(dg_low, full_gate)
        part = part.reshape(nquad, 2 * seg, dm)
        d_hone = d_hone + sum_rel([part[k] for k in range(nquad)], quad, nquad)
        g_down = tdot(mixed_low, dm_low).reshape(ny * nw * nc, ffb, dm)
        g_down = halve(jnp.take(g_down, reorder("cyw", "ywc"), axis=0), stages)[0]

        def ff_scatter(left, right):
            part = tdot(left, right).reshape(ndev, rows, ffq)
            part = jnp.take(part, reorder("cywxz", "yxwzc"), axis=0)
            part = halve(part.reshape(ny * nw * nc, nquad, rows, ffq), stages)[0].astype(BF)
            got = place(exchange_rel([part[k] for k in range(nquad)], quad, nquad), quad_at)
            got = got.reshape(nx, nz, rows, ny, nw, nc, ffb).transpose(2, 3, 0, 4, 1, 5, 6)
            return got.reshape(rows, ff).astype(F32)

        g_up, g_gate = ff_scatter(h_low, du_low), ff_scatter(h_low, dg_low)

        d_hattn, d_tokens, g_alpha_attn = attn_pull(d_hone)
        dh_low = d_hattn.astype(BF)

        def to_owner(part, kind=BF):
            part = jnp.take(part, reorder("cyxwz", "yxwzc"), axis=0)
            part = halve(part.reshape((nc, ny * nx, nline) + part.shape[1:]), bits("c", nc), kind)[0]
            part = sum_rel([part[k] for k in range(ny * nx)], ("y", "x"), ny * nx, kind)
            return sum_rel([part[k] for k in range(nline)], line, nline, kind)

        g_out = to_owner(tdot(att_mine, dh_low).reshape(ndev, rows, dm))
        d_att = dot_t(dh_low, full_out).astype(BF).reshape(2 * seg, nline, hcols).transpose(1, 0, 2)
        d_att = jnp.concatenate(
            exchange_rel(pick(d_att, line_at, nline), line, nline), axis=0
        ).reshape(nt, nheads, HEAD_DIM)
        delta = jnp.sum(d_att.astype(F32) * attended, axis=-1)
        d_probs = jnp.einsum("qhd,khd->hqk", d_att, v_low, preferred_element_type=F32)
        d_scores = (probs * (d_probs - delta.T[:, :, None])).astype(BF)
        d_q = score_scale * jnp.einsum("hqk,khd->qhd", d_scores, k_low, preferred_element_type=F32)
        d_k = score_scale * jnp.einsum("hqk,qhd->khd", d_scores, q_low, preferred_element_type=F32)
        d_v = jnp.einsum("hqk,qhd->khd", p_low, d_att, preferred_element_type=F32)
        d_qpre, d_kpre, g_sqk = unit_pull((d_q, d_k))
        d_qkv = jnp.concatenate([d_qpre, d_kpre, d_v.reshape(nt, hcols)], axis=1).astype(BF)
        part = dot_t(d_qkv, full_qkv).reshape(nline, 2 * seg, dm)
        tokens_grad = d_tokens + sum_rel([part[k] for k in range(nline)], line, nline)
        tokens_grad = from_row(tokens_grad, BF)
        g_qkv = tdot(row_tokens, d_qkv).reshape(ndev, rows, 3 * hcols)
        g_qkv = jnp.take(g_qkv, reorder("cyxwz", "yxwzc"), axis=0)
        g_qkv = halve(g_qkv.reshape(nc, ny * nx, nline, rows, 3 * hcols), bits("c", nc))[0]
        g_qkv = sum_rel([g_qkv[k] for k in range(ny * nx)], ("y", "x"), ny * nx).astype(BF)
        got = place(exchange_rel([g_qkv[k] for k in range(nline)], line, nline), line_at)
        got = got.reshape(nline, rows, 3, hcols).transpose(2, 1, 0, 3).reshape(3, rows, dm)
        g_query, g_key, g_value = got.astype(F32)

        def spread(vec, rank, count):
            return jnp.where(jnp.arange(count)[:, None] == rank, vec[None], 0.0)

        def ff_order(vec):
            v = spread(vec, quad_at, nquad).reshape(nx, nz, ny, nw, nc, ffb)
            return v.transpose(2, 0, 3, 1, 4, 5).reshape(ndev, ffb)

        vecs = jnp.concatenate(
            [
                spread(g_sqk, line_at, nline).reshape(ndev, -1),
                g_alpha_attn.reshape(ndev, -1),
                ff_order(g_s_up),
                ff_order(g_s_gate),
                g_alpha_mlp.reshape(ndev, -1),
            ],
            axis=1,
        )
        vecs = to_owner(vecs, F32)
        cuts = [rows, 2 * rows, 2 * rows + ffb, 2 * rows + 2 * ffb]
        g_sqk, g_alpha_attn, g_s_up, g_s_gate, g_alpha_mlp = jnp.split(vecs, cuts)
        return (
            hidden_out, tokens_grad, g_query, g_key, g_value, g_out, g_up, g_gate, g_down,
            g_sqk, g_alpha_attn, g_s_up, g_s_gate, g_alpha_mlp,
        )

    return body


VM = pl.BlockSpec(memory_space=pltpu.VMEM)
SM = pl.BlockSpec(memory_space=pltpu.SMEM)
HB = pl.BlockSpec(memory_space=pltpu.HBM)


def call(kernel, outs, args, hbm=(), hbm_out=(), scratch=(), flops=0, mib=60, after=()):
    moved = sum(math.prod(a.shape) * a.dtype.itemsize for a in args)
    moved += sum(math.prod(s) * jnp.dtype(d).itemsize for s, d in outs)
    count = len(args)

    def run(*refs):
        kernel(*refs[:count], *refs[count + len(after) :])

    specs = [SM] + [HB if i in hbm else VM for i in range(1, count)]
    specs += [pl.BlockSpec(memory_space=pl.ANY)] * len(after)
    return pl.pallas_call(
        run,
        out_shape=[jax.ShapeDtypeStruct(s, d) for s, d in outs],
        in_specs=specs,
        out_specs=[HB if i in hbm_out else VM for i in range(len(outs))],
        scratch_shapes=list(scratch),
        compiler_params=pltpu.CompilerParams(vmem_limit_bytes=mib << 20),
        cost_estimate=pl.CostEstimate(flops=flops, bytes_accessed=moved, transcendentals=0),
    )(*args, *after)


def row_norm(v):
    return lax.rsqrt(jnp.mean(v * v, axis=-1, keepdims=True) + EPS)


def sphere_back(dy, y, norm):
    return (dy - y * jnp.mean(dy * y, axis=-1, keepdims=True)) * norm


def make_kernels(sizes):
    ny, nx, nw, nz, nc = sizes
    ndev = ny * nx * nw * nz * nc
    nyx, nline = ny * nx, nw * nz
    ndpc = nyx * nc
    line, yx, dpc = ("w", "z"), ("y", "x"), ("y", "x", "c")

    def swap(value, axes, count, k):
        return lax.ppermute(value, axes, [(i, i ^ k) for i in range(count)])

    def exchange(chunks, axes, count):
        return [chunks[0]] + [swap(chunks[k], axes, count, k) for k in range(1, count)]

    def gather(value, axes, count):
        return exchange([value] * count, axes, count)

    def body(
        tokens, doc_ids, w_query, w_key, w_value, w_out, w_up, w_gate, w_down,
        s_qk, alpha_attn, s_up, s_gate, alpha_mlp, cotangent,
    ):
        nseq, seg, dm = tokens.shape
        rows = w_query.shape[0]
        ff = w_up.shape[1]
        ffq, ffb = ff // nline, ff // ndev
        sub = nc * ffb
        hc = dm // nline
        nheads = HEADS // nline
        nt = nline * 2 * seg
        tk = 2 * seg
        pad = 16
        ext = seg + pad
        scale = math.sqrt(HEAD_DIM)
        tile = 256

        at = [lax.axis_index(a) for a in "yxwzc"]
        ranks = jnp.stack(at + [lax.axis_index(yx), lax.axis_index(line)])
        ranks = ranks.astype(jnp.int32)

        def pack_tokens(rk, tok, docs, keep, send):
            c = rk[4]
            first = lax.broadcasted_iota(jnp.int32, (pad, dm), 0) == 0
            for out, which in ((keep, c), (send, 1 - c)):
                out[:seg] = tok[which]
                out[seg:] = jnp.where(first, docs[which], 0.0).astype(BF)

        def ff_cols(rk, k):
            runs = [(d * nline + (rk[6] ^ k)) * sub for d in range(nyx)]
            return [pl.ds(pl.multiple_of(run, 128), sub) for run in runs]

        def pack_qkv(rk, wq, wk, wv, *outs):
            for k in range(nline):
                cols = pl.ds(pl.multiple_of((rk[6] ^ k) * hc, 128), hc)
                for i, w in enumerate((wq, wk, wv)):
                    outs[k][:, i * hc : (i + 1) * hc] = w[:, cols].astype(BF)

        def pack_weights(rk, wu, wg, wo, gain, su, sg, *outs):
            for k in range(nline):
                out_ff = outs[k]
                for d, cols in enumerate(ff_cols(rk, k)):
                    for i, w in enumerate((wu, wg)):
                        here = i * ffq + d * sub
                        out_ff[:, here : here + sub] = w[:, cols].astype(BF)
                out_ff[:, 2 * ffq :] = wo[...].astype(BF)
            outs[nline][...] = gain[:, pl.ds(pl.multiple_of(rk[6] * hc, 128), hc)]
            for d, cols in enumerate(ff_cols(rk, 0)):
                here = slice(d * sub, (d + 1) * sub)
                outs[nline + 1][:, here] = su[:, cols]
                outs[nline + 2][:, here] = sg[:, cols]

        docs = jnp.pad(doc_ids.astype(F32), ((0, 0), (0, dm - seg))).reshape(nseq, 1, dm)
        packed = call(
            pack_qkv, [((rows, 3 * hc), BF)] * nline, (ranks, w_query, w_key, w_value)
        )
        keep, send = call(pack_tokens, [((ext, dm), BF)] * 2, (ranks, tokens, docs), after=(packed[0],))

        def join_tokens(rk, near, far, out):
            out[:seg] = near[:seg]
            out[seg:tk] = far[:seg]
            row = lax.broadcasted_iota(jnp.int32, (pad, dm), 0)
            ids = far[seg:].astype(F32)[:1]
            out[tk:] = jnp.where(row == 1, ids, near[seg:].astype(F32)).astype(BF)

        (mine,) = call(join_tokens, [((tk + pad, dm), BF)], (ranks, keep, swap(send, "c", nc, 1)))
        packed_ff = call(
            pack_weights,
            [((rows, 2 * ffq + dm), BF)] * nline
            + [((1, hc), F32)]
            + [((1, ffq), F32)] * 2,
            (ranks, w_up, w_gate, w_out, s_qk.reshape(1, dm))
            + (s_up.reshape(1, ff), s_gate.reshape(1, ff)),
            after=(keep,),
        )
        packed_ff, (my_gain, my_su, my_sg) = packed_ff[:nline], packed_ff[nline:]

        w_got = exchange(packed, line, nline)
        ff_got = exchange(packed_ff, line, nline)
        pieces = gather(mine, line, nline)

        def stack(rk, *refs):
            for k in range(nline):
                refs[nline][k * rows : (k + 1) * rows, :] = refs[k][...]

        (got,) = call(stack, [((ffb, 3 * hc), BF)], (ranks, *w_got))
        qkv_full = lax.all_gather(got, dpc, axis=0, tiled=True)

        def stack_ff(rk, *refs):
            parts, (wd, out) = refs[:nline], refs[nline:]
            for k in range(nline):
                out[k * rows : (k + 1) * rows, : 2 * ffq + dm] = parts[k][...]
            out[:, 2 * ffq + dm :] = wd[...].astype(BF)

        (got,) = call(
            stack_ff,
            [((ffb, 2 * ffq + 2 * dm), BF)],
            (ranks, *ff_got, w_down),
            after=(got, mine),
        )
        ff_full = lax.all_gather(got, dpc, axis=0, tiled=True)

        place = jnp.arange(nt, dtype=F32)[:, None]
        freq = 10000.0 ** (-jnp.arange(HEAD_DIM // 2, dtype=F32) / (HEAD_DIM // 2))
        angles = place * freq
        cosines, sines = jnp.cos(angles), jnp.sin(angles)
        reps = 128 // HEAD_DIM
        table = jnp.concatenate(
            [cosines] * (2 * reps) + [-sines, sines] * reps, axis=1
        )
        table_hi = table.astype(BF)
        table_lo = (table - table_hi.astype(F32)).astype(BF)

        def natural(rk, src, cols, dst, sems):
            copies = []
            for b in range(ndpc):
                for k in range(nline):
                    row = ((b // nc) * nline + (rk[6] ^ k)) * nc + b % nc
                    row = pl.ds(pl.multiple_of(row * rows, 32), rows)
                    block = src.at[pl.ds((b * nline + k) * rows, rows), cols]
                    copies.append(pltpu.make_async_copy(block, dst.at[row], sems.at[len(copies)]))
            return copies

        def heads_swap(v, low):
            width = v.shape[1]
            half = HEAD_DIM // 2
            return jnp.where(low, pltpu.roll(v, width - half, 1), pltpu.roll(v, half, 1))

        def low_half():
            lane = lax.broadcasted_iota(jnp.int32, (nt, hc), 1)
            return lane % HEAD_DIM < HEAD_DIM // 2

        def token_index(rk, axis, shape):
            t = lax.broadcasted_iota(jnp.int32, shape, axis)
            peer = (t // tk) ^ rk[6]
            core = ((t // seg) % 2) ^ rk[4]
            return (peer * 2 + core) * seg + t % seg

        def allowed_keys(rk, start):
            key = token_index(rk, 1, (1, nt))
            query = token_index(rk, 0, (nt, 1))
            return (key <= query) & (key.astype(F32) >= start)

        def attn_forward(rk, *refs):
            ext_refs, refs = refs[:nline], refs[nline:]
            stack, gain, t_hi, t_lo = refs[:4]
            att_ref, refs = refs[4], refs[5:]
            x_ref, w_ref, rq_ref, rk_ref, q_ref, k_ref, v_ref, bias_ref, cs_ref = refs[:9]
            full_ref, inv_ref, sems = refs[9:]
            copies = natural(rk, stack, pl.ds(0, 3 * hc), w_ref, sems)
            for copy in copies:
                copy.start()
            ids = []
            for k in range(nline):
                x_ref[k * tk : (k + 1) * tk, :] = ext_refs[k][:tk, :]
                tail = ext_refs[k][tk:, :128].astype(F32)
                ids += [tail[:1, :seg], tail[1:2, :seg]]
            ids = jnp.concatenate(ids, axis=1)
            same = lax.broadcasted_iota(jnp.int32, (nt, nt), 0) == lax.broadcasted_iota(
                jnp.int32, (nt, nt), 1
            )
            ids_col = jnp.sum(jnp.where(same, ids, 0.0), axis=1, keepdims=True)
            start = jnp.sum(jnp.where(ids < ids_col, 1.0, 0.0), axis=1, keepdims=True)
            pos = token_index(rk, 0, (nt, 1)) - start.astype(jnp.int32)
            hot = (lax.broadcasted_iota(jnp.int32, (nt, nt), 1) == pos).astype(F32).astype(BF)
            cs = dot(hot, t_hi[...]) + dot(hot, t_lo[...])
            cs_ref[...] = cs
            cos = jnp.concatenate([cs[:, :128]] * (hc // 128), axis=1)
            sin = jnp.concatenate([cs[:, 128:]] * (hc // 128), axis=1)
            bias_ref[...] = jnp.where(allowed_keys(rk, start), 0.0, NEG).astype(BF)
            for copy in copies:
                copy.wait()
            low = low_half()
            for i, (raw_ref, unit_ref) in enumerate(((rq_ref, q_ref), (rk_ref, k_ref))):
                pre = dot(x_ref[...], w_ref[:, i * hc : (i + 1) * hc])
                turned = pre * cos + heads_swap(pre, low) * sin
                raw_ref[...] = turned
                for h in range(nheads):
                    at_h = slice(h * HEAD_DIM, (h + 1) * HEAD_DIM)
                    part = turned[:, at_h]
                    norm = lax.rsqrt(jnp.sum(part * part, axis=1, keepdims=True) + EPS)
                    unit = (gain[:, at_h] * part * norm).astype(BF)
                    unit_ref[:, at_h] = unit * (scale if i == 0 else 1)
            v_ref[...] = dot(x_ref[...], w_ref[:, 2 * hc :]).astype(BF)
            for h in range(nheads):
                at_h = slice(h * HEAD_DIM, (h + 1) * HEAD_DIM)
                raw = jnp.exp(dot_t(q_ref[:, at_h], k_ref[:, at_h]) + bias_ref[...].astype(F32))
                inv = 1.0 / jnp.sum(raw, axis=1, keepdims=True)
                att_h = dot(raw.astype(BF), v_ref[:, at_h]) * inv
                full_ref[:, at_h] = att_h
                att_ref[:, at_h] = att_h.astype(BF)
                inv_ref[:, h : h + 1] = inv

        unit = ((nt, hc), BF)
        outs = call(
            attn_forward,
            [unit, ((nt, dm), BF), ((dm, 3 * hc), BF), ((nt, hc), F32), ((nt, hc), F32)]
            + [unit, unit, unit, ((nt, nt), BF), ((nt, 256), F32), ((nt, hc), F32), ((nt, 128), F32)],
            (ranks, *pieces, qkv_full, my_gain, table_hi, table_lo),
            hbm=(1 + nline,),
            scratch=[pltpu.SemaphoreType.DMA((ndev,))],
            flops=2 * nt * dm * 3 * hc + 4 * nt * nt * hc,
        )
        att, outs = outs[0], outs[1:]
        x_all, w_qkv, r_q, r_k, q_low, k_low, v_low, bias, cs, att_full, inv = outs
        att_got = gather(att, line, nline)

        def own_x(ext_ref):
            return ext_ref[:tk].astype(F32)

        alpha_a, alpha_m = alpha_attn.reshape(1, dm), alpha_mlp.reshape(1, dm)
        full = ((tk, dm), F32)

        def load_out(rk, stack, wo, sems):
            return natural(rk, stack, pl.ds(2 * ffq, dm), wo, sems)

        def load_ff(rk, stack, scratch):
            wug, wd, sems, sem_d = scratch
            down = stack.at[:, pl.ds(2 * ffq + dm, dm)]
            return (
                natural(rk, stack, pl.ds(0, 2 * ffq), wug, sems),
                [pltpu.make_async_copy(down, wd, sem_d.at[0])],
            )

        w_scratch = [pltpu.VMEM((dm, 2 * ffq), BF), pltpu.VMEM((ffq, dm), BF)]
        w_scratch += [pltpu.SemaphoreType.DMA((ndev,)), pltpu.SemaphoreType.DMA((1,))]
        out_scratch = [pltpu.VMEM((dm, dm), BF), pltpu.SemaphoreType.DMA((ndev,))]

        def gate_terms(gate, sg):
            v = sg * gate
            s = 1.0 / (1.0 + jnp.exp(-v))
            return v, s

        def forward(rk, *refs):
            att_refs, refs = refs[:nline], refs[nline:]
            x_ref, alpha, stack, su, sg = refs[:5]
            parts, refs = refs[5 : 5 + nline], refs[5 + nline :]
            h_all, up_ref, gate_ref, mixed_ref, one_ref, raw_ref = refs[:6]
            scratch = refs[6:]
            wug, wd = scratch[:2]
            w, a_ref = scratch[4], scratch[6]
            first, third = load_ff(rk, stack, scratch[:4])
            out_copies = load_out(rk, stack, w, scratch[5])
            for copy in out_copies + first + third:
                copy.start()
            for k in range(nline):
                spot = pl.ds(pl.multiple_of((rk[6] ^ k) * hc, hc), hc)
                for m in range(nline):
                    block = att_refs[k][(m ^ k) * tk : ((m ^ k) + 1) * tk, :]
                    a_ref[m * tk : (m + 1) * tk, spot] = block
            for copy in out_copies:
                copy.wait()
            for m in range(nline):
                total = dot(a_ref[m * tk : (m + 1) * tk, :], w[...])
                x = x_ref[m * tk : (m + 1) * tk, :].astype(F32)
                z = x + alpha[...] * (total * row_norm(total) - x)
                one = z * row_norm(z)
                h_all[m * tk : (m + 1) * tk, :] = one.astype(BF)
                if m == 0:
                    one_ref[...] = one
                    raw_ref[...] = total
            for copy in first:
                copy.wait()

            @pl.loop(0, ffq // tile, unroll=True)
            def _(j):
                cols = pl.ds(pl.multiple_of(j * tile, tile), tile)
                up = dot(h_all[...], wug[:, cols])
                gate = dot(h_all[...], wug[:, pl.ds(pl.multiple_of(ffq + j * tile, tile), tile)])
                up_ref[:, cols] = up.astype(BF)
                gate_ref[:, cols] = gate.astype(BF)
                v, s = gate_terms(gate, sg[:, cols])
                mixed_ref[:, cols] = (su[:, cols] * up * (v * s)).astype(BF)

            for copy in third:
                copy.wait()

            @pl.loop(0, dm // tile, unroll=True)
            def _(j):
                cols = pl.ds(pl.multiple_of(j * tile, tile), tile)
                part = dot(mixed_ref[...], wd[:, cols])
                for k in range(nline):
                    parts[k][:, cols] = part[k * tk : (k + 1) * tk].astype(parts[k].dtype)

        part_shapes = [((tk, dm), F32)] + [((tk, dm), BF)] * (nline - 1)
        outs = call(
            forward,
            part_shapes
            + [((nt, dm), BF), ((nt, ffq), BF), ((nt, ffq), BF), ((nt, ffq), BF), full, full],
            (ranks, *att_got, x_all, alpha_a, ff_full, my_su, my_sg),
            hbm=(3 + nline,),
            scratch=w_scratch + out_scratch + [pltpu.VMEM((nt, dm), BF)],
            flops=6 * nt * dm * ffq + 2 * nt * dm * dm,
        )
        mlp_parts, (h_all, up, gate, mixed, h_one, h_attn) = outs[:nline], outs[nline:]
        mlp_got = exchange(mlp_parts, line, nline)

        def split_rows(rk, cot, keep, send):
            keep[...] = cot[rk[4]]
            send[...] = cot[1 - rk[4]]

        half_low = ((seg, dm), BF)
        cot_keep, cot_send = call(split_rows, [half_low] * 2, (ranks, cotangent))
        cot_recv = swap(cot_send, "c", nc, 1)

        def mlp_update(rk, *refs):
            parts, refs = refs[:nline], refs[nline:]
            one_ref, alpha_ref, ck, cr, hid_keep, hid_send, dm_ref, direct, g_alpha = refs
            h = parts[0][...]
            for k in range(1, nline):
                h = h + parts[k][...].astype(F32)
            one, alpha = one_ref[...], alpha_ref[...]
            norm_h = row_norm(h)
            b = h * norm_h
            gap = b - one
            z = one + alpha * gap
            norm_z = row_norm(z)
            y = z * norm_z
            low = y.astype(BF)
            hid_keep[...] = low[:seg]
            hid_send[...] = low[seg:]
            dy = jnp.concatenate([ck[...], cr[...]], axis=0).astype(F32)
            dz = sphere_back(dy, y, norm_z)
            g_alpha[...] = jnp.sum(dz * gap, axis=0, keepdims=True)
            direct[...] = dz * (1.0 - alpha)
            dm_ref[...] = sphere_back(dz * alpha, b, norm_h).astype(BF)

        outs = call(
            mlp_update,
            [half_low, half_low, ((tk, dm), BF), full, ((1, dm), F32)],
            (ranks, *mlp_got, h_one, alpha_m, cot_keep, cot_recv),
        )
        hid_keep, hid_send, dm_low, d_one_direct, g_alpha_mlp = outs
        hid_recv = swap(hid_send, "c", nc, 1)
        dm_got = gather(dm_low, line, nline)

        def ff_back(rk, late, *refs):
            d_refs, stack = refs[:nline], refs[nline]
            su_ref, sg_ref, up_ref, gate_ref = refs[nline + 1 : nline + 5]
            refs = refs[nline + 5 :]
            parts, (d_all, dug, g_su, g_sg) = refs[:nline], refs[nline : nline + 4]
            scratch = refs[nline + 4 :]
            wug, wd = scratch[:2]
            first, third = load_ff(rk, stack, scratch)
            for copy in third + late[:2] + first + late[2:]:
                copy.start()
            for k in range(nline):
                d_all[k * tk : (k + 1) * tk, :] = d_refs[k][...]
            for copy in third + late[:2]:
                copy.wait()

            @pl.loop(0, ffq // tile)
            def _(j):
                cols = pl.ds(pl.multiple_of(j * tile, tile), tile)
                d_mixed = dot_t(d_all[...], wd[cols, :])
                up, gate = up_ref[:, cols].astype(F32), gate_ref[:, cols].astype(F32)
                su, sg = su_ref[:, cols], sg_ref[:, cols]
                v, s = gate_terms(gate, sg)
                silu = v * s
                dug[:, cols] = (d_mixed * su * silu).astype(BF)
                slope = d_mixed * su * up * (s * (1.0 + v * (1.0 - s)))
                other = pl.ds(pl.multiple_of(ffq + j * tile, tile), tile)
                dug[:, other] = (slope * sg).astype(BF)
                g_su[:, cols] = jnp.sum(d_mixed * up * silu, axis=0, keepdims=True)
                g_sg[:, cols] = jnp.sum(slope * gate, axis=0, keepdims=True)

            for copy in first:
                copy.wait()

            @pl.loop(0, dm // tile)
            def _(j):
                cols = pl.ds(pl.multiple_of(j * tile, tile), tile)
                part = dot_t(dug[...], wug[cols, :])
                for k in range(nline):
                    parts[k][:, cols] = part[k * tk : (k + 1) * tk].astype(parts[k].dtype)


        def stored(rk, g_ref, out, width, block, sems):
            d, peer, c = block // (nline * nc), (block // nc) % nline, block % nc
            spot = ((d * nc + c) * nline + (peer ^ rk[6])) * rows
            src = g_ref.at[pl.ds(pl.multiple_of(block * rows, 32), rows)]
            dst = out.at[pl.ds(pl.multiple_of(spot, 32), rows), pl.ds(0, width)]
            return pltpu.make_async_copy(src, dst, sems.at[block])

        def outer_ff(rk, h, dug, mixed_ref, d_all, out, g_ref, g_down_ref, sems, sem_d):
            def store(block):
                return stored(rk, g_ref, out, 2 * ffq, block, sems)

            @pl.loop(0, dm // tile, unroll=True)
            def _(j):
                cols = pl.ds(pl.multiple_of(j * tile, tile), tile)
                g_ref[cols, :] = tdot(h[:, cols], dug[...]).astype(BF)
                for i in range(tile // rows):
                    store(j * (tile // rows) + i).start()

            @pl.loop(0, ffq // tile, unroll=True)
            def _(j):
                cols = pl.ds(pl.multiple_of(j * tile, tile), tile)
                g_down_ref[cols, :] = tdot(mixed_ref[:, cols], d_all[...]).astype(BF)

            down = pltpu.make_async_copy(g_down_ref, out.at[:, pl.ds(2 * ffq, dm)], sem_d.at[0])
            down.start()
            down.wait()

            @pl.loop(0, ndev)
            def _(block):
                store(block).wait()

        def ff_back_all(rk, *refs):
            ins, refs = list(refs[: nline + 7]), refs[nline + 7 :]
            parts, (g_su, g_sg, out) = refs[:nline], refs[nline : nline + 3]
            d_all, dug, wug, wd, s_u, s_d, g_ref, g_down_ref, sems, sem_d = refs[nline + 3 : nline + 13]
            *held, late_sems = refs[nline + 13 :]
            late = []
            for i, dst in enumerate(held):
                late.append(pltpu.make_async_copy(ins[nline + 3 + i], dst, late_sems.at[i]))
            ins[nline + 3 :] = held
            scratch = (d_all, dug, g_su, g_sg, wug, wd, s_u, s_d)
            ff_back(rk, late, *ins[: nline + 5], *parts, *scratch)
            h, mixed_ref = ins[nline + 5 :]
            for copy in late[2:]:
                copy.wait()
            outer_ff(rk, h, dug, mixed_ref, d_all, out, g_ref, g_down_ref, sems, sem_d)

        *one_parts, g_su, g_sg, g_ff = call(
            ff_back_all,
            part_shapes + [((1, ffq), F32)] * 2 + [((dm, 2 * ffq + dm), BF)],
            (ranks, *dm_got, ff_full, my_su, my_sg, up, gate, h_all, mixed),
            hbm=(1 + nline, 4 + nline, 5 + nline, 6 + nline, 7 + nline),
            hbm_out=(nline + 2,),
            scratch=[pltpu.VMEM((nt, dm), BF), pltpu.VMEM((nt, 2 * ffq), BF)]
            + w_scratch
            + [pltpu.VMEM((dm, 2 * ffq), BF), pltpu.VMEM((ffq, dm), BF)]
            + [pltpu.SemaphoreType.DMA((ndev,)), pltpu.SemaphoreType.DMA((1,))]
            + [pltpu.VMEM((nt, ffq), BF)] * 2
            + [pltpu.VMEM((nt, dm), BF), pltpu.VMEM((nt, ffq), BF)]
            + [pltpu.SemaphoreType.DMA((4,))],
            flops=12 * nt * dm * ffq,
        )
        one_got = exchange(one_parts, line, nline)
        g_ff = lax.psum_scatter(g_ff, dpc, scatter_dimension=0, tiled=True)
        def attn_update_back(rk, *refs):
            parts, refs = refs[:nline], refs[nline:]
            direct_in, one_ref, raw_ref, ext_ref, alpha_ref, stack = refs[:6]
            d_outs, (dh_ref, direct, g_alpha, w, sems) = refs[6 : 6 + nline], refs[6 + nline :]
            copies = load_out(rk, stack, w, sems)
            for copy in copies:
                copy.start()
            d = direct_in[...] + parts[0][...]
            for k in range(1, nline):
                d = d + parts[k][...].astype(F32)
            one, raw, alpha = one_ref[...], raw_ref[...], alpha_ref[...]
            x = own_x(ext_ref)
            norm_raw = row_norm(raw)
            b = raw * norm_raw
            gap = b - x
            norm_z = row_norm(x + alpha * gap)
            dz = sphere_back(d, one, norm_z)
            g_alpha[...] = jnp.sum(dz * gap, axis=0, keepdims=True)
            direct[...] = dz * (1.0 - alpha)
            dh_ref[...] = sphere_back(dz * alpha, b, norm_raw).astype(BF)
            for copy in copies:
                copy.wait()
            for k in range(nline):
                w_k = w[pl.ds(pl.multiple_of((rk[6] ^ k) * hc, hc), hc), :]
                d_outs[k][...] = dot_t(dh_ref[...], w_k).astype(BF)

        outs = call(
            attn_update_back,
            [((tk, hc), BF)] * nline + [((tk, dm), BF), full, ((1, dm), F32)],
            (ranks, *one_got, d_one_direct, h_one, h_attn, mine, alpha_a, ff_full),
            hbm=(6 + nline,),
            scratch=out_scratch,
            flops=2 * tk * dm * dm,
        )
        d_att_parts, (dh_low, d_x_direct, g_alpha_attn) = outs[:nline], outs[nline:]
        d_att = exchange(d_att_parts, line, nline)

        def outer_out(rk, dh, *refs):
            parts, outs, (g_ref, sems) = refs[:nline], refs[nline : nline + 2], refs[nline + 2 :]
            for k in range(nline):
                spot = pl.ds(pl.multiple_of((rk[6] ^ k) * hc, hc), hc)
                own = parts[k][k * tk : (k + 1) * tk, :]
                g_ref[spot, :] = tdot(own, dh[...]).astype(BF)
            copies = []
            for cr in range(nc):
                for a in range(nyx):
                    for b in range(nline):
                        row = ((rk[5] ^ a) * nline + (rk[6] ^ b)) * nc + (rk[4] ^ cr)
                        src = g_ref.at[pl.ds(pl.multiple_of(row * rows, 32), rows)]
                        dst = outs[cr].at[pl.ds((a * nline + b) * rows, rows)]
                        copies.append(pltpu.make_async_copy(src, dst, sems.at[len(copies)]))
            for copy in copies:
                copy.start()
            for copy in copies:
                copy.wait()

        keep, send = call(
            outer_out,
            [((dm // nc, dm), BF)] * nc,
            (ranks, dh_low, *att_got),
            hbm_out=(0, 1),
            scratch=[pltpu.VMEM((dm, dm), BF), pltpu.SemaphoreType.DMA((ndev,))],
            flops=2 * tk * dm * dm,
        )

        def attn_back(rk, late, *refs):
            d_refs, refs = refs[:nline], refs[nline:]
            w_ref, rq_ref, rk_ref, q_ref, k_ref, v_ref, bias_ref, cs_ref, gain = refs[:9]
            full_ref, inv_ref, refs = refs[9], refs[10], refs[11:]
            parts, (d_ref, g_gain, do_ref, dq_ref, dk_ref) = refs[:nline], refs[nline:]
            for k in range(nline):
                do_ref[k * tk : (k + 1) * tk, :] = d_refs[k][...]
            for h in range(nheads):
                at_h = slice(h * HEAD_DIM, (h + 1) * HEAD_DIM)
                q, key, do = q_ref[:, at_h], k_ref[:, at_h], do_ref[:, at_h]
                raw = jnp.exp(dot_t(q, key) + bias_ref[...].astype(F32))
                p = raw * inv_ref[:, h : h + 1]
                delta = jnp.sum(do.astype(F32) * full_ref[:, at_h], axis=1, keepdims=True)
                ds = (p * (dot_t(do, v_ref[:, at_h]) - delta)).astype(BF)
                p = p.astype(BF)
                at_v = slice(2 * hc + h * HEAD_DIM, 2 * hc + (h + 1) * HEAD_DIM)
                d_ref[:, at_v] = tdot(p, do).astype(BF)
                dq_ref[:, at_h] = scale * dot(ds, key)
                dk_ref[:, at_h] = tdot(ds, q)
            for copy in late:
                copy.wait()
            cs = cs_ref[...]
            cos = jnp.concatenate([cs[:, :128]] * (hc // 128), axis=1)
            sin = jnp.concatenate([cs[:, 128:]] * (hc // 128), axis=1)
            low = low_half()
            for i, (raw_ref, g_ref) in enumerate(((rq_ref, dq_ref), (rk_ref, dk_ref))):
                for h in range(nheads):
                    at_h = slice(h * HEAD_DIM, (h + 1) * HEAD_DIM)
                    turned, g = raw_ref[:, at_h], g_ref[:, at_h]
                    norm = lax.rsqrt(jnp.sum(turned * turned, axis=1, keepdims=True) + EPS)
                    unit = turned * norm
                    term = jnp.sum(g * unit, axis=0, keepdims=True)
                    g_gain[:, at_h] = term if i == 0 else g_gain[:, at_h] + term
                    g = g * gain[:, at_h]
                    g_ref[:, at_h] = norm * (g - unit * jnp.sum(unit * g, axis=1, keepdims=True))
                g = g_ref[...]
                d_ref[:, i * hc : (i + 1) * hc] = (g * cos - heads_swap(g, low) * sin).astype(BF)

            @pl.loop(0, dm // tile)
            def _(j):
                cols = pl.ds(pl.multiple_of(j * tile, tile), tile)
                part = dot_t(d_ref[...], w_ref[cols, :])
                for k in range(nline):
                    parts[k][:, cols] = part[k * tk : (k + 1) * tk].astype(parts[k].dtype)


        at_line = ranks[6]
        mine_ff = (jnp.arange(nline) == at_line)[None, :, None, None]

        def ff_owner(vec):
            return jnp.where(mine_ff, vec.reshape(nyx, 1, nc, ffb), 0.0).reshape(ndev, ffb)

        misc = [v.reshape(ndev, rows) for v in (g_alpha_attn, g_alpha_mlp)]
        misc = jnp.pad(jnp.concatenate(misc, axis=1), ((0, 0), (0, ffb - 2 * rows)))
        vecs = jnp.stack([ff_owner(g_su), ff_owner(g_sg), misc], axis=1).astype(BF)
        vecs = jnp.pad(vecs, ((0, 0), (0, rows - 3), (0, 0))).reshape(dm, ffb)

        wide = 3 * hc + ffb

        def core_add(rk, a, b, *outs):
            for i in range(nyx):
                here = slice(i * ffb, (i + 1) * ffb)
                outs[i][...] = (a[here, :].astype(F32) + b[here, :].astype(F32)).astype(BF)

        out_sum = call(
            core_add, [((ffb, dm), BF)] * nyx, (ranks, keep, swap(send, "c", nc, 1))
        )
        out_got = exchange(out_sum, yx, nyx)

        def outer_last(rk, x_ref, d_ref, vec_ref, g_gain, out, g_ref, sems):

            def store(block):
                return stored(rk, g_ref, out, wide, block, sems)

            g_ref[:, 3 * hc : wide] = vec_ref[...]
            third = lax.broadcasted_iota(jnp.int32, (16, ffb), 0) == 2
            for i in range(hc // rows):
                spot = pl.ds(pl.multiple_of((rk[6] * (hc // rows) + i) * rows, 32), 16)
                run = [jnp.zeros((1, 2 * rows), F32), g_gain[:, i * rows : (i + 1) * rows]]
                run = jnp.concatenate(run + [jnp.zeros((1, ffb - 3 * rows), F32)], axis=1)
                held = g_ref[spot, 3 * hc : wide].astype(F32)
                g_ref[spot, 3 * hc : wide] = (held + jnp.where(third, run, 0.0)).astype(BF)

            @pl.loop(0, dm // tile)
            def _(j):
                cols = pl.ds(pl.multiple_of(j * tile, tile), tile)
                g_ref[cols, : 3 * hc] = tdot(x_ref[:, cols], d_ref[...]).astype(BF)
                for i in range(tile // rows):
                    store(j * (tile // rows) + i).start()

            @pl.loop(0, ndev)
            def _(block):
                store(block).wait()

        def attn_back_all(rk, *refs):
            ins, refs = list(refs[: nline + 13]), refs[nline + 13 :]
            parts, out = refs[:nline], refs[nline]
            d_ref, g_gain, do_ref, dq_ref, dk_ref, g_ref, sems = refs[nline + 1 : nline + 8]
            *held, late_sems = refs[nline + 8 :]
            late = []
            for i, (at_in, dst) in enumerate(zip(late_back, held)):
                late.append(pltpu.make_async_copy(ins[at_in - 1], dst, late_sems.at[i]))
                ins[at_in - 1] = dst
            for copy in late:
                copy.start()
            x_ref, vec_ref = ins[nline + 11 :]
            scratch = (d_ref, g_gain, do_ref, dq_ref, dk_ref)
            attn_back(rk, late, *ins[: nline + 11], *parts, *scratch)
            outer_last(rk, x_ref, d_ref, vec_ref, g_gain, out, g_ref, sems)

        late_back = [1 + nline, 2 + nline, 3 + nline, 8 + nline, 12 + nline]
        late_shapes = [((dm, 3 * hc), BF), ((nt, hc), F32), ((nt, hc), F32), ((nt, 256), F32)]
        late_shapes.append(((nt, dm), BF))

        *x_parts, g_last = call(
            attn_back_all,
            part_shapes + [((dm, wide), BF)],
            (ranks, *d_att, w_qkv, r_q, r_k, q_low, k_low, v_low, bias, cs, my_gain, att_full, inv)
            + (x_all, vecs),
            hbm=late_back,
            hbm_out=(nline,),
            after=(keep,),
            scratch=[
                pltpu.VMEM((nt, 3 * hc), BF), pltpu.VMEM((1, hc), F32),
                pltpu.VMEM((nt, hc), BF), pltpu.VMEM((nt, hc), F32), pltpu.VMEM((nt, hc), F32),
                pltpu.VMEM((dm, wide), BF), pltpu.SemaphoreType.DMA((ndev,)),
                *[pltpu.VMEM(*shape) for shape in late_shapes], pltpu.SemaphoreType.DMA((5,)),
            ],
            flops=4 * nt * dm * 3 * hc + 10 * nt * nt * hc,
        )
        x_got = exchange(x_parts, line, nline)


        g_last = lax.psum_scatter(g_last, dpc, scatter_dimension=0, tiled=True)

        def split_ff(rk, *refs):
            parts, (g_ref, down), outs = refs[:nyx], refs[nyx : nyx + 2], refs[nyx + 2 :]
            down[...] = g_ref[:, 2 * ffq :].astype(F32)
            for k in range(nline):
                here = slice(k * rows, (k + 1) * rows)
                outs[k][:, : 2 * ffq] = g_ref[here, : 2 * ffq]
                total = parts[0][here, :].astype(F32)
                for j in range(1, nyx):
                    total = total + parts[j][here, :].astype(F32)
                outs[k][:, 2 * ffq :] = total.astype(BF)

        g_down, *g_parts = call(
            split_ff,
            [((ffb, dm), F32)] + [((rows, 2 * ffq + dm), BF)] * nline,
            (ranks, *out_got, g_ff),
            after=tuple(x_got[1:]),
        )
        g_parts = exchange(g_parts, line, nline)

        def place_ff(rk, *refs):
            parts, outs, g_o = refs[:nline], refs[nline : nline + 2], refs[nline + 2]
            total = parts[0][:, 2 * ffq :].astype(F32)
            for k in range(nline):
                for d, cols in enumerate(ff_cols(rk, k)):
                    for i in range(2):
                        here = i * ffq + d * sub
                        outs[i][:, cols] = parts[k][:, here : here + sub].astype(F32)
                if k:
                    total = total + parts[k][:, 2 * ffq :].astype(F32)
            g_o[...] = total

        g_up, g_gate, g_out = call(
            place_ff, [((rows, ff), F32)] * 2 + [((rows, dm), F32)], (ranks, *g_parts)
        )

        def finish_tokens(rk, *refs):
            parts, (direct, keep, send) = refs[:nline], refs[nline:]
            d = direct[...] + parts[0][...]
            for k in range(1, nline):
                d = d + parts[k][...].astype(F32)
            keep[...] = d[:seg]
            send[...] = d[seg:].astype(BF)

        x_keep, x_send = call(
            finish_tokens, [((seg, dm), F32), half_low], (ranks, *x_got, d_x_direct)
        )
        x_recv = swap(x_send, "c", nc, 1)

        def join_rows(rk, keep, recv, out):
            out[rk[4]] = keep[...].astype(out.dtype)
            out[1 - rk[4]] = recv[...].astype(out.dtype)

        (tokens_grad,) = call(join_rows, [((nseq, seg, dm), F32)], (ranks, x_keep, x_recv))
        (hidden_out,) = call(join_rows, [((nseq, seg, dm), BF)], (ranks, hid_keep, hid_recv))

        def split_last(rk, g_ref, *outs):
            for k in range(nline):
                outs[k][...] = g_ref[k * rows : (k + 1) * rows, :]

        last = call(
            split_last,
            [((rows, wide), BF)] * nline,
            (ranks, g_last),
            after=(tokens_grad, hidden_out, g_parts[1]),
        )
        last = exchange(last, line, nline)

        def place_last(rk, *refs):
            parts, outs, vec_outs = refs[:nline], refs[nline : nline + 3], refs[nline + 3 :]
            v_sum = None
            for k in range(nline):
                cols = pl.ds(pl.multiple_of((rk[6] ^ k) * hc, 128), hc)
                for i in range(3):
                    outs[i][:, cols] = parts[k][:, i * hc : (i + 1) * hc].astype(F32)
                vec = parts[k][:16, 3 * hc : wide].astype(F32)
                v_sum = vec if v_sum is None else v_sum + vec
            vec_outs[0][...] = v_sum[:1]
            vec_outs[1][...] = v_sum[1:2]
            for i in range(3):
                vec_outs[2 + i][...] = v_sum[2:3, i * rows : (i + 1) * rows]

        g_query, g_key, g_value, *vecs = call(
            place_last,
            [((rows, dm), F32)] * 3
            + [((1, ffb), F32)] * 2
            + [((1, rows), F32)] * 3,
            (ranks, *last),
        )
        g_s_up, g_s_gate, g_aa, g_am, g_sqk = [v.reshape(-1) for v in vecs]
        return (
            hidden_out, tokens_grad, g_query, g_key, g_value, g_out, g_up, g_gate, g_down,
            g_sqk, g_aa, g_s_up, g_s_gate, g_am,
        )

    return body


def make_body(sizes):
    plain, kernels = make_plain(sizes), make_kernels(sizes)
    ndev = math.prod(sizes)
    nline = sizes[2] * sizes[3]

    def body(*args):
        tokens, w_query, w_up = args[0], args[2], args[6]
        fits = w_query.shape[0] % 32 == 0 and (w_up.shape[1] // ndev) % 128 == 0
        fits = fits and (tokens.shape[2] // nline) % 256 == 0 and tokens.shape[1] == 64
        return (kernels if fits else plain)(*args)

    return body


def solution(mesh):
    ndp, nblk = mesh.shape["dp"], mesh.shape["blk"]
    sizes = (ndp // 2, 2, nblk // 4, 2, 2)
    fine = Mesh(mesh.devices.reshape(sizes), ("y", "x", "w", "z", "c"))
    rows, cols = ("y", "x"), ("w", "z", "c")
    flat = rows + cols
    seq = P(rows, cols, None)
    weight = P(flat, None)
    return jax.shard_map(
        make_body(sizes),
        mesh=fine,
        in_specs=(seq, P(rows, cols)) + (weight,) * 7 + (P(),) * 5 + (seq,),
        out_specs=(seq, seq) + (weight,) * 7 + (P(flat),) * 5,
        check_vma=False,
    )
```

```python
import math

import jax
import jax.numpy as jnp
from jax import lax
from jax.experimental import pallas as pl
from jax.experimental.pallas import tpu as pltpu
from jax.sharding import Mesh
from jax.sharding import PartitionSpec as P

HEADS = 16
HEAD_DIM = 64
EPS = 1e-06
NEG = -1e30
BF = jnp.bfloat16
F32 = jnp.float32


def dot(a, b):
    return jnp.dot(a, b, preferred_element_type=F32)


def dot_t(a, b):
    return lax.dot_general(a, b, (((1,), (1,)), ((), ())), preferred_element_type=F32)


def tdot(a, b):
    return lax.dot_general(a, b, (((0,), (0,)), ((), ())), preferred_element_type=F32)


def rotate(tensor, cosines, sines):
    half_dim = tensor.shape[-1] // 2
    front = tensor[..., :half_dim]
    behind = tensor[..., half_dim:]
    return jnp.concatenate(
        [front * cosines - behind * sines, behind * cosines + front * sines], axis=-1
    )


def sphere(tensor):
    return tensor * lax.rsqrt(jnp.mean(tensor * tensor, axis=-1, keepdims=True) + EPS)


def head_unit(tensor, gains):
    return gains * tensor * lax.rsqrt(jnp.sum(tensor * tensor, axis=-1, keepdims=True) + EPS)


def residual_step(branch, residual_in, alpha):
    return sphere(residual_in + alpha * (sphere(branch) - residual_in))


def gating(up_proj, gate_proj, scale_up, scale_gate):
    return scale_up * up_proj * jax.nn.silu(scale_gate * gate_proj)


def make_plain(sizes):
    ny, nx, nw, nz, nc = sizes
    ndev = ny * nx * nw * nz * nc
    line = ("w", "z")
    nline = nw * nz
    quad = ("x", "z")
    nquad = nx * nz

    def swap(value, axes, count, k):
        return lax.ppermute(value, axes, [(i, i ^ k) for i in range(count)])

    def gather_rel(value, axes, count):
        return [value] + [swap(value, axes, count, k) for k in range(1, count)]

    def exchange_rel(chunks, axes, count):
        return [chunks[0]] + [swap(chunks[k], axes, count, k) for k in range(1, count)]

    def sum_rel(chunks, axes, count, kind=BF):
        got = exchange_rel([c.astype(kind) for c in chunks], axes, count)
        total = chunks[0].astype(F32)
        for piece in got[1:]:
            total = total + piece.astype(F32)
        return total

    def double(value, stages):
        for axis, count, k in stages:
            value = jnp.concatenate([value, swap(value, axis, count, k)], axis=0)
        return value

    def halve(value, stages, kind=BF):
        for axis, count, k in stages[::-1]:
            half = value.shape[0] // 2
            other = swap(value[half:].astype(kind), axis, count, k)
            value = value[:half].astype(F32) + other.astype(F32)
        return value

    def bits(axis, count):
        return [(axis, count, 1 << b) for b in range(count.bit_length() - 1)]

    def ranks(order):
        count = dict(y=ny, x=nx, w=nw, z=nz, c=nc)
        shape = [count[axis] for axis in order]
        found = {}
        for i, axis in enumerate(order):
            shifted = jnp.arange(count[axis]) ^ lax.axis_index(axis)
            found[axis] = shifted.reshape((-1,) + (1,) * (len(order) - 1 - i))
        flat = jnp.zeros(shape, jnp.int32)
        return found, flat

    def reorder(order, target):
        found, flat = ranks(order)
        count = dict(y=ny, x=nx, w=nw, z=nz, c=nc)
        index = flat
        for axis in target:
            index = index * count[axis] + found[axis]
        return index.reshape(-1)

    def place(pieces, rank):
        stack = jnp.stack(pieces)
        order = rank ^ jnp.arange(len(pieces))
        return jnp.take(stack, order, axis=0)

    def pick(array, rank, count):
        return [lax.dynamic_index_in_dim(array, rank ^ k, 0, False) for k in range(count)]

    def body(
        tokens, doc_ids, w_query, w_key, w_value, w_out, w_up, w_gate, w_down,
        s_qk, alpha_attn, s_up, s_gate, alpha_mlp, cotangent,
    ):
        nseq, seg, dm = tokens.shape
        rows = w_query.shape[0]
        ff = w_up.shape[1]
        ffq = ff // nquad
        ffb = ff // ndev
        hcols = dm // nline
        nheads = HEADS // nline
        score_scale = math.sqrt(HEAD_DIM)
        c_at = lax.axis_index("c")
        line_at = lax.axis_index(line)
        quad_at = lax.axis_index(quad)

        def by_line(w):
            return w.astype(BF).reshape(rows, nline, hcols)

        w_qkv = jnp.stack([by_line(w_query), by_line(w_key), by_line(w_value)], axis=2)
        w_qkv = w_qkv.transpose(1, 0, 2, 3).reshape(nline, rows, 3 * hcols)
        got = jnp.stack(exchange_rel(pick(w_qkv, line_at, nline), line, nline))
        got = jnp.stack(gather_rel(got, ("y", "x"), ny * nx))
        full = double(got[None], bits("c", nc)).reshape(ndev, rows, 3 * hcols)
        full_qkv = jnp.take(full, reorder("yxwzc", "cyxwz"), axis=0).reshape(dm, 3 * hcols)
        full_out = lax.all_gather(w_out.astype(BF), ("y", "x", "w", "z", "c"), axis=0, tiled=True)

        def by_quad(w):
            w = w.astype(BF).reshape(rows, ny, nx, nw, nz, nc, ffb)
            return w.transpose(2, 4, 0, 1, 3, 5, 6).reshape(nquad, rows, ffq)

        w_ug = jnp.concatenate([by_quad(w_up), by_quad(w_gate)], axis=2)
        got = jnp.stack(exchange_rel(pick(w_ug, quad_at, nquad), quad, nquad))
        stages = bits("w", nw) + bits("y", ny) + bits("c", nc)

        def ff_full(part):
            full = double(part[None], stages).reshape(ndev, rows, ffq)
            return jnp.take(full, reorder("yxwzc", "cywxz"), axis=0).reshape(dm, ffq)

        full_up, full_gate = ff_full(got[:, :, :ffq]), ff_full(got[:, :, ffq:])
        full_down = double(w_down.astype(BF)[None], stages)
        full_down = jnp.take(full_down, reorder("ywc", "cyw"), axis=0).reshape(ffq, dm)

        def my_ff(vec):
            v = vec.reshape(ny, nx, nw, nz, nc, ffb).transpose(1, 3, 0, 2, 4, 5)
            return lax.dynamic_index_in_dim(v.reshape(nquad, ffq), quad_at, 0, False)

        my_s_up, my_s_gate = my_ff(s_up), my_ff(s_gate)
        my_gain = lax.dynamic_index_in_dim(s_qk.reshape(nline, hcols), line_at, 0, False)

        def to_row(value):
            keep = lax.dynamic_index_in_dim(value, c_at, 0, False)
            send = lax.dynamic_index_in_dim(value, 1 - c_at, 0, False)
            return jnp.concatenate([keep, lax.ppermute(send, "c", [(0, 1), (1, 0)])], axis=0)

        def from_row(value, send_type):
            keep, send = value[:seg], value[seg:]
            other = lax.ppermute(send.astype(send_type), "c", [(0, 1), (1, 0)])
            pair = jnp.stack([keep, other.astype(value.dtype)])
            return jnp.where(c_at == 0, pair, pair[::-1])

        docs = doc_ids.astype(BF)
        extra = jnp.zeros((nseq, 16, dm), BF).at[:, 0, :seg].set(docs)
        ext = jnp.concatenate([tokens, extra], axis=1)
        mine = to_row(ext).reshape(2, seg + 16, dm)
        everyone = jnp.stack(gather_rel(mine, line, nline))
        row_tokens = everyone[:, :, :seg].reshape(nline * 2 * seg, dm)
        row_docs = everyone[:, :, seg, :seg].reshape(-1).astype(F32)
        peers = line_at ^ jnp.arange(nline)
        seg_at = 2 * peers[:, None] + jnp.stack([c_at, 1 - c_at])[None, :]
        index = (seg_at[:, :, None] * seg + jnp.arange(seg)).reshape(-1)
        start = jnp.sum((row_docs[None, :] < row_docs[:, None]).astype(jnp.int32), axis=1)
        pos = index - start
        allowed = (index[None, :] <= index[:, None]) & (index[None, :] >= start[:, None])
        frequency = 10000.0 ** (-jnp.arange(HEAD_DIM // 2, dtype=F32) / (HEAD_DIM // 2))
        angles = pos.astype(F32)[:, None] * frequency
        cosines, sines = jnp.cos(angles)[:, None, :], jnp.sin(angles)[:, None, :]
        nt = row_tokens.shape[0]
        x_low = mine[:, :seg].reshape(2 * seg, dm)
        x_row = x_low.astype(F32)

        pre = dot(row_tokens, full_qkv)

        def heads(t):
            return t.reshape(nt, nheads, HEAD_DIM)

        def unit_pair(q_pre, k_pre, gains):
            gains = gains.reshape(nheads, HEAD_DIM)
            return (
                head_unit(rotate(heads(q_pre), cosines, sines), gains),
                head_unit(rotate(heads(k_pre), cosines, sines), gains),
            )

        (q_unit, k_unit), unit_pull = jax.vjp(
            unit_pair, pre[:, :hcols], pre[:, hcols : 2 * hcols], my_gain
        )
        q_low, k_low = q_unit.astype(BF), k_unit.astype(BF)
        v_low = heads(pre[:, 2 * hcols :].astype(BF))
        scores = jnp.einsum("qhd,khd->hqk", q_low, k_low, preferred_element_type=F32) * score_scale
        scores = jnp.where(allowed[None], scores, NEG)
        peak = jnp.max(scores, axis=-1, keepdims=True)
        raw = jnp.where(allowed[None], jnp.exp(scores - peak), 0.0)
        probs = raw / jnp.sum(raw, axis=-1, keepdims=True)
        p_low = probs.astype(BF)
        attended = jnp.einsum("hqk,khd->qhd", p_low, v_low, preferred_element_type=F32)
        att_low = attended.astype(BF).reshape(nline, 2 * seg, hcols)
        got = place(exchange_rel([att_low[k] for k in range(nline)], line, nline), line_at)
        att_mine = got.transpose(1, 0, 2).reshape(2 * seg, dm)

        h_attn = dot(att_mine, full_out)
        h_one, attn_pull = jax.vjp(residual_step, h_attn, x_row, alpha_attn)
        h_low = jnp.concatenate(gather_rel(h_one.astype(BF), quad, nquad), axis=0)
        up, gate = dot(h_low, full_up), dot(h_low, full_gate)
        mixed, gate_pull = jax.vjp(gating, up, gate, my_s_up, my_s_gate)
        mixed_low = mixed.astype(BF)
        part = dot(mixed_low, full_down).reshape(nquad, 2 * seg, dm)
        h_mlp = sum_rel([part[k] for k in range(nquad)], quad, nquad)
        result, out_pull = jax.vjp(residual_step, h_mlp, h_one, alpha_mlp)
        hidden_out = from_row(result.astype(BF), BF)

        d_result = to_row(cotangent).astype(F32)
        d_hmlp, d_hone, g_alpha_mlp = out_pull(d_result)
        dm_low = jnp.concatenate(gather_rel(d_hmlp.astype(BF), quad, nquad), axis=0)
        d_mixed = dot_t(dm_low, full_down)
        d_up, d_gate, g_s_up, g_s_gate = gate_pull(d_mixed)
        du_low, dg_low = d_up.astype(BF), d_gate.astype(BF)
        part = dot_t(du_low, full_up) + dot_t(dg_low, full_gate)
        part = part.reshape(nquad, 2 * seg, dm)
        d_hone = d_hone + sum_rel([part[k] for k in range(nquad)], quad, nquad)
        g_down = tdot(mixed_low, dm_low).reshape(ny * nw * nc, ffb, dm)
        g_down = halve(jnp.take(g_down, reorder("cyw", "ywc"), axis=0), stages)[0]

        def ff_scatter(left, right):
            part = tdot(left, right).reshape(ndev, rows, ffq)
            part = jnp.take(part, reorder("cywxz", "yxwzc"), axis=0)
            part = halve(part.reshape(ny * nw * nc, nquad, rows, ffq), stages)[0].astype(BF)
            got = place(exchange_rel([part[k] for k in range(nquad)], quad, nquad), quad_at)
            got = got.reshape(nx, nz, rows, ny, nw, nc, ffb).transpose(2, 3, 0, 4, 1, 5, 6)
            return got.reshape(rows, ff).astype(F32)

        g_up, g_gate = ff_scatter(h_low, du_low), ff_scatter(h_low, dg_low)

        d_hattn, d_tokens, g_alpha_attn = attn_pull(d_hone)
        dh_low = d_hattn.astype(BF)

        def to_owner(part, kind=BF):
            part = jnp.take(part, reorder("cyxwz", "yxwzc"), axis=0)
            part = halve(part.reshape((nc, ny * nx, nline) + part.shape[1:]), bits("c", nc), kind)[0]
            part = sum_rel([part[k] for k in range(ny * nx)], ("y", "x"), ny * nx, kind)
            return sum_rel([part[k] for k in range(nline)], line, nline, kind)

        g_out = to_owner(tdot(att_mine, dh_low).reshape(ndev, rows, dm))
        d_att = dot_t(dh_low, full_out).astype(BF).reshape(2 * seg, nline, hcols).transpose(1, 0, 2)
        d_att = jnp.concatenate(
            exchange_rel(pick(d_att, line_at, nline), line, nline), axis=0
        ).reshape(nt, nheads, HEAD_DIM)
        delta = jnp.sum(d_att.astype(F32) * attended, axis=-1)
        d_probs = jnp.einsum("qhd,khd->hqk", d_att, v_low, preferred_element_type=F32)
        d_scores = (probs * (d_probs - delta.T[:, :, None])).astype(BF)
        d_q = score_scale * jnp.einsum("hqk,khd->qhd", d_scores, k_low, preferred_element_type=F32)
        d_k = score_scale * jnp.einsum("hqk,qhd->khd", d_scores, q_low, preferred_element_type=F32)
        d_v = jnp.einsum("hqk,qhd->khd", p_low, d_att, preferred_element_type=F32)
        d_qpre, d_kpre, g_sqk = unit_pull((d_q, d_k))
        d_qkv = jnp.concatenate([d_qpre, d_kpre, d_v.reshape(nt, hcols)], axis=1).astype(BF)
        part = dot_t(d_qkv, full_qkv).reshape(nline, 2 * seg, dm)
        tokens_grad = d_tokens + sum_rel([part[k] for k in range(nline)], line, nline)
        tokens_grad = from_row(tokens_grad, BF)
        g_qkv = tdot(row_tokens, d_qkv).reshape(ndev, rows, 3 * hcols)
        g_qkv = jnp.take(g_qkv, reorder("cyxwz", "yxwzc"), axis=0)
        g_qkv = halve(g_qkv.reshape(nc, ny * nx, nline, rows, 3 * hcols), bits("c", nc))[0]
        g_qkv = sum_rel([g_qkv[k] for k in range(ny * nx)], ("y", "x"), ny * nx).astype(BF)
        got = place(exchange_rel([g_qkv[k] for k in range(nline)], line, nline), line_at)
        got = got.reshape(nline, rows, 3, hcols).transpose(2, 1, 0, 3).reshape(3, rows, dm)
        g_query, g_key, g_value = got.astype(F32)

        def spread(vec, rank, count):
            return jnp.where(jnp.arange(count)[:, None] == rank, vec[None], 0.0)

        def ff_order(vec):
            v = spread(vec, quad_at, nquad).reshape(nx, nz, ny, nw, nc, ffb)
            return v.transpose(2, 0, 3, 1, 4, 5).reshape(ndev, ffb)

        vecs = jnp.concatenate(
            [
                spread(g_sqk, line_at, nline).reshape(ndev, -1),
                g_alpha_attn.reshape(ndev, -1),
                ff_order(g_s_up),
                ff_order(g_s_gate),
                g_alpha_mlp.reshape(ndev, -1),
            ],
            axis=1,
        )
        vecs = to_owner(vecs, F32)
        cuts = [rows, 2 * rows, 2 * rows + ffb, 2 * rows + 2 * ffb]
        g_sqk, g_alpha_attn, g_s_up, g_s_gate, g_alpha_mlp = jnp.split(vecs, cuts)
        return (
            hidden_out, tokens_grad, g_query, g_key, g_value, g_out, g_up, g_gate, g_down,
            g_sqk, g_alpha_attn, g_s_up, g_s_gate, g_alpha_mlp,
        )

    return body


VM = pl.BlockSpec(memory_space=pltpu.VMEM)
SM = pl.BlockSpec(memory_space=pltpu.SMEM)
HB = pl.BlockSpec(memory_space=pltpu.HBM)


def call(kernel, outs, args, hbm=(), hbm_out=(), scratch=(), flops=0, mib=60, after=()):
    moved = sum(math.prod(a.shape) * a.dtype.itemsize for a in args)
    moved += sum(math.prod(s) * jnp.dtype(d).itemsize for s, d in outs)
    count = len(args)

    def run(*refs):
        kernel(*refs[:count], *refs[count + len(after) :])

    specs = [SM] + [HB if i in hbm else VM for i in range(1, count)]
    specs += [pl.BlockSpec(memory_space=pl.ANY)] * len(after)
    return pl.pallas_call(
        run,
        out_shape=[jax.ShapeDtypeStruct(s, d) for s, d in outs],
        in_specs=specs,
        out_specs=[HB if i in hbm_out else VM for i in range(len(outs))],
        scratch_shapes=list(scratch),
        compiler_params=pltpu.CompilerParams(vmem_limit_bytes=mib << 20),
        cost_estimate=pl.CostEstimate(flops=flops, bytes_accessed=moved, transcendentals=0),
    )(*args, *after)


def row_norm(v):
    return lax.rsqrt(jnp.mean(v * v, axis=-1, keepdims=True) + EPS)


def sphere_back(dy, y, norm):
    return (dy - y * jnp.mean(dy * y, axis=-1, keepdims=True)) * norm


def make_kernels(sizes):
    ny, nx, nw, nz, nc = sizes
    ndev = ny * nx * nw * nz * nc
    nyx, nline = ny * nx, nw * nz
    ndpc = nyx * nc
    line, yx, dpc = ("w", "z"), ("y", "x"), ("y", "x", "c")

    def swap(value, axes, count, k):
        return lax.ppermute(value, axes, [(i, i ^ k) for i in range(count)])

    def exchange(chunks, axes, count):
        return [chunks[0]] + [swap(chunks[k], axes, count, k) for k in range(1, count)]

    def gather(value, axes, count):
        return exchange([value] * count, axes, count)

    def body(
        tokens, doc_ids, w_query, w_key, w_value, w_out, w_up, w_gate, w_down,
        s_qk, alpha_attn, s_up, s_gate, alpha_mlp, cotangent,
    ):
        nseq, seg, dm = tokens.shape
        rows = w_query.shape[0]
        ff = w_up.shape[1]
        ffq, ffb = ff // nline, ff // ndev
        sub = nc * ffb
        hc = dm // nline
        nheads = HEADS // nline
        nt = nline * 2 * seg
        tk = 2 * seg
        pad = 16
        ext = seg + pad
        scale = math.sqrt(HEAD_DIM)
        tile = 512

        at = [lax.axis_index(a) for a in "yxwzc"]
        ranks = jnp.stack(at + [lax.axis_index(yx), lax.axis_index(line)])
        ranks = ranks.astype(jnp.int32)

        def pack_tokens(rk, tok, docs, keep, send):
            c = rk[4]
            first = lax.broadcasted_iota(jnp.int32, (pad, dm), 0) == 0
            for out, which in ((keep, c), (send, 1 - c)):
                out[:seg] = tok[which]
                out[seg:] = jnp.where(first, docs[which], 0.0).astype(BF)

        def ff_cols(rk, k):
            runs = [(d * nline + (rk[6] ^ k)) * sub for d in range(nyx)]
            return [pl.ds(pl.multiple_of(run, 128), sub) for run in runs]

        def pack_qkv(rk, wq, wk, wv, *outs):
            for k in range(nline):
                cols = pl.ds(pl.multiple_of((rk[6] ^ k) * hc, 128), hc)
                for i, w in enumerate((wq, wk, wv)):
                    outs[k][:, i * hc : (i + 1) * hc] = w[:, cols].astype(BF)

        def pack_weights(rk, wu, wg, wo, gain, su, sg, *outs):
            for k in range(nline):
                out_ff = outs[k]
                for d, cols in enumerate(ff_cols(rk, k)):
                    for i, w in enumerate((wu, wg)):
                        here = i * ffq + d * sub
                        out_ff[:, here : here + sub] = w[:, cols].astype(BF)
                out_ff[:, 2 * ffq :] = wo[...].astype(BF)
            outs[nline][...] = gain[:, pl.ds(pl.multiple_of(rk[6] * hc, 128), hc)]
            for d, cols in enumerate(ff_cols(rk, 0)):
                here = slice(d * sub, (d + 1) * sub)
                outs[nline + 1][:, here] = su[:, cols]
                outs[nline + 2][:, here] = sg[:, cols]

        docs = jnp.pad(doc_ids.astype(F32), ((0, 0), (0, dm - seg))).reshape(nseq, 1, dm)
        packed = call(
            pack_qkv, [((rows, 3 * hc), BF)] * nline, (ranks, w_query, w_key, w_value)
        )
        keep, send = call(pack_tokens, [((ext, dm), BF)] * 2, (ranks, tokens, docs), after=(packed[0],))

        def join_tokens(rk, near, far, out):
            out[:seg] = near[:seg]
            out[seg:tk] = far[:seg]
            row = lax.broadcasted_iota(jnp.int32, (pad, dm), 0)
            ids = far[seg:].astype(F32)[:1]
            out[tk:] = jnp.where(row == 1, ids, near[seg:].astype(F32)).astype(BF)

        (mine,) = call(join_tokens, [((tk + pad, dm), BF)], (ranks, keep, swap(send, "c", nc, 1)))
        packed_ff = call(
            pack_weights,
            [((rows, 2 * ffq + dm), BF)] * nline
            + [((1, hc), F32)]
            + [((1, ffq), F32)] * 2,
            (ranks, w_up, w_gate, w_out, s_qk.reshape(1, dm))
            + (s_up.reshape(1, ff), s_gate.reshape(1, ff)),
            after=(keep,),
        )
        packed_ff, (my_gain, my_su, my_sg) = packed_ff[:nline], packed_ff[nline:]

        w_got = exchange(packed, line, nline)
        ff_got = exchange(packed_ff, line, nline)
        pieces = gather(mine, line, nline)

        def stack(rk, *refs):
            for k in range(nline):
                refs[nline][k * rows : (k + 1) * rows, :] = refs[k][...]

        (got,) = call(stack, [((ffb, 3 * hc), BF)], (ranks, *w_got))
        qkv_full = lax.all_gather(got, dpc, axis=0, tiled=True)

        def stack_ff(rk, *refs):
            parts, (wd, out) = refs[:nline], refs[nline:]
            for k in range(nline):
                out[k * rows : (k + 1) * rows, : 2 * ffq + dm] = parts[k][...]
            out[:, 2 * ffq + dm :] = wd[...].astype(BF)

        (got,) = call(
            stack_ff,
            [((ffb, 2 * ffq + 2 * dm), BF)],
            (ranks, *ff_got, w_down),
            after=(got, mine),
        )
        ff_full = lax.all_gather(got, dpc, axis=0, tiled=True)

        place = jnp.arange(nt, dtype=F32)[:, None]
        freq = 10000.0 ** (-jnp.arange(HEAD_DIM // 2, dtype=F32) / (HEAD_DIM // 2))
        angles = place * freq
        cosines, sines = jnp.cos(angles), jnp.sin(angles)
        reps = 128 // HEAD_DIM
        table = jnp.concatenate(
            [cosines] * (2 * reps) + [-sines, sines] * reps, axis=1
        )
        table_hi = table.astype(BF)
        table_lo = (table - table_hi.astype(F32)).astype(BF)

        def natural(rk, src, cols, dst, sems):
            copies = []
            for b in range(ndpc):
                for k in range(nline):
                    row = ((b // nc) * nline + (rk[6] ^ k)) * nc + b % nc
                    row = pl.ds(pl.multiple_of(row * rows, 32), rows)
                    block = src.at[pl.ds((b * nline + k) * rows, rows), cols]
                    copies.append(pltpu.make_async_copy(block, dst.at[row], sems.at[len(copies)]))
            return copies

        def heads_swap(v, low):
            width = v.shape[1]
            half = HEAD_DIM // 2
            return jnp.where(low, pltpu.roll(v, width - half, 1), pltpu.roll(v, half, 1))

        def low_half():
            lane = lax.broadcasted_iota(jnp.int32, (nt, hc), 1)
            return lane % HEAD_DIM < HEAD_DIM // 2

        def token_index(rk, axis, shape):
            t = lax.broadcasted_iota(jnp.int32, shape, axis)
            peer = (t // tk) ^ rk[6]
            core = ((t // seg) % 2) ^ rk[4]
            return (peer * 2 + core) * seg + t % seg

        def allowed_keys(rk, start):
            key = token_index(rk, 1, (1, nt))
            query = token_index(rk, 0, (nt, 1))
            return (key <= query) & (key.astype(F32) >= start)

        def attn_forward(rk, *refs):
            ext_refs, refs = refs[:nline], refs[nline:]
            stack, gain, t_hi, t_lo = refs[:4]
            att_ref, refs = refs[4], refs[5:]
            x_ref, w_ref, rq_ref, rk_ref, q_ref, k_ref, v_ref, bias_ref, cs_ref = refs[:9]
            full_ref, inv_ref, sems = refs[9:]
            copies = natural(rk, stack, pl.ds(0, 3 * hc), w_ref, sems)
            for copy in copies:
                copy.start()
            ids = []
            for k in range(nline):
                x_ref[k * tk : (k + 1) * tk, :] = ext_refs[k][:tk, :]
                tail = ext_refs[k][tk:, :128].astype(F32)
                ids += [tail[:1, :seg], tail[1:2, :seg]]
            ids = jnp.concatenate(ids, axis=1)
            same = lax.broadcasted_iota(jnp.int32, (nt, nt), 0) == lax.broadcasted_iota(
                jnp.int32, (nt, nt), 1
            )
            ids_col = jnp.sum(jnp.where(same, ids, 0.0), axis=1, keepdims=True)
            start = jnp.sum(jnp.where(ids < ids_col, 1.0, 0.0), axis=1, keepdims=True)
            pos = token_index(rk, 0, (nt, 1)) - start.astype(jnp.int32)
            hot = (lax.broadcasted_iota(jnp.int32, (nt, nt), 1) == pos).astype(F32).astype(BF)
            cs = dot(hot, t_hi[...]) + dot(hot, t_lo[...])
            cs_ref[...] = cs
            cos = jnp.concatenate([cs[:, :128]] * (hc // 128), axis=1)
            sin = jnp.concatenate([cs[:, 128:]] * (hc // 128), axis=1)
            bias_ref[...] = jnp.where(allowed_keys(rk, start), 0.0, NEG).astype(BF)
            for copy in copies:
                copy.wait()
            low = low_half()
            for i, (raw_ref, unit_ref) in enumerate(((rq_ref, q_ref), (rk_ref, k_ref))):
                pre = dot(x_ref[...], w_ref[:, i * hc : (i + 1) * hc])
                turned = pre * cos + heads_swap(pre, low) * sin
                raw_ref[...] = turned
                for h in range(nheads):
                    at_h = slice(h * HEAD_DIM, (h + 1) * HEAD_DIM)
                    part = turned[:, at_h]
                    norm = lax.rsqrt(jnp.sum(part * part, axis=1, keepdims=True) + EPS)
                    unit = (gain[:, at_h] * part * norm).astype(BF)
                    unit_ref[:, at_h] = unit * (scale if i == 0 else 1)
            v_ref[...] = dot(x_ref[...], w_ref[:, 2 * hc :]).astype(BF)
            for h in range(nheads):
                at_h = slice(h * HEAD_DIM, (h + 1) * HEAD_DIM)
                raw = jnp.exp(dot_t(q_ref[:, at_h], k_ref[:, at_h]) + bias_ref[...].astype(F32))
                inv = 1.0 / jnp.sum(raw, axis=1, keepdims=True)
                att_h = dot(raw.astype(BF), v_ref[:, at_h]) * inv
                full_ref[:, at_h] = att_h
                att_ref[:, at_h] = att_h.astype(BF)
                inv_ref[:, h : h + 1] = inv

        unit = ((nt, hc), BF)
        outs = call(
            attn_forward,
            [unit, ((nt, dm), BF), ((dm, 3 * hc), BF), ((nt, hc), F32), ((nt, hc), F32)]
            + [unit, unit, unit, ((nt, nt), BF), ((nt, 256), F32), ((nt, hc), F32), ((nt, 128), F32)],
            (ranks, *pieces, qkv_full, my_gain, table_hi, table_lo),
            hbm=(1 + nline,),
            scratch=[pltpu.SemaphoreType.DMA((ndev,))],
            flops=2 * nt * dm * 3 * hc + 4 * nt * nt * hc,
        )
        att, outs = outs[0], outs[1:]
        x_all, w_qkv, r_q, r_k, q_low, k_low, v_low, bias, cs, att_full, inv = outs
        att_got = gather(att, line, nline)

        def own_x(ext_ref):
            return ext_ref[:tk].astype(F32)

        alpha_a, alpha_m = alpha_attn.reshape(1, dm), alpha_mlp.reshape(1, dm)
        full = ((tk, dm), F32)

        def load_out(rk, stack, wo, sems):
            return natural(rk, stack, pl.ds(2 * ffq, dm), wo, sems)

        def load_ff(rk, stack, scratch):
            wug, wd, sems, sem_d = scratch
            down = stack.at[:, pl.ds(2 * ffq + dm, dm)]
            return (
                natural(rk, stack, pl.ds(0, 2 * ffq), wug, sems),
                [pltpu.make_async_copy(down, wd, sem_d.at[0])],
            )

        w_scratch = [pltpu.VMEM((dm, 2 * ffq), BF), pltpu.VMEM((ffq, dm), BF)]
        w_scratch += [pltpu.SemaphoreType.DMA((ndev,)), pltpu.SemaphoreType.DMA((1,))]
        out_scratch = [pltpu.VMEM((dm, dm), BF), pltpu.SemaphoreType.DMA((ndev,))]

        def gate_terms(gate, sg):
            v = sg * gate
            s = 1.0 / (1.0 + jnp.exp(-v))
            return v, s

        def forward(rk, *refs):
            att_refs, refs = refs[:nline], refs[nline:]
            x_ref, alpha, stack, su, sg = refs[:5]
            parts, refs = refs[5 : 5 + nline], refs[5 + nline :]
            h_all, up_ref, gate_ref, mixed_ref, one_ref, raw_ref = refs[:6]
            scratch = refs[6:]
            wug, wd = scratch[:2]
            w, a_ref = scratch[4], scratch[6]
            first, third = load_ff(rk, stack, scratch[:4])
            out_copies = load_out(rk, stack, w, scratch[5])
            for copy in out_copies + first + third:
                copy.start()
            for k in range(nline):
                spot = pl.ds(pl.multiple_of((rk[6] ^ k) * hc, hc), hc)
                for m in range(nline):
                    block = att_refs[k][(m ^ k) * tk : ((m ^ k) + 1) * tk, :]
                    a_ref[m * tk : (m + 1) * tk, spot] = block
            for copy in out_copies:
                copy.wait()
            for m in range(nline):
                total = dot(a_ref[m * tk : (m + 1) * tk, :], w[...])
                x = x_ref[m * tk : (m + 1) * tk, :].astype(F32)
                z = x + alpha[...] * (total * row_norm(total) - x)
                one = z * row_norm(z)
                h_all[m * tk : (m + 1) * tk, :] = one.astype(BF)
                if m == 0:
                    one_ref[...] = one
                    raw_ref[...] = total
            for copy in first:
                copy.wait()

            @pl.loop(0, ffq // tile, unroll=True)
            def _(j):
                cols = pl.ds(pl.multiple_of(j * tile, tile), tile)
                up = dot(h_all[...], wug[:, cols])
                gate = dot(h_all[...], wug[:, pl.ds(pl.multiple_of(ffq + j * tile, tile), tile)])
                up_ref[:, cols] = up.astype(BF)
                gate_ref[:, cols] = gate.astype(BF)
                v, s = gate_terms(gate, sg[:, cols])
                mixed_ref[:, cols] = (su[:, cols] * up * (v * s)).astype(BF)

            for copy in third:
                copy.wait()

            @pl.loop(0, dm // tile, unroll=True)
            def _(j):
                cols = pl.ds(pl.multiple_of(j * tile, tile), tile)
                part = dot(mixed_ref[...], wd[:, cols])
                for k in range(nline):
                    parts[k][:, cols] = part[k * tk : (k + 1) * tk].astype(parts[k].dtype)

        part_shapes = [((tk, dm), F32)] + [((tk, dm), BF)] * (nline - 1)
        outs = call(
            forward,
            part_shapes
            + [((nt, dm), BF), ((nt, ffq), BF), ((nt, ffq), BF), ((nt, ffq), BF), full, full],
            (ranks, *att_got, x_all, alpha_a, ff_full, my_su, my_sg),
            hbm=(3 + nline,),
            scratch=w_scratch + out_scratch + [pltpu.VMEM((nt, dm), BF)],
            flops=6 * nt * dm * ffq + 2 * nt * dm * dm,
        )
        mlp_parts, (h_all, up, gate, mixed, h_one, h_attn) = outs[:nline], outs[nline:]
        mlp_got = exchange(mlp_parts, line, nline)

        def split_rows(rk, cot, keep, send):
            keep[...] = cot[rk[4]]
            send[...] = cot[1 - rk[4]]

        half_low = ((seg, dm), BF)
        cot_keep, cot_send = call(split_rows, [half_low] * 2, (ranks, cotangent))
        cot_recv = swap(cot_send, "c", nc, 1)

        def mlp_update(rk, *refs):
            parts, refs = refs[:nline], refs[nline:]
            one_ref, alpha_ref, ck, cr, hid_keep, hid_send, dm_ref, direct, g_alpha = refs
            h = parts[0][...]
            for k in range(1, nline):
                h = h + parts[k][...].astype(F32)
            one, alpha = one_ref[...], alpha_ref[...]
            norm_h = row_norm(h)
            b = h * norm_h
            gap = b - one
            z = one + alpha * gap
            norm_z = row_norm(z)
            y = z * norm_z
            low = y.astype(BF)
            hid_keep[...] = low[:seg]
            hid_send[...] = low[seg:]
            dy = jnp.concatenate([ck[...], cr[...]], axis=0).astype(F32)
            dz = sphere_back(dy, y, norm_z)
            g_alpha[...] = jnp.sum(dz * gap, axis=0, keepdims=True)
            direct[...] = dz * (1.0 - alpha)
            dm_ref[...] = sphere_back(dz * alpha, b, norm_h).astype(BF)

        outs = call(
            mlp_update,
            [half_low, half_low, ((tk, dm), BF), full, ((1, dm), F32)],
            (ranks, *mlp_got, h_one, alpha_m, cot_keep, cot_recv),
        )
        hid_keep, hid_send, dm_low, d_one_direct, g_alpha_mlp = outs
        hid_recv = swap(hid_send, "c", nc, 1)
        dm_got = gather(dm_low, line, nline)

        def ff_back(rk, late, *refs):
            d_refs, stack = refs[:nline], refs[nline]
            su_ref, sg_ref, up_ref, gate_ref = refs[nline + 1 : nline + 5]
            refs = refs[nline + 5 :]
            parts, (d_all, dug, g_su, g_sg) = refs[:nline], refs[nline : nline + 4]
            scratch = refs[nline + 4 :]
            wug, wd = scratch[:2]
            first, third = load_ff(rk, stack, scratch)
            for copy in third + late[:2] + first + late[2:]:
                copy.start()
            for k in range(nline):
                d_all[k * tk : (k + 1) * tk, :] = d_refs[k][...]
            for copy in third + late[:2]:
                copy.wait()

            @pl.loop(0, ffq // tile)
            def _(j):
                cols = pl.ds(pl.multiple_of(j * tile, tile), tile)
                d_mixed = dot_t(d_all[...], wd[cols, :])
                up, gate = up_ref[:, cols].astype(F32), gate_ref[:, cols].astype(F32)
                su, sg = su_ref[:, cols], sg_ref[:, cols]
                v, s = gate_terms(gate, sg)
                silu = v * s
                dug[:, cols] = (d_mixed * su * silu).astype(BF)
                slope = d_mixed * su * up * (s * (1.0 + v * (1.0 - s)))
                other = pl.ds(pl.multiple_of(ffq + j * tile, tile), tile)
                dug[:, other] = (slope * sg).astype(BF)
                g_su[:, cols] = jnp.sum(d_mixed * up * silu, axis=0, keepdims=True)
                g_sg[:, cols] = jnp.sum(slope * gate, axis=0, keepdims=True)

            for copy in first:
                copy.wait()

            @pl.loop(0, dm // tile)
            def _(j):
                cols = pl.ds(pl.multiple_of(j * tile, tile), tile)
                part = dot_t(dug[...], wug[cols, :])
                for k in range(nline):
                    parts[k][:, cols] = part[k * tk : (k + 1) * tk].astype(parts[k].dtype)


        def stored(rk, g_ref, out, width, block, sems):
            d, peer, c = block // (nline * nc), (block // nc) % nline, block % nc
            spot = ((d * nc + c) * nline + (peer ^ rk[6])) * rows
            src = g_ref.at[pl.ds(pl.multiple_of(block * rows, 32), rows)]
            dst = out.at[pl.ds(pl.multiple_of(spot, 32), rows), pl.ds(0, width)]
            return pltpu.make_async_copy(src, dst, sems.at[block])

        def outer_ff(rk, h, dug, mixed_ref, d_all, out, g_ref, g_down_ref, sems, sem_d):
            def store(block):
                return stored(rk, g_ref, out, 2 * ffq, block, sems)

            @pl.loop(0, dm // tile, unroll=True)
            def _(j):
                cols = pl.ds(pl.multiple_of(j * tile, tile), tile)
                g_ref[cols, :] = tdot(h[:, cols], dug[...]).astype(BF)
                for i in range(tile // rows):
                    store(j * (tile // rows) + i).start()

            @pl.loop(0, ffq // tile, unroll=True)
            def _(j):
                cols = pl.ds(pl.multiple_of(j * tile, tile), tile)
                g_down_ref[cols, :] = tdot(mixed_ref[:, cols], d_all[...]).astype(BF)

            down = pltpu.make_async_copy(g_down_ref, out.at[:, pl.ds(2 * ffq, dm)], sem_d.at[0])
            down.start()
            down.wait()

            @pl.loop(0, ndev)
            def _(block):
                store(block).wait()

        def ff_back_all(rk, *refs):
            ins, refs = list(refs[: nline + 7]), refs[nline + 7 :]
            parts, (g_su, g_sg, out) = refs[:nline], refs[nline : nline + 3]
            d_all, dug, wug, wd, s_u, s_d, g_ref, g_down_ref, sems, sem_d = refs[nline + 3 : nline + 13]
            *held, late_sems = refs[nline + 13 :]
            late = []
            for i, dst in enumerate(held):
                late.append(pltpu.make_async_copy(ins[nline + 3 + i], dst, late_sems.at[i]))
            ins[nline + 3 :] = held
            scratch = (d_all, dug, g_su, g_sg, wug, wd, s_u, s_d)
            ff_back(rk, late, *ins[: nline + 5], *parts, *scratch)
            h, mixed_ref = ins[nline + 5 :]
            for copy in late[2:]:
                copy.wait()
            outer_ff(rk, h, dug, mixed_ref, d_all, out, g_ref, g_down_ref, sems, sem_d)

        *one_parts, g_su, g_sg, g_ff = call(
            ff_back_all,
            part_shapes + [((1, ffq), F32)] * 2 + [((dm, 2 * ffq + dm), BF)],
            (ranks, *dm_got, ff_full, my_su, my_sg, up, gate, h_all, mixed),
            hbm=(1 + nline, 4 + nline, 5 + nline, 6 + nline, 7 + nline),
            hbm_out=(nline + 2,),
            scratch=[pltpu.VMEM((nt, dm), BF), pltpu.VMEM((nt, 2 * ffq), BF)]
            + w_scratch
            + [pltpu.VMEM((dm, 2 * ffq), BF), pltpu.VMEM((ffq, dm), BF)]
            + [pltpu.SemaphoreType.DMA((ndev,)), pltpu.SemaphoreType.DMA((1,))]
            + [pltpu.VMEM((nt, ffq), BF)] * 2
            + [pltpu.VMEM((nt, dm), BF), pltpu.VMEM((nt, ffq), BF)]
            + [pltpu.SemaphoreType.DMA((4,))],
            flops=12 * nt * dm * ffq,
        )
        one_got = exchange(one_parts, line, nline)
        g_ff = lax.psum_scatter(g_ff, dpc, scatter_dimension=0, tiled=True)
        def attn_update_back(rk, *refs):
            parts, refs = refs[:nline], refs[nline:]
            direct_in, one_ref, raw_ref, ext_ref, alpha_ref, stack = refs[:6]
            d_outs, (dh_ref, direct, g_alpha, w, sems) = refs[6 : 6 + nline], refs[6 + nline :]
            copies = load_out(rk, stack, w, sems)
            for copy in copies:
                copy.start()
            d = direct_in[...] + parts[0][...]
            for k in range(1, nline):
                d = d + parts[k][...].astype(F32)
            one, raw, alpha = one_ref[...], raw_ref[...], alpha_ref[...]
            x = own_x(ext_ref)
            norm_raw = row_norm(raw)
            b = raw * norm_raw
            gap = b - x
            norm_z = row_norm(x + alpha * gap)
            dz = sphere_back(d, one, norm_z)
            g_alpha[...] = jnp.sum(dz * gap, axis=0, keepdims=True)
            direct[...] = dz * (1.0 - alpha)
            dh_ref[...] = sphere_back(dz * alpha, b, norm_raw).astype(BF)
            for copy in copies:
                copy.wait()
            for k in range(nline):
                w_k = w[pl.ds(pl.multiple_of((rk[6] ^ k) * hc, hc), hc), :]
                d_outs[k][...] = dot_t(dh_ref[...], w_k).astype(BF)

        outs = call(
            attn_update_back,
            [((tk, hc), BF)] * nline + [((tk, dm), BF), full, ((1, dm), F32)],
            (ranks, *one_got, d_one_direct, h_one, h_attn, mine, alpha_a, ff_full),
            hbm=(6 + nline,),
            scratch=out_scratch,
            flops=2 * tk * dm * dm,
        )
        d_att_parts, (dh_low, d_x_direct, g_alpha_attn) = outs[:nline], outs[nline:]
        d_att = exchange(d_att_parts, line, nline)

        def outer_out(rk, dh, *refs):
            parts, outs, (g_ref, sems) = refs[:nline], refs[nline : nline + 2], refs[nline + 2 :]
            for k in range(nline):
                spot = pl.ds(pl.multiple_of((rk[6] ^ k) * hc, hc), hc)
                own = parts[k][k * tk : (k + 1) * tk, :]
                g_ref[spot, :] = tdot(own, dh[...]).astype(BF)
            copies = []
            for cr in range(nc):
                for a in range(nyx):
                    for b in range(nline):
                        row = ((rk[5] ^ a) * nline + (rk[6] ^ b)) * nc + (rk[4] ^ cr)
                        src = g_ref.at[pl.ds(pl.multiple_of(row * rows, 32), rows)]
                        dst = outs[cr].at[pl.ds((a * nline + b) * rows, rows)]
                        copies.append(pltpu.make_async_copy(src, dst, sems.at[len(copies)]))
            for copy in copies:
                copy.start()
            for copy in copies:
                copy.wait()

        keep, send = call(
            outer_out,
            [((dm // nc, dm), BF)] * nc,
            (ranks, dh_low, *att_got),
            hbm_out=(0, 1),
            scratch=[pltpu.VMEM((dm, dm), BF), pltpu.SemaphoreType.DMA((ndev,))],
            flops=2 * tk * dm * dm,
        )

        def attn_back(rk, late, *refs):
            d_refs, refs = refs[:nline], refs[nline:]
            w_ref, rq_ref, rk_ref, q_ref, k_ref, v_ref, bias_ref, cs_ref, gain = refs[:9]
            full_ref, inv_ref, refs = refs[9], refs[10], refs[11:]
            parts, (d_ref, g_gain, do_ref, dq_ref, dk_ref) = refs[:nline], refs[nline:]
            for k in range(nline):
                do_ref[k * tk : (k + 1) * tk, :] = d_refs[k][...]
            for h in range(nheads):
                at_h = slice(h * HEAD_DIM, (h + 1) * HEAD_DIM)
                q, key, do = q_ref[:, at_h], k_ref[:, at_h], do_ref[:, at_h]
                raw = jnp.exp(dot_t(q, key) + bias_ref[...].astype(F32))
                p = raw * inv_ref[:, h : h + 1]
                delta = jnp.sum(do.astype(F32) * full_ref[:, at_h], axis=1, keepdims=True)
                ds = (p * (dot_t(do, v_ref[:, at_h]) - delta)).astype(BF)
                p = p.astype(BF)
                at_v = slice(2 * hc + h * HEAD_DIM, 2 * hc + (h + 1) * HEAD_DIM)
                d_ref[:, at_v] = tdot(p, do).astype(BF)
                dq_ref[:, at_h] = scale * dot(ds, key)
                dk_ref[:, at_h] = tdot(ds, q)
            for copy in late:
                copy.wait()
            cs = cs_ref[...]
            cos = jnp.concatenate([cs[:, :128]] * (hc // 128), axis=1)
            sin = jnp.concatenate([cs[:, 128:]] * (hc // 128), axis=1)
            low = low_half()
            for i, (raw_ref, g_ref) in enumerate(((rq_ref, dq_ref), (rk_ref, dk_ref))):
                for h in range(nheads):
                    at_h = slice(h * HEAD_DIM, (h + 1) * HEAD_DIM)
                    turned, g = raw_ref[:, at_h], g_ref[:, at_h]
                    norm = lax.rsqrt(jnp.sum(turned * turned, axis=1, keepdims=True) + EPS)
                    unit = turned * norm
                    term = jnp.sum(g * unit, axis=0, keepdims=True)
                    g_gain[:, at_h] = term if i == 0 else g_gain[:, at_h] + term
                    g = g * gain[:, at_h]
                    g_ref[:, at_h] = norm * (g - unit * jnp.sum(unit * g, axis=1, keepdims=True))
                g = g_ref[...]
                d_ref[:, i * hc : (i + 1) * hc] = (g * cos - heads_swap(g, low) * sin).astype(BF)

            @pl.loop(0, dm // tile)
            def _(j):
                cols = pl.ds(pl.multiple_of(j * tile, tile), tile)
                part = dot_t(d_ref[...], w_ref[cols, :])
                for k in range(nline):
                    parts[k][:, cols] = part[k * tk : (k + 1) * tk].astype(parts[k].dtype)


        at_line = ranks[6]
        mine_ff = (jnp.arange(nline) == at_line)[None, :, None, None]

        def ff_owner(vec):
            return jnp.where(mine_ff, vec.reshape(nyx, 1, nc, ffb), 0.0).reshape(ndev, ffb)

        misc = [v.reshape(ndev, rows) for v in (g_alpha_attn, g_alpha_mlp)]
        misc = jnp.pad(jnp.concatenate(misc, axis=1), ((0, 0), (0, ffb - 2 * rows)))
        vecs = jnp.stack([ff_owner(g_su), ff_owner(g_sg), misc], axis=1).astype(BF)
        vecs = jnp.pad(vecs, ((0, 0), (0, rows - 3), (0, 0))).reshape(dm, ffb)

        wide = 3 * hc + ffb

        def core_add(rk, a, b, *outs):
            for i in range(nyx):
                here = slice(i * ffb, (i + 1) * ffb)
                outs[i][...] = (a[here, :].astype(F32) + b[here, :].astype(F32)).astype(BF)

        out_sum = call(
            core_add, [((ffb, dm), BF)] * nyx, (ranks, keep, swap(send, "c", nc, 1))
        )
        out_got = exchange(out_sum, yx, nyx)

        def outer_last(rk, x_ref, d_ref, vec_ref, g_gain, out, g_ref, sems):

            def store(block):
                return stored(rk, g_ref, out, wide, block, sems)

            g_ref[:, 3 * hc : wide] = vec_ref[...]
            third = lax.broadcasted_iota(jnp.int32, (16, ffb), 0) == 2
            for i in range(hc // rows):
                spot = pl.ds(pl.multiple_of((rk[6] * (hc // rows) + i) * rows, 32), 16)
                run = [jnp.zeros((1, 2 * rows), F32), g_gain[:, i * rows : (i + 1) * rows]]
                run = jnp.concatenate(run + [jnp.zeros((1, ffb - 3 * rows), F32)], axis=1)
                held = g_ref[spot, 3 * hc : wide].astype(F32)
                g_ref[spot, 3 * hc : wide] = (held + jnp.where(third, run, 0.0)).astype(BF)

            @pl.loop(0, dm // tile)
            def _(j):
                cols = pl.ds(pl.multiple_of(j * tile, tile), tile)
                g_ref[cols, : 3 * hc] = tdot(x_ref[:, cols], d_ref[...]).astype(BF)
                for i in range(tile // rows):
                    store(j * (tile // rows) + i).start()

            @pl.loop(0, ndev)
            def _(block):
                store(block).wait()

        def attn_back_all(rk, *refs):
            ins, refs = list(refs[: nline + 13]), refs[nline + 13 :]
            parts, out = refs[:nline], refs[nline]
            d_ref, g_gain, do_ref, dq_ref, dk_ref, g_ref, sems = refs[nline + 1 : nline + 8]
            *held, late_sems = refs[nline + 8 :]
            late = []
            for i, (at_in, dst) in enumerate(zip(late_back, held)):
                late.append(pltpu.make_async_copy(ins[at_in - 1], dst, late_sems.at[i]))
                ins[at_in - 1] = dst
            for copy in late:
                copy.start()
            x_ref, vec_ref = ins[nline + 11 :]
            scratch = (d_ref, g_gain, do_ref, dq_ref, dk_ref)
            attn_back(rk, late, *ins[: nline + 11], *parts, *scratch)
            outer_last(rk, x_ref, d_ref, vec_ref, g_gain, out, g_ref, sems)

        late_back = [1 + nline, 2 + nline, 3 + nline, 8 + nline, 12 + nline]
        late_shapes = [((dm, 3 * hc), BF), ((nt, hc), F32), ((nt, hc), F32), ((nt, 256), F32)]
        late_shapes.append(((nt, dm), BF))

        *x_parts, g_last = call(
            attn_back_all,
            part_shapes + [((dm, wide), BF)],
            (ranks, *d_att, w_qkv, r_q, r_k, q_low, k_low, v_low, bias, cs, my_gain, att_full, inv)
            + (x_all, vecs),
            hbm=late_back,
            hbm_out=(nline,),
            after=(keep,),
            scratch=[
                pltpu.VMEM((nt, 3 * hc), BF), pltpu.VMEM((1, hc), F32),
                pltpu.VMEM((nt, hc), BF), pltpu.VMEM((nt, hc), F32), pltpu.VMEM((nt, hc), F32),
                pltpu.VMEM((dm, wide), BF), pltpu.SemaphoreType.DMA((ndev,)),
                *[pltpu.VMEM(*shape) for shape in late_shapes], pltpu.SemaphoreType.DMA((5,)),
            ],
            flops=4 * nt * dm * 3 * hc + 10 * nt * nt * hc,
        )
        x_got = exchange(x_parts, line, nline)


        g_last = lax.psum_scatter(g_last, dpc, scatter_dimension=0, tiled=True)

        def split_ff(rk, *refs):
            parts, (g_ref, down), outs = refs[:nyx], refs[nyx : nyx + 2], refs[nyx + 2 :]
            down[...] = g_ref[:, 2 * ffq :].astype(F32)
            for k in range(nline):
                here = slice(k * rows, (k + 1) * rows)
                outs[k][:, : 2 * ffq] = g_ref[here, : 2 * ffq]
                total = parts[0][here, :].astype(F32)
                for j in range(1, nyx):
                    total = total + parts[j][here, :].astype(F32)
                outs[k][:, 2 * ffq :] = total.astype(BF)

        g_down, *g_parts = call(
            split_ff,
            [((ffb, dm), F32)] + [((rows, 2 * ffq + dm), BF)] * nline,
            (ranks, *out_got, g_ff),
            after=tuple(x_got[1:]),
        )
        g_parts = exchange(g_parts, line, nline)

        def place_ff(rk, *refs):
            parts, outs, g_o = refs[:nline], refs[nline : nline + 2], refs[nline + 2]
            total = parts[0][:, 2 * ffq :].astype(F32)
            for k in range(nline):
                for d, cols in enumerate(ff_cols(rk, k)):
                    for i in range(2):
                        here = i * ffq + d * sub
                        outs[i][:, cols] = parts[k][:, here : here + sub].astype(F32)
                if k:
                    total = total + parts[k][:, 2 * ffq :].astype(F32)
            g_o[...] = total

        g_up, g_gate, g_out = call(
            place_ff, [((rows, ff), F32)] * 2 + [((rows, dm), F32)], (ranks, *g_parts)
        )

        def finish_tokens(rk, *refs):
            parts, (direct, keep, send) = refs[:nline], refs[nline:]
            d = direct[...] + parts[0][...]
            for k in range(1, nline):
                d = d + parts[k][...].astype(F32)
            keep[...] = d[:seg]
            send[...] = d[seg:].astype(BF)

        x_keep, x_send = call(
            finish_tokens, [((seg, dm), F32), half_low], (ranks, *x_got, d_x_direct)
        )
        x_recv = swap(x_send, "c", nc, 1)

        def join_rows(rk, keep, recv, out):
            out[rk[4]] = keep[...].astype(out.dtype)
            out[1 - rk[4]] = recv[...].astype(out.dtype)

        (tokens_grad,) = call(join_rows, [((nseq, seg, dm), F32)], (ranks, x_keep, x_recv))
        (hidden_out,) = call(join_rows, [((nseq, seg, dm), BF)], (ranks, hid_keep, hid_recv))

        def split_last(rk, g_ref, *outs):
            for k in range(nline):
                outs[k][...] = g_ref[k * rows : (k + 1) * rows, :]

        last = call(
            split_last,
            [((rows, wide), BF)] * nline,
            (ranks, g_last),
            after=(tokens_grad, hidden_out, g_parts[1]),
        )
        last = exchange(last, line, nline)

        def place_last(rk, *refs):
            parts, outs, vec_outs = refs[:nline], refs[nline : nline + 3], refs[nline + 3 :]
            v_sum = None
            for k in range(nline):
                cols = pl.ds(pl.multiple_of((rk[6] ^ k) * hc, 128), hc)
                for i in range(3):
                    outs[i][:, cols] = parts[k][:, i * hc : (i + 1) * hc].astype(F32)
                vec = parts[k][:16, 3 * hc : wide].astype(F32)
                v_sum = vec if v_sum is None else v_sum + vec
            vec_outs[0][...] = v_sum[:1]
            vec_outs[1][...] = v_sum[1:2]
            for i in range(3):
                vec_outs[2 + i][...] = v_sum[2:3, i * rows : (i + 1) * rows]

        g_query, g_key, g_value, *vecs = call(
            place_last,
            [((rows, dm), F32)] * 3
            + [((1, ffb), F32)] * 2
            + [((1, rows), F32)] * 3,
            (ranks, *last),
        )
        g_s_up, g_s_gate, g_aa, g_am, g_sqk = [v.reshape(-1) for v in vecs]
        return (
            hidden_out, tokens_grad, g_query, g_key, g_value, g_out, g_up, g_gate, g_down,
            g_sqk, g_aa, g_s_up, g_s_gate, g_am,
        )

    return body


def make_body(sizes):
    plain, kernels = make_plain(sizes), make_kernels(sizes)
    ndev = math.prod(sizes)
    nline = sizes[2] * sizes[3]

    def body(*args):
        tokens, w_query, w_up = args[0], args[2], args[6]
        fits = w_query.shape[0] % 32 == 0 and (w_up.shape[1] // ndev) % 128 == 0
        fits = fits and (tokens.shape[2] // nline) % 256 == 0 and tokens.shape[1] == 64
        return (kernels if fits else plain)(*args)

    return body


def solution(mesh):
    ndp, nblk = mesh.shape["dp"], mesh.shape["blk"]
    sizes = (ndp // 2, 2, nblk // 4, 2, 2)
    fine = Mesh(mesh.devices.reshape(sizes), ("y", "x", "w", "z", "c"))
    rows, cols = ("y", "x"), ("w", "z", "c")
    flat = rows + cols
    seq = P(rows, cols, None)
    weight = P(flat, None)
    return jax.shard_map(
        make_body(sizes),
        mesh=fine,
        in_specs=(seq, P(rows, cols)) + (weight,) * 7 + (P(),) * 5 + (seq,),
        out_specs=(seq, seq) + (weight,) * 7 + (P(flat),) * 5,
        check_vma=False,
    )
```
